32 devices in a mesh: dp: 8 (over z, y), fsdp: 4 (over x, core).
Axes of the slice: x: 2, y: 2, z: 4, core: 2. Of those that a mesh axis runs over, the one named last changes fastest.
Arguments:
- tokens: bfloat16 [32768, 768], P(('dp', 'fsdp')), may hold values from -6 to 6
- lengths: int32 [32, 5], P(('dp', 'fsdp')), may hold values from 0 to 768, as said below
- ln1_gain: bfloat16 [768], P(('dp', 'fsdp')), may hold values from 0.099609375 to 1.8984375
- ln1_bias: bfloat16 [768], P(('dp', 'fsdp')), may hold values from -4 to 4
- w_qkv: bfloat16 [768, 2304], P(('dp', 'fsdp')), may hold values from -0.21875 to 0.21875
- qv_bias: bfloat16 [1536], P(('dp', 'fsdp')), may hold values from -4 to 4
- w_proj: bfloat16 [768, 768], P(('dp', 'fsdp')), may hold values from -6 to 6
- proj_bias: bfloat16 [768], P(('dp', 'fsdp')), may hold values from -6 to 6
- ln2_gain: bfloat16 [768], P(('dp', 'fsdp')), may hold values from 0.099609375 to 1.8984375
- ln2_bias: bfloat16 [768], P(('dp', 'fsdp')), may hold values from -4 to 4
- w_fc: bfloat16 [768, 3072], P(('dp', 'fsdp')), may hold values from -0.21875 to 0.21875
- fc_bias: bfloat16 [3072], P(('dp', 'fsdp')), may hold values from -6 to 6
- w_out: bfloat16 [3072, 768], P(('dp', 'fsdp')), may hold values from -3 to 3
- out_bias: bfloat16 [768], P(('dp', 'fsdp')), may hold values from -6 to 6
- cotangent: bfloat16 [32768, 768], P(('dp', 'fsdp')), may hold values from -6 to 6
Outputs:
- block_out: bfloat16 [32768, 768], P(('dp', 'fsdp'))
- grad_tokens: bfloat16 [32768, 768], P(('dp', 'fsdp'))
- grad_ln1_gain: float32 [768], P(('dp', 'fsdp'))
- grad_ln1_bias: float32 [768], P(('dp', 'fsdp'))
- grad_w_qkv: float32 [768, 2304], P(('dp', 'fsdp'))
- grad_qv_bias: float32 [1536], P(('dp', 'fsdp'))
- grad_w_proj: float32 [768, 768], P(('dp', 'fsdp'))
- grad_proj_bias: float32 [768], P(('dp', 'fsdp'))
- grad_ln2_gain: float32 [768], P(('dp', 'fsdp'))
- grad_ln2_bias: float32 [768], P(('dp', 'fsdp'))
- grad_w_fc: float32 [768, 3072], P(('dp', 'fsdp'))
- grad_fc_bias: float32 [3072], P(('dp', 'fsdp'))
- grad_w_out: float32 [3072, 768], P(('dp', 'fsdp'))
- grad_out_bias: float32 [768], P(('dp', 'fsdp'))
The draws below stay inside these ranges and needn't reach their ends.
Inputs may be any that keep to these rules, and one draw needn't show every extreme that they name: Row r lists, in order, the lengths of the 4 sequences of pack r, each 64 or more, and, last, the number of pad rows after them, below 64; each row sums to 1024, and in every row one sequence has exactly 768 rows.
All inputs are finite; a program needn't handle non-finite values.
Results may differ from the reference program's by a relative error of at most 0.012.
Values may be sent and summed in bfloat16 or wider, within the bound.
No kernel may reach another device: no remote copies, remote signals or barrier semaphores. Data moves between devices by JAX's collectives and lax.ppermute only.
A program may use at most 256 MiB of HBM per device.

```python
import math
import jax
import jax.numpy as jnp
from jax import lax

D = 768
H = 12
HD = 64
FF = 3072
TOK_DEV = 1024
SEQS = 4
MINLEN = 64
PADMAX = 64
MAXLEN = 768
TOKENS = 32768
N_DP = 8
N_FSDP = 4


def draw_lengths(key, part):
    key = jax.random.fold_in(key, 11)
    packs = N_DP * N_FSDP
    others_count = SEQS - 1
    pad_key = jax.random.fold_in(key, 1)
    empty_key = jax.random.fold_in(key, 2)
    cut_key = jax.random.fold_in(key, 3)
    slot_key = jax.random.fold_in(key, 4)
    pad_rows = jax.random.randint(pad_key, (packs,), 0, PADMAX).astype(jnp.int32)
    empty_pack = jax.random.randint(empty_key, (), 0, packs).astype(jnp.int32)
    pad_rows = jnp.where(jnp.arange(packs, dtype=jnp.int32) == empty_pack, 0, pad_rows).astype(jnp.int32)
    spare = (TOK_DEV - MAXLEN - others_count * MINLEN - pad_rows).astype(jnp.int32)
    raw_cuts = jax.random.randint(cut_key, (packs, others_count - 1), 0, 1 << 20).astype(jnp.int32)
    cuts = jnp.sort(raw_cuts % (spare[:, None] + 1), axis=1).astype(jnp.int32)
    bounds = jnp.concatenate([jnp.zeros((packs, 1), jnp.int32), cuts, spare[:, None]], axis=1)
    others = (bounds[:, 1:] - bounds[:, :-1] + MINLEN).astype(jnp.int32)
    long_slot = jax.random.randint(slot_key, (packs, 1), 0, SEQS).astype(jnp.int32)
    slot = jnp.arange(SEQS, dtype=jnp.int32)[None, :]
    source = jnp.clip(jnp.where(slot < long_slot, slot, slot - 1), 0, others_count - 1).astype(jnp.int32)
    picked = jnp.take_along_axis(others, jnp.broadcast_to(source, (packs, SEQS)), axis=1)
    sequences = jnp.where(slot == long_slot, MAXLEN, picked).astype(jnp.int32)
    return jnp.concatenate([sequences, pad_rows[:, None]], axis=1).astype(jnp.int32)


def strengthened(array, stream_key, source, target, blocks, factor):
    owner, partner = [(jnp.arange(array.shape[axis_at]) // (array.shape[axis_at] // blocks)).reshape([-1 if axis == axis_at else 1 for axis in range(array.ndim)]) for axis_at in (source, target)]
    chosen = jax.random.permutation(stream_key, blocks)[partner]
    strong = (owner == chosen) | (owner == (partner + blocks // 2) % blocks)
    return jnp.where(strong, factor * array, array)


def level_of(own_key, dims, pieces, smallest, top_value):
    def one(axis_at, parts):
        draws = jax.random.uniform(jax.random.fold_in(jax.random.fold_in(own_key, 6), axis_at), (parts,), jnp.float32, smallest / len(pieces), top_value / len(pieces))
        return jnp.repeat(jnp.exp(draws), dims[axis_at] // parts).reshape((-1,) + (1,) * (len(dims) - axis_at - 1))

    factor_of = one(*pieces[0])
    for cut in pieces[1:]:
        factor_of = factor_of * one(*cut)
    return factor_of


def gaussian(key, extent, scale, limit, cuts=(), kind=jnp.bfloat16):
    array = jax.random.normal(key, extent, jnp.float32) * scale
    if len(cuts) > 0:
        array = level_of(key, extent, cuts, -0.22, 0.18) * array
    return jnp.clip(array, min=-limit, max=limit).astype(kind)


def gaussian_with(stream_key, dims, width, most, cuts, heavy, kind=jnp.bfloat16):
    drawn = width * jax.random.normal(stream_key, dims, jnp.float32)
    if cuts:
        drawn = drawn * level_of(stream_key, dims, cuts, -0.22, 0.18)
    return jnp.clip(strengthened(drawn, jax.random.fold_in(stream_key, 3), *heavy), -most, most).astype(kind)


def setup_inputs(seed: int = 0) -> dict:
    seeds = jax.random.split(jax.random.key(seed), 16)
    return {
        "tokens": gaussian_with(seeds[0], (TOKENS, D), 1.0, 6.0, ((0, 32),), (0, 1, 32, 2.75)),
        "lengths": draw_lengths(jax.random.fold_in(seeds[15], 71), 0),
        "ln1_gain": jnp.clip(1.0 + 0.18 * jax.random.normal(seeds[2], (D,), jnp.float32), 0.099609375, 1.8984375).astype(jnp.bfloat16),
        "ln1_bias": gaussian(seeds[3], (D,), 0.3, 4.0, ((0, 32),)),
        "w_qkv": gaussian(seeds[4], (D, 3 * D), D ** -0.5, 0.21875, ((0, 32),)),
        "qv_bias": gaussian(seeds[5], (2 * D,), 0.3, 4.0, ((0, 32),)),
        "w_proj": gaussian(seeds[6], (D, D), 1.0, 6.0, ((0, 32),)),
        "proj_bias": gaussian(seeds[7], (D,), 2.0, 6.0, ((0, 32),)),
        "ln2_gain": jnp.clip(1.0 + 0.18 * jax.random.normal(seeds[8], (D,), jnp.float32), 0.099609375, 1.8984375).astype(jnp.bfloat16),
        "ln2_bias": gaussian(seeds[9], (D,), 0.3, 4.0, ((0, 32),)),
        "w_fc": gaussian(seeds[10], (D, FF), D ** -0.5, 0.21875, ((0, 32),)),
        "fc_bias": gaussian(seeds[11], (FF,), 0.5, 6.0, ((0, 32),)),
        "w_out": gaussian(seeds[12], (FF, D), 0.2, 3.0, ((0, 32),)),
        "out_bias": gaussian(seeds[13], (D,), 2.0, 6.0, ((0, 32),)),
        "cotangent": gaussian(seeds[14], (TOKENS, D), 1.0, 6.0, ((0, 32),)),
    }


@jax.custom_vjp
def low(v):
    return lax.optimization_barrier(v.astype(jnp.bfloat16)).astype(jnp.float32)

@jax.custom_vjp
def low_back(v):
    return v

def low_keep(v):
    return (low(v), None)

def low_pass(kept, grad):
    return (grad,)

def back_keep(v):
    return (v, None)

def back_low(kept, grad):
    return (low(grad),)
low.defvjp(low_keep, low_pass)
low_back.defvjp(back_keep, back_low)
epsilon = 1e-05
branch_scale = 1.0 / math.sqrt(48.0)
highest = lax.Precision.HIGHEST
masked_score = -1e+30

def layer_norm(values, gain, bias):
    centred = values - lax.optimization_barrier(jnp.mean(values, axis=-1, keepdims=True))
    variance = lax.optimization_barrier(jnp.mean(centred * centred, axis=-1, keepdims=True))
    return centred * lax.rsqrt(variance + epsilon) * gain + bias

def pack_layout(counts, row_count):
    seq_ends = jnp.cumsum(counts).astype(jnp.int32)
    position = jnp.arange(row_count, dtype=jnp.int32)
    segment = lax.optimization_barrier(jnp.sum((position[:, None] >= seq_ends[None, :]).astype(jnp.int32), axis=1)).astype(jnp.int32)
    row_valid = segment < counts.shape[0] - 1
    return (position, segment, row_valid)

def permitted(position, segment, row_valid, first_row, block_rows):
    query_pos = lax.dynamic_slice_in_dim(position, first_row, block_rows)
    query_seg = lax.dynamic_slice_in_dim(segment, first_row, block_rows)
    same_seq = (query_seg[:, None] == segment[None, :]) & (query_pos[:, None] >= position[None, :]) & row_valid[None, :]
    return same_seq | (query_pos[:, None] == position[None, :])

def matmul(left_side, right_side):
    return jnp.dot(left_side, right_side, precision=highest, preferred_element_type=jnp.float32)

def residual_block(inputs, counts, params):
    gain_one, bias_one, w_qkv, qv_bias, w_proj, proj_bias, gain_two, bias_two, w_fc, fc_bias, w_out, out_bias = params
    row_count = inputs.shape[0]
    position, segment, row_valid = pack_layout(counts, row_count)
    allowed = permitted(position, segment, row_valid, 0, row_count)
    normed = low(layer_norm(inputs, gain_one, bias_one))
    qkv_bias = jnp.concatenate([qv_bias[:D], jnp.zeros_like(qv_bias[:D]), qv_bias[D:]])
    joined = low(low_back(matmul(normed, w_qkv) + qkv_bias))
    queries = joined[:, :D].reshape(row_count, H, HD)
    key_heads = joined[:, D:2 * D].reshape(row_count, H, HD)
    value_heads = joined[:, 2 * D:].reshape(row_count, H, HD)
    scores = jnp.einsum('qhd,khd->hqk', queries, key_heads, precision=highest) * HD ** (-0.5)
    scores = low_back(jnp.where(allowed[None], scores, masked_score))
    weights = low(jax.nn.softmax(scores, axis=-1))
    attended = jnp.einsum('hqk,khd->qhd', weights, value_heads, precision=highest).reshape(row_count, D)
    attended = low(low_back(attended))
    branch = low_back(matmul(attended, w_proj) + proj_bias)
    middle = inputs + branch_scale * branch
    normed_two = low(layer_norm(middle, gain_two, bias_two))
    pre_act = low_back(matmul(normed_two, w_fc) + fc_bias)
    activated = low(jax.nn.gelu(pre_act, approximate=True))
    mlp_out = low_back(matmul(activated, w_out) + out_bias)
    return middle + branch_scale * mlp_out

def reference(tokens, lengths, ln1_gain, ln1_bias, w_qkv, qv_bias, w_proj, proj_bias, ln2_gain, ln2_bias, w_fc, fc_bias, w_out, out_bias, cotangent):
    packs = N_DP * N_FSDP
    params = tuple((entry.astype(jnp.float32) for entry in (ln1_gain, ln1_bias, w_qkv, qv_bias, w_proj, proj_bias, ln2_gain, ln2_bias, w_fc, fc_bias, w_out, out_bias)))
    inputs = tokens.astype(jnp.float32).reshape(packs, TOK_DEV, D)

    def forward(packed, *weight_list):

        def one_pack(state_in, pack_item):
            return (state_in, jax.checkpoint(residual_block)(pack_item[0], pack_item[1], weight_list))
        return lax.scan(one_pack, None, (packed, lengths))[1]
    outputs, pull_back = jax.vjp(forward, inputs, *params)

    def valid_rows(counts):
        return pack_layout(counts, TOK_DEV)[2]
    row_valid = jax.vmap(valid_rows)(lengths)
    seed_grad = cotangent.astype(jnp.float32).reshape(packs, TOK_DEV, D) * row_valid[:, :, None].astype(jnp.float32)
    gradients = pull_back(seed_grad)
    return (outputs.reshape(TOKENS, D).astype(jnp.bfloat16), gradients[0].reshape(TOKENS, D).astype(jnp.bfloat16), gradients[1], gradients[2], gradients[3], gradients[4], gradients[5], gradients[6], gradients[7], gradients[8], gradients[9], gradients[10], gradients[11], gradients[12])
```

```python
import functools
import math

import jax
import jax.numpy as jnp
from jax import lax
from jax.experimental import pallas as pl
from jax.experimental.pallas import tpu as pltpu
from jax.sharding import PartitionSpec as P

HD = 64
LONG = 768
EPS = 1e-05
BS = 1.0 / math.sqrt(48.0)
NEG = -1e30
F32 = jnp.float32
BF = jnp.bfloat16
VMEM_LIMIT = 58 * 1024 * 1024
AXES = ("dp", "fsdp")
GC0 = math.sqrt(2.0 / math.pi)
GC1 = 0.044715


def dot(a, b):
    return lax.dot_general(a, b, (((1,), (0,)), ((), ())), preferred_element_type=F32)


def dot_t(a, b):
    return lax.dot_general(a, b, (((1,), (1,)), ((), ())), preferred_element_type=F32)


def dot_0(a, b):
    return lax.dot_general(a, b, (((0,), (0,)), ((), ())), preferred_element_type=F32)


def params(grid_len=1):
    return pltpu.CompilerParams(
        dimension_semantics=("arbitrary",) * grid_len, vmem_limit_bytes=VMEM_LIMIT
    )


def cost(flops, nbytes, trans=0):
    return pl.CostEstimate(flops=int(flops), bytes_accessed=int(nbytes), transcendentals=int(trans))


def normalize(values):
    centred = values - jnp.mean(values, axis=-1, keepdims=True)
    rstd = lax.rsqrt(jnp.mean(centred * centred, axis=-1, keepdims=True) + EPS)
    return centred * rstd, rstd


def ln_back(dy, xhat, rstd, gain):
    dx = dy * gain
    m1 = jnp.mean(dx, axis=-1, keepdims=True)
    m2 = jnp.mean(dx * xhat, axis=-1, keepdims=True)
    return rstd * (dx - m1 - xhat * m2)


def full_spec(shape):
    return pl.BlockSpec(shape, lambda *_: (0,) * len(shape))


def qkv_kernel(x_ref, g_ref, b_ref, w_ref, bias_ref, o_ref, n_ref):
    rows = x_ref.shape[0]

    @pl.when(pl.program_id(0) == 0)
    def _():
        for r in range(0, rows, 256):
            xhat, _ = normalize(x_ref[r : r + 256, :].astype(F32))
            n_ref[r : r + 256, :] = (xhat * g_ref[...] + b_ref[...]).astype(BF)

    for r in range(0, rows, 256):
        o_ref[r : r + 256, :] = (dot(n_ref[r : r + 256, :], w_ref[...]) + bias_ref[...]).astype(BF)


def qkv_call(x, g, b, w, bias):
    rows, d = x.shape
    cols = w.shape[1]
    bc = 384
    return pl.pallas_call(
        qkv_kernel,
        grid=(cols // bc,),
        in_specs=[
            full_spec((rows, d)),
            full_spec((1, d)),
            full_spec((1, d)),
            pl.BlockSpec((d, bc), lambda j: (0, j)),
            pl.BlockSpec((1, bc), lambda j: (0, j)),
        ],
        out_specs=pl.BlockSpec((rows, bc), lambda j: (0, j)),
        out_shape=jax.ShapeDtypeStruct((rows, cols), BF),
        scratch_shapes=[pltpu.VMEM((rows, d), BF)],
        compiler_params=params(),
        cost_estimate=cost(2 * rows * d * cols, rows * d * 8 + d * cols * 2),
        name="qkv",
    )(x, g, b, w, bias)


def lane_masks(rows):
    lane = lax.broadcasted_iota(jnp.int32, (rows, 128), 1)
    return lane < HD


def split_heads(block):
    low = lane_masks(block.shape[0])
    zero = jnp.zeros_like(block)
    return jnp.where(low, block, zero), jnp.where(low, zero, block)


def q_tiles(rows):
    tiles = [(r, 0, r + 256, True) for r in range(0, LONG, 256)]
    tiles += [(LONG, LONG, rows, False)]
    return tiles


def diag_allowed(is_long, seg_row, seg_col):
    kv = lax.broadcasted_iota(jnp.int32, (256, 256), 0)
    qp = lax.broadcasted_iota(jnp.int32, (256, 256), 1)
    allowed = kv <= qp
    if not is_long:
        allowed = allowed & (seg_col == seg_row)
    return allowed


def attn_kernel(q_ref, k_ref, v_ref, segr_ref, segc_ref, o_ref, lse_ref):
    rows = q_ref.shape[0]
    k0, k1 = split_heads(k_ref[...] * BF(HD**-0.5))
    v0, v1 = split_heads(v_ref[...])
    for q0, kv0, kv1, is_long in q_tiles(rows):
        q = q_ref[q0 : q0 + 256, :]
        allowed = diag_allowed(is_long, segr_ref[...], segc_ref[...])
        outs = []
        for h, (k, v) in enumerate(((k0, v0), (k1, v1))):
            s = dot_t(k[kv0:kv1], q)
            diag = jnp.where(allowed, s[q0 - kv0 : q0 - kv0 + 256], NEG)
            parts = [diag] if kv1 - kv0 == 256 else [s[: q0 - kv0], diag]
            top = functools.reduce(
                jnp.maximum, [jnp.max(p, axis=0, keepdims=True) for p in parts]
            )
            exps = [jnp.exp(p - top) for p in parts]
            total = functools.reduce(
                jnp.add, [jnp.sum(e, axis=0, keepdims=True) for e in exps]
            )
            lse_ref[0, h : h + 1, q0 : q0 + 256] = top + jnp.log(total)
            probs = jnp.concatenate([e.astype(BF) for e in exps], axis=0)
            outs.append(dot_0(v[kv0:kv1], probs) * (1.0 / total))
        o_ref[q0 : q0 + 256, :] = (outs[0] + outs[1]).T.astype(BF)


def attn_call(joined, seg_row, seg_col):
    rows = joined.shape[0]
    pairs = joined.shape[1] // 384
    return pl.pallas_call(
        attn_kernel,
        grid=(pairs,),
        in_specs=[
            pl.BlockSpec((rows, 128), lambda p: (0, p)),
            pl.BlockSpec((rows, 128), lambda p: (0, pairs + p)),
            pl.BlockSpec((rows, 128), lambda p: (0, 2 * pairs + p)),
            full_spec((1, 256)),
            full_spec((256, 1)),
        ],
        out_specs=[
            pl.BlockSpec((rows, 128), lambda p: (0, p)),
            pl.BlockSpec((1, 2, rows), lambda p: (p, 0, 0)),
        ],
        out_shape=[
            jax.ShapeDtypeStruct((rows, pairs * 128), BF),
            jax.ShapeDtypeStruct((pairs, 2, rows), F32),
        ],
        compiler_params=params(),
        cost_estimate=cost(12e9, 8e6, 5.5e6),
        name="attn",
    )(joined, joined, joined, seg_row, seg_col)


def attn_back_kernel(
    q_ref, k_ref, v_ref, do_ref, lse_ref, del_ref, segr_ref, segc_ref, dq_ref, dk_ref, dv_ref,
    dk_acc, dv_acc,
):
    rows = q_ref.shape[0]
    scale = HD**-0.5
    k0, k1 = split_heads(k_ref[...] * BF(scale))
    v0, v1 = split_heads(v_ref[...])
    for q0, kv0, kv1, is_long in q_tiles(rows)[::-1]:
        q = q_ref[q0 : q0 + 256, :]
        do = do_ref[q0 : q0 + 256, :]
        qh = split_heads(q)
        doh = split_heads(do)
        allowed = diag_allowed(is_long, segr_ref[...], segc_ref[...])
        low_p, low_s = [], []
        dq = None
        for h, (k, v) in enumerate(((k0, v0), (k1, v1))):
            s = dot_t(k[kv0:kv1], q)
            dp = dot_t(v[kv0:kv1], do)
            lse = lse_ref[0, h : h + 1, q0 : q0 + 256]
            dlt = del_ref[0, h : h + 1, q0 : q0 + 256]
            diag = jnp.where(allowed, s[q0 - kv0 : q0 - kv0 + 256], NEG)
            parts = [diag] if kv1 - kv0 == 256 else [s[: q0 - kv0], diag]
            probs = jnp.concatenate([jnp.exp(p - lse) for p in parts], axis=0)
            ds = (probs * (dp - dlt)).astype(BF)
            low_p.append(probs.astype(BF))
            low_s.append(ds)
            part = dot_0(k[kv0:kv1], ds)
            dq = part if dq is None else dq + part
        dq_ref[q0 : q0 + 256, :] = dq.T.astype(BF)
        dv = dot(jnp.concatenate(low_p, axis=1), jnp.concatenate(doh, axis=0))
        dk = dot(jnp.concatenate(low_s, axis=1), jnp.concatenate(qh, axis=0))
        if q0 in (LONG, LONG - 256):
            dk_acc[kv0:kv1, :] = dk
            dv_acc[kv0:kv1, :] = dv
        else:
            dk_acc[kv0:kv1, :] += dk
            dv_acc[kv0:kv1, :] += dv
    dk_ref[...] = (dk_acc[...] * scale).astype(BF)
    dv_ref[...] = dv_acc[...].astype(BF)


def attn_back_call(joined, grad_att, lse, delta, seg_row, seg_col):
    rows = joined.shape[0]
    pairs = joined.shape[1] // 384
    blk = lambda off: pl.BlockSpec((rows, 128), lambda p: (0, off + p))
    stat = pl.BlockSpec((1, 2, rows), lambda p: (p, 0, 0))
    return pl.pallas_call(
        attn_back_kernel,
        grid=(pairs,),
        in_specs=[
            blk(0), blk(pairs), blk(2 * pairs), blk(0), stat, stat,
            full_spec((1, 256)), full_spec((256, 1)),
        ],
        out_specs=[blk(0), blk(0), blk(0)],
        out_shape=[jax.ShapeDtypeStruct((rows, pairs * 128), BF)] * 3,
        scratch_shapes=[pltpu.VMEM((rows, 128), F32)] * 2,
        compiler_params=params(),
        cost_estimate=cost(30e9, 12e6, 5.5e6),
        name="attn_back",
    )(joined, joined, joined, grad_att, lse, delta, seg_row, seg_col)


def proj_kernel(x_ref, a_ref, w_ref, pb_ref, g_ref, b_ref, mid_ref, n_ref):
    branch = dot(a_ref[...], w_ref[...]) + pb_ref[...]
    middle = x_ref[...].astype(F32) + BS * branch
    mid_ref[...] = middle
    xhat, _ = normalize(middle)
    n_ref[...] = (xhat * g_ref[...] + b_ref[...]).astype(BF)


def proj_call(x, att, w, pb, g, b):
    rows, d = x.shape
    br = 256
    row = pl.BlockSpec((br, d), lambda i: (i, 0))
    return pl.pallas_call(
        proj_kernel,
        grid=(rows // br,),
        in_specs=[row, row, full_spec((d, d)), full_spec((1, d)), full_spec((1, d)), full_spec((1, d))],
        out_specs=[row, row],
        out_shape=[jax.ShapeDtypeStruct((rows, d), F32), jax.ShapeDtypeStruct((rows, d), BF)],
        compiler_params=params(),
        cost_estimate=cost(2 * rows * d * d, rows * d * 10 + d * d * 2),
        name="proj",
    )(x, att, w, pb, g, b)


def mlp_kernel(
    n_ref, c_ref, mid_ref, wf_ref, fb_ref, wo_ref, ob_ref,
    out_ref, gn_ref, gwf_ref, gwo_ref, gfb_ref, gob_ref,
    nt_scr, mg_scr, acc_scr, act_scr, gp_scr,
):
    j = pl.program_id(0)
    rows = n_ref.shape[0]
    br = 256

    @pl.when(j == 0)
    def _():
        nt_scr[...] = n_ref[...].T
        total = jnp.zeros_like(gob_ref)
        for r in range(0, rows, br):
            mg = (BS * c_ref[r : r + br, :].astype(F32)).astype(BF)
            mg_scr[r : r + br, :] = mg
            total += jnp.sum(mg.astype(F32), axis=0, keepdims=True)
        gob_ref[...] = total

    bias_sum = jnp.zeros_like(gfb_ref)
    for r in range(0, rows, br):
        rr = slice(r, r + br)
        pre = dot(n_ref[rr, :], wf_ref[...]) + fb_ref[...]
        ga = dot_t(mg_scr[rr, :], wo_ref[...])
        sq = pre * pre
        t = jnp.tanh(GC0 * pre * (1.0 + GC1 * sq))
        half = 0.5 * (1.0 + t)
        act = (pre * half).astype(BF)
        slope = half + (0.5 * GC0) * pre * (1.0 - t * t) * (1.0 + (3.0 * GC1) * sq)
        gp = (slope * ga).astype(BF)
        act_scr[rr, :] = act
        gp_scr[rr, :] = gp
        bias_sum += jnp.sum(gp.astype(F32), axis=0, keepdims=True)
        fwd = dot(act, wo_ref[...])
        back = dot_t(gp, wf_ref[...])

        @pl.when(j == 0)
        def _():
            acc_scr[rr, :] = fwd
            gn_ref[rr, :] = back

        @pl.when(j > 0)
        def _():
            acc_scr[rr, :] += fwd
            gn_ref[rr, :] += back

    gfb_ref[...] = bias_sum
    gwf_ref[...] = dot(nt_scr[...], gp_scr[...]).astype(BF)
    gwo_ref[...] = dot_0(act_scr[...], mg_scr[...]).astype(BF)

    @pl.when(j == pl.num_programs(0) - 1)
    def _():
        for r in range(0, rows, br):
            rr = slice(r, r + br)
            out_ref[rr, :] = (mid_ref[rr, :] + BS * (acc_scr[rr, :] + ob_ref[...])).astype(BF)


def mlp_call(normed, cot, middle, w_fc, fc_bias, w_out, out_bias):
    rows, d = normed.shape
    ff = w_fc.shape[1]
    bc = 512
    return pl.pallas_call(
        mlp_kernel,
        grid=(ff // bc,),
        in_specs=[
            full_spec((rows, d)), full_spec((rows, d)), full_spec((rows, d)),
            pl.BlockSpec((d, bc), lambda j: (0, j)),
            pl.BlockSpec((1, bc), lambda j: (0, j)),
            pl.BlockSpec((bc, d), lambda j: (j, 0)),
            full_spec((1, d)),
        ],
        out_specs=[
            full_spec((rows, d)), full_spec((rows, d)),
            pl.BlockSpec((d, bc), lambda j: (0, j)),
            pl.BlockSpec((bc, d), lambda j: (j, 0)),
            pl.BlockSpec((1, bc), lambda j: (0, j)),
            full_spec((1, d)),
        ],
        out_shape=[
            jax.ShapeDtypeStruct((rows, d), BF),
            jax.ShapeDtypeStruct((rows, d), F32),
            jax.ShapeDtypeStruct((d, ff), BF),
            jax.ShapeDtypeStruct((ff, d), BF),
            jax.ShapeDtypeStruct((1, ff), F32),
            jax.ShapeDtypeStruct((1, d), F32),
        ],
        scratch_shapes=[
            pltpu.VMEM((d, rows), BF), pltpu.VMEM((rows, d), BF), pltpu.VMEM((rows, d), F32),
            pltpu.VMEM((rows, bc), BF), pltpu.VMEM((rows, bc), BF),
        ],
        compiler_params=params(),
        cost_estimate=cost(12 * rows * d * ff, 30e6, rows * ff),
        name="mlp",
    )(normed, cot, middle, w_fc, fc_bias, w_out, out_bias)


def proj_back_kernel(
    gn_ref, mid_ref, c_ref, a_ref, w_ref, g_ref, ind_ref,
    gm_ref, ga_ref, gw_ref, del_ref, gg_ref, gb_ref, gpb_ref, gw_acc,
):
    i = pl.program_id(0)

    @pl.when(i == 0)
    def _():
        gw_acc[...] = jnp.zeros_like(gw_acc)
        gg_ref[...] = jnp.zeros_like(gg_ref)
        gb_ref[...] = jnp.zeros_like(gb_ref)
        gpb_ref[...] = jnp.zeros_like(gpb_ref)

    dy = gn_ref[...]
    xhat, rstd = normalize(mid_ref[...])
    gg_ref[...] += jnp.sum(dy * xhat, axis=0, keepdims=True)
    gb_ref[...] += jnp.sum(dy, axis=0, keepdims=True)
    gm = c_ref[...].astype(F32) + ln_back(dy, xhat, rstd, g_ref[...])
    gm_ref[...] = gm
    pg = (BS * gm).astype(BF)
    gpb_ref[...] += jnp.sum(pg.astype(F32), axis=0, keepdims=True)
    gw_acc[...] += dot_0(a_ref[...], pg)
    ga = dot_t(pg, w_ref[...]).astype(BF)
    ga_ref[...] = ga
    prod = ga.astype(F32) * a_ref[...].astype(F32)
    high = prod.astype(BF)
    low = (prod - high.astype(F32)).astype(BF)
    del_ref[...] = dot_t(ind_ref[...], high) + dot_t(ind_ref[...], low)

    @pl.when(i == pl.num_programs(0) - 1)
    def _():
        gw_ref[...] = gw_acc[...].astype(BF)


def proj_back_call(gn, middle, cot, att, w, g, heads):
    rows, d = middle.shape
    br = 256
    row = pl.BlockSpec((br, d), lambda i: (i, 0))
    ind = (jnp.arange(16)[:, None] == jnp.arange(d)[None, :] // HD).astype(BF)
    vec = full_spec((1, d))
    vshape = jax.ShapeDtypeStruct((1, d), F32)
    return pl.pallas_call(
        proj_back_kernel,
        grid=(rows // br,),
        in_specs=[row, row, row, row, full_spec((d, d)), vec, full_spec((16, d))],
        out_specs=[row, row, full_spec((d, d)), pl.BlockSpec((16, br), lambda i: (0, i)), vec, vec, vec],
        out_shape=[
            jax.ShapeDtypeStruct((rows, d), F32),
            jax.ShapeDtypeStruct((rows, d), BF),
            jax.ShapeDtypeStruct((d, d), BF),
            jax.ShapeDtypeStruct((16, rows), F32),
            vshape, vshape, vshape,
        ],
        scratch_shapes=[pltpu.VMEM((d, d), F32)],
        compiler_params=params(),
        cost_estimate=cost(4 * rows * d * d, rows * d * 16),
        name="proj_back",
    )(gn, middle, cot, att, w, g, ind)


def qkv_back_kernel(
    x_ref, gm_ref, gq_ref, gk_ref, gv_ref, w_ref, g_ref, b_ref,
    gx_ref, gw_ref, gg_ref, gb_ref, gqb_ref, gvb_ref, nt_scr, acc_scr,
):
    j = pl.program_id(0)
    rows, d = x_ref.shape
    br = 256

    def block(src):
        gw_ref[...] = dot(nt_scr[...], src[...]).astype(BF)

        for r in range(0, rows, br):
            rr = slice(r, r + br)
            back = dot_t(src[rr, :], w_ref[...])

            @pl.when(j == 0)
            def _():
                acc_scr[rr, :] = back

            @pl.when(j > 0)
            def _():
                acc_scr[rr, :] += back

    def column_sum(src):
        total = jnp.zeros((1, d), F32)
        for r in range(0, rows, br):
            total += jnp.sum(src[r : r + br, :].astype(F32), axis=0, keepdims=True)
        return total

    @pl.when(j == 0)
    def _():
        for r in range(0, rows, br):
            xhat, _ = normalize(x_ref[r : r + br, :].astype(F32))
            nt_scr[:, r : r + br] = (xhat * g_ref[...] + b_ref[...]).astype(BF).T
        gqb_ref[...] = column_sum(gq_ref)
        gvb_ref[...] = column_sum(gv_ref)
        block(gq_ref)

    @pl.when(j == 1)
    def _():
        block(gk_ref)

    @pl.when(j == 2)
    def _():
        block(gv_ref)
        gg = jnp.zeros((1, d), F32)
        gb = jnp.zeros((1, d), F32)
        for r in range(0, rows, br):
            rr = slice(r, r + br)
            xhat, rstd = normalize(x_ref[rr, :].astype(F32))
            dy = acc_scr[rr, :]
            gg += jnp.sum(dy * xhat, axis=0, keepdims=True)
            gb += jnp.sum(dy, axis=0, keepdims=True)
            gx_ref[rr, :] = (gm_ref[rr, :] + ln_back(dy, xhat, rstd, g_ref[...])).astype(BF)
        gg_ref[...] = gg
        gb_ref[...] = gb


def qkv_back_call(x, gm, gq, gk, gv, w, g, b):
    rows, d = x.shape
    act = full_spec((rows, d))
    vec = full_spec((1, d))
    vshape = jax.ShapeDtypeStruct((1, d), F32)
    return pl.pallas_call(
        qkv_back_kernel,
        grid=(3,),
        in_specs=[act, act, act, act, act, pl.BlockSpec((d, d), lambda j: (0, j)), vec, vec],
        out_specs=[act, pl.BlockSpec((d, d), lambda j: (0, j)), vec, vec, vec, vec],
        out_shape=[
            jax.ShapeDtypeStruct((rows, d), BF),
            jax.ShapeDtypeStruct((d, 3 * d), BF),
            vshape, vshape, vshape, vshape,
        ],
        scratch_shapes=[pltpu.VMEM((d, rows), BF), pltpu.VMEM((rows, d), F32)],
        compiler_params=params(),
        cost_estimate=cost(12 * rows * d * d, rows * d * 20),
        name="qkv_back",
    )(x, gm, gq, gk, gv, w, g, b)


def pack_plan(counts, rows):
    c = [counts[i] for i in range(counts.shape[0])]
    ends, run = [], jnp.int32(0)
    for v in c:
        run = run + v
        ends.append(run)
    start = jnp.int32(0)
    for i in range(len(c) - 1):
        start = jnp.where(c[i] == LONG, ends[i] - c[i], start)
    rolled = jnp.arange(rows, dtype=jnp.int32)
    pos = rolled + start
    pos = jnp.where(pos >= rows, pos - rows, pos)
    seg = functools.reduce(jnp.add, [(pos >= e).astype(jnp.int32) for e in ends])
    valid = seg < len(c) - 1
    seg = jnp.where(valid, seg, 1000 + rolled)
    return start, seg[LONG:], valid


def roll_rows(array, shift):
    return lax.dynamic_slice_in_dim(jnp.concatenate([array, array], axis=0), shift, array.shape[0])


def per_device(
    tokens, lengths, ln1_gain, ln1_bias, w_qkv, qv_bias, w_proj, proj_bias, ln2_gain, ln2_bias,
    w_fc, fc_bias, w_out, out_bias, cotangent,
):
    rows, d = tokens.shape
    heads = d // HD
    r = w_qkv.shape[0]
    devices = d // r
    gather = lambda v: lax.all_gather(v, AXES, axis=0, tiled=True)
    scatter = lambda v: lax.psum_scatter(v, AXES, scatter_dimension=0, tiled=True)

    start, seg, valid = pack_plan(lengths[0], rows)
    seg_row, seg_col = seg[None, :], seg[:, None]
    x = roll_rows(tokens, start)
    cot = jnp.where(valid[:, None], roll_rows(cotangent, start), BF(0))

    vectors = [ln1_gain, ln1_bias, qv_bias, proj_bias, ln2_gain, ln2_bias, fc_bias, out_bias]
    flat = jnp.concatenate(vectors)
    flat = jnp.pad(flat, (0, r * 128 - flat.shape[0])).reshape(r, 128)
    first = gather(jnp.concatenate([w_qkv, w_proj, flat], axis=1))
    w_fc_all = gather(w_fc)
    w_out_all = gather(w_out)
    w_qkv_all = first[:, : 3 * d]
    w_proj_all = first[:, 3 * d : 4 * d]
    table = first[:, 4 * d :].reshape(devices, r * 128)
    rows_of, at = [], 0
    for v in vectors:
        size = v.shape[0]
        rows_of.append(table[:, at : at + size].reshape(1, -1).astype(F32))
        at += size
    g1, b1, qvb, pb, g2, b2, fb, ob = rows_of
    bias = jnp.concatenate([qvb[:, :d], jnp.zeros((1, d), F32), qvb[:, d:]], axis=1)

    joined = qkv_call(x, g1, b1, w_qkv_all, bias)
    att, lse = attn_call(joined, seg_row, seg_col)
    middle, normed_two = proj_call(x, att, w_proj_all, pb, g2, b2)
    out, gn, gw_fc, gw_out, gfb, gob = mlp_call(normed_two, cot, middle, w_fc_all, fb, w_out_all, ob)
    rs_fc = scatter(gw_fc)
    rs_out = scatter(gw_out)
    gm, ga, gw_proj, delta, gg2, gb2, gpb = proj_back_call(gn, middle, cot, att, w_proj_all, g2, heads)
    delta = delta[:heads].reshape(heads // 2, 2, rows)
    gq, gk, gv = attn_back_call(joined, ga, lse, delta, seg_row, seg_col)
    gx, gw_qkv, gg1, gb1, gqb, gvb = qkv_back_call(x, gm, gq, gk, gv, w_qkv_all, g1, b1)
    gqv = jnp.concatenate([gqb, gvb], axis=1)
    grads = [gg1, gb1, gqv, gpb, gg2, gb2, gfb, gob]
    back = jnp.concatenate([v.reshape(devices, -1) for v in grads], axis=1)
    back = jnp.pad(back, ((0, 0), (0, r * 128 - back.shape[1]))).reshape(d, 128)
    last = scatter(jnp.concatenate([gw_qkv, gw_proj, back.astype(BF)], axis=1))
    small = last[:, 4 * d :].reshape(-1).astype(F32)
    shares, at = [], 0
    for v in vectors:
        shares.append(small[at : at + v.shape[0]])
        at += v.shape[0]
    rg1, rb1, rqv, rpb, rg2, rb2, rfb, rob = shares
    restore = rows - start
    return (
        roll_rows(out, restore),
        roll_rows(gx, restore),
        rg1, rb1, last[:, : 3 * d].astype(F32), rqv, last[:, 3 * d : 4 * d].astype(F32), rpb,
        rg2, rb2, rs_fc.astype(F32), rfb, rs_out.astype(F32), rob,
    )


def solution(mesh):
    row, vec = P(AXES, None), P(AXES)
    in_specs = (row, row, vec, vec, row, vec, row, vec, vec, vec, row, vec, row, vec, row)
    out_specs = (row, row, vec, vec, row, vec, row, vec, vec, vec, row, vec, row, vec)
    return jax.shard_map(
        per_device, mesh=mesh, in_specs=in_specs, out_specs=out_specs, check_vma=False
    )
```

```python
import functools
import math

import jax
import jax.numpy as jnp
from jax import lax
from jax.experimental import pallas as pl
from jax.experimental.pallas import tpu as pltpu
from jax.sharding import PartitionSpec as P

HD = 64
LONG = 768
EPS = 1e-05
BS = 1.0 / math.sqrt(48.0)
NEG = -1e30
F32 = jnp.float32
BF = jnp.bfloat16
VMEM_LIMIT = 58 * 1024 * 1024
AXES = ("dp", "fsdp")
GC0 = math.sqrt(2.0 / math.pi)
GC1 = 0.044715


def dot(a, b):
    return lax.dot_general(a, b, (((1,), (0,)), ((), ())), preferred_element_type=F32)


def dot_t(a, b):
    return lax.dot_general(a, b, (((1,), (1,)), ((), ())), preferred_element_type=F32)


def dot_0(a, b):
    return lax.dot_general(a, b, (((0,), (0,)), ((), ())), preferred_element_type=F32)


def params(grid_len=1):
    return pltpu.CompilerParams(
        dimension_semantics=("arbitrary",) * grid_len, vmem_limit_bytes=VMEM_LIMIT
    )


def cost(flops, nbytes, trans=0):
    return pl.CostEstimate(flops=int(flops), bytes_accessed=int(nbytes), transcendentals=int(trans))


def normalize(values):
    centred = values - jnp.mean(values, axis=-1, keepdims=True)
    rstd = lax.rsqrt(jnp.mean(centred * centred, axis=-1, keepdims=True) + EPS)
    return centred * rstd, rstd


def ln_back(dy, xhat, rstd, gain):
    dx = dy * gain
    m1 = jnp.mean(dx, axis=-1, keepdims=True)
    m2 = jnp.mean(dx * xhat, axis=-1, keepdims=True)
    return rstd * (dx - m1 - xhat * m2)


def full_spec(shape):
    return pl.BlockSpec(shape, lambda *_: (0,) * len(shape))


def lane_masks(rows):
    lane = lax.broadcasted_iota(jnp.int32, (rows, 128), 1)
    return lane < HD


def split_heads(block):
    low = lane_masks(block.shape[0])
    zero = jnp.zeros_like(block)
    return jnp.where(low, block, zero), jnp.where(low, zero, block)


def q_tiles(rows):
    tiles = [(r, 0, r + 256, True) for r in range(0, LONG, 256)]
    tiles += [(LONG, LONG, rows, False)]
    return tiles


def diag_allowed(is_long, seg_row, seg_col):
    kv = lax.broadcasted_iota(jnp.int32, (256, 256), 0)
    qp = lax.broadcasted_iota(jnp.int32, (256, 256), 1)
    allowed = kv <= qp
    if not is_long:
        allowed = allowed & (seg_col == seg_row)
    return allowed


def attn_kernel(q_ref, k_ref, v_ref, segr_ref, segc_ref, o_ref, lse_ref):
    rows = q_ref.shape[0]
    k0, k1 = split_heads(k_ref[...] * BF(HD**-0.5))
    v0, v1 = split_heads(v_ref[...])
    for q0, kv0, kv1, is_long in q_tiles(rows):
        q = q_ref[q0 : q0 + 256, :]
        allowed = diag_allowed(is_long, segr_ref[...], segc_ref[...])
        outs = []
        for h, (k, v) in enumerate(((k0, v0), (k1, v1))):
            s = dot_t(k[kv0:kv1], q)
            diag = jnp.where(allowed, s[q0 - kv0 : q0 - kv0 + 256], NEG)
            parts = [diag] if kv1 - kv0 == 256 else [s[: q0 - kv0], diag]
            top = functools.reduce(
                jnp.maximum, [jnp.max(p, axis=0, keepdims=True) for p in parts]
            )
            exps = [jnp.exp(p - top) for p in parts]
            total = functools.reduce(
                jnp.add, [jnp.sum(e, axis=0, keepdims=True) for e in exps]
            )
            lse_ref[0, h : h + 1, q0 : q0 + 256] = top + jnp.log(total)
            probs = jnp.concatenate([e.astype(BF) for e in exps], axis=0)
            outs.append(dot_0(v[kv0:kv1], probs) * (1.0 / total))
        o_ref[q0 : q0 + 256, :] = (outs[0] + outs[1]).T.astype(BF)


def attn_call(joined, seg_row, seg_col):
    rows = joined.shape[0]
    pairs = joined.shape[1] // 384
    return pl.pallas_call(
        attn_kernel,
        grid=(pairs,),
        in_specs=[pl.BlockSpec((rows, 128), lambda p, t=t: (0, pair_block(p, pairs) * 3 + t)) for t in range(3)]
        + [full_spec((1, 256)), full_spec((256, 1))],
        out_specs=[
            pl.BlockSpec((rows, 128), lambda p: (0, p)),
            pl.BlockSpec((1, 2, rows), lambda p: (p, 0, 0)),
        ],
        out_shape=[
            jax.ShapeDtypeStruct((rows, pairs * 128), BF),
            jax.ShapeDtypeStruct((pairs, 2, rows), F32),
        ],
        compiler_params=params(),
        cost_estimate=cost(24e9, 8e6, 5.5e6),
        name="attn",
    )(joined, joined, joined, seg_row, seg_col)


def pair_block(p, pairs):
    return (p % 2) * (pairs // 2) + p // 2


ANY = pl.BlockSpec(memory_space=pl.ANY)
SMEM = pl.BlockSpec(memory_space=pltpu.SMEM)


def local_copy(src, dst, sem):
    return pltpu.make_async_copy(src, dst, sem)


def chips_of(dims, where_ref):
    z_n, y_n, x_n = dims
    zi, yi, xi = [where_ref[i] for i in range(3)]
    for i in range(y_n * x_n):
        for j in range(z_n):
            yield i, j, lax.rem(zi + j, z_n), lax.rem(yi + i // x_n, y_n), lax.rem(xi + i % x_n, x_n)


def piece_at(dims, arrays, i, j):
    at = i * dims[0] + j
    for a in arrays:
        if at < a.shape[0]:
            return a.at[at]
        at -= a.shape[0]


def load_columns(dims, where_ref, own, oth, first, cols, dst, sem):
    ci = where_ref[3]
    for i, j, z, y, x in chips_of(dims, where_ref):
        for half, src in ((ci, own), (1 - ci, oth)):
            block = piece_at(dims, src, i, j).at[:, pl.ds(first, cols)]
            local_copy(block, dst.at[half, z, y, x], sem.at[half, z, y, x]).start()


def wait_columns(dims, dst, sem, half):
    for z in range(dims[0]):
        for y in range(dims[1]):
            for x in range(dims[2]):
                block = dst.at[half, z, y, x]
                local_copy(block, block, sem.at[half, z, y, x]).wait()


def flat2(value):
    return value.reshape(-1, value.shape[-1])


def store_columns(dims, where_ref, src, own, oth, half, first, cols, sem):
    ci = where_ref[3]
    for other, out in ((False, own), (True, oth)):

        @pl.when((half != ci) if other else (half == ci))
        def _():
            for i, j, z, y, x in chips_of(dims, where_ref):
                local_copy(src.at[z, y, x], out.at[i, j, :, pl.ds(first, cols)], sem.at[i, j]).start()


def wait_store(dims, src, out, first, cols, sem):
    for i in range(dims[1] * dims[2]):
        for j in range(dims[0]):
            local_copy(src.at[0, 0, 0], out.at[i, j, :, pl.ds(first, cols)], sem.at[i, j]).wait()


def weight_scratch(dims, n, cols):
    return [
        pltpu.VMEM((2,) + dims + (n, cols), BF),
        pltpu.SemaphoreType.DMA((2,) + dims),
    ]


def vector_plan(d, devices):
    r = d // devices
    return {
        "g1": (0, 0, r), "b1": (0, r, r), "qv": (0, 2 * r, 2 * r), "fb": (1, 0, 4 * r),
        "pb": (2, 0, r), "g2": (2, r, r), "b2": (2, 2 * r, r), "ob": (2, 3 * r, r),
    }


VECTOR_ROWS = ("g1", "b1", "qv", "pb", "g2", "b2", "fb", "ob")


def owner_of(shape, size, axis):
    c = lax.broadcasted_iota(jnp.int32, shape, axis).astype(F32)
    owner = jnp.floor((c + 0.5) * (1.0 / size))
    return owner, c - owner * size


def row_pick(devices, d, row):
    r = d // devices
    at = lax.broadcasted_iota(jnp.int32, (devices, d), 1)
    dev = lax.broadcasted_iota(jnp.int32, (devices, d), 0)
    return (at == dev * r + row).astype(BF)


def vector_maps(devices, n, first, size):
    owner, place = owner_of((devices, n), size, 1)
    mine = owner == lax.broadcasted_iota(jnp.int32, (devices, n), 0).astype(F32)
    _, place = owner_of((128, n), size, 1)
    spot = (place + first == lax.broadcasted_iota(jnp.int32, (128, n), 0).astype(F32)).astype(BF)
    return mine, spot


def unpack_vectors(table, d, devices, out_ref):
    plan = vector_plan(d, devices)
    picked = [dot(row_pick(devices, d, k), table).astype(BF) for k in range(3)]
    for i, name in enumerate(VECTOR_ROWS):
        k, first, size = plan[name]
        n = size * devices
        mine, spot = vector_maps(devices, n, first, size)
        spread = dot(picked[k], spot)
        out_ref[i : i + 1, :n] = jnp.sum(jnp.where(mine, spread, 0.0), axis=0, keepdims=True)


def pack_vectors(rows, d, devices):
    plan = vector_plan(d, devices)
    parts = [None] * 3
    for name in VECTOR_ROWS:
        k, first, size = plan[name]
        n = size * devices
        mine, spot = vector_maps(devices, n, first, size)
        part = dot_t(jnp.where(mine, rows[name], 0.0).astype(BF), spot)
        parts[k] = part if parts[k] is None else parts[k] + part
    total = None
    for k in range(3):
        piece = dot_0(row_pick(devices, d, k), parts[k].astype(BF))
        total = piece if total is None else total + piece
    return total.astype(BF)


def qkv_kernel(dims, count, devices, where_ref, x_ref, *refs):
    own, oth = refs[:count], refs[count : 2 * count]
    o_ref, vec_ref, w_scr, w_sem, t_scr, t_sem, n_scr, bias_scr = refs[2 * count :]
    rows, d = x_ref.shape
    cols = w_scr.shape[-1]
    table_at = own[0].shape[-1] - 128
    step = pl.program_id(0)

    @pl.when(step == 0)
    def _():
        for i, j, z, y, x in chips_of(dims, where_ref):
            block = piece_at(dims, own, i, j).at[:, pl.ds(table_at, 128)]
            local_copy(block, t_scr.at[z, y, x], t_sem.at[z, y, x]).start()
        load_columns(dims, where_ref, own, oth, 0, cols, w_scr, w_sem)
        for z in range(dims[0]):
            for y in range(dims[1]):
                for x in range(dims[2]):
                    block = t_scr.at[z, y, x]
                    local_copy(block, block, t_sem.at[z, y, x]).wait()
        vec_ref[...] = jnp.zeros_like(vec_ref)
        unpack_vectors(flat2(t_scr[...]), d, devices, vec_ref)
        zero = jnp.zeros((1, 128), F32)
        pairs = d // 128
        for p in range(pairs):
            at = pair_block(p, pairs) * 384
            half, at = at // cols, at % cols
            bias_scr[half, :, at : at + 128] = vec_ref[2:3, p * 128 : (p + 1) * 128]
            bias_scr[half, :, at + 128 : at + 256] = zero
            bias_scr[half, :, at + 256 : at + 384] = vec_ref[2:3, d + p * 128 : d + (p + 1) * 128]
        for r in range(0, rows, 256):
            xhat, _ = normalize(x_ref[r : r + 256, :].astype(F32))
            n_scr[r : r + 256, :] = (xhat * vec_ref[0:1, :d] + vec_ref[1:2, :d]).astype(BF)
        wait_columns(dims, w_scr, w_sem, 0)

    @pl.when(step == 1)
    def _():
        wait_columns(dims, w_scr, w_sem, 1)

    w = flat2(w_scr[step])
    for r in range(0, rows, 256):
        o_ref[r : r + 256, :] = (dot(n_scr[r : r + 256, :], w) + bias_scr[step]).astype(BF)


def qkv_call(dims, where, x, own, oth, devices):
    rows, d = x.shape
    n = own[0].shape[1]
    cols = 3 * d // 2
    return pl.pallas_call(
        functools.partial(qkv_kernel, dims, len(own), devices),
        grid=(2,),
        in_specs=[SMEM, full_spec((rows, d))] + [ANY] * (2 * len(own)),
        out_specs=[pl.BlockSpec((rows, cols), lambda j: (0, j)), full_spec((8, 4 * d))],
        out_shape=[
            jax.ShapeDtypeStruct((rows, 2 * cols), BF), jax.ShapeDtypeStruct((8, 4 * d), F32)
        ],
        scratch_shapes=weight_scratch(dims, n, cols)
        + [
            pltpu.VMEM(dims + (n, 128), BF), pltpu.SemaphoreType.DMA(dims),
            pltpu.VMEM((rows, d), BF), pltpu.VMEM((2, 1, cols), F32),
        ],
        compiler_params=params(),
        cost_estimate=cost(4 * rows * d * cols, rows * d * 8 + d * cols * 4),
        name="qkv",
    )(where, x, *own, *oth)


def proj_kernel(dims, count, first, where_ref, x_ref, a_ref, vec_ref, *refs):
    own, oth = refs[:count], refs[count : 2 * count]
    mid_ref, n_ref, w_scr, w_sem = refs[2 * count :]
    d = x_ref.shape[1]

    @pl.when(pl.program_id(0) == 0)
    def _():
        load_columns(dims, where_ref, own, oth, first, w_scr.shape[-1], w_scr, w_sem)
        for h in range(2):
            wait_columns(dims, w_scr, w_sem, h)

    a = a_ref[...]
    branch = jnp.concatenate([dot(a, flat2(w_scr[h])) for h in range(2)], axis=1) + vec_ref[3:4, :d]
    middle = x_ref[...].astype(F32) + BS * branch
    mid_ref[...] = middle
    xhat, _ = normalize(middle)
    n_ref[...] = (xhat * vec_ref[4:5, :d] + vec_ref[5:6, :d]).astype(BF)


def proj_call(dims, where, x, att, vec, own, oth):
    rows, d = x.shape
    br = 256
    row = pl.BlockSpec((br, d), lambda i: (i, 0))
    return pl.pallas_call(
        functools.partial(proj_kernel, dims, len(own), 3 * d // 2),
        grid=(rows // br,),
        in_specs=[SMEM, row, row, full_spec(vec.shape)] + [ANY] * (2 * len(own)),
        out_specs=[row, row],
        out_shape=[jax.ShapeDtypeStruct((rows, d), F32), jax.ShapeDtypeStruct((rows, d), BF)],
        scratch_shapes=weight_scratch(dims, own[0].shape[1], d // 2),
        compiler_params=params(),
        cost_estimate=cost(2 * rows * d * d, rows * d * 10 + d * d * 2),
        name="proj",
    )(where, x, att, vec, *own, *oth)


def hidden_parts(dims, n, d):
    per = min(n, d)
    return per, d // per


def mlp_kernel(dims, count, where_ref, n_ref, c_ref, mid_ref, vec_ref, *refs):
    fc_own, fc_oth = refs[: count[0]], refs[count[0] : 2 * count[0]]
    refs = refs[2 * count[0] :]
    out_own, out_oth = refs[: count[1]], refs[count[1] : 2 * count[1]]
    (
        out_ref, gn_ref, gfb_ref, gob_ref, gf_own, gf_oth, go_own, go_oth,
        nt_scr, mg_scr, acc_scr, act_scr, gp_scr, f_scr, f_sem, o_scr, o_sem, gf_scr, gf_sem, go_scr, go_sem,
    ) = refs[2 * count[1] :]
    z_n, y_n, x_n = dims
    zi, yi, xi, ci = [where_ref[i] for i in range(4)]
    j = pl.program_id(0)
    blocks = o_scr.shape[0]
    rows, d = n_ref.shape
    n = out_own[0].shape[1]
    per, parts = hidden_parts(dims, n, d)
    br = 256

    @pl.when(j == 0)
    def _():
        load_columns(dims, where_ref, fc_own, fc_oth, 0, f_scr.shape[-1], f_scr, f_sem)
        for i, s, z, y, x in chips_of(dims, where_ref):
            for core, src in ((ci, out_own), (1 - ci, out_oth)):
                for q in range(n // per):
                    at = (((z * y_n + y) * x_n + x) * 2 + core) * n + q * per
                    blk, off = at // d, lax.rem(at, d)
                    local_copy(
                        piece_at(dims, src, i, s).at[pl.ds(q * per, per), :],
                        o_scr.at[blk, pl.ds(pl.multiple_of(off, 16), per), :],
                        o_sem.at[blk, off // per],
                    ).start()
        nt_scr[...] = n_ref[...].T
        total = jnp.zeros_like(gob_ref)
        for r in range(0, rows, br):
            mg = (BS * c_ref[r : r + br, :].astype(F32)).astype(BF)
            mg_scr[r : r + br, :] = mg
            total += jnp.sum(mg.astype(F32), axis=0, keepdims=True)
        gob_ref[...] = total
        wait_columns(dims, f_scr, f_sem, 0)

    @pl.when(j == blocks // 2)
    def _():
        wait_columns(dims, f_scr, f_sem, 1)

    for q in range(parts):
        part = o_scr.at[j, pl.ds(q * per, per), :]
        local_copy(part, part, o_sem.at[j, q]).wait()

    half = j // (blocks // 2)
    first = pl.multiple_of(lax.rem(j, blocks // 2) * d, 128)
    wf = flat2(f_scr[half, :, :, :, :, pl.ds(first, d)])
    wo = o_scr[j]
    fb = vec_ref[6:7, pl.ds(pl.multiple_of(j * d, 128), d)]
    bias_sum = jnp.zeros((1, d), F32)
    for r in range(0, rows, br):
        rr = slice(r, r + br)
        pre = dot(n_ref[rr, :], wf) + fb
        ga = dot_t(mg_scr[rr, :], wo)
        sq = pre * pre
        t = jnp.tanh(GC0 * pre * (1.0 + GC1 * sq))
        half_t = 0.5 * (1.0 + t)
        act = (pre * half_t).astype(BF)
        slope = half_t + (0.5 * GC0) * pre * (1.0 - t * t) * (1.0 + (3.0 * GC1) * sq)
        gp = (slope * ga).astype(BF)
        act_scr[rr, :] = act
        gp_scr[rr, :] = gp
        bias_sum += jnp.sum(gp.astype(F32), axis=0, keepdims=True)
        fwd = dot(act, wo)
        back = dot_t(gp, wf)

        @pl.when(j == 0)
        def _():
            acc_scr[rr, :] = fwd
            gn_ref[rr, :] = back

        @pl.when(j > 0)
        def _():
            acc_scr[rr, :] += fwd
            gn_ref[rr, :] += back

    gfb_ref[...] = bias_sum
    gf_scr[j] = dot(nt_scr[...], gp_scr[...]).astype(BF).reshape(gf_scr.shape[1:])
    store_columns(dims, where_ref, gf_scr.at[j], gf_own, gf_oth, half, first, d, gf_sem.at[j])
    go_scr[j] = dot_0(act_scr[...], mg_scr[...]).astype(BF)
    for q in range(parts):
        at = j * d + q * per
        dev = at // n
        core = lax.rem(dev, 2)
        x = lax.rem(dev // 2, x_n)
        y = lax.rem(dev // (2 * x_n), y_n)
        z = dev // (2 * x_n * y_n)
        piece = lax.rem(y - yi + y_n, y_n) * x_n + lax.rem(x - xi + x_n, x_n)
        slot = lax.rem(z - zi + z_n, z_n)
        off = pl.multiple_of(lax.rem(at, n), 16)
        for other, out in ((False, go_own), (True, go_oth)):

            @pl.when((core != ci) if other else (core == ci))
            def _():
                local_copy(
                    go_scr.at[j, pl.ds(q * per, per), :], out.at[piece, slot, pl.ds(off, per), :], go_sem.at[j, q]
                ).start()

    @pl.when(j == blocks - 1)
    def _():
        for r in range(0, rows, br):
            rr = slice(r, r + br)
            out_ref[rr, :] = (mid_ref[rr, :] + BS * (acc_scr[rr, :] + vec_ref[7:8, :d])).astype(BF)
        for b in range(blocks):
            wait_store(dims, gf_scr.at[b], gf_own, 0, d, gf_sem.at[b])
            for q in range(parts):
                part = go_scr.at[b, pl.ds(q * per, per), :]
                local_copy(part, part, go_sem.at[b, q]).wait()


def mlp_call(dims, where, normed, cot, middle, vec, fc, out):
    rows, d = normed.shape
    n, half = fc[0][0].shape[1:]
    blocks = 2 * half // d
    n_out = out[0][0].shape[1]
    per, parts = hidden_parts(dims, n_out, d)
    count = dims[1] * dims[2]
    act = full_spec((rows, d))
    f_piece = jax.ShapeDtypeStruct((count, dims[0], n, half), BF)
    o_piece = jax.ShapeDtypeStruct((count, dims[0], n_out, d), BF)
    return pl.pallas_call(
        functools.partial(mlp_kernel, dims, (len(fc[0]), len(out[0]))),
        grid=(blocks,),
        in_specs=[SMEM, act, act, act, full_spec(vec.shape)] + [ANY] * (2 * (len(fc[0]) + len(out[0]))),
        out_specs=[act, act, pl.BlockSpec((1, d), lambda j: (0, j)), full_spec((1, d))] + [ANY] * 4,
        out_shape=[
            jax.ShapeDtypeStruct((rows, d), BF),
            jax.ShapeDtypeStruct((rows, d), F32),
            jax.ShapeDtypeStruct((1, 2 * half), F32),
            jax.ShapeDtypeStruct((1, d), F32),
            f_piece, f_piece, o_piece, o_piece,
        ],
        scratch_shapes=[
            pltpu.VMEM((d, rows), BF), pltpu.VMEM((rows, d), BF), pltpu.VMEM((rows, d), F32),
            pltpu.VMEM((rows, d), BF), pltpu.VMEM((rows, d), BF),
        ]
        + weight_scratch(dims, n, half)
        + [
            pltpu.VMEM((blocks, d, d), BF), pltpu.SemaphoreType.DMA((blocks, parts)),
            pltpu.VMEM((blocks,) + dims + (n, d), BF), pltpu.SemaphoreType.DMA((blocks, count, dims[0])),
            pltpu.VMEM((blocks, d, d), BF), pltpu.SemaphoreType.DMA((blocks, parts)),
        ],
        compiler_params=params(),
        cost_estimate=cost(24 * rows * d * half, 30e6, rows * half),
        name="mlp",
    )(where, normed, cot, middle, vec, *fc[0], *fc[1], *out[0], *out[1])


def proj_back_kernel(dims, count, first, where_ref, gn_ref, mid_ref, c_ref, a_ref, vec_ref, ind_ref, *refs):
    own, oth = refs[:count], refs[count : 2 * count]
    (
        gm_ref, ga_ref, gw_ref, del_ref, gg_ref, gb_ref, gpb_ref, gw_acc, w_scr, w_sem,
    ) = refs[2 * count :]
    i = pl.program_id(0)
    d = mid_ref.shape[1]
    m = d // 2

    @pl.when(i == 0)
    def _():
        load_columns(dims, where_ref, own, oth, first, m, w_scr, w_sem)
        gw_acc[...] = jnp.zeros_like(gw_acc)
        gg_ref[...] = jnp.zeros_like(gg_ref)
        gb_ref[...] = jnp.zeros_like(gb_ref)
        gpb_ref[...] = jnp.zeros_like(gpb_ref)
        for h in range(2):
            wait_columns(dims, w_scr, w_sem, h)

    dy = gn_ref[...]
    xhat, rstd = normalize(mid_ref[...])
    gg_ref[...] += jnp.sum(dy * xhat, axis=0, keepdims=True)
    gb_ref[...] += jnp.sum(dy, axis=0, keepdims=True)
    gm = c_ref[...].astype(F32) + ln_back(dy, xhat, rstd, vec_ref[4:5, :d])
    gm_ref[...] = gm
    pg = (BS * gm).astype(BF)
    gpb_ref[...] += jnp.sum(pg.astype(F32), axis=0, keepdims=True)
    gw_acc[...] += dot_0(a_ref[...], pg)
    ga = (dot_t(pg[:, :m], flat2(w_scr[0])) + dot_t(pg[:, m:], flat2(w_scr[1]))).astype(BF)
    ga_ref[...] = ga
    prod = ga.astype(F32) * a_ref[...].astype(F32)
    high = prod.astype(BF)
    low = (prod - high.astype(F32)).astype(BF)
    del_ref[...] = dot_t(ind_ref[...], high) + dot_t(ind_ref[...], low)

    @pl.when(i == pl.num_programs(0) - 1)
    def _():
        gw_ref[...] = gw_acc[...].astype(BF)


def proj_back_call(dims, where, gn, middle, cot, att, vec, own, oth):
    rows, d = middle.shape
    br = 256
    row = pl.BlockSpec((br, d), lambda i: (i, 0))
    ind = (jnp.arange(16)[:, None] == jnp.arange(d)[None, :] // HD).astype(BF)
    one = full_spec((1, d))
    vshape = jax.ShapeDtypeStruct((1, d), F32)
    return pl.pallas_call(
        functools.partial(proj_back_kernel, dims, len(own), 3 * d // 2),
        grid=(rows // br,),
        in_specs=[SMEM, row, row, row, row, full_spec(vec.shape), full_spec((16, d))] + [ANY] * (2 * len(own)),
        out_specs=[row, row, full_spec((d, d)), pl.BlockSpec((16, br), lambda i: (0, i)), one, one, one],
        out_shape=[
            jax.ShapeDtypeStruct((rows, d), F32),
            jax.ShapeDtypeStruct((rows, d), BF),
            jax.ShapeDtypeStruct((d, d), BF),
            jax.ShapeDtypeStruct((16, rows), F32),
            vshape, vshape, vshape,
        ],
        scratch_shapes=[pltpu.VMEM((d, d), F32)] + weight_scratch(dims, own[0].shape[1], d // 2),
        compiler_params=params(),
        cost_estimate=cost(4 * rows * d * d, rows * d * 16),
        name="proj_back",
    )(where, gn, middle, cot, att, vec, ind, *own, *oth)


def pair_back(j_ref, do_ref, lse_ref, del_ref, segr_ref, segc_ref, dj_ref, dk_acc, dv_acc):
    rows = j_ref.shape[0]
    scale = HD**-0.5
    k0, k1 = split_heads(j_ref[:, 128:256] * BF(scale))
    v0, v1 = split_heads(j_ref[:, 256:384])
    for q0, kv0, kv1, is_long in q_tiles(rows)[::-1]:
        q = j_ref[q0 : q0 + 256, 0:128]
        do = do_ref[q0 : q0 + 256, :]
        qh = split_heads(q)
        doh = split_heads(do)
        allowed = diag_allowed(is_long, segr_ref[...], segc_ref[...])
        low_p, low_s = [], []
        dq = None
        for h, (k, v) in enumerate(((k0, v0), (k1, v1))):
            s = dot_t(k[kv0:kv1], q)
            dp = dot_t(v[kv0:kv1], do)
            lse = lse_ref[0, h : h + 1, q0 : q0 + 256]
            dlt = del_ref[0, h : h + 1, q0 : q0 + 256]
            diag = jnp.where(allowed, s[q0 - kv0 : q0 - kv0 + 256], NEG)
            parts = [diag] if kv1 - kv0 == 256 else [s[: q0 - kv0], diag]
            probs = jnp.concatenate([jnp.exp(p - lse) for p in parts], axis=0)
            low_p.append(probs.astype(BF))
            ds = (probs * (dp - dlt)).astype(BF)
            low_s.append(ds)
            part = dot_0(k[kv0:kv1], ds)
            dq = part if dq is None else dq + part
        dj_ref[q0 : q0 + 256, 0:128] = dq.T.astype(BF)
        dv = dot(jnp.concatenate(low_p, axis=1), jnp.concatenate(doh, axis=0))
        dk = dot(jnp.concatenate(low_s, axis=1), jnp.concatenate(qh, axis=0))
        if q0 in (LONG, LONG - 256):
            dk_acc[kv0:kv1, :] = dk
            dv_acc[kv0:kv1, :] = dv
        else:
            dk_acc[kv0:kv1, :] += dk
            dv_acc[kv0:kv1, :] += dv
    dj_ref[:, 128:256] = (dk_acc[...] * scale).astype(BF)
    dj_ref[:, 256:384] = dv_acc[...].astype(BF)


def attn_back_kernel(
    dims, count, group0, groups, last, devices, where_ref, j_ref, do_ref, lse_ref, del_ref, segr_ref, segc_ref,
    x_ref, vec_ref, *refs,
):
    own, oth, refs = refs[:count], refs[count : 2 * count], refs[2 * count :]
    if last:
        gnin_ref, qvin_ref, gm_ref, gfb_ref, gob_ref, gg2_ref, gb2_ref, gpb_ref = refs[:8]
        gx_ref, g_own, g_oth = refs[8:11]
        refs = refs[11:]
    else:
        gwp_ref, gn_out, qv_out, g_own, g_oth = refs[:5]
        refs = refs[5:]
    w_scr, w_sem, nt_scr, gn_scr, dj_scr, dk_acc, dv_acc, gw_scr, gw_sem, e_scr, e_sem, qv_scr = refs
    i = pl.program_id(0)
    rows, d = x_ref.shape
    half, group = lax.rem(i, 2), i // 2
    br = 256
    extra_at = groups * 384

    @pl.when(i == 0)
    def _():
        load_columns(dims, where_ref, own, oth, group0 * 384, groups * 384, w_scr, w_sem)
        if not last:
            for h in range(2):
                e_scr[h] = gwp_ref[:, h * (d // 2) : (h + 1) * (d // 2)].reshape(e_scr.shape[1:])
                store_columns(dims, where_ref, e_scr.at[h], g_own, g_oth, h, extra_at, d // 2, e_sem.at[h])
            qv_scr[...] = jnp.zeros_like(qv_scr)
            gn_scr[...] = jnp.zeros_like(gn_scr)
        else:
            qv_scr[...] = qvin_ref[...]
            gn_scr[...] = gnin_ref[...]
        for r in range(0, rows, br):
            xhat, _ = normalize(x_ref[r : r + br, :].astype(F32))
            nt_scr[:, r : r + br] = (xhat * vec_ref[0:1, :d] + vec_ref[1:2, :d]).astype(BF).T
        for h in range(2):
            wait_columns(dims, w_scr, w_sem, h)

    pair_back(j_ref, do_ref, lse_ref, del_ref, segr_ref, segc_ref, dj_scr, dk_acc, dv_acc)
    first = pl.multiple_of(group * 384, 128)
    dj = dj_scr[...]
    pair = group0 * 2 + i
    qv_scr[:, pl.ds(pl.multiple_of(pair * 128, 128), 128)] = jnp.sum(
        dj[:, 0:128].astype(F32), axis=0, keepdims=True
    )
    qv_scr[:, pl.ds(pl.multiple_of(d + pair * 128, 128), 128)] = jnp.sum(
        dj[:, 256:384].astype(F32), axis=0, keepdims=True
    )
    gw_scr[i] = dot(nt_scr[...], dj).astype(BF).reshape(gw_scr.shape[1:])
    store_columns(dims, where_ref, gw_scr.at[i], g_own, g_oth, half, first, 384, gw_sem.at[i])
    w = flat2(w_scr[half, :, :, :, :, pl.ds(first, 384)])
    for r in range(0, rows, br):
        gn_scr[r : r + br, :] += dot_t(dj[r : r + br, :], w)

    @pl.when(i == 2 * groups - 1)
    def _():
        if last:
            gg = jnp.zeros((1, d), F32)
            gb = jnp.zeros((1, d), F32)
            for r in range(0, rows, br):
                rr = slice(r, r + br)
                xhat, rstd = normalize(x_ref[rr, :].astype(F32))
                dy = gn_scr[rr, :]
                gg += jnp.sum(dy * xhat, axis=0, keepdims=True)
                gb += jnp.sum(dy, axis=0, keepdims=True)
                gx_ref[rr, :] = (gm_ref[rr, :] + ln_back(dy, xhat, rstd, vec_ref[0:1, :d])).astype(BF)
            table = pack_vectors(
                {
                    "g1": gg, "b1": gb, "qv": qv_scr[...], "fb": gfb_ref[...], "pb": gpb_ref[...],
                    "g2": gg2_ref[...], "b2": gb2_ref[...], "ob": gob_ref[...],
                },
                d, devices,
            ).reshape(e_scr.shape[1:])
            for h in range(2):
                e_scr[h] = table
                store_columns(dims, where_ref, e_scr.at[h], g_own, g_oth, h, extra_at, 128, e_sem.at[h])
        else:
            gn_out[...] = gn_scr[...]
            qv_out[...] = qv_scr[...]
        for b in range(2 * groups):
            wait_store(dims, gw_scr.at[b], g_own, 0, 384, gw_sem.at[b])
        for h in range(2):
            wait_store(dims, e_scr.at[h], g_own, extra_at, e_scr.shape[-1], e_sem.at[h])


def attn_back_call(dims, where, joined, ga, lse, delta, seg_row, seg_col, x, vec, own, oth, group0, groups, extra, last, devices):
    rows, d = x.shape
    n = own[0].shape[1]
    pairs = d // 128
    act = full_spec((rows, d))
    one = full_spec((1, d))
    wide = d // 2 if not last else 128
    stat = pl.BlockSpec((1, 2, rows), lambda i: (group0 * 2 + i, 0, 0))
    arrays, count = len(own), dims[1] * dims[2]
    piece = jax.ShapeDtypeStruct((count, dims[0], n, groups * 384 + wide), BF)
    in_specs = [
        SMEM,
        pl.BlockSpec((rows, 384), lambda i: (0, pair_block(group0 * 2 + i, pairs))),
        pl.BlockSpec((rows, 128), lambda i: (0, group0 * 2 + i)),
        stat, stat, full_spec((1, 256)), full_spec((256, 1)), act, full_spec(vec.shape),
    ] + [ANY] * (2 * arrays)
    if last:
        in_specs += [act, full_spec((1, 2 * d)), act, full_spec((1, 4 * d))] + [one] * 4
        out_specs = [act, ANY, ANY]
        out_shape = [jax.ShapeDtypeStruct((rows, d), BF), piece, piece]
    else:
        in_specs += [full_spec((d, d))]
        out_specs = [act, full_spec((1, 2 * d)), ANY, ANY]
        out_shape = [jax.ShapeDtypeStruct((rows, d), F32), jax.ShapeDtypeStruct((1, 2 * d), F32), piece, piece]
    return pl.pallas_call(
        functools.partial(attn_back_kernel, dims, arrays, group0, groups, last, devices),
        grid=(2 * groups,),
        in_specs=in_specs,
        out_specs=out_specs,
        out_shape=out_shape,
        scratch_shapes=weight_scratch(dims, n, groups * 384)
        + [
            pltpu.VMEM((d, rows), BF), pltpu.VMEM((rows, d), F32), pltpu.VMEM((rows, 384), BF),
            pltpu.VMEM((rows, 128), F32), pltpu.VMEM((rows, 128), F32),
            pltpu.VMEM((2 * groups,) + dims + (n, 384), BF), pltpu.SemaphoreType.DMA((2 * groups, count, dims[0])),
            pltpu.VMEM((2,) + dims + (n, wide), BF), pltpu.SemaphoreType.DMA((2, count, dims[0])),
            pltpu.VMEM((1, 2 * d), F32),
        ],
        compiler_params=params(),
        cost_estimate=cost(groups * 20e9, 12e6, 5.5e6),
        name="attn_back_last" if last else "attn_back",
    )(where, joined, ga, lse, delta, seg_row, seg_col, x, vec, *own, *oth, *extra)


def pack_plan(counts, rows):
    c = [counts[i] for i in range(counts.shape[0])]
    ends, run = [], jnp.int32(0)
    for v in c:
        run = run + v
        ends.append(run)
    start = jnp.int32(0)
    for i in range(len(c) - 1):
        start = jnp.where(c[i] == LONG, ends[i] - c[i], start)
    rolled = jnp.arange(rows, dtype=jnp.int32)
    pos = rolled + start
    pos = jnp.where(pos >= rows, pos - rows, pos)
    seg = functools.reduce(jnp.add, [(pos >= e).astype(jnp.int32) for e in ends])
    valid = seg < len(c) - 1
    seg = jnp.where(valid, seg, 1000 + rolled)
    return start, seg[LONG:], valid


def roll_rows(array, shift):
    return lax.dynamic_slice_in_dim(jnp.concatenate([array, array], axis=0), shift, array.shape[0])


def half_columns(w, h, joined=False):
    r, cols = w.shape
    if not joined:
        return w[:, h * (cols // 2) : (h + 1) * (cols // 2)]
    pairs = cols // 384
    parts = w.reshape(r, 3, pairs // 2, 2, 128)[:, :, :, h]
    return jnp.swapaxes(parts, 1, 2).reshape(r, cols // 2)


def join_columns(left, right):
    r, m = left.shape
    both = jnp.stack([v.reshape(r, m // 384, 3, 128) for v in (left, right)], axis=2)
    return both.transpose(0, 3, 1, 2, 4).reshape(r, 2 * m)


def add_all(values):
    return functools.reduce(jnp.add, [v.astype(F32) for v in values])


class Plain:
    def __init__(self, dp, fsdp):
        self.dims = (1, 1, 1)
        index = lax.axis_index("dp") * fsdp + lax.axis_index("fsdp")
        self.ci = index % 2

    def where(self):
        zero = jnp.zeros((), jnp.int32)
        return jnp.stack([zero, zero, zero, self.ci.astype(jnp.int32)])

    def pick(self, pair):
        return jnp.where(self.ci == 0, pair[0], pair[1]), jnp.where(self.ci == 0, pair[1], pair[0])

    def gather(self, w_qkv, w_proj, table, w_fc, w_out):
        whole = lambda v: lax.all_gather(v, AXES, axis=0, tiled=True)
        attn = whole(jnp.concatenate([w_qkv, w_proj, table], axis=1))
        cut = w_qkv.shape[1], w_qkv.shape[1] + w_proj.shape[1]
        fc, out = whole(w_fc), whole(w_out)
        first = [
            jnp.concatenate(
                [half_columns(attn[:, : cut[0]], h, True), half_columns(attn[:, cut[0] : cut[1]], h), attn[:, cut[1] :]],
                axis=1,
            )
            for h in range(2)
        ]
        second = [half_columns(fc, h) for h in range(2)]
        third = [out[: out.shape[0] // 2], out[out.shape[0] // 2 :]]
        listed = []
        for pair in (first, second, third):
            own, oth = self.pick(pair)
            listed.append(([own[None]], [oth[None]]))
        return listed

    def scatter(self, own, oth, rows=False):
        pair = self.pick([own[0, 0], oth[0, 0]])
        if rows:
            return lax.psum_scatter(jnp.concatenate(pair, axis=0), AXES, scatter_dimension=0, tiled=True).astype(F32)
        m = pair[0].shape[1]
        mine = lax.psum_scatter(jnp.concatenate(pair, axis=1), AXES, scatter_dimension=0, tiled=True).astype(F32)
        return mine[:, :m], mine[:, m:]


class Chips:
    def __init__(self, dp, fsdp):
        x_n, z_n = fsdp // 2, 4
        self.dims = (z_n, dp // z_n, x_n)
        index = lax.axis_index("dp") * fsdp + lax.axis_index("fsdp")
        self.ci = index % 2
        self.at = (index // (2 * x_n * self.dims[1]), (index // (2 * x_n)) % self.dims[1], (index // 2) % x_n, self.ci)

    def where(self):
        return jnp.stack(self.at).astype(jnp.int32)

    def pick(self, pair):
        return jnp.where(self.ci == 0, pair[0], pair[1]), jnp.where(self.ci == 0, pair[1], pair[0])

    def send(self, array, dz=0, dy=0, dx=0, dc=0):
        z_n, y_n, x_n = self.dims
        pairs = []
        for z in range(z_n):
            for y in range(y_n):
                for x in range(x_n):
                    for c in range(2):
                        here = ((z * y_n + y) * x_n + x) * 2 + c
                        there = (((z + dz) % z_n * y_n + (y + dy) % y_n) * x_n + (x + dx) % x_n) * 2 + (c + dc) % 2
                        pairs.append((here, there))
        return lax.ppermute(array, AXES, pairs)

    def cut_halves(self, w_qkv, w_proj, table, w_fc):
        halves = [
            jnp.concatenate(
                [half_columns(w_qkv, h, True), half_columns(w_proj, h), table, half_columns(w_fc, h)], axis=1
            )
            for h in range(2)
        ]
        keep, give = self.pick(halves)
        rows = jnp.concatenate(self.pick([keep, self.send(give, dc=1)]), axis=0)
        cut = (w_qkv.shape[1] + w_proj.shape[1]) // 2 + 128
        return rows[:, :cut], rows[:, cut:]

    def along_z(self, piece):
        return jnp.stack([piece] + [self.send(piece, dz=-k) for k in range(1, self.dims[0])])

    def swap(self, arrays):
        return [self.send(v, dc=1) for v in arrays]

    def add_core(self, own, theirs):
        return [add_all([own[i], theirs[i]]).astype(BF) for i in range(own.shape[0])]

    def add_chips(self, block, arrived):
        return [add_all([block[j]] + [a[j] for a in arrived]).astype(BF) for j in range(self.dims[0])]

    def sum_z(self, column):
        return add_all([column[0]] + [self.send(column[j], dz=j) for j in range(1, self.dims[0])])

    def rows_back(self, total):
        n = total.shape[0] // 2
        mine, give = self.pick([total[:n], total[n:]])
        return self.pick([mine, self.send(give, dc=1)])


def together(*trees):
    return lax.optimization_barrier(trees)


def prepare(tokens, lengths, cotangent):
    start, seg, valid = pack_plan(lengths[0], tokens.shape[0])
    x = roll_rows(tokens, start)
    cot = jnp.where(valid[:, None], roll_rows(cotangent, start), BF(0))
    return start, seg[None, :], seg[:, None], x, cot


def vector_table(r, ln1_gain, ln1_bias, qv_bias, proj_bias, ln2_gain, ln2_bias, fc_bias, out_bias):
    flat = [
        jnp.concatenate([ln1_gain, ln1_bias, qv_bias]), fc_bias,
        jnp.concatenate([proj_bias, ln2_gain, ln2_bias, out_bias]),
    ]
    return jnp.pad(jnp.stack(flat), ((0, r - 3), (0, 128 - 4 * r)))


def results(r, start, out, gx, s_fc, s_out, s_one, s_two):
    rows = out.shape[0]
    wide = 2 * 384
    s_qkv = join_columns(*[jnp.concatenate([a[:, :wide], b[:, :-128]], axis=1) for a, b in zip(s_one, s_two)])
    s_proj = jnp.concatenate([v[:, wide:] for v in s_one], axis=1)
    small = s_two[0][:, -128:]
    row0, row1, row2 = [small[k, : 4 * r] for k in range(3)]
    restore = rows - start
    return (
        roll_rows(out, restore), roll_rows(gx, restore),
        row0[:r], row0[r : 2 * r], s_qkv, row0[2 * r :], s_proj, row2[:r],
        row2[r : 2 * r], row2[2 * r : 3 * r], jnp.concatenate(s_fc, axis=1), row1, s_out, row2[3 * r :],
    )


def block_plain(
    links, tokens, lengths, ln1_gain, ln1_bias, w_qkv, qv_bias, w_proj, proj_bias, ln2_gain, ln2_bias,
    w_fc, fc_bias, w_out, out_bias, cotangent,
):
    rows, d = tokens.shape
    r = w_qkv.shape[0]
    devices = d // r
    dims, where = links.dims, links.where()
    table = vector_table(r, ln1_gain, ln1_bias, qv_bias, proj_bias, ln2_gain, ln2_bias, fc_bias, out_bias)
    attn_w, fc_w, out_w = links.gather(w_qkv, w_proj, table, w_fc, w_out)
    start, seg_row, seg_col, x, cot = prepare(tokens, lengths, cotangent)
    joined, vec = qkv_call(dims, where, x, *attn_w, devices)
    att, lse = attn_call(joined, seg_row, seg_col)
    middle, normed_two = proj_call(dims, where, x, att, vec, *attn_w)
    out, gn, gfb, gob, gf_own, gf_oth, go_own, go_oth = mlp_call(
        dims, where, normed_two, cot, middle, vec, fc_w, out_w
    )
    s_fc = links.scatter(gf_own, gf_oth)
    s_out = links.scatter(go_own, go_oth, rows=True)
    gm, ga, gw_proj, delta, gg2, gb2, gpb = proj_back_call(dims, where, gn, middle, cot, att, vec, *attn_w)
    delta = delta[: d // HD].reshape(d // 128, 2, rows)
    shared = (dims, where, joined, ga, lse, delta, seg_row, seg_col, x, vec, *attn_w)
    gn1, qv1, g_own, g_oth = attn_back_call(*shared, 0, 2, (gw_proj,), False, devices)
    s_one = links.scatter(g_own, g_oth)
    gx, g_own, g_oth = attn_back_call(
        *shared, 2, d // 256 - 2, (gn1, qv1, gm, gfb, gob, gg2, gb2, gpb), True, devices
    )
    s_two = links.scatter(g_own, g_oth)
    return results(r, start, out, gx, s_fc, s_out, s_one, s_two)


def block_chips(
    links, tokens, lengths, ln1_gain, ln1_bias, w_qkv, qv_bias, w_proj, proj_bias, ln2_gain, ln2_bias,
    w_fc, fc_bias, w_out, out_bias, cotangent,
):
    rows, d = tokens.shape
    r = w_qkv.shape[0]
    devices = d // r
    dims, where, send = links.dims, links.where(), links.send
    table = vector_table(r, ln1_gain, ln1_bias, qv_bias, proj_bias, ln2_gain, ln2_bias, fc_bias, out_bias)
    a, b = links.cut_halves(w_qkv, w_proj, table, w_fc)
    start, seg_row, seg_col, x, cot = prepare(tokens, lengths, cotangent)

    a0 = links.along_z(a)
    a0, b, c = together(a0, b, w_out)
    ax, ay = send(a0, dx=1), send(a0, dy=1)
    b0 = links.along_z(b)
    ax, ay, b0, c = together(ax, ay, b0, c)
    ad = [send(ax[:2], dy=1), send(ay[2:], dx=1)]
    a_oth = links.swap([a0, ax, ay])
    c0 = links.along_z(c)
    ad, a_oth, c0, b0 = together(ad, a_oth, c0, b0)
    attn_w = [a0, ax, ay] + ad, a_oth + links.swap(ad)
    attn_w, b0, c0, x = together(attn_w, b0, c0, x)

    joined, vec = qkv_call(dims, where, x, *attn_w, devices)
    bx, by = send(b0, dx=1), send(b0, dy=1)
    joined, bx, by, c0 = together(joined, bx, by, c0)

    att, lse = attn_call(joined, seg_row, seg_col)
    bd = send(bx, dy=1)
    cx, cy = send(c0, dx=1), send(c0, dy=1)
    b_oth = links.swap([b0, bx, by])
    att, bd, cx, cy, b_oth = together(att, bd, cx, cy, b_oth)

    middle, normed_two = proj_call(dims, where, x, att, vec, *attn_w)
    cd = send(cy, dx=1)
    b_oth = b_oth + links.swap([bd])
    c_oth = links.swap([c0, cx, cy])
    normed_two, cd, b_oth, c_oth = together(normed_two, cd, b_oth, c_oth)
    c_oth = c_oth + links.swap([cd])

    out, gn, gfb, gob, gf_own, gf_oth, go_own, go_oth = mlp_call(
        dims, where, normed_two, cot, middle, vec, ([b0, bx, by, bd], b_oth), ([c0, cx, cy, cd], c_oth)
    )

    gm, ga, gw_proj, delta, gg2, gb2, gpb = proj_back_call(dims, where, gn, middle, cot, att, vec, *attn_w)
    delta = delta[: d // HD].reshape(d // 128, 2, rows)
    gf_oth, go_oth = links.swap([gf_oth, go_oth])
    fc = links.add_core(gf_own, gf_oth)
    wo = links.add_core(go_own, go_oth)
    ga, fc, wo = together(ga, fc, wo)

    shared = (dims, where, joined, ga, lse, delta, seg_row, seg_col, x, vec, *attn_w)
    gn1, qv1, g_own, g_oth = attn_back_call(*shared, 0, 2, (gw_proj,), False, devices)
    fd, fy = send(fc[3], dy=1), send(fc[2], dy=1)
    wd, wx = send(wo[3], dx=1), send(wo[1], dx=1)
    fcx = add_all([fc[1], fd]).astype(BF)
    woy = add_all([wo[2], wd]).astype(BF)
    gn1, g_own, g_oth, fcx, woy, fy, wx = together(gn1, g_own, g_oth, fcx, woy, fy, wx)

    gx, h_own, h_oth = attn_back_call(
        *shared, 2, d // 256 - 2, (gn1, qv1, gm, gfb, gob, gg2, gb2, gpb), True, devices
    )
    fx, wy = send(fcx, dx=1), send(woy, dy=1)
    (g_oth,) = links.swap([g_oth])
    fc = links.add_chips(fc[0], [fx, fy])
    wo = links.add_chips(wo[0], [wx, wy])
    one = links.add_core(g_own, g_oth)
    gx, h_own, h_oth, fc, wo, one = together(gx, h_own, h_oth, fc, wo, one)

    fc, wo = links.sum_z(fc), links.sum_z(wo)
    one = links.add_chips(one[0], [send(one[1], dx=1), send(one[2], dy=1), send(one[3], dx=1, dy=1)])
    (h_oth,) = links.swap([h_oth])
    two = links.add_core(h_own, h_oth)
    two, one, fc, wo = together(two, one, fc, wo)
    two = links.add_chips(two[0], [send(two[1], dx=1), send(two[2], dy=1), send(two[3], dx=1, dy=1)])
    one = links.sum_z(one)
    s_fc = links.rows_back(fc)
    two, one, s_fc = together(two, one, s_fc)
    s_two = links.rows_back(links.sum_z(two))
    s_one = links.rows_back(one)
    return results(r, start, out, gx, s_fc, wo, s_one, s_two)


def solution(mesh):
    dp, fsdp = mesh.shape["dp"], mesh.shape["fsdp"]

    def per_device(*args):
        if (dp, fsdp) == (8, 4) and args[4].shape[0] % 8 == 0:
            return block_chips(Chips(dp, fsdp), *args)
        return block_plain(Plain(dp, fsdp), *args)

    row, vec = P(AXES, None), P(AXES)
    in_specs = (row, row, vec, vec, row, vec, row, vec, vec, vec, row, vec, row, vec, row)
    out_specs = (row, row, vec, vec, row, vec, row, vec, vec, vec, row, vec, row, vec)
    return jax.shard_map(
        per_device, mesh=mesh, in_specs=in_specs, out_specs=out_specs, check_vma=False
    )
```

```python
import functools
import math

import jax
import jax.numpy as jnp
from jax import lax
from jax.experimental import pallas as pl
from jax.experimental.pallas import tpu as pltpu
from jax.sharding import PartitionSpec as P

HD = 64
LONG = 768
EPS = 1e-05
BS = 1.0 / math.sqrt(48.0)
NEG = -1e30
F32 = jnp.float32
BF = jnp.bfloat16
VMEM_LIMIT = 58 * 1024 * 1024
AXES = ("dp", "fsdp")
GC0 = math.sqrt(2.0 / math.pi)
GC1 = 0.044715


def dot(a, b):
    return lax.dot_general(a, b, (((1,), (0,)), ((), ())), preferred_element_type=F32)


def dot_t(a, b):
    return lax.dot_general(a, b, (((1,), (1,)), ((), ())), preferred_element_type=F32)


def dot_0(a, b):
    return lax.dot_general(a, b, (((0,), (0,)), ((), ())), preferred_element_type=F32)


def params(grid_len=1):
    return pltpu.CompilerParams(
        dimension_semantics=("arbitrary",) * grid_len, vmem_limit_bytes=VMEM_LIMIT
    )


def cost(flops, nbytes, trans=0):
    return pl.CostEstimate(flops=int(flops), bytes_accessed=int(nbytes), transcendentals=int(trans))


def normalize(values):
    centred = values - jnp.mean(values, axis=-1, keepdims=True)
    rstd = lax.rsqrt(jnp.mean(centred * centred, axis=-1, keepdims=True) + EPS)
    return centred * rstd, rstd


def ln_back(dy, xhat, rstd, gain):
    dx = dy * gain
    m1 = jnp.mean(dx, axis=-1, keepdims=True)
    m2 = jnp.mean(dx * xhat, axis=-1, keepdims=True)
    return rstd * (dx - m1 - xhat * m2)


def full_spec(shape):
    return pl.BlockSpec(shape, lambda *_: (0,) * len(shape), pipeline_mode=pl.Buffered(1))


def lane_masks(rows):
    lane = lax.broadcasted_iota(jnp.int32, (rows, 128), 1)
    return lane < HD


def split_heads(block):
    low = lane_masks(block.shape[0])
    zero = jnp.zeros_like(block)
    return jnp.where(low, block, zero), jnp.where(low, zero, block)


def q_tiles(rows):
    tiles = [(r, 0, r + 256, True) for r in range(0, LONG, 256)]
    tiles += [(LONG, LONG, rows, False)]
    return tiles


def diag_allowed(is_long, seg_row, seg_col):
    kv = lax.broadcasted_iota(jnp.int32, (256, 256), 0)
    qp = lax.broadcasted_iota(jnp.int32, (256, 256), 1)
    allowed = kv <= qp
    if not is_long:
        allowed = allowed & (seg_col == seg_row)
    return allowed


def attn_kernel(q_ref, k_ref, v_ref, segr_ref, segc_ref, o_ref, lse_ref):
    rows = q_ref.shape[0]
    k0, k1 = split_heads(k_ref[...] * BF(HD**-0.5))
    v0, v1 = split_heads(v_ref[...])
    for q0, kv0, kv1, is_long in q_tiles(rows):
        q = q_ref[q0 : q0 + 256, :]
        allowed = diag_allowed(is_long, segr_ref[...], segc_ref[...])
        outs = []
        for h, (k, v) in enumerate(((k0, v0), (k1, v1))):
            s = dot_t(k[kv0:kv1], q)
            diag = jnp.where(allowed, s[q0 - kv0 : q0 - kv0 + 256], NEG)
            parts = [diag] if kv1 - kv0 == 256 else [s[: q0 - kv0], diag]
            top = functools.reduce(
                jnp.maximum, [jnp.max(p, axis=0, keepdims=True) for p in parts]
            )
            exps = [jnp.exp(p - top) for p in parts]
            total = functools.reduce(
                jnp.add, [jnp.sum(e, axis=0, keepdims=True) for e in exps]
            )
            lse_ref[0, h : h + 1, q0 : q0 + 256] = top + jnp.log(total)
            probs = jnp.concatenate([e.astype(BF) for e in exps], axis=0)
            outs.append(dot_0(v[kv0:kv1], probs) * (1.0 / total))
        o_ref[q0 : q0 + 256, :] = (outs[0] + outs[1]).T.astype(BF)


def attn_call(joined, seg_row, seg_col, group0, groups):
    rows = joined.shape[0]
    pairs = joined.shape[1] // 384
    at = lambda t: pl.BlockSpec((rows, 128), lambda p: (0, pair_block(group0 * 2 + p, pairs) * 3 + t))
    return pl.pallas_call(
        attn_kernel,
        grid=(2 * groups,),
        in_specs=[at(0), at(1), at(2), full_spec((1, 256)), full_spec((256, 1))],
        out_specs=[
            pl.BlockSpec((rows, 128), lambda p: (0, p)),
            pl.BlockSpec((1, 2, rows), lambda p: (p, 0, 0)),
        ],
        out_shape=[
            jax.ShapeDtypeStruct((rows, groups * 256), BF),
            jax.ShapeDtypeStruct((2 * groups, 2, rows), F32),
        ],
        compiler_params=params(),
        cost_estimate=cost(groups * 8e9, 8e6, 5.5e6),
        name="attn",
    )(joined, joined, joined, seg_row, seg_col)


def pair_block(p, pairs):
    return (p % 2) * (pairs // 2) + p // 2


ANY = pl.BlockSpec(memory_space=pl.ANY)
SMEM = pl.BlockSpec(memory_space=pltpu.SMEM)


def local_copy(src, dst, sem):
    return pltpu.make_async_copy(src, dst, sem)


def chips_of(dims, where_ref):
    z_n, y_n, x_n = dims
    zi, yi, xi = [where_ref[i] for i in range(3)]
    for i in range(y_n * x_n):
        for j in range(z_n):
            yield i, j, lax.rem(zi + j, z_n), lax.rem(yi + i // x_n, y_n), lax.rem(xi + i % x_n, x_n)


def piece_at(dims, arrays, i, j):
    at = i * dims[0] + j
    for a in arrays:
        if at < a.shape[0]:
            return a.at[at]
        at -= a.shape[0]


def load_columns(dims, where_ref, own, oth, first, cols, dst, sem):
    ci = where_ref[3]
    for i, j, z, y, x in chips_of(dims, where_ref):
        for half, src in ((ci, own), (1 - ci, oth)):
            block = piece_at(dims, src, i, j).at[:, pl.ds(first, cols)]
            local_copy(block, dst.at[half, z, y, x], sem.at[half, z, y, x]).start()


def wait_columns(dims, dst, sem, half):
    for z in range(dims[0]):
        for y in range(dims[1]):
            for x in range(dims[2]):
                block = dst.at[half, z, y, x]
                local_copy(block, block, sem.at[half, z, y, x]).wait()


def flat2(value):
    return value.reshape(-1, value.shape[-1])


def store_columns(dims, where_ref, src, own, oth, half, first, cols, sem):
    ci = where_ref[3]
    for other, out in ((False, own), (True, oth)):

        @pl.when((half != ci) if other else (half == ci))
        def _():
            for i, j, z, y, x in chips_of(dims, where_ref):
                local_copy(src.at[z, y, x], out.at[i, j, :, pl.ds(first, cols)], sem.at[i, j]).start()


def wait_store(dims, src, out, first, cols, sem):
    for i in range(dims[1] * dims[2]):
        for j in range(dims[0]):
            local_copy(src.at[0, 0, 0], out.at[i, j, :, pl.ds(first, cols)], sem.at[i, j]).wait()


def weight_scratch(dims, n, cols):
    return [
        pltpu.VMEM((2,) + dims + (n, cols), BF),
        pltpu.SemaphoreType.DMA((2,) + dims),
    ]


def vector_plan(d, devices):
    r = d // devices
    return {
        "g1": (0, 0, r), "b1": (0, r, r), "qv": (0, 2 * r, 2 * r), "fb": (1, 0, 4 * r),
        "pb": (2, 0, r), "g2": (2, r, r), "b2": (2, 2 * r, r), "ob": (2, 3 * r, r),
    }


VECTOR_ROWS = {"g1": 0, "b1": 1, "qv": 2, "pb": 3, "g2": 4, "b2": 5, "fb": 6, "ob": 7}


def owner_of(shape, size, axis):
    c = lax.broadcasted_iota(jnp.int32, shape, axis).astype(F32)
    owner = jnp.floor((c + 0.5) * (1.0 / size))
    return owner, c - owner * size


def row_pick(devices, d, row):
    r = d // devices
    at = lax.broadcasted_iota(jnp.int32, (devices, d), 1)
    dev = lax.broadcasted_iota(jnp.int32, (devices, d), 0)
    return (at == dev * r + row).astype(BF)


def vector_maps(devices, n, first, size):
    owner, place = owner_of((devices, n), size, 1)
    mine = owner == lax.broadcasted_iota(jnp.int32, (devices, n), 0).astype(F32)
    _, place = owner_of((128, n), size, 1)
    spot = (place + first == lax.broadcasted_iota(jnp.int32, (128, n), 0).astype(F32)).astype(BF)
    return mine, spot


def unpack_vectors(table, d, devices, out_ref):
    plan = vector_plan(d, devices)
    picked = [dot(row_pick(devices, d, k), table).astype(BF) for k in range(3)]
    for name, i in VECTOR_ROWS.items():
        k, first, size = plan[name]
        n = size * devices
        mine, spot = vector_maps(devices, n, first, size)
        spread = dot(picked[k], spot)
        out_ref[i : i + 1, :n] = jnp.sum(jnp.where(mine, spread, 0.0), axis=0, keepdims=True)


def pack_vectors(rows, d, devices):
    plan = vector_plan(d, devices)
    parts = [None] * 3
    for name in VECTOR_ROWS:
        k, first, size = plan[name]
        n = size * devices
        mine, spot = vector_maps(devices, n, first, size)
        part = dot_t(jnp.where(mine, rows[name], 0.0).astype(BF), spot)
        parts[k] = part if parts[k] is None else parts[k] + part
    total = None
    for k in range(3):
        piece = dot_0(row_pick(devices, d, k), parts[k].astype(BF))
        total = piece if total is None else total + piece
    return total.astype(BF)


def cut_kernel(where_ref, w_ref, p_ref, t_ref, keep_ref, give_ref):
    ci = where_ref[3]
    pairs = w_ref.shape[1] // 384
    half = p_ref.shape[1] // 2
    for h in range(2):
        for other, out in ((False, keep_ref), (True, give_ref)):

            @pl.when((ci != h) if other else (ci == h))
            def _():
                at = 0
                for p in range(h, pairs, 2):
                    for t in range(3):
                        first = (t * pairs + p) * 128
                        out[:, at : at + 128] = w_ref[:, first : first + 128]
                        at += 128
                out[:, at : at + half] = p_ref[:, h * half : (h + 1) * half]
                out[:, at + half :] = t_ref[...]


def cut_call(where, w_qkv, w_proj, table):
    r = w_qkv.shape[0]
    cols = (w_qkv.shape[1] + w_proj.shape[1]) // 2 + 128
    shapes = [full_spec(v.shape) for v in (w_qkv, w_proj, table)]
    return pl.pallas_call(
        cut_kernel,
        grid=(1,),
        in_specs=[SMEM] + shapes,
        out_specs=[full_spec((r, cols))] * 2,
        out_shape=[jax.ShapeDtypeStruct((r, cols), BF)] * 2,
        compiler_params=params(),
        cost_estimate=cost(0, 4 * r * cols),
        name="cut",
    )(where, w_qkv, w_proj, table)


def qkv_kernel(dims, count, devices, where_ref, x_ref, *refs):
    own, oth = refs[:count], refs[count : 2 * count]
    o_ref, vec_ref, w_scr, w_sem, t_scr, t_sem, n_scr, bias_scr = refs[2 * count :]
    rows, d = x_ref.shape
    cols = w_scr.shape[-1]
    table_at = own[0].shape[-1] - 128
    step = pl.program_id(0)

    @pl.when(step == 0)
    def _():
        for i, j, z, y, x in chips_of(dims, where_ref):
            block = piece_at(dims, own, i, j).at[:, pl.ds(table_at, 128)]
            local_copy(block, t_scr.at[z, y, x], t_sem.at[z, y, x]).start()
        load_columns(dims, where_ref, own, oth, 0, cols, w_scr, w_sem)
        for z in range(dims[0]):
            for y in range(dims[1]):
                for x in range(dims[2]):
                    block = t_scr.at[z, y, x]
                    local_copy(block, block, t_sem.at[z, y, x]).wait()
        vec_ref[...] = jnp.zeros_like(vec_ref)
        unpack_vectors(flat2(t_scr[...]), d, devices, vec_ref)
        zero = jnp.zeros((1, 128), F32)
        pairs = d // 128
        for p in range(pairs):
            at = pair_block(p, pairs) * 384
            half, at = at // cols, at % cols
            bias_scr[half, :, at : at + 128] = vec_ref[2:3, p * 128 : (p + 1) * 128]
            bias_scr[half, :, at + 128 : at + 256] = zero
            bias_scr[half, :, at + 256 : at + 384] = vec_ref[2:3, d + p * 128 : d + (p + 1) * 128]
        for r in range(0, rows, 256):
            xhat, _ = normalize(x_ref[r : r + 256, :].astype(F32))
            n_scr[r : r + 256, :] = (xhat * vec_ref[0:1, :d] + vec_ref[1:2, :d]).astype(BF)
        wait_columns(dims, w_scr, w_sem, 0)

    @pl.when(step == 1)
    def _():
        wait_columns(dims, w_scr, w_sem, 1)

    w = flat2(w_scr[step])
    for r in range(0, rows, 256):
        o_ref[r : r + 256, :] = (dot(n_scr[r : r + 256, :], w) + bias_scr[step]).astype(BF)


def qkv_call(dims, where, x, own, oth, devices):
    rows, d = x.shape
    n = own[0].shape[1]
    cols = 3 * d // 2
    return pl.pallas_call(
        functools.partial(qkv_kernel, dims, len(own), devices),
        grid=(2,),
        in_specs=[SMEM, full_spec((rows, d))] + [ANY] * (2 * len(own)),
        out_specs=[pl.BlockSpec((rows, cols), lambda j: (0, j)), full_spec((8, 4 * d))],
        out_shape=[
            jax.ShapeDtypeStruct((rows, 2 * cols), BF), jax.ShapeDtypeStruct((8, 4 * d), F32)
        ],
        scratch_shapes=weight_scratch(dims, n, cols)
        + [
            pltpu.VMEM(dims + (n, 128), BF), pltpu.SemaphoreType.DMA(dims),
            pltpu.VMEM((rows, d), BF), pltpu.VMEM((2, 1, cols), F32),
        ],
        compiler_params=params(),
        cost_estimate=cost(4 * rows * d * cols, rows * d * 8 + d * cols * 4),
        name="qkv",
    )(where, x, *own, *oth)


def proj_kernel(dims, count, first, where_ref, x_ref, a0_ref, a1_ref, vec_ref, *refs):
    own, oth = refs[:count], refs[count : 2 * count]
    mid_ref, n_ref, w_scr, w_sem = refs[2 * count :]
    d = x_ref.shape[1]

    @pl.when(pl.program_id(0) == 0)
    def _():
        load_columns(dims, where_ref, own, oth, first, w_scr.shape[-1], w_scr, w_sem)
        for h in range(2):
            wait_columns(dims, w_scr, w_sem, h)

    a = jnp.concatenate([a0_ref[...], a1_ref[...]], axis=1)
    branch = jnp.concatenate([dot(a, flat2(w_scr[h])) for h in range(2)], axis=1) + vec_ref[3:4, :d]
    middle = x_ref[...].astype(F32) + BS * branch
    mid_ref[...] = middle
    xhat, _ = normalize(middle)
    n_ref[...] = (xhat * vec_ref[4:5, :d] + vec_ref[5:6, :d]).astype(BF)


def proj_call(dims, where, x, att, vec, own, oth):
    rows, d = x.shape
    br = 256
    row = pl.BlockSpec((br, d), lambda i: (i, 0))
    return pl.pallas_call(
        functools.partial(proj_kernel, dims, len(own), 3 * d // 2),
        grid=(rows // br,),
        in_specs=[SMEM, row] + [pl.BlockSpec((br, v.shape[1]), lambda i: (i, 0)) for v in att]
        + [full_spec(vec.shape)] + [ANY] * (2 * len(own)),
        out_specs=[row, row],
        out_shape=[jax.ShapeDtypeStruct((rows, d), F32), jax.ShapeDtypeStruct((rows, d), BF)],
        scratch_shapes=weight_scratch(dims, own[0].shape[1], d // 2),
        compiler_params=params(),
        cost_estimate=cost(2 * rows * d * d, rows * d * 10 + d * d * 2),
        name="proj",
    )(where, x, *att, vec, *own, *oth)


def mlp_kernel(dims, count, where_ref, n_ref, c_ref, mid_ref, vec_ref, *refs):
    own, oth = refs[:count], refs[count : 2 * count]
    (
        out_ref, gn_ref, gfb_ref, gob_ref, g_own, g_oth,
        nt_scr, mg_scr, acc_scr, act_scr, gp_scr, f_scr, f_sem, o_scr, o_sem, gf_scr, gf_sem, go_scr, go_sem,
    ) = refs[2 * count :]
    z_n, y_n, x_n = dims
    zi, yi, xi, ci = [where_ref[i] for i in range(4)]
    j = pl.program_id(0)
    blocks = o_scr.shape[0]
    rows, d = n_ref.shape
    n = own[0].shape[1]
    wide = f_scr.shape[-1]
    parts = d // n
    br = 256

    @pl.when(j == 0)
    def _():
        load_columns(dims, where_ref, own, oth, 0, wide, f_scr, f_sem)
        for i, s, z, y, x in chips_of(dims, where_ref):
            for core, src in ((ci, own), (1 - ci, oth)):
                for t in range(2):
                    at = (((z * y_n + y) * x_n + x) * 2 + core) * 2 + t
                    q = lax.rem(at, parts)
                    local_copy(
                        piece_at(dims, src, i, s).at[:, pl.ds(wide + t * d, d)],
                        o_scr.at[at // parts, pl.ds(pl.multiple_of(q * n, 16), n), :],
                        o_sem.at[at // parts, q],
                    ).start()
        nt_scr[...] = n_ref[...].T
        total = jnp.zeros_like(gob_ref)
        for r in range(0, rows, br):
            mg = (BS * c_ref[r : r + br, :].astype(F32)).astype(BF)
            mg_scr[r : r + br, :] = mg
            total += jnp.sum(mg.astype(F32), axis=0, keepdims=True)
        gob_ref[...] = total
        wait_columns(dims, f_scr, f_sem, 0)

    @pl.when(j == blocks // 2)
    def _():
        wait_columns(dims, f_scr, f_sem, 1)

    for q in range(parts):
        part = o_scr.at[j, pl.ds(q * n, n), :]
        local_copy(part, part, o_sem.at[j, q]).wait()

    half = j // (blocks // 2)
    first = pl.multiple_of(lax.rem(j, blocks // 2) * d, 128)
    wf = flat2(f_scr[half, :, :, :, :, pl.ds(first, d)])
    wo = o_scr[j]
    fb = vec_ref[6:7, pl.ds(pl.multiple_of(j * d, 128), d)]
    bias_sum = jnp.zeros((1, d), F32)
    for r in range(0, rows, br):
        rr = slice(r, r + br)
        pre = dot(n_ref[rr, :], wf) + fb
        ga = dot_t(mg_scr[rr, :], wo)
        sq = pre * pre
        t = jnp.tanh(GC0 * pre * (1.0 + GC1 * sq))
        half_t = 0.5 * (1.0 + t)
        act = (pre * half_t).astype(BF)
        slope = half_t + (0.5 * GC0) * pre * (1.0 - t * t) * (1.0 + (3.0 * GC1) * sq)
        gp = (slope * ga).astype(BF)
        act_scr[rr, :] = act
        gp_scr[rr, :] = gp
        bias_sum += jnp.sum(gp.astype(F32), axis=0, keepdims=True)
        fwd = dot(act, wo)
        back = dot_t(gp, wf)

        @pl.when(j == 0)
        def _():
            acc_scr[rr, :] = fwd
            gn_ref[rr, :] = back

        @pl.when(j > 0)
        def _():
            acc_scr[rr, :] += fwd
            gn_ref[rr, :] += back

    gfb_ref[...] = bias_sum
    gf_scr[j] = dot(nt_scr[...], gp_scr[...]).astype(BF).reshape(gf_scr.shape[1:])
    store_columns(dims, where_ref, gf_scr.at[j], g_own, g_oth, half, first, d, gf_sem.at[j])
    go_scr[j] = dot_0(act_scr[...], mg_scr[...]).astype(BF)
    for q in range(parts):
        at = j * parts + q
        dev, t = at // 2, lax.rem(at, 2)
        core = lax.rem(dev, 2)
        x = lax.rem(dev // 2, x_n)
        y = lax.rem(dev // (2 * x_n), y_n)
        z = dev // (2 * x_n * y_n)
        piece = lax.rem(y - yi + y_n, y_n) * x_n + lax.rem(x - xi + x_n, x_n)
        slot = lax.rem(z - zi + z_n, z_n)
        to = pl.ds(pl.multiple_of(wide + t * d, 128), d)
        for other, out in ((False, g_own), (True, g_oth)):

            @pl.when((core != ci) if other else (core == ci))
            def _():
                local_copy(go_scr.at[j, pl.ds(q * n, n), :], out.at[piece, slot, :, to], go_sem.at[j, q]).start()

    @pl.when(j == blocks - 1)
    def _():
        for r in range(0, rows, br):
            rr = slice(r, r + br)
            out_ref[rr, :] = (mid_ref[rr, :] + BS * (acc_scr[rr, :] + vec_ref[7:8, :d])).astype(BF)
        for b in range(blocks):
            wait_store(dims, gf_scr.at[b], g_own, 0, d, gf_sem.at[b])
            for q in range(parts):
                part = go_scr.at[b, pl.ds(q * n, n), :]
                local_copy(part, part, go_sem.at[b, q]).wait()


def mlp_call(dims, where, normed, cot, middle, vec, own, oth):
    rows, d = normed.shape
    n, cols = own[0].shape[1:]
    wide = cols - 2 * d
    blocks = 2 * wide // d
    count = dims[1] * dims[2]
    act = full_spec((rows, d))
    piece = jax.ShapeDtypeStruct((count, dims[0], n, cols), BF)
    return pl.pallas_call(
        functools.partial(mlp_kernel, dims, len(own)),
        grid=(blocks,),
        in_specs=[SMEM, act, act, act, full_spec(vec.shape)] + [ANY] * (2 * len(own)),
        out_specs=[act, act, pl.BlockSpec((1, d), lambda j: (0, j)), full_spec((1, d))] + [ANY] * 2,
        out_shape=[
            jax.ShapeDtypeStruct((rows, d), BF),
            jax.ShapeDtypeStruct((rows, d), F32),
            jax.ShapeDtypeStruct((1, blocks * d), F32),
            jax.ShapeDtypeStruct((1, d), F32),
            piece, piece,
        ],
        scratch_shapes=[
            pltpu.VMEM((d, rows), BF), pltpu.VMEM((rows, d), BF), pltpu.VMEM((rows, d), F32),
            pltpu.VMEM((rows, d), BF), pltpu.VMEM((rows, d), BF),
        ]
        + weight_scratch(dims, n, wide)
        + [
            pltpu.VMEM((blocks, d, d), BF), pltpu.SemaphoreType.DMA((blocks, d // n)),
            pltpu.VMEM((blocks,) + dims + (n, d), BF), pltpu.SemaphoreType.DMA((blocks, count, dims[0])),
            pltpu.VMEM((blocks, d, d), BF), pltpu.SemaphoreType.DMA((blocks, d // n)),
        ],
        compiler_params=params(),
        cost_estimate=cost(24 * rows * d * wide, 30e6, 2 * rows * wide),
        name="mlp",
    )(where, normed, cot, middle, vec, *own, *oth)


def proj_back_kernel(dims, count, first, where_ref, gn_ref, mid_ref, c_ref, a0_ref, a1_ref, vec_ref, ind_ref, *refs):
    own, oth = refs[:count], refs[count : 2 * count]
    (
        gm_ref, ga_ref, gw_ref, del_ref, gg_ref, gb_ref, gpb_ref, gw_acc, w_scr, w_sem,
    ) = refs[2 * count :]
    i = pl.program_id(0)
    d = mid_ref.shape[1]
    m = d // 2

    @pl.when(i == 0)
    def _():
        load_columns(dims, where_ref, own, oth, first, m, w_scr, w_sem)
        gw_acc[...] = jnp.zeros_like(gw_acc)
        gg_ref[...] = jnp.zeros_like(gg_ref)
        gb_ref[...] = jnp.zeros_like(gb_ref)
        gpb_ref[...] = jnp.zeros_like(gpb_ref)
        for h in range(2):
            wait_columns(dims, w_scr, w_sem, h)

    dy = gn_ref[...]
    xhat, rstd = normalize(mid_ref[...])
    gg_ref[...] += jnp.sum(dy * xhat, axis=0, keepdims=True)
    gb_ref[...] += jnp.sum(dy, axis=0, keepdims=True)
    gm = c_ref[...].astype(F32) + ln_back(dy, xhat, rstd, vec_ref[4:5, :d])
    gm_ref[...] = gm
    pg = (BS * gm).astype(BF)
    gpb_ref[...] += jnp.sum(pg.astype(F32), axis=0, keepdims=True)
    a = jnp.concatenate([a0_ref[...], a1_ref[...]], axis=1)
    gw_acc[...] += dot_0(a, pg)
    ga = (dot_t(pg[:, :m], flat2(w_scr[0])) + dot_t(pg[:, m:], flat2(w_scr[1]))).astype(BF)
    ga_ref[...] = ga
    prod = ga.astype(F32) * a.astype(F32)
    high = prod.astype(BF)
    low = (prod - high.astype(F32)).astype(BF)
    del_ref[...] = dot_t(ind_ref[...], high) + dot_t(ind_ref[...], low)

    @pl.when(i == pl.num_programs(0) - 1)
    def _():
        gw_ref[...] = gw_acc[...].astype(BF)


def proj_back_call(dims, where, gn, middle, cot, att, vec, own, oth):
    rows, d = middle.shape
    br = 256
    row = pl.BlockSpec((br, d), lambda i: (i, 0))
    ind = (jnp.arange(16)[:, None] == jnp.arange(d)[None, :] // HD).astype(BF)
    one = full_spec((1, d))
    vshape = jax.ShapeDtypeStruct((1, d), F32)
    return pl.pallas_call(
        functools.partial(proj_back_kernel, dims, len(own), 3 * d // 2),
        grid=(rows // br,),
        in_specs=[SMEM, row, row, row] + [pl.BlockSpec((br, v.shape[1]), lambda i: (i, 0)) for v in att]
        + [full_spec(vec.shape), full_spec((16, d))] + [ANY] * (2 * len(own)),
        out_specs=[row, row, full_spec((d, d)), pl.BlockSpec((16, br), lambda i: (0, i)), one, one, one],
        out_shape=[
            jax.ShapeDtypeStruct((rows, d), F32),
            jax.ShapeDtypeStruct((rows, d), BF),
            jax.ShapeDtypeStruct((d, d), BF),
            jax.ShapeDtypeStruct((16, rows), F32),
            vshape, vshape, vshape,
        ],
        scratch_shapes=[pltpu.VMEM((d, d), F32)] + weight_scratch(dims, own[0].shape[1], d // 2),
        compiler_params=params(),
        cost_estimate=cost(4 * rows * d * d, rows * d * 16),
        name="proj_back",
    )(where, gn, middle, cot, *att, vec, ind, *own, *oth)


def pair_back(j_ref, do_ref, lse_ref, del_ref, segr_ref, segc_ref, dj_ref, dk_acc, dv_acc):
    rows = j_ref.shape[0]
    scale = HD**-0.5
    k0, k1 = split_heads(j_ref[:, 128:256] * BF(scale))
    v0, v1 = split_heads(j_ref[:, 256:384])
    for q0, kv0, kv1, is_long in q_tiles(rows)[::-1]:
        q = j_ref[q0 : q0 + 256, 0:128]
        do = do_ref[q0 : q0 + 256, :]
        qh = split_heads(q)
        doh = split_heads(do)
        allowed = diag_allowed(is_long, segr_ref[...], segc_ref[...])
        low_p, low_s = [], []
        dq = None
        for h, (k, v) in enumerate(((k0, v0), (k1, v1))):
            s = dot_t(k[kv0:kv1], q)
            dp = dot_t(v[kv0:kv1], do)
            lse = lse_ref[0, h : h + 1, q0 : q0 + 256]
            dlt = del_ref[0, h : h + 1, q0 : q0 + 256]
            diag = jnp.where(allowed, s[q0 - kv0 : q0 - kv0 + 256], NEG)
            parts = [diag] if kv1 - kv0 == 256 else [s[: q0 - kv0], diag]
            probs = jnp.concatenate([jnp.exp(p - lse) for p in parts], axis=0)
            low_p.append(probs.astype(BF))
            ds = (probs * (dp - dlt)).astype(BF)
            low_s.append(ds)
            part = dot_0(k[kv0:kv1], ds)
            dq = part if dq is None else dq + part
        dj_ref[q0 : q0 + 256, 0:128] = dq.T.astype(BF)
        dv = dot(jnp.concatenate(low_p, axis=1), jnp.concatenate(doh, axis=0))
        dk = dot(jnp.concatenate(low_s, axis=1), jnp.concatenate(qh, axis=0))
        if q0 in (LONG, LONG - 256):
            dk_acc[kv0:kv1, :] = dk
            dv_acc[kv0:kv1, :] = dv
        else:
            dk_acc[kv0:kv1, :] += dk
            dv_acc[kv0:kv1, :] += dv
    dj_ref[:, 128:256] = (dk_acc[...] * scale).astype(BF)
    dj_ref[:, 256:384] = dv_acc[...].astype(BF)


def attn_back_kernel(
    dims, count, group0, groups, last, devices, where_ref, j_ref, do_ref, lse_ref, del_ref, segr_ref, segc_ref,
    x_ref, vec_ref, *refs,
):
    own, oth, refs = refs[:count], refs[count : 2 * count], refs[2 * count :]
    if last:
        gnin_ref, qvin_ref, gm_ref, gfb_ref, gob_ref, gg2_ref, gb2_ref, gpb_ref = refs[:8]
        gx_ref, g_own, g_oth = refs[8:11]
        refs = refs[11:]
    else:
        gwp_ref, gn_out, qv_out, g_own, g_oth = refs[:5]
        refs = refs[5:]
    w_scr, w_sem, nt_scr, gn_scr, dj_scr, dk_acc, dv_acc, gw_scr, gw_sem, e_scr, e_sem, qv_scr = refs
    i = pl.program_id(0)
    rows, d = x_ref.shape
    half, group = lax.rem(i, 2), i // 2
    br = 256
    extra_at = groups * 384

    @pl.when(i == 0)
    def _():
        load_columns(dims, where_ref, own, oth, group0 * 384, groups * 384, w_scr, w_sem)
        if not last:
            for h in range(2):
                e_scr[h] = gwp_ref[:, h * (d // 2) : (h + 1) * (d // 2)].reshape(e_scr.shape[1:])
                store_columns(dims, where_ref, e_scr.at[h], g_own, g_oth, h, extra_at, d // 2, e_sem.at[h])
            qv_scr[...] = jnp.zeros_like(qv_scr)
            gn_scr[...] = jnp.zeros_like(gn_scr)
        else:
            qv_scr[...] = qvin_ref[...]
            gn_scr[...] = gnin_ref[...]
        for r in range(0, rows, br):
            xhat, _ = normalize(x_ref[r : r + br, :].astype(F32))
            nt_scr[:, r : r + br] = (xhat * vec_ref[0:1, :d] + vec_ref[1:2, :d]).astype(BF).T
        for h in range(2):
            wait_columns(dims, w_scr, w_sem, h)

    pair_back(j_ref, do_ref, lse_ref, del_ref, segr_ref, segc_ref, dj_scr, dk_acc, dv_acc)
    first = pl.multiple_of(group * 384, 128)
    dj = dj_scr[...]
    pair = group0 * 2 + i
    qv_scr[:, pl.ds(pl.multiple_of(pair * 128, 128), 128)] = jnp.sum(
        dj[:, 0:128].astype(F32), axis=0, keepdims=True
    )
    qv_scr[:, pl.ds(pl.multiple_of(d + pair * 128, 128), 128)] = jnp.sum(
        dj[:, 256:384].astype(F32), axis=0, keepdims=True
    )
    gw_scr[i] = dot(nt_scr[...], dj).astype(BF).reshape(gw_scr.shape[1:])
    store_columns(dims, where_ref, gw_scr.at[i], g_own, g_oth, half, first, 384, gw_sem.at[i])
    w = flat2(w_scr[half, :, :, :, :, pl.ds(first, 384)])
    for r in range(0, rows, br):
        gn_scr[r : r + br, :] += dot_t(dj[r : r + br, :], w)

    @pl.when(i == 2 * groups - 1)
    def _():
        if last:
            gg = jnp.zeros((1, d), F32)
            gb = jnp.zeros((1, d), F32)
            for r in range(0, rows, br):
                rr = slice(r, r + br)
                xhat, rstd = normalize(x_ref[rr, :].astype(F32))
                dy = gn_scr[rr, :]
                gg += jnp.sum(dy * xhat, axis=0, keepdims=True)
                gb += jnp.sum(dy, axis=0, keepdims=True)
                gx_ref[rr, :] = (gm_ref[rr, :] + ln_back(dy, xhat, rstd, vec_ref[0:1, :d])).astype(BF)
            table = pack_vectors(
                {
                    "g1": gg, "b1": gb, "qv": qv_scr[...], "fb": gfb_ref[...], "pb": gpb_ref[...],
                    "g2": gg2_ref[...], "b2": gb2_ref[...], "ob": gob_ref[...],
                },
                d, devices,
            ).reshape(e_scr.shape[1:])
            for h in range(2):
                e_scr[h] = table
                store_columns(dims, where_ref, e_scr.at[h], g_own, g_oth, h, extra_at, 128, e_sem.at[h])
        else:
            gn_out[...] = gn_scr[...]
            qv_out[...] = qv_scr[...]
        for b in range(2 * groups):
            wait_store(dims, gw_scr.at[b], g_own, 0, 384, gw_sem.at[b])
        for h in range(2):
            wait_store(dims, e_scr.at[h], g_own, extra_at, e_scr.shape[-1], e_sem.at[h])


def attn_back_call(dims, where, joined, ga, lse, delta, seg_row, seg_col, x, vec, own, oth, group0, groups, extra, last, devices):
    rows, d = x.shape
    n = own[0].shape[1]
    pairs = d // 128
    act = full_spec((rows, d))
    one = full_spec((1, d))
    wide = d // 2 if not last else 128
    stat = pl.BlockSpec((1, 2, rows), lambda i: (group0 * 2 + i, 0, 0))
    arrays, count = len(own), dims[1] * dims[2]
    piece = jax.ShapeDtypeStruct((count, dims[0], n, groups * 384 + wide), BF)
    in_specs = [
        SMEM,
        pl.BlockSpec((rows, 384), lambda i: (0, pair_block(group0 * 2 + i, pairs))),
        pl.BlockSpec((rows, 128), lambda i: (0, group0 * 2 + i)),
        pl.BlockSpec((1, 2, rows), lambda i: (i, 0, 0)), stat, full_spec((1, 256)), full_spec((256, 1)), act, full_spec(vec.shape),
    ] + [ANY] * (2 * arrays)
    if last:
        in_specs += [act, full_spec((1, 2 * d)), act, full_spec((1, 4 * d))] + [one] * 4
        out_specs = [act, ANY, ANY]
        out_shape = [jax.ShapeDtypeStruct((rows, d), BF), piece, piece]
    else:
        in_specs += [full_spec((d, d))]
        out_specs = [act, full_spec((1, 2 * d)), ANY, ANY]
        out_shape = [jax.ShapeDtypeStruct((rows, d), F32), jax.ShapeDtypeStruct((1, 2 * d), F32), piece, piece]
    return pl.pallas_call(
        functools.partial(attn_back_kernel, dims, arrays, group0, groups, last, devices),
        grid=(2 * groups,),
        in_specs=in_specs,
        out_specs=out_specs,
        out_shape=out_shape,
        scratch_shapes=weight_scratch(dims, n, groups * 384)
        + [
            pltpu.VMEM((d, rows), BF), pltpu.VMEM((rows, d), F32), pltpu.VMEM((rows, 384), BF),
            pltpu.VMEM((rows, 128), F32), pltpu.VMEM((rows, 128), F32),
            pltpu.VMEM((2 * groups,) + dims + (n, 384), BF), pltpu.SemaphoreType.DMA((2 * groups, count, dims[0])),
            pltpu.VMEM((2,) + dims + (n, wide), BF), pltpu.SemaphoreType.DMA((2, count, dims[0])),
            pltpu.VMEM((1, 2 * d), F32),
        ],
        compiler_params=params(),
        cost_estimate=cost(groups * 20e9, 12e6, 5.5e6),
        name="attn_back_last" if last else "attn_back",
    )(where, joined, ga, lse, delta, seg_row, seg_col, x, vec, *own, *oth, *extra)


def pack_plan(counts, rows):
    c = [counts[i] for i in range(counts.shape[0])]
    ends, run = [], jnp.int32(0)
    for v in c:
        run = run + v
        ends.append(run)
    start = jnp.int32(0)
    for i in range(len(c) - 1):
        start = jnp.where(c[i] == LONG, ends[i] - c[i], start)
    rolled = jnp.arange(rows, dtype=jnp.int32)
    pos = rolled + start
    pos = jnp.where(pos >= rows, pos - rows, pos)
    seg = functools.reduce(jnp.add, [(pos >= e).astype(jnp.int32) for e in ends])
    valid = seg < len(c) - 1
    seg = jnp.where(valid, seg, 1000 + rolled)
    return start, seg[LONG:], valid


def roll_rows(array, shift):
    return lax.dynamic_slice_in_dim(jnp.concatenate([array, array], axis=0), shift, array.shape[0])


def half_columns(w, h, joined=False):
    r, cols = w.shape
    if not joined:
        return w[:, h * (cols // 2) : (h + 1) * (cols // 2)]
    pairs = cols // 384
    starts = [(t * pairs + p) * 128 for p in range(h, pairs, 2) for t in range(3)]
    return jnp.concatenate([w[:, s : s + 128] for s in starts], axis=1)


def join_columns(left, right):
    r, m = left.shape
    both = jnp.stack([v.reshape(r, m // 384, 3, 128) for v in (left, right)], axis=2)
    return both.transpose(0, 3, 1, 2, 4).reshape(r, 2 * m)


def add_all(values):
    return functools.reduce(jnp.add, [v.astype(F32) for v in values])


class Plain:
    def __init__(self, dp, fsdp):
        self.dims = (1, 1, 1)
        index = lax.axis_index("dp") * fsdp + lax.axis_index("fsdp")
        self.ci = index % 2

    def where(self):
        zero = jnp.zeros((), jnp.int32)
        return jnp.stack([zero, zero, zero, self.ci.astype(jnp.int32)])

    def pick(self, pair):
        return jnp.where(self.ci == 0, pair[0], pair[1]), jnp.where(self.ci == 0, pair[1], pair[0])

    def gather(self, w_qkv, w_proj, table, w_fc, w_out):
        whole = lambda v: lax.all_gather(v, AXES, axis=0, tiled=True)
        attn = whole(jnp.concatenate([w_qkv, w_proj, table], axis=1))
        cut = w_qkv.shape[1], w_qkv.shape[1] + w_proj.shape[1]
        fc, out = whole(w_fc), whole(w_out)
        d = out.shape[1]
        lists = [[], []]
        for h in range(2):
            qkv, proj, table = attn[:, : cut[0]], attn[:, cut[0] : cut[1]], attn[:, cut[1] :]
            lists[0].append(jnp.concatenate([half_columns(qkv, h, True), half_columns(proj, h), table], axis=1))
            lists[1].append(
                jnp.concatenate([half_columns(fc, h)] + [out[(2 * h + t) * d : (2 * h + t + 1) * d] for t in range(2)], axis=1)
            )
        listed = []
        for pair in lists:
            own, oth = self.pick(pair)
            listed.append(([own[None]], [oth[None]]))
        return listed

    def scatter(self, own, oth):
        pair = self.pick([own[0, 0], oth[0, 0]])
        m = pair[0].shape[1]
        mine = lax.psum_scatter(jnp.concatenate(pair, axis=1), AXES, scatter_dimension=0, tiled=True).astype(F32)
        return mine[:, :m], mine[:, m:]

    def scatter_hidden(self, own, oth):
        pair = self.pick([own[0, 0], oth[0, 0]])
        d = pair[0].shape[0]
        wide = pair[0].shape[1] - 2 * d
        fc = self.scatter(own[..., :wide], oth[..., :wide])
        out = jnp.concatenate([v[:, wide + t * d : wide + (t + 1) * d] for v in pair for t in range(2)], axis=0)
        return fc, lax.psum_scatter(out, AXES, scatter_dimension=0, tiled=True).astype(F32)


class Chips:
    def __init__(self, dp, fsdp):
        x_n, z_n = fsdp // 2, 4
        self.dims = (z_n, dp // z_n, x_n)
        index = lax.axis_index("dp") * fsdp + lax.axis_index("fsdp")
        self.ci = index % 2
        self.at = (index // (2 * x_n * self.dims[1]), (index // (2 * x_n)) % self.dims[1], (index // 2) % x_n, self.ci)

    def where(self):
        return jnp.stack(self.at).astype(jnp.int32)

    def pick(self, pair):
        return jnp.where(self.ci == 0, pair[0], pair[1]), jnp.where(self.ci == 0, pair[1], pair[0])

    def send(self, array, dz=0, dy=0, dx=0, dc=0):
        z_n, y_n, x_n = self.dims
        pairs = []
        for z in range(z_n):
            for y in range(y_n):
                for x in range(x_n):
                    for c in range(2):
                        here = ((z * y_n + y) * x_n + x) * 2 + c
                        there = (((z + dz) % z_n * y_n + (y + dy) % y_n) * x_n + (x + dx) % x_n) * 2 + (c + dc) % 2
                        pairs.append((here, there))
        return lax.ppermute(array, AXES, pairs)

    def trade(self, halves):
        return self.rows_of(*self.pick(halves))

    def rows_of(self, keep, give):
        return jnp.concatenate(self.pick([keep, self.send(give, dc=1)]), axis=0)

    def along_z(self, piece):
        return [piece] + [self.send(piece, dz=-k) for k in range(1, self.dims[0])]

    def swap(self, arrays):
        return [self.send(v, dc=1) for v in arrays]

    def add_core(self, own, theirs):
        return [add_all([own[i], theirs[i]]).astype(BF) for i in range(own.shape[0])]

    def rows_back(self, total):
        n = total.shape[0] // 2
        mine, give = self.pick([total[:n], total[n:]])
        return self.pick([mine, self.send(give, dc=1)])


def together(*trees):
    return lax.optimization_barrier(trees)


def prepare(tokens, lengths, cotangent):
    start, seg, valid = pack_plan(lengths[0], tokens.shape[0])
    x = roll_rows(tokens, start)
    cot = jnp.where(valid[:, None], roll_rows(cotangent, start), BF(0))
    return start, seg[None, :], seg[:, None], x, cot


def vector_table(r, ln1_gain, ln1_bias, qv_bias, proj_bias, ln2_gain, ln2_bias, fc_bias, out_bias):
    flat = [
        jnp.concatenate([ln1_gain, ln1_bias, qv_bias]), fc_bias,
        jnp.concatenate([proj_bias, ln2_gain, ln2_bias, out_bias]),
    ]
    return jnp.pad(jnp.stack(flat), ((0, r - 3), (0, 128 - 4 * r)))


def results(r, start, out, gx, s_fc, s_out, s_attn):
    rows, d = out.shape
    cut = 3 * d // 2
    s_qkv = join_columns(*[v[:, :cut] for v in s_attn])
    s_proj = jnp.concatenate([v[:, cut:-128] for v in s_attn], axis=1)
    row0, row1, row2 = [s_attn[0][k, 2 * d : 2 * d + 4 * r] for k in range(3)]
    restore = rows - start
    return (
        roll_rows(out, restore), roll_rows(gx, restore),
        row0[:r], row0[r : 2 * r], s_qkv, row0[2 * r :], s_proj, row2[:r],
        row2[r : 2 * r], row2[2 * r : 3 * r], jnp.concatenate(s_fc, axis=1), row1, s_out, row2[3 * r :],
    )


def merge_parts(one, two):
    a, b = one.shape[-1], two.shape[-1]
    return jnp.concatenate([one[..., : 2 * 384], two[..., : b - 128], one[..., 2 * 384 : a], two[..., b - 128 :]], axis=-1)


def block_plain(
    links, tokens, lengths, ln1_gain, ln1_bias, w_qkv, qv_bias, w_proj, proj_bias, ln2_gain, ln2_bias,
    w_fc, fc_bias, w_out, out_bias, cotangent,
):
    rows, d = tokens.shape
    r = w_qkv.shape[0]
    devices = d // r
    dims, where = links.dims, links.where()
    table = vector_table(r, ln1_gain, ln1_bias, qv_bias, proj_bias, ln2_gain, ln2_bias, fc_bias, out_bias)
    attn_w, mlp_w = links.gather(w_qkv, w_proj, table, w_fc, w_out)
    start, seg_row, seg_col, x, cot = prepare(tokens, lengths, cotangent)
    joined, vec = qkv_call(dims, where, x, *attn_w, devices)
    att0, lse0 = attn_call(joined, seg_row, seg_col, 0, 2)
    att1, lse1 = attn_call(joined, seg_row, seg_col, 2, d // 256 - 2)
    att = att0, att1
    middle, normed_two = proj_call(dims, where, x, att, vec, *attn_w)
    out, gn, gfb, gob, *m_g = mlp_call(dims, where, normed_two, cot, middle, vec, *mlp_w)
    s_fc, s_out = links.scatter_hidden(*m_g)
    gm, ga, gw_proj, delta, gg2, gb2, gpb = proj_back_call(dims, where, gn, middle, cot, att, vec, *attn_w)
    delta = delta[: d // HD].reshape(d // 128, 2, rows)
    stats = (delta, seg_row, seg_col, x, vec, *attn_w)
    gn1, qv1, g_own, g_oth = attn_back_call(dims, where, joined, ga, lse0, *stats, 0, 2, (gw_proj,), False, devices)
    gx, h_own, h_oth = attn_back_call(
        dims, where, joined, ga, lse1, *stats, 2, d // 256 - 2, (gn1, qv1, gm, gfb, gob, gg2, gb2, gpb), True, devices
    )
    s_attn = links.scatter(merge_parts(g_own, h_own), merge_parts(g_oth, h_oth))
    return results(r, start, out, gx, s_fc, s_out, s_attn)


def block_chips(
    links, tokens, lengths, ln1_gain, ln1_bias, w_qkv, qv_bias, w_proj, proj_bias, ln2_gain, ln2_bias,
    w_fc, fc_bias, w_out, out_bias, cotangent,
):
    rows, d = tokens.shape
    r = w_qkv.shape[0]
    devices = d // r
    dims, where, send, swap = links.dims, links.where(), links.send, links.swap
    table = vector_table(r, ln1_gain, ln1_bias, qv_bias, proj_bias, ln2_gain, ln2_bias, fc_bias, out_bias)

    def xy(column):
        return send(column, dx=1), send(column, dy=1)

    def corner(x_part, y_part):
        return [send(x_part[:2], dy=1), send(y_part[2:], dx=1)]

    a = links.rows_of(*cut_call(where, w_qkv, w_proj, table))
    a, tokens, lengths, cotangent, w_fc = together(a, tokens, lengths, cotangent, w_fc)
    a0 = links.along_z(a)
    fc = links.trade([half_columns(w_fc, h) for h in range(2)])
    m = jnp.concatenate([fc, w_out[: 2 * r], w_out[2 * r :]], axis=1)
    prep = prepare(tokens, lengths, cotangent)
    a0, prep, m = together(a0, prep, m)
    start, seg_row, seg_col, x, cot = prep
    a0 = jnp.stack(a0)
    ax, ay = xy(a0)
    m1, m3 = send(m, dz=-1), send(m, dz=-3)
    ax, ay, m, m1, m3 = together(ax, ay, m, m1, m3)
    ad = corner(ax, ay)
    a_oth = swap([a0, ax, ay])
    m2 = send(m, dz=-2)
    ad, a_oth, m2 = together(ad, a_oth, m2)
    m0 = jnp.stack([m, m1, m2, m3])
    attn_w = [a0, ax, ay] + ad, a_oth + swap(ad)
    m0, x, attn_w = together(m0, x, attn_w)

    joined, vec = qkv_call(dims, where, x, *attn_w, devices)
    att0, lse0 = attn_call(joined, seg_row, seg_col, 0, 2)
    mx, my = xy(m0)
    att0, joined, mx, my = together(att0, joined, mx, my)
    att1, lse1 = attn_call(joined, seg_row, seg_col, 2, d // 256 - 2)
    att = att0, att1

    middle, normed_two = proj_call(dims, where, x, att, vec, *attn_w)
    md = corner(mx, my)
    m_oth = swap([m0, mx, my])
    normed_two, md, m_oth = together(normed_two, md, m_oth)
    mlp_w = [m0, mx, my] + md, m_oth + swap(md)

    out, gn, gfb, gob, m_own, m_oth = mlp_call(dims, where, normed_two, cot, middle, vec, *mlp_w)
    gm, ga, gw_proj, delta, gg2, gb2, gpb = proj_back_call(dims, where, gn, middle, cot, att, vec, *attn_w)
    (m_oth,) = swap([m_oth])
    ga, delta, m_own, m_oth = together(ga, delta, m_own, m_oth)
    delta = delta[: d // HD].reshape(d // 128, 2, rows)
    b = links.add_core(m_own, m_oth)
    b, ga, delta = together(b, ga, delta)
    stats = (delta, seg_row, seg_col, x, vec, *attn_w)
    first = send(b[3][:2], dy=1), send(b[3][2:], dx=1), send(b[1][2:], dx=1), send(b[2][:2], dy=1)
    gn1, qv1, g_own, g_oth = attn_back_call(dims, where, joined, ga, lse0, *stats, 0, 2, (gw_proj,), False, devices)
    gn1, g_own, g_oth, first = together(gn1, g_own, g_oth, first)

    by_y, by_x, x_high, y_low = first
    sums = add_all([b[1][:2], by_y]).astype(BF), add_all([b[2][2:], by_x]).astype(BF)
    sums, gn1, g_own, g_oth = together(sums, gn1, g_own, g_oth)
    x_low, y_high = send(sums[0], dx=1), send(sums[1], dy=1)
    (g_oth,) = swap([g_oth])
    gx, h_own, h_oth = attn_back_call(
        dims, where, joined, ga, lse1, *stats, 2, d // 256 - 2, (gn1, qv1, gm, gfb, gob, gg2, gb2, gpb), True, devices
    )
    gx, h_own, h_oth, x_low, y_high, g_oth = together(gx, h_own, h_oth, x_low, y_high, g_oth)

    (h_oth,) = swap([h_oth])
    column = [add_all([b[0][j], x_low[j], y_low[j]]).astype(BF) for j in range(2)]
    column += [add_all([b[0][j + 2], x_high[j], y_high[j]]).astype(BF) for j in range(2)]
    column, h_oth = together(column, h_oth)
    arrived = [column[0]] + [send(column[j], dz=j) for j in range(1, dims[0])]
    e = links.add_core(merge_parts(g_own, h_own), merge_parts(g_oth, h_oth))
    near = send(e[1], dx=1), send(e[2], dy=1), send(e[3], dx=1, dy=1)
    near, arrived, out, gx = together(near, arrived, out, gx)

    column = [add_all([e[0][j]] + [a[j] for a in near]).astype(BF) for j in range(dims[0])]
    total = add_all(arrived)
    s_fc = links.rows_back(total[:, : w_fc.shape[1] // 2])
    s_out = jnp.concatenate([total[:, -2 * d : -d], total[:, -d:]], axis=0)
    s_attn = links.rows_back(add_all([column[0]] + [send(column[j], dz=j) for j in range(1, dims[0])]))
    return results(r, start, out, gx, s_fc, s_out, s_attn)


def solution(mesh):
    dp, fsdp = mesh.shape["dp"], mesh.shape["fsdp"]

    def per_device(*args):
        if (dp, fsdp) == (8, 4) and args[4].shape[0] % 8 == 0:
            return block_chips(Chips(dp, fsdp), *args)
        return block_plain(Plain(dp, fsdp), *args)

    row, vec = P(AXES, None), P(AXES)
    in_specs = (row, row, vec, vec, row, vec, row, vec, vec, vec, row, vec, row, vec, row)
    out_specs = (row, row, vec, vec, row, vec, row, vec, vec, vec, row, vec, row, vec)
    return jax.shard_map(
        per_device, mesh=mesh, in_specs=in_specs, out_specs=out_specs, check_vma=False
    )
```

```python
import functools
import math

import jax
import jax.numpy as jnp
from jax import lax
from jax.experimental import pallas as pl
from jax.experimental.pallas import tpu as pltpu
from jax.sharding import PartitionSpec as P

HD = 64
LONG = 768
EPS = 1e-05
BS = 1.0 / math.sqrt(48.0)
NEG = -1e30
F32 = jnp.float32
BF = jnp.bfloat16
VMEM_LIMIT = 58 * 1024 * 1024
AXES = ("dp", "fsdp")
GC0 = math.sqrt(2.0 / math.pi)
GC1 = 0.044715


def dot(a, b):
    return lax.dot_general(a, b, (((1,), (0,)), ((), ())), preferred_element_type=F32)


def dot_t(a, b):
    return lax.dot_general(a, b, (((1,), (1,)), ((), ())), preferred_element_type=F32)


def dot_0(a, b):
    return lax.dot_general(a, b, (((0,), (0,)), ((), ())), preferred_element_type=F32)


def params(grid_len=1):
    return pltpu.CompilerParams(
        dimension_semantics=("arbitrary",) * grid_len, vmem_limit_bytes=VMEM_LIMIT
    )


def cost(flops, nbytes, trans=0):
    return pl.CostEstimate(flops=int(flops), bytes_accessed=int(nbytes), transcendentals=int(trans))


def normalize(values):
    centred = values - jnp.mean(values, axis=-1, keepdims=True)
    rstd = lax.rsqrt(jnp.mean(centred * centred, axis=-1, keepdims=True) + EPS)
    return centred * rstd, rstd


def ln_back(dy, xhat, rstd, gain):
    dx = dy * gain
    m1 = jnp.mean(dx, axis=-1, keepdims=True)
    m2 = jnp.mean(dx * xhat, axis=-1, keepdims=True)
    return rstd * (dx - m1 - xhat * m2)


def full_spec(shape):
    return pl.BlockSpec(shape, lambda *_: (0,) * len(shape), pipeline_mode=pl.Buffered(1))


def lane_masks(rows):
    lane = lax.broadcasted_iota(jnp.int32, (rows, 128), 1)
    return lane < HD


def split_heads(block):
    low = lane_masks(block.shape[0])
    zero = jnp.zeros_like(block)
    return jnp.where(low, block, zero), jnp.where(low, zero, block)


def q_tiles(rows):
    tiles = [(r, 0, r + 256, True) for r in range(0, LONG, 256)]
    tiles += [(LONG, LONG, rows, False)]
    return tiles


def diag_allowed(is_long, seg_row, seg_col):
    kv = lax.broadcasted_iota(jnp.int32, (256, 256), 0)
    qp = lax.broadcasted_iota(jnp.int32, (256, 256), 1)
    allowed = kv <= qp
    if not is_long:
        allowed = allowed & (seg_col == seg_row)
    return allowed


def attn_kernel(q_ref, k_ref, v_ref, segr_ref, segc_ref, o_ref, lse_ref):
    rows = q_ref.shape[0]
    ks = split_heads(k_ref[...] * BF(HD**-0.5))
    vt = v_ref[...].T
    items = [(tile, h) for tile in q_tiles(rows) for h in range(2)]

    def score(item):
        (q0, kv0, kv1, _), h = item
        return dot_t(ks[h][kv0:kv1], q_ref[q0 : q0 + 256, :])

    queue = [score(it) for it in items[:3]]
    outs = []
    for n, ((q0, kv0, kv1, is_long), h) in enumerate(items):
        if n + 3 < len(items):
            queue.append(score(items[n + 3]))
        s, queue[n] = queue[n], None
        parts = mask_diagonal(s, q0 - kv0, is_long, segr_ref, segc_ref)
        top = functools.reduce(jnp.maximum, [jnp.max(p, axis=0, keepdims=True) for p in parts])
        exps = [jnp.exp(p - top) for p in parts]
        total = functools.reduce(jnp.add, [jnp.sum(e, axis=0, keepdims=True) for e in exps])
        lse_ref[0, h : h + 1, q0 : q0 + 256] = top + jnp.log(total)
        probs = jnp.concatenate([e.astype(BF) for e in exps], axis=0)
        outs.append(dot(vt[h * HD : (h + 1) * HD, kv0:kv1], probs) * (1.0 / total))
        if h == 1:
            o_ref[q0 : q0 + 256, :] = jnp.concatenate(outs, axis=0).T.astype(BF)
            outs = []


def mask_diagonal(s, at, is_long, segr_ref, segc_ref):
    allowed = diag_allowed(is_long, segr_ref[...], segc_ref[...])
    diag = jnp.where(allowed, s[at:], NEG)
    return [s[:at], diag] if at else [diag]


def attn_call(joined, seg_row, seg_col, group0, groups):
    rows = joined.shape[0]
    pairs = joined.shape[1] // 384
    at = lambda t: pl.BlockSpec((rows, 128), lambda p: (0, pair_block(group0 * 2 + p, pairs) * 3 + t))
    return pl.pallas_call(
        attn_kernel,
        grid=(2 * groups,),
        in_specs=[at(0), at(1), at(2), full_spec((1, 256)), full_spec((256, 1))],
        out_specs=[
            pl.BlockSpec((rows, 128), lambda p: (0, p)),
            pl.BlockSpec((1, 2, rows), lambda p: (p, 0, 0)),
        ],
        out_shape=[
            jax.ShapeDtypeStruct((rows, groups * 256), BF),
            jax.ShapeDtypeStruct((2 * groups, 2, rows), F32),
        ],
        compiler_params=params(),
        cost_estimate=cost(groups * 8e9, 8e6, 5.5e6),
        name="attn",
    )(joined, joined, joined, seg_row, seg_col)


def pair_block(p, pairs):
    return (p % 2) * (pairs // 2) + p // 2


ANY = pl.BlockSpec(memory_space=pl.ANY)
SMEM = pl.BlockSpec(memory_space=pltpu.SMEM)


def local_copy(src, dst, sem):
    return pltpu.make_async_copy(src, dst, sem)


def chips_of(dims, where_ref):
    z_n, y_n, x_n = dims
    zi, yi, xi = [where_ref[i] for i in range(3)]
    for i in range(y_n * x_n):
        for j in range(z_n):
            yield i, j, lax.rem(zi + j, z_n), lax.rem(yi + i // x_n, y_n), lax.rem(xi + i % x_n, x_n)


def piece_at(dims, arrays, i, j):
    at = i * dims[0] + j
    for a in arrays:
        if at < a.shape[0]:
            return a.at[at]
        at -= a.shape[0]


def load_columns(dims, where_ref, own, oth, first, cols, dst, sem):
    ci = where_ref[3]
    for i, j, z, y, x in chips_of(dims, where_ref):
        for half, src in ((ci, own), (1 - ci, oth)):
            block = piece_at(dims, src, i, j).at[:, pl.ds(first, cols)]
            local_copy(block, dst.at[half, z, y, x], sem.at[half, z, y, x]).start()


def wait_columns(dims, dst, sem, half):
    for z in range(dims[0]):
        for y in range(dims[1]):
            for x in range(dims[2]):
                block = dst.at[half, z, y, x]
                local_copy(block, block, sem.at[half, z, y, x]).wait()


def flat2(value):
    return value.reshape(-1, value.shape[-1])


def store_columns(dims, where_ref, src, own, oth, half, first, cols, sem):
    ci = where_ref[3]
    for other, out in ((False, own), (True, oth)):

        @pl.when((half != ci) if other else (half == ci))
        def _():
            for i, j, z, y, x in chips_of(dims, where_ref):
                local_copy(src.at[z, y, x], out.at[i, j, :, pl.ds(first, cols)], sem.at[i, j]).start()


def wait_store(dims, src, out, first, cols, sem):
    for i in range(dims[1] * dims[2]):
        for j in range(dims[0]):
            local_copy(src.at[0, 0, 0], out.at[i, j, :, pl.ds(first, cols)], sem.at[i, j]).wait()


def weight_scratch(dims, n, cols):
    return [
        pltpu.VMEM((2,) + dims + (n, cols), BF),
        pltpu.SemaphoreType.DMA((2,) + dims),
    ]


def vector_plan(d, devices):
    r = d // devices
    return {
        "g1": (0, 0, r), "b1": (0, r, r), "qv": (0, 2 * r, 2 * r), "fb": (1, 0, 4 * r),
        "pb": (2, 0, r), "g2": (2, r, r), "b2": (2, 2 * r, r), "ob": (2, 3 * r, r),
    }


VECTOR_ROWS = {"g1": 0, "b1": 1, "qv": 2, "pb": 3, "g2": 4, "b2": 5, "fb": 6, "ob": 7}


def owner_of(shape, size, axis):
    c = lax.broadcasted_iota(jnp.int32, shape, axis).astype(F32)
    owner = jnp.floor((c + 0.5) * (1.0 / size))
    return owner, c - owner * size


def row_pick(devices, d, row):
    r = d // devices
    at = lax.broadcasted_iota(jnp.int32, (devices, d), 1)
    dev = lax.broadcasted_iota(jnp.int32, (devices, d), 0)
    return (at == dev * r + row).astype(BF)


def vector_maps(devices, n, first, size):
    owner, place = owner_of((devices, n), size, 1)
    mine = owner == lax.broadcasted_iota(jnp.int32, (devices, n), 0).astype(F32)
    _, place = owner_of((128, n), size, 1)
    spot = (place + first == lax.broadcasted_iota(jnp.int32, (128, n), 0).astype(F32)).astype(BF)
    return mine, spot


def unpack_vectors(table, d, devices, out_ref):
    plan = vector_plan(d, devices)
    picked = [dot(row_pick(devices, d, k), table).astype(BF) for k in range(3)]
    for name, i in VECTOR_ROWS.items():
        k, first, size = plan[name]
        n = size * devices
        mine, spot = vector_maps(devices, n, first, size)
        spread = dot(picked[k], spot)
        out_ref[i : i + 1, :n] = jnp.sum(jnp.where(mine, spread, 0.0), axis=0, keepdims=True)


def pack_vectors(rows, d, devices):
    plan = vector_plan(d, devices)
    parts = [None] * 3
    for name in VECTOR_ROWS:
        k, first, size = plan[name]
        n = size * devices
        mine, spot = vector_maps(devices, n, first, size)
        part = dot_t(jnp.where(mine, rows[name], 0.0).astype(BF), spot)
        parts[k] = part if parts[k] is None else parts[k] + part
    total = None
    for k in range(3):
        piece = dot_0(row_pick(devices, d, k), parts[k].astype(BF))
        total = piece if total is None else total + piece
    return total.astype(BF)


def cut_kernel(where_ref, w_ref, t_ref, keep_ref, give_ref):
    ci = where_ref[3]
    pairs = w_ref.shape[1] // 384
    for h in range(2):
        for other, out in ((False, keep_ref), (True, give_ref)):

            @pl.when((ci != h) if other else (ci == h))
            def _():
                at = 0
                for p in range(h, pairs, 2):
                    for t in range(3):
                        first = (t * pairs + p) * 128
                        out[:, at : at + 128] = w_ref[:, first : first + 128]
                        at += 128
                out[:, at:] = t_ref[...]


def cut_call(where, w_qkv, table):
    r = w_qkv.shape[0]
    cols = w_qkv.shape[1] // 2 + 128
    return pl.pallas_call(
        cut_kernel,
        grid=(1,),
        in_specs=[SMEM, full_spec(w_qkv.shape), full_spec(table.shape)],
        out_specs=[full_spec((r, cols))] * 2,
        out_shape=[jax.ShapeDtypeStruct((r, cols), BF)] * 2,
        compiler_params=params(),
        cost_estimate=cost(0, 4 * r * cols),
        name="cut",
    )(where, w_qkv, table)


def qkv_kernel(dims, count, devices, where_ref, x_ref, *refs):
    own, oth = refs[:count], refs[count : 2 * count]
    o_ref, vec_ref, w_scr, w_sem, t_scr, t_sem, n_scr, bias_scr = refs[2 * count :]
    rows, d = x_ref.shape
    cols = w_scr.shape[-1]
    table_at = own[0].shape[-1] - 128
    step = pl.program_id(0)

    @pl.when(step == 0)
    def _():
        for i, j, z, y, x in chips_of(dims, where_ref):
            block = piece_at(dims, own, i, j).at[:, pl.ds(table_at, 128)]
            local_copy(block, t_scr.at[z, y, x], t_sem.at[z, y, x]).start()
        load_columns(dims, where_ref, own, oth, 0, cols, w_scr, w_sem)
        for z in range(dims[0]):
            for y in range(dims[1]):
                for x in range(dims[2]):
                    block = t_scr.at[z, y, x]
                    local_copy(block, block, t_sem.at[z, y, x]).wait()
        vec_ref[...] = jnp.zeros_like(vec_ref)
        unpack_vectors(flat2(t_scr[...]), d, devices, vec_ref)
        zero = jnp.zeros((1, 128), F32)
        pairs = d // 128
        for p in range(pairs):
            at = pair_block(p, pairs) * 384
            half, at = at // cols, at % cols
            bias_scr[half, :, at : at + 128] = vec_ref[2:3, p * 128 : (p + 1) * 128]
            bias_scr[half, :, at + 128 : at + 256] = zero
            bias_scr[half, :, at + 256 : at + 384] = vec_ref[2:3, d + p * 128 : d + (p + 1) * 128]
        for r in range(0, rows, 256):
            xhat, _ = normalize(x_ref[r : r + 256, :].astype(F32))
            n_scr[r : r + 256, :] = (xhat * vec_ref[0:1, :d] + vec_ref[1:2, :d]).astype(BF)
        wait_columns(dims, w_scr, w_sem, 0)

    @pl.when(step == 1)
    def _():
        wait_columns(dims, w_scr, w_sem, 1)

    w = flat2(w_scr[step])
    for r in range(0, rows, 256):
        o_ref[r : r + 256, :] = (dot(n_scr[r : r + 256, :], w) + bias_scr[step]).astype(BF)


def qkv_call(dims, where, x, own, oth, devices):
    rows, d = x.shape
    n = own[0].shape[1]
    cols = 3 * d // 2
    return pl.pallas_call(
        functools.partial(qkv_kernel, dims, len(own), devices),
        grid=(2,),
        in_specs=[SMEM, full_spec((rows, d))] + [ANY] * (2 * len(own)),
        out_specs=[pl.BlockSpec((rows, cols), lambda j: (0, j)), full_spec((8, 4 * d))],
        out_shape=[
            jax.ShapeDtypeStruct((rows, 2 * cols), BF), jax.ShapeDtypeStruct((8, 4 * d), F32)
        ],
        scratch_shapes=weight_scratch(dims, n, cols)
        + [
            pltpu.VMEM(dims + (n, 128), BF), pltpu.SemaphoreType.DMA(dims),
            pltpu.VMEM((rows, d), BF), pltpu.VMEM((2, 1, cols), F32),
        ],
        compiler_params=params(),
        cost_estimate=cost(4 * rows * d * cols, rows * d * 8 + d * cols * 4),
        name="qkv",
    )(where, x, *own, *oth)


def proj_kernel(x_ref, a0_ref, a1_ref, vec_ref, w_ref, mid_ref, n_ref):
    d = x_ref.shape[1]
    a = jnp.concatenate([a0_ref[...], a1_ref[...]], axis=1)
    branch = dot(a, w_ref[...]) + vec_ref[3:4, :d]
    middle = x_ref[...].astype(F32) + BS * branch
    mid_ref[...] = middle
    xhat, _ = normalize(middle)
    n_ref[...] = (xhat * vec_ref[4:5, :d] + vec_ref[5:6, :d]).astype(BF)


def proj_call(x, att, vec, w):
    rows, d = x.shape
    br = 256
    row = pl.BlockSpec((br, d), lambda i: (i, 0))
    return pl.pallas_call(
        proj_kernel,
        grid=(rows // br,),
        in_specs=[row] + [pl.BlockSpec((br, v.shape[1]), lambda i: (i, 0)) for v in att]
        + [full_spec(vec.shape), full_spec((d, d))],
        out_specs=[row, row],
        out_shape=[jax.ShapeDtypeStruct((rows, d), F32), jax.ShapeDtypeStruct((rows, d), BF)],
        compiler_params=params(),
        cost_estimate=cost(2 * rows * d * d, rows * d * 10 + d * d * 2),
        name="proj",
    )(x, *att, vec, w)


def mlp_kernel(dims, count, take, where_ref, n_ref, c_ref, mid_ref, vec_ref, wo_ref, *refs):
    own, oth = refs[:count], refs[count : 2 * count]
    (
        out_ref, gn_ref, gfb_ref, gob_ref, go_ref, g_own, g_oth,
        nt_scr, mg_scr, acc_scr, act_scr, gp_scr, f_scr, f_sem, gf_scr, gf_sem,
    ) = refs[2 * count :]
    j = pl.program_id(0)
    rows, d = n_ref.shape
    wide = f_scr.shape[-1]
    blocks = 2 * wide // d
    br = 512

    @pl.when(j == 0)
    def _():
        load_columns(dims, where_ref, own, oth, 0, wide, f_scr, f_sem)
        nt_scr[...] = n_ref[...].T
        total = jnp.zeros_like(gob_ref)
        for r in range(0, rows, br):
            mg = (BS * c_ref[r : r + br, :].astype(F32)).astype(BF)
            mg_scr[r : r + br, :] = mg
            total += jnp.sum(mg.astype(F32), axis=0, keepdims=True)
        gob_ref[...] = total
        wait_columns(dims, f_scr, f_sem, 0)

    @pl.when(j == blocks // 2)
    def _():
        wait_columns(dims, f_scr, f_sem, 1)

    half = j // (blocks // 2)
    first = pl.multiple_of(lax.rem(j, blocks // 2) * d, 128)
    wf = flat2(f_scr[half, :, :, :, :, pl.ds(first, d)])
    wo = wo_ref[:, :take, :].reshape(d, d)
    fb = vec_ref[6:7, pl.ds(pl.multiple_of(j * d, 128), d)]
    bias_sum = jnp.zeros((1, d), F32)
    starts = list(range(0, rows, br))

    def ahead_of(r):
        return dot(n_ref[r : r + br, :], wf), dot_t(mg_scr[r : r + br, :], wo)

    def behind(r, act, gp):
        rr = slice(r, r + br)
        fwd = dot(act, wo)
        back = dot_t(gp, wf)
        acc_scr[rr, :] = jnp.where(j == 0, fwd, acc_scr[rr, :] + fwd)
        gn_ref[rr, :] = jnp.where(j == 0, back, gn_ref[rr, :] + back)

    queue = [ahead_of(starts[0])]
    waiting = None
    for i, r in enumerate(starts):
        rr = slice(r, r + br)
        if i + 1 < len(starts):
            queue.append(ahead_of(starts[i + 1]))
        (pre, ga), queue[i] = queue[i], None
        pre = pre + fb
        sq = pre * pre
        t = jnp.tanh(GC0 * pre * (1.0 + GC1 * sq))
        half_t = 0.5 * (1.0 + t)
        act = (pre * half_t).astype(BF)
        slope = half_t + (0.5 * GC0) * pre * (1.0 - t * t) * (1.0 + (3.0 * GC1) * sq)
        gp = (slope * ga).astype(BF)
        act_scr[rr, :] = act
        gp_scr[rr, :] = gp
        bias_sum += jnp.sum(gp.astype(F32), axis=0, keepdims=True)
        if waiting is not None:
            behind(*waiting)
        waiting = r, act, gp
    behind(*waiting)

    gfb_ref[...] = bias_sum
    gf_scr[j] = dot(nt_scr[...], gp_scr[...]).astype(BF).reshape(gf_scr.shape[1:])
    store_columns(dims, where_ref, gf_scr.at[j], g_own, g_oth, half, first, d, gf_sem.at[j])
    go_ref[...] = dot_0(act_scr[...], mg_scr[...]).astype(BF)

    @pl.when(j == blocks - 1)
    def _():
        for r in range(0, rows, br):
            rr = slice(r, r + br)
            out_ref[rr, :] = (mid_ref[rr, :] + BS * (acc_scr[rr, :] + vec_ref[7:8, :d])).astype(BF)
        for b in range(blocks):
            wait_store(dims, gf_scr.at[b], g_own, 0, d, gf_sem.at[b])


def mlp_call(dims, where, normed, cot, middle, vec, w_out, take, own, oth):
    rows, d = normed.shape
    n, wide = own[0].shape[1:]
    blocks = 2 * wide // d
    count = dims[1] * dims[2]
    act = full_spec((rows, d))
    piece = jax.ShapeDtypeStruct((count, dims[0], n, wide), BF)
    block = pl.BlockSpec((d, d), lambda j: (j, 0))
    whole = pl.BlockSpec((d // take,) + w_out.shape[1:], lambda j: (j, 0, 0))
    return pl.pallas_call(
        functools.partial(mlp_kernel, dims, len(own), take),
        grid=(blocks,),
        in_specs=[SMEM, act, act, act, full_spec(vec.shape), whole] + [ANY] * (2 * len(own)),
        out_specs=[act, act, pl.BlockSpec((1, d), lambda j: (0, j)), full_spec((1, d)), block] + [ANY] * 2,
        out_shape=[
            jax.ShapeDtypeStruct((rows, d), BF),
            jax.ShapeDtypeStruct((rows, d), F32),
            jax.ShapeDtypeStruct((1, blocks * d), F32),
            jax.ShapeDtypeStruct((1, d), F32),
            jax.ShapeDtypeStruct((blocks * d, d), BF),
            piece, piece,
        ],
        scratch_shapes=[
            pltpu.VMEM((d, rows), BF), pltpu.VMEM((rows, d), BF), pltpu.VMEM((rows, d), F32),
            pltpu.VMEM((rows, d), BF), pltpu.VMEM((rows, d), BF),
        ]
        + weight_scratch(dims, n, wide)
        + [
            pltpu.VMEM((blocks,) + dims + (n, d), BF), pltpu.SemaphoreType.DMA((blocks, count, dims[0])),
        ],
        compiler_params=params(),
        cost_estimate=cost(24 * rows * d * wide, 30e6, 2 * rows * wide),
        name="mlp",
    )(where, normed, cot, middle, vec, w_out, *own, *oth)


def proj_back_kernel(
    gn_ref, mid_ref, c_ref, a0_ref, a1_ref, vec_ref, ind_ref, w_ref,
    gm_ref, ga_ref, gw_ref, del_ref, gg_ref, gb_ref, gpb_ref, gw_acc,
):
    i = pl.program_id(0)
    d = mid_ref.shape[1]

    @pl.when(i == 0)
    def _():
        gw_acc[...] = jnp.zeros_like(gw_acc)
        gg_ref[...] = jnp.zeros_like(gg_ref)
        gb_ref[...] = jnp.zeros_like(gb_ref)
        gpb_ref[...] = jnp.zeros_like(gpb_ref)

    dy = gn_ref[...]
    xhat, rstd = normalize(mid_ref[...])
    gg_ref[...] += jnp.sum(dy * xhat, axis=0, keepdims=True)
    gb_ref[...] += jnp.sum(dy, axis=0, keepdims=True)
    gm = c_ref[...].astype(F32) + ln_back(dy, xhat, rstd, vec_ref[4:5, :d])
    gm_ref[...] = gm
    pg = (BS * gm).astype(BF)
    gpb_ref[...] += jnp.sum(pg.astype(F32), axis=0, keepdims=True)
    a = jnp.concatenate([a0_ref[...], a1_ref[...]], axis=1)
    gw_acc[...] += dot_0(a, pg)
    ga = dot_t(pg, w_ref[...]).astype(BF)
    ga_ref[...] = ga
    prod = ga.astype(F32) * a.astype(F32)
    high = prod.astype(BF)
    low = (prod - high.astype(F32)).astype(BF)
    del_ref[...] = dot_t(ind_ref[...], high) + dot_t(ind_ref[...], low)

    @pl.when(i == pl.num_programs(0) - 1)
    def _():
        gw_ref[...] = gw_acc[...].astype(BF)


def proj_back_call(gn, middle, cot, att, vec, w):
    rows, d = middle.shape
    br = 256
    row = pl.BlockSpec((br, d), lambda i: (i, 0))
    ind = (jnp.arange(16)[:, None] == jnp.arange(d)[None, :] // HD).astype(BF)
    one = full_spec((1, d))
    vshape = jax.ShapeDtypeStruct((1, d), F32)
    return pl.pallas_call(
        proj_back_kernel,
        grid=(rows // br,),
        in_specs=[row, row, row] + [pl.BlockSpec((br, v.shape[1]), lambda i: (i, 0)) for v in att]
        + [full_spec(vec.shape), full_spec((16, d)), full_spec((d, d))],
        out_specs=[row, row, full_spec((d, d)), pl.BlockSpec((16, br), lambda i: (0, i)), one, one, one],
        out_shape=[
            jax.ShapeDtypeStruct((rows, d), F32),
            jax.ShapeDtypeStruct((rows, d), BF),
            jax.ShapeDtypeStruct((d, d), BF),
            jax.ShapeDtypeStruct((16, rows), F32),
            vshape, vshape, vshape,
        ],
        scratch_shapes=[pltpu.VMEM((d, d), F32)],
        compiler_params=params(),
        cost_estimate=cost(4 * rows * d * d, rows * d * 16),
        name="proj_back",
    )(gn, middle, cot, *att, vec, ind, w)


def pair_back(j_ref, do_ref, lse_ref, del_ref, row, segr_ref, segc_ref, pair, dj_ref, dk_acc, dv_acc):
    rows = j_ref.shape[0]
    scale = HD**-0.5
    lanes = slice(pair * 128, (pair + 1) * 128)
    base = pair * 384
    k = j_ref[:, 128:256] * BF(scale)
    ks = split_heads(k)
    kt = k.T
    vs = split_heads(j_ref[:, 256:384])
    qt = j_ref[:, 0:128].T
    dot_do = do_ref[:, lanes].T
    items = [(tile, h) for tile in q_tiles(rows)[::-1] for h in range(2)]

    def ahead_of(item):
        (q0, kv0, kv1, _), h = item
        q = j_ref[q0 : q0 + 256, 0:128]
        do = do_ref[q0 : q0 + 256, lanes]
        return dot_t(ks[h][kv0:kv1], q), dot_t(vs[h][kv0:kv1], do)

    def behind(tile, h, probs, ds):
        q0, kv0, kv1, _ = tile
        hh = slice(h * HD, (h + 1) * HD)
        qq = slice(q0, q0 + 256)
        dv = dot_t(dot_do[hh, qq], probs)
        dk = dot_t(qt[hh, qq], ds)
        if q0 in (LONG, LONG - 256):
            dk_acc[hh, kv0:kv1] = dk
            dv_acc[hh, kv0:kv1] = dv
        else:
            dk_acc[hh, kv0:kv1] += dk
            dv_acc[hh, kv0:kv1] += dv
        return dot(kt[hh, kv0:kv1], ds)

    queue = [ahead_of(it) for it in items[:2]]
    waiting, dqs = None, []

    def settle():
        tile, h = waiting[:2]
        dqs.append(behind(*waiting))
        if h == 1:
            q0 = tile[0]
            dj_ref[q0 : q0 + 256, base : base + 128] = jnp.concatenate(dqs[-2:], axis=0).T.astype(BF)

    for n, (tile, h) in enumerate(items):
        q0, kv0, kv1, is_long = tile
        if n + 2 < len(items):
            queue.append(ahead_of(items[n + 2]))
        (s, dp), queue[n] = queue[n], None
        lse = lse_ref[pair, h : h + 1, q0 : q0 + 256]
        dlt = del_ref[pl.ds(row + h, 1), q0 : q0 + 256]
        parts = mask_diagonal(s, q0 - kv0, is_long, segr_ref, segc_ref)
        probs = jnp.concatenate([jnp.exp(p - lse) for p in parts], axis=0)
        ds = (probs * (dp - dlt)).astype(BF)
        if waiting is not None:
            settle()
        waiting = tile, h, probs.astype(BF), ds
    settle()
    dj_ref[:, base + 128 : base + 256] = (dk_acc[...] * scale).T.astype(BF)
    dj_ref[:, base + 256 : base + 384] = dv_acc[...].T.astype(BF)


def attn_back_kernel(
    dims, count, devices, where_ref, j0_ref, j1_ref, do_ref, lse_ref, del_ref, segr_ref, segc_ref,
    x_ref, vec_ref, gwp_ref, gfb_ref, gob_ref, gg2_ref, gb2_ref, gpb_ref, gm_ref, *refs,
):
    own, oth, refs = refs[:count], refs[count : 2 * count], refs[2 * count :]
    gx_ref, g_own, g_oth = refs[:3]
    (
        w_scr, w_sem, nt_scr, gn_scr, gm_scr, gm_sem, dj_scr, dk_acc, dv_acc, gw_scr, gw_sem,
        p_scr, p_sem, t_scr, t_sem, qv_scr,
    ) = refs[3:]
    i = pl.program_id(0)
    groups = gw_scr.shape[0]
    rows, d = x_ref.shape
    br = 256
    proj_at = groups * 384
    table_at = proj_at + d // 2

    @pl.when(i == 0)
    def _():
        load_columns(dims, where_ref, own, oth, 0, groups * 384, w_scr, w_sem)
        local_copy(gm_ref, gm_scr, gm_sem).start()
        for h in range(2):
            p_scr[h] = gwp_ref[:, h * (d // 2) : (h + 1) * (d // 2)].reshape(p_scr.shape[1:])
            store_columns(dims, where_ref, p_scr.at[h], g_own, g_oth, h, proj_at, d // 2, p_sem.at[h])
        for r in range(0, rows, br):
            xhat, _ = normalize(x_ref[r : r + br, :].astype(F32))
            nt_scr[:, r : r + br] = (xhat * vec_ref[0:1, :d] + vec_ref[1:2, :d]).astype(BF).T

    for h, j_ref in enumerate((j0_ref, j1_ref)):
        row = (i * 2 + h) * 2
        pair_back(j_ref, do_ref, lse_ref, del_ref, row, segr_ref, segc_ref, h, dj_scr, dk_acc, dv_acc)

    @pl.when(i == 0)
    def _():
        for h in range(2):
            wait_columns(dims, w_scr, w_sem, h)

    first = pl.multiple_of(i * 384, 128)
    dj = dj_scr[...]
    for h in range(2):
        for t, off in ((0, 0), (2, d)):
            part = dj[:, h * 384 + t * 128 : h * 384 + (t + 1) * 128].astype(F32)
            qv_scr[:, pl.ds(pl.multiple_of(off + (i * 2 + h) * 128, 128), 128)] = jnp.sum(part, axis=0, keepdims=True)
    gw = dot(nt_scr[...], dj).astype(BF)
    for h in range(2):
        gw_scr[i, h] = gw[:, h * 384 : (h + 1) * 384].reshape(gw_scr.shape[2:])
        store_columns(dims, where_ref, gw_scr.at[i, h], g_own, g_oth, h, first, 384, gw_sem.at[i, h])
    w = jnp.concatenate([flat2(w_scr[h, :, :, :, :, pl.ds(first, 384)]) for h in range(2)], axis=1)
    for r in range(0, rows, br):
        back = dot_t(dj[r : r + br, :], w)
        gn_scr[r : r + br, :] = jnp.where(i == 0, back, gn_scr[r : r + br, :] + back)

    @pl.when(i == groups - 1)
    def _():
        local_copy(gm_ref, gm_scr, gm_sem).wait()
        gg = jnp.zeros((1, d), F32)
        gb = jnp.zeros((1, d), F32)
        for r in range(0, rows, br):
            rr = slice(r, r + br)
            xhat, rstd = normalize(x_ref[rr, :].astype(F32))
            dy = gn_scr[rr, :]
            gg += jnp.sum(dy * xhat, axis=0, keepdims=True)
            gb += jnp.sum(dy, axis=0, keepdims=True)
            gx_ref[rr, :] = (gm_scr[rr, :] + ln_back(dy, xhat, rstd, vec_ref[0:1, :d])).astype(BF)
        table = pack_vectors(
            {
                "g1": gg, "b1": gb, "qv": qv_scr[...], "fb": gfb_ref[...], "pb": gpb_ref[...],
                "g2": gg2_ref[...], "b2": gb2_ref[...], "ob": gob_ref[...],
            },
            d, devices,
        ).reshape(t_scr.shape)
        t_scr[...] = table
        for h in range(2):
            store_columns(dims, where_ref, t_scr, g_own, g_oth, h, table_at, 128, t_sem.at[h])
        for h in range(2):
            for b in range(groups):
                wait_store(dims, gw_scr.at[b, h], g_own, 0, 384, gw_sem.at[b, h])
            wait_store(dims, p_scr.at[h], g_own, proj_at, d // 2, p_sem.at[h])
            wait_store(dims, t_scr, g_own, table_at, 128, t_sem.at[h])


def attn_back_call(dims, where, joined, ga, lse, delta, seg_row, seg_col, x, vec, own, oth, vectors, gm, devices):
    rows, d = x.shape
    n = own[0].shape[1]
    groups = d // 256
    act = full_spec((rows, d))
    count = dims[1] * dims[2]
    piece = jax.ShapeDtypeStruct((count, dims[0], n, groups * 384 + d // 2 + 128), BF)
    return pl.pallas_call(
        functools.partial(attn_back_kernel, dims, len(own), devices),
        grid=(groups,),
        in_specs=[
            SMEM,
            pl.BlockSpec((rows, 384), lambda i: (0, i)),
            pl.BlockSpec((rows, 384), lambda i: (0, groups + i)),
            pl.BlockSpec((rows, 256), lambda i: (0, i)),
            pl.BlockSpec((2, 2, rows), lambda i: (i, 0, 0)),
            full_spec(delta.shape), full_spec((1, 256)), full_spec((256, 1)), act, full_spec(vec.shape),
        ]
        + [full_spec(v.shape) for v in vectors] + [ANY] * (1 + 2 * len(own)),
        out_specs=[act, ANY, ANY],
        out_shape=[jax.ShapeDtypeStruct((rows, d), BF), piece, piece],
        scratch_shapes=weight_scratch(dims, n, groups * 384)
        + [
            pltpu.VMEM((d, rows), BF), pltpu.VMEM((rows, d), F32),
            pltpu.VMEM((rows, d), F32), pltpu.SemaphoreType.DMA(()), pltpu.VMEM((rows, 768), BF),
            pltpu.VMEM((128, rows), F32), pltpu.VMEM((128, rows), F32),
            pltpu.VMEM((groups, 2) + dims + (n, 384), BF), pltpu.SemaphoreType.DMA((groups, 2, count, dims[0])),
            pltpu.VMEM((2,) + dims + (n, d // 2), BF), pltpu.SemaphoreType.DMA((2, count, dims[0])),
            pltpu.VMEM(dims + (n, 128), BF), pltpu.SemaphoreType.DMA((2, count, dims[0])),
            pltpu.VMEM((1, 2 * d), F32),
        ],
        compiler_params=params(),
        cost_estimate=cost(60e9, 20e6, 5.5e6),
        name="attn_back",
    )(where, joined, joined, ga, lse, delta, seg_row, seg_col, x, vec, *vectors, gm, *own, *oth)


def pack_plan(counts, rows):
    c = [counts[i] for i in range(counts.shape[0])]
    ends, run = [], jnp.int32(0)
    for v in c:
        run = run + v
        ends.append(run)
    start = jnp.int32(0)
    for i in range(len(c) - 1):
        start = jnp.where(c[i] == LONG, ends[i] - c[i], start)
    rolled = jnp.arange(rows, dtype=jnp.int32)
    pos = rolled + start
    pos = jnp.where(pos >= rows, pos - rows, pos)
    seg = functools.reduce(jnp.add, [(pos >= e).astype(jnp.int32) for e in ends])
    valid = seg < len(c) - 1
    seg = jnp.where(valid, seg, 1000 + rolled)
    return start, seg[LONG:], valid


def roll_rows(array, shift):
    return lax.dynamic_slice_in_dim(jnp.concatenate([array, array], axis=0), shift, array.shape[0])


def half_columns(w, h, joined=False):
    r, cols = w.shape
    if not joined:
        return w[:, h * (cols // 2) : (h + 1) * (cols // 2)]
    pairs = cols // 384
    starts = [(t * pairs + p) * 128 for p in range(h, pairs, 2) for t in range(3)]
    return jnp.concatenate([w[:, s : s + 128] for s in starts], axis=1)


def join_columns(left, right):
    r, m = left.shape
    both = jnp.stack([v.reshape(r, m // 384, 3, 128) for v in (left, right)], axis=2)
    return both.transpose(0, 3, 1, 2, 4).reshape(r, 2 * m)


def add_all(values):
    return functools.reduce(jnp.add, [v.astype(F32) for v in values])


class Plain:
    def __init__(self, dp, fsdp):
        self.dims = (1, 1, 1)
        index = lax.axis_index("dp") * fsdp + lax.axis_index("fsdp")
        self.ci = index % 2

    def where(self):
        zero = jnp.zeros((), jnp.int32)
        return jnp.stack([zero, zero, zero, self.ci.astype(jnp.int32)])

    def pick(self, pair):
        return jnp.where(self.ci == 0, pair[0], pair[1]), jnp.where(self.ci == 0, pair[1], pair[0])

    def gather(self, w_qkv, table, w_fc):
        whole = lambda v: lax.all_gather(v, AXES, axis=0, tiled=True)
        attn, fc = whole(jnp.concatenate([w_qkv, table], axis=1)), whole(w_fc)
        qkv, table = attn[:, : w_qkv.shape[1]], attn[:, w_qkv.shape[1] :]
        first = [jnp.concatenate([half_columns(qkv, h, True), table], axis=1) for h in range(2)]
        listed = []
        for pair in (first, [half_columns(fc, h) for h in range(2)]):
            own, oth = self.pick(pair)
            listed.append(([own[None]], [oth[None]]))
        return listed

    def scatter(self, own, oth):
        pair = self.pick([own[0, 0], oth[0, 0]])
        m = pair[0].shape[1]
        mine = lax.psum_scatter(jnp.concatenate(pair, axis=1), AXES, scatter_dimension=0, tiled=True).astype(F32)
        return mine[:, :m], mine[:, m:]


class Chips:
    def __init__(self, dp, fsdp):
        x_n, z_n = fsdp // 2, 4
        self.dims = (z_n, dp // z_n, x_n)
        index = lax.axis_index("dp") * fsdp + lax.axis_index("fsdp")
        self.ci = index % 2
        self.at = (index // (2 * x_n * self.dims[1]), (index // (2 * x_n)) % self.dims[1], (index // 2) % x_n, self.ci)

    def where(self):
        return jnp.stack(self.at).astype(jnp.int32)

    def pick(self, pair):
        return jnp.where(self.ci == 0, pair[0], pair[1]), jnp.where(self.ci == 0, pair[1], pair[0])

    def send(self, array, dz=0, dy=0, dx=0, dc=0):
        z_n, y_n, x_n = self.dims
        pairs = []
        for z in range(z_n):
            for y in range(y_n):
                for x in range(x_n):
                    for c in range(2):
                        here = ((z * y_n + y) * x_n + x) * 2 + c
                        there = (((z + dz) % z_n * y_n + (y + dy) % y_n) * x_n + (x + dx) % x_n) * 2 + (c + dc) % 2
                        pairs.append((here, there))
        return lax.ppermute(array, AXES, pairs)

    def trade(self, halves):
        return self.rows_of(*self.pick(halves))

    def rows_of(self, keep, give):
        return jnp.concatenate(self.pick([keep, self.send(give, dc=1)]), axis=0)

    def along_z(self, piece):
        return [piece] + [self.send(piece, dz=-k) for k in range(1, self.dims[0])]

    def swap(self, arrays):
        return [self.send(v, dc=1) for v in arrays]

    def add_core(self, own, theirs):
        return [add_all([own[i], theirs[i]]).astype(BF) for i in range(own.shape[0])]

    def rows_back(self, total):
        n = total.shape[0] // 2
        mine, give = self.pick([total[:n], total[n:]])
        return self.pick([mine, self.send(give, dc=1)])


def together(*trees):
    return lax.optimization_barrier(trees)


def prepare(tokens, lengths, cotangent):
    start, seg, valid = pack_plan(lengths[0], tokens.shape[0])
    x = roll_rows(tokens, start)
    cot = jnp.where(valid[:, None], roll_rows(cotangent, start), BF(0))
    return start, seg[None, :], seg[:, None], x, cot


def vector_table(r, ln1_gain, ln1_bias, qv_bias, proj_bias, ln2_gain, ln2_bias, fc_bias, out_bias):
    flat = [
        jnp.concatenate([ln1_gain, ln1_bias, qv_bias]), fc_bias,
        jnp.concatenate([proj_bias, ln2_gain, ln2_bias, out_bias]),
    ]
    return jnp.pad(jnp.stack(flat), ((0, r - 3), (0, 128 - 4 * r)))


def results(r, out, gx, s_fc, s_out, s_attn):
    d = out.shape[1]
    cut = 3 * d // 2
    s_qkv = join_columns(*[v[:, :cut] for v in s_attn])
    s_proj = jnp.concatenate([v[:, cut:-128] for v in s_attn], axis=1)
    row0, row1, row2 = [s_attn[0][k, -128:][: 4 * r] for k in range(3)]
    return (
        out, gx,
        row0[:r], row0[r : 2 * r], s_qkv, row0[2 * r :], s_proj, row2[:r],
        row2[r : 2 * r], row2[2 * r : 3 * r], jnp.concatenate(s_fc, axis=1), row1, s_out, row2[3 * r :],
    )


def block_plain(
    links, tokens, lengths, ln1_gain, ln1_bias, w_qkv, qv_bias, w_proj, proj_bias, ln2_gain, ln2_bias,
    w_fc, fc_bias, w_out, out_bias, cotangent,
):
    rows, d = tokens.shape
    r = w_qkv.shape[0]
    devices = d // r
    dims, where = links.dims, links.where()
    table = vector_table(r, ln1_gain, ln1_bias, qv_bias, proj_bias, ln2_gain, ln2_bias, fc_bias, out_bias)
    attn_w, fc_w = links.gather(w_qkv, table, w_fc)
    proj = lax.all_gather(w_proj, AXES, axis=0, tiled=True)
    w_out_all = lax.all_gather(w_out, AXES, axis=0, tiled=True).reshape(-1, d, d)
    start, seg_row, seg_col, x, cot = prepare(tokens, lengths, cotangent)
    joined, vec = qkv_call(dims, where, x, *attn_w, devices)
    att0, lse0 = attn_call(joined, seg_row, seg_col, 0, 2)
    att1, lse1 = attn_call(joined, seg_row, seg_col, 2, d // 256 - 2)
    att = att0, att1
    middle, normed_two = proj_call(x, att, vec, proj)
    out, gn, gfb, gob, gw_out, *fc_g = mlp_call(dims, where, normed_two, cot, middle, vec, w_out_all, d, *fc_w)
    s_fc = links.scatter(*fc_g)
    s_out = lax.psum_scatter(gw_out, AXES, scatter_dimension=0, tiled=True).astype(F32)
    gm, ga, gw_proj, delta, gg2, gb2, gpb = proj_back_call(gn, middle, cot, att, vec, proj)
    gx, *g = attn_back_call(
        dims, where, joined, ga, jnp.concatenate([lse0, lse1]), delta, seg_row, seg_col, x, vec, *attn_w,
        (gw_proj, gfb, gob, gg2, gb2, gpb), gm, devices,
    )
    restore = rows - start
    return results(r, roll_rows(out, restore), roll_rows(gx, restore), s_fc, s_out, links.scatter(*g))


def block_chips(
    links, tokens, lengths, ln1_gain, ln1_bias, w_qkv, qv_bias, w_proj, proj_bias, ln2_gain, ln2_bias,
    w_fc, fc_bias, w_out, out_bias, cotangent,
):
    rows, d = tokens.shape
    r = w_qkv.shape[0]
    devices = d // r
    dims, where, send, swap = links.dims, links.where(), links.send, links.swap
    table = vector_table(r, ln1_gain, ln1_bias, qv_bias, proj_bias, ln2_gain, ln2_bias, fc_bias, out_bias)

    def xy(column):
        return send(column, dx=1), send(column, dy=1)

    hidden = w_out.shape[0]
    rest = lax.all_gather(jnp.concatenate([w_out, w_proj], axis=0), AXES, axis=0, tiled=True)
    rest = rest.reshape(devices, hidden + r, d)
    a = links.rows_of(*cut_call(where, w_qkv, table))
    a, tokens, lengths, cotangent, w_fc = together(a, tokens, lengths, cotangent, w_fc)
    a0 = links.along_z(a)
    fc = links.trade([half_columns(w_fc, h) for h in range(2)])
    prep = prepare(tokens, lengths, cotangent)
    a0, prep, fc = together(a0, prep, fc)
    start, seg_row, seg_col, x, cot = prep
    a0 = jnp.stack(a0)
    a_own = [a0, send(a0, dx=1), send(a0, dy=1), send(a0, dx=1, dy=1)]
    fc = links.along_z(fc)
    a_own, fc = together(a_own, fc)
    fc0 = jnp.stack(fc)
    attn_w = a_own, swap(a_own)
    fc0, x, attn_w = together(fc0, x, attn_w)

    joined, vec = qkv_call(dims, where, x, *attn_w, devices)
    att0, lse0 = attn_call(joined, seg_row, seg_col, 0, 2)
    fx, fy = xy(fc0)
    att0, joined, fx, fy = together(att0, joined, fx, fy)
    att1, lse1 = attn_call(joined, seg_row, seg_col, 2, d // 256 - 2)
    att = att0, att1
    proj = rest[:, hidden:].reshape(d, d)
    middle, normed_two = proj_call(x, att, vec, proj)
    fd = [send(fx[:2], dy=1), send(fy[2:], dx=1)]
    f_oth = swap([fc0, fx, fy])
    lse = jnp.concatenate([lse0, lse1])
    normed_two, fd, f_oth, lse = together(normed_two, fd, f_oth, lse)
    fc_w = [fc0, fx, fy] + fd, f_oth + swap(fd)

    out, gn, gfb, gob, gw_out, f_own, f_oth = mlp_call(dims, where, normed_two, cot, middle, vec, rest, hidden, *fc_w)
    s_out = lax.psum_scatter(gw_out, AXES, scatter_dimension=0, tiled=True).astype(F32)
    gm, ga, gw_proj, delta, gg2, gb2, gpb = proj_back_call(gn, middle, cot, att, vec, proj)
    (f_oth,) = swap([f_oth])
    restore = rows - start
    out = roll_rows(out, restore)
    ga, delta, f_own, f_oth, out = together(ga, delta, f_own, f_oth, out)

    def near(b):
        return send(b[1], dx=1), send(b[2], dy=1), send(b[3], dx=1, dy=1)

    def column(b, arrived):
        return [add_all([b[0][j]] + [v[j] for v in arrived]).astype(BF) for j in range(dims[0])]

    def far(parts):
        return [parts[0]] + [send(parts[j], dz=j) for j in range(1, dims[0])]

    b = links.add_core(f_own, f_oth)
    b, ga, delta = together(b, ga, delta)
    b_near = near(b)
    gx, g_own, g_oth = attn_back_call(
        dims, where, joined, ga, lse, delta, seg_row, seg_col, x, vec, *attn_w,
        (gw_proj, gfb, gob, gg2, gb2, gpb), gm, devices,
    )
    gx, g_own, g_oth, b_near, b = together(gx, g_own, g_oth, b_near, b)

    (g_oth,) = swap([g_oth])
    b = column(b, b_near)
    g_oth, b, gx = together(g_oth, b, gx)
    e = links.add_core(g_own, g_oth)
    e_near, b = near(e), far(b)
    gx = roll_rows(gx, restore)
    e_near, b, e, gx = together(e_near, b, e, gx)

    e = far(column(e, e_near))
    s_fc = links.rows_back(add_all(b))
    e, s_fc = together(e, s_fc)
    return results(r, out, gx, s_fc, s_out, links.rows_back(add_all(e)))


def solution(mesh):
    dp, fsdp = mesh.shape["dp"], mesh.shape["fsdp"]

    def per_device(*args):
        if (dp, fsdp) == (8, 4) and args[4].shape[0] % 8 == 0:
            return block_chips(Chips(dp, fsdp), *args)
        return block_plain(Plain(dp, fsdp), *args)

    row, vec = P(AXES, None), P(AXES)
    in_specs = (row, row, vec, vec, row, vec, row, vec, vec, vec, row, vec, row, vec, row)
    out_specs = (row, row, vec, vec, row, vec, row, vec, vec, vec, row, vec, row, vec)
    return jax.shard_map(
        per_device, mesh=mesh, in_specs=in_specs, out_specs=out_specs, check_vma=False
    )
```

```python
import functools
import math

import jax
import jax.numpy as jnp
import numpy as np
from jax import lax
from jax.experimental import pallas as pl
from jax.experimental.pallas import tpu as pltpu
from jax.sharding import PartitionSpec as P

HD = 64
LONG = 768
EPS = 1e-05
BS = 1.0 / math.sqrt(48.0)
NEG = -1e30
F32 = jnp.float32
BF = jnp.bfloat16
VMEM_LIMIT = 58 * 1024 * 1024
AXES = ("dp", "fsdp")
GC0 = math.sqrt(2.0 / math.pi)
GC1 = 0.044715


def dot(a, b):
    return lax.dot_general(a, b, (((1,), (0,)), ((), ())), preferred_element_type=F32)


def dot_t(a, b):
    return lax.dot_general(a, b, (((1,), (1,)), ((), ())), preferred_element_type=F32)


def dot_0(a, b):
    return lax.dot_general(a, b, (((0,), (0,)), ((), ())), preferred_element_type=F32)


def params(grid_len=1):
    return pltpu.CompilerParams(
        dimension_semantics=("arbitrary",) * grid_len, vmem_limit_bytes=VMEM_LIMIT
    )


def cost(flops, nbytes, trans=0):
    return pl.CostEstimate(flops=int(flops), bytes_accessed=int(nbytes), transcendentals=int(trans))


def normalize(values):
    centred = values - jnp.mean(values, axis=-1, keepdims=True)
    rstd = lax.rsqrt(jnp.mean(centred * centred, axis=-1, keepdims=True) + EPS)
    return centred * rstd, rstd


def ln_back(dy, xhat, rstd, gain):
    dx = dy * gain
    m1 = jnp.mean(dx, axis=-1, keepdims=True)
    m2 = jnp.mean(dx * xhat, axis=-1, keepdims=True)
    return rstd * (dx - m1 - xhat * m2)


def full_spec(shape):
    return pl.BlockSpec(shape, lambda *_: (0,) * len(shape), pipeline_mode=pl.Buffered(1))


def lane_masks(rows):
    lane = lax.broadcasted_iota(jnp.int32, (rows, 128), 1)
    return lane < HD


def split_heads(block):
    low = lane_masks(block.shape[0])
    zero = jnp.zeros_like(block)
    return jnp.where(low, block, zero), jnp.where(low, zero, block)


def q_tiles(rows):
    tiles = [(r, 0, r + 256, True) for r in range(0, LONG, 256)]
    tiles += [(LONG, LONG, rows, False)]
    return tiles


def diag_allowed(is_long, seg_row, seg_col):
    kv = lax.broadcasted_iota(jnp.int32, (256, 256), 0)
    qp = lax.broadcasted_iota(jnp.int32, (256, 256), 1)
    allowed = kv <= qp
    if not is_long:
        allowed = allowed & (seg_col == seg_row)
    return allowed


def attn_kernel(q_ref, k_ref, v_ref, segr_ref, segc_ref, o_ref, lse_ref):
    rows = q_ref.shape[0]
    ks = split_heads(k_ref[...] * BF(HD**-0.5))
    vt = v_ref[...].T
    items = [(tile, h) for tile in q_tiles(rows) for h in range(2)]

    def score(item):
        (q0, kv0, kv1, _), h = item
        return dot_t(ks[h][kv0:kv1], q_ref[q0 : q0 + 256, :])

    queue = [score(it) for it in items[:3]]
    outs = []
    for n, ((q0, kv0, kv1, is_long), h) in enumerate(items):
        if n + 3 < len(items):
            queue.append(score(items[n + 3]))
        s, queue[n] = queue[n], None
        parts = mask_diagonal(s, q0 - kv0, is_long, segr_ref, segc_ref)
        top = functools.reduce(jnp.maximum, [jnp.max(p, axis=0, keepdims=True) for p in parts])
        exps = [jnp.exp(p - top) for p in parts]
        total = functools.reduce(jnp.add, [jnp.sum(e, axis=0, keepdims=True) for e in exps])
        lse_ref[0, h : h + 1, q0 : q0 + 256] = top + jnp.log(total)
        probs = jnp.concatenate([e.astype(BF) for e in exps], axis=0)
        outs.append(dot(vt[h * HD : (h + 1) * HD, kv0:kv1], probs) * (1.0 / total))
        if h == 1:
            o_ref[q0 : q0 + 256, :] = jnp.concatenate(outs, axis=0).T.astype(BF)
            outs = []


def mask_diagonal(s, at, is_long, segr_ref, segc_ref):
    allowed = diag_allowed(is_long, segr_ref[...], segc_ref[...])
    diag = jnp.where(allowed, s[at:], NEG)
    return [s[:at], diag] if at else [diag]


def attn_call(joined, seg_row, seg_col, group0, groups):
    rows = joined.shape[0]
    pairs = joined.shape[1] // 384
    at = lambda t: pl.BlockSpec((rows, 128), lambda p: (0, pair_block(group0 * 2 + p, pairs) * 3 + t))
    return pl.pallas_call(
        attn_kernel,
        grid=(2 * groups,),
        in_specs=[at(0), at(1), at(2), full_spec((1, 256)), full_spec((256, 1))],
        out_specs=[
            pl.BlockSpec((rows, 128), lambda p: (0, p)),
            pl.BlockSpec((1, 2, rows), lambda p: (p, 0, 0)),
        ],
        out_shape=[
            jax.ShapeDtypeStruct((rows, groups * 256), BF),
            jax.ShapeDtypeStruct((2 * groups, 2, rows), F32),
        ],
        compiler_params=params(),
        cost_estimate=cost(groups * 8e9, 8e6, 5.5e6),
        name="attn",
    )(joined, joined, joined, seg_row, seg_col)


def pair_block(p, pairs):
    return (p % 2) * (pairs // 2) + p // 2


ANY = pl.BlockSpec(memory_space=pl.ANY)
SMEM = pl.BlockSpec(memory_space=pltpu.SMEM)


def local_copy(src, dst, sem):
    return pltpu.make_async_copy(src, dst, sem)


def chips_of(dims, where_ref):
    z_n, y_n, x_n = dims
    zi, yi, xi = [where_ref[i] for i in range(3)]
    for i in range(y_n * x_n):
        for j in range(z_n):
            yield i, j, lax.rem(zi + j, z_n), lax.rem(yi + i // x_n, y_n), lax.rem(xi + i % x_n, x_n)


def piece_at(dims, arrays, i, j):
    at = i * dims[0] + j
    for a in arrays:
        if at < a.shape[0]:
            return a.at[at]
        at -= a.shape[0]


def load_columns(dims, where_ref, own, oth, first, cols, dst, sem):
    ci = where_ref[3]
    for i, j, z, y, x in chips_of(dims, where_ref):
        for half, src in ((ci, own), (1 - ci, oth)):
            block = piece_at(dims, src, i, j).at[:, pl.ds(first, cols)]
            local_copy(block, dst.at[half, z, y, x], sem.at[half, z, y, x]).start()


def wait_columns(dims, dst, sem, half):
    for z in range(dims[0]):
        for y in range(dims[1]):
            for x in range(dims[2]):
                block = dst.at[half, z, y, x]
                local_copy(block, block, sem.at[half, z, y, x]).wait()


def flat2(value):
    return value.reshape(-1, value.shape[-1])


def store_columns(dims, where_ref, src, own, oth, half, first, cols, sem):
    ci = where_ref[3]
    for other, out in ((False, own), (True, oth)):

        @pl.when((half != ci) if other else (half == ci))
        def _():
            for i, j, z, y, x in chips_of(dims, where_ref):
                local_copy(src.at[z, y, x], out.at[i, j, :, pl.ds(first, cols)], sem.at[i, j]).start()


def wait_store(dims, src, out, first, cols, sem):
    for i in range(dims[1] * dims[2]):
        for j in range(dims[0]):
            local_copy(src.at[0, 0, 0], out.at[i, j, :, pl.ds(first, cols)], sem.at[i, j]).wait()


def weight_scratch(dims, n, cols):
    return [
        pltpu.VMEM((2,) + dims + (n, cols), BF),
        pltpu.SemaphoreType.DMA((2,) + dims),
    ]


def vector_plan(d, devices):
    r = d // devices
    return {
        "g1": (0, 0, r), "b1": (0, r, r), "qv": (0, 2 * r, 2 * r), "fb": (1, 0, 4 * r),
        "pb": (2, 0, r), "g2": (2, r, r), "b2": (2, 2 * r, r), "ob": (2, 3 * r, r),
    }


VECTOR_ROWS = {"g1": 0, "b1": 1, "qv": 2, "pb": 3, "g2": 4, "b2": 5, "fb": 6, "ob": 7}


def owner_of(shape, size, axis):
    c = lax.broadcasted_iota(jnp.int32, shape, axis).astype(F32)
    owner = jnp.floor((c + 0.5) * (1.0 / size))
    return owner, c - owner * size


def row_pick(devices, d, row):
    r = d // devices
    at = lax.broadcasted_iota(jnp.int32, (devices, d), 1)
    dev = lax.broadcasted_iota(jnp.int32, (devices, d), 0)
    return (at == dev * r + row).astype(BF)


def vector_maps(devices, n, first, size):
    owner, place = owner_of((devices, n), size, 1)
    mine = owner == lax.broadcasted_iota(jnp.int32, (devices, n), 0).astype(F32)
    _, place = owner_of((128, n), size, 1)
    spot = (place + first == lax.broadcasted_iota(jnp.int32, (128, n), 0).astype(F32)).astype(BF)
    return mine, spot


def unpack_vectors(table, d, devices, out_ref):
    plan = vector_plan(d, devices)
    picked = [dot(row_pick(devices, d, k), table).astype(BF) for k in range(3)]
    for name, i in VECTOR_ROWS.items():
        k, first, size = plan[name]
        n = size * devices
        mine, spot = vector_maps(devices, n, first, size)
        spread = dot(picked[k], spot)
        out_ref[i : i + 1, :n] = jnp.sum(jnp.where(mine, spread, 0.0), axis=0, keepdims=True)


def pack_vectors(rows, d, devices):
    plan = vector_plan(d, devices)
    parts = [None] * 3
    for name in VECTOR_ROWS:
        k, first, size = plan[name]
        n = size * devices
        mine, spot = vector_maps(devices, n, first, size)
        part = dot_t(jnp.where(mine, rows[name], 0.0).astype(BF), spot)
        parts[k] = part if parts[k] is None else parts[k] + part
    total = None
    for k in range(3):
        piece = dot_0(row_pick(devices, d, k), parts[k].astype(BF))
        total = piece if total is None else total + piece
    return total.astype(BF)


def cut_kernel(where_ref, w_ref, p_ref, t_ref, keep_ref, give_ref):
    ci = where_ref[3]
    pairs = w_ref.shape[1] // 384
    half = p_ref.shape[1] // 2
    for h in range(2):
        for other, out in ((False, keep_ref), (True, give_ref)):

            @pl.when((ci != h) if other else (ci == h))
            def _():
                at = 0
                for p in range(h, pairs, 2):
                    for t in range(3):
                        first = (t * pairs + p) * 128
                        out[:, at : at + 128] = w_ref[:, first : first + 128]
                        at += 128
                out[:, at : at + half] = p_ref[:, h * half : (h + 1) * half]
                out[:, at + half :] = t_ref[...]


def cut_call(where, w_qkv, w_proj, table):
    r = w_qkv.shape[0]
    cols = (w_qkv.shape[1] + w_proj.shape[1]) // 2 + 128
    shapes = [full_spec(v.shape) for v in (w_qkv, w_proj, table)]
    return pl.pallas_call(
        cut_kernel,
        grid=(1,),
        in_specs=[SMEM] + shapes,
        out_specs=[full_spec((r, cols))] * 2,
        out_shape=[jax.ShapeDtypeStruct((r, cols), BF)] * 2,
        compiler_params=params(),
        cost_estimate=cost(0, 4 * r * cols),
        name="cut",
    )(where, w_qkv, w_proj, table)


def first_norm_kernel(dims, count, devices, where_ref, x_ref, *refs):
    own = refs[:count]
    n_ref, nt_ref, vec_ref, t_scr, t_sem = refs[count:]
    rows, d = x_ref.shape
    table_at = own[0].shape[-1] - 128
    for i, j, z, y, x in chips_of(dims, where_ref):
        block = piece_at(dims, own, i, j).at[:, pl.ds(table_at, 128)]
        local_copy(block, t_scr.at[z, y, x], t_sem.at[z, y, x]).start()
    for z in range(dims[0]):
        for y in range(dims[1]):
            for x in range(dims[2]):
                block = t_scr.at[z, y, x]
                local_copy(block, block, t_sem.at[z, y, x]).wait()
    vec_ref[...] = jnp.zeros_like(vec_ref)
    unpack_vectors(flat2(t_scr[...]), d, devices, vec_ref)
    for r in range(0, rows, 256):
        xhat, _ = normalize(x_ref[r : r + 256, :].astype(F32))
        normed = (xhat * vec_ref[0:1, :d] + vec_ref[1:2, :d]).astype(BF)
        n_ref[r : r + 256, :] = normed
        nt_ref[:, r : r + 256] = normed.T


def first_norm_call(dims, where, x, own, devices):
    rows, d = x.shape
    return pl.pallas_call(
        functools.partial(first_norm_kernel, dims, len(own), devices),
        grid=(1,),
        in_specs=[SMEM, full_spec((rows, d))] + [ANY] * len(own),
        out_specs=[full_spec((rows, d)), full_spec((d, rows)), full_spec((8, 4 * d))],
        out_shape=[
            jax.ShapeDtypeStruct((rows, d), BF), jax.ShapeDtypeStruct((d, rows), BF),
            jax.ShapeDtypeStruct((8, 4 * d), F32),
        ],
        scratch_shapes=[pltpu.VMEM(dims + (own[0].shape[1], 128), BF), pltpu.SemaphoreType.DMA(dims)],
        compiler_params=params(),
        cost_estimate=cost(1e9, rows * d * 6),
        name="first_norm",
    )(where, x, *own)


def qkv_kernel(dims, count, where_ref, n_ref, vec_ref, *refs):
    own, oth = refs[:count], refs[count : 2 * count]
    o_ref, w_scr, w_sem, bias_scr = refs[2 * count :]
    rows, d = n_ref.shape
    cols = w_scr.shape[-1]
    step = pl.program_id(0)

    @pl.when(step == 0)
    def _():
        load_columns(dims, where_ref, own, oth, 0, cols, w_scr, w_sem)
        zero = jnp.zeros((1, 128), F32)
        pairs = d // 128
        for p in range(pairs):
            at = pair_block(p, pairs) * 384
            half, at = at // cols, at % cols
            bias_scr[half, :, at : at + 128] = vec_ref[2:3, p * 128 : (p + 1) * 128]
            bias_scr[half, :, at + 128 : at + 256] = zero
            bias_scr[half, :, at + 256 : at + 384] = vec_ref[2:3, d + p * 128 : d + (p + 1) * 128]
        wait_columns(dims, w_scr, w_sem, 0)

    @pl.when(step == 1)
    def _():
        wait_columns(dims, w_scr, w_sem, 1)

    w = flat2(w_scr[step])
    for r in range(0, rows, 256):
        o_ref[r : r + 256, :] = (dot(n_ref[r : r + 256, :], w) + bias_scr[step]).astype(BF)


def qkv_call(dims, where, normed, vec, own, oth):
    rows, d = normed.shape
    n = own[0].shape[1]
    cols = 3 * d // 2
    return pl.pallas_call(
        functools.partial(qkv_kernel, dims, len(own)),
        grid=(2,),
        in_specs=[SMEM, full_spec((rows, d)), full_spec(vec.shape)] + [ANY] * (2 * len(own)),
        out_specs=pl.BlockSpec((rows, cols), lambda j: (0, j)),
        out_shape=jax.ShapeDtypeStruct((rows, 2 * cols), BF),
        scratch_shapes=weight_scratch(dims, n, cols) + [pltpu.VMEM((2, 1, cols), F32)],
        compiler_params=params(),
        cost_estimate=cost(4 * rows * d * cols, rows * d * 8 + d * cols * 4),
        name="qkv",
    )(where, normed, vec, *own, *oth)


def proj_kernel(dims, count, first, where_ref, x_ref, a0_ref, a1_ref, vec_ref, *refs):
    own, oth = refs[:count], refs[count : 2 * count]
    mid_ref, n_ref, w_scr, w_sem = refs[2 * count :]
    d = x_ref.shape[1]

    @pl.when(pl.program_id(0) == 0)
    def _():
        load_columns(dims, where_ref, own, oth, first, w_scr.shape[-1], w_scr, w_sem)
        for h in range(2):
            wait_columns(dims, w_scr, w_sem, h)

    a = jnp.concatenate([a0_ref[...], a1_ref[...]], axis=1)
    branch = jnp.concatenate([dot(a, flat2(w_scr[h])) for h in range(2)], axis=1) + vec_ref[3:4, :d]
    middle = x_ref[...].astype(F32) + BS * branch
    mid_ref[...] = middle
    xhat, _ = normalize(middle)
    n_ref[...] = (xhat * vec_ref[4:5, :d] + vec_ref[5:6, :d]).astype(BF)


def proj_call(dims, where, x, att, vec, own, oth):
    rows, d = x.shape
    br = 256
    row = pl.BlockSpec((br, d), lambda i: (i, 0))
    return pl.pallas_call(
        functools.partial(proj_kernel, dims, len(own), 3 * d // 2),
        grid=(rows // br,),
        in_specs=[SMEM, row] + [pl.BlockSpec((br, v.shape[1]), lambda i: (i, 0)) for v in att]
        + [full_spec(vec.shape)] + [ANY] * (2 * len(own)),
        out_specs=[row, row],
        out_shape=[jax.ShapeDtypeStruct((rows, d), F32), jax.ShapeDtypeStruct((rows, d), BF)],
        scratch_shapes=weight_scratch(dims, own[0].shape[1], d // 2),
        compiler_params=params(),
        cost_estimate=cost(2 * rows * d * d, rows * d * 10 + d * d * 2),
        name="proj",
    )(where, x, *att, vec, *own, *oth)


def mlp_kernel(dims, count, where_ref, n_ref, c_ref, mid_ref, vec_ref, *refs):
    own, oth = refs[:count], refs[count : 2 * count]
    (
        out_ref, gn_ref, gfb_ref, gob_ref, g_own, g_oth,
        mid_scr, mid_sem, nt_scr, mg_scr, acc_scr, act_scr, gp_scr, f_scr, f_sem, o_scr, o_sem, gf_scr, gf_sem, go_scr, go_sem,
    ) = refs[2 * count :]
    z_n, y_n, x_n = dims
    zi, yi, xi, ci = [where_ref[i] for i in range(4)]
    j = pl.program_id(0)
    blocks = o_scr.shape[0]
    rows, d = n_ref.shape
    n = own[0].shape[1]
    wide = f_scr.shape[-1]
    parts = d // n
    br = 512

    @pl.when(j == 0)
    def _():
        load_columns(dims, where_ref, own, oth, 0, wide, f_scr, f_sem)
        for i, s, z, y, x in chips_of(dims, where_ref):
            for core, src in ((ci, own), (1 - ci, oth)):
                for t in range(2):
                    at = (((z * y_n + y) * x_n + x) * 2 + core) * 2 + t
                    q = lax.rem(at, parts)
                    local_copy(
                        piece_at(dims, src, i, s).at[:, pl.ds(wide + t * d, d)],
                        o_scr.at[at // parts, pl.ds(pl.multiple_of(q * n, 16), n), :],
                        o_sem.at[at // parts, q],
                    ).start()
        local_copy(mid_ref, mid_scr, mid_sem).start()
        nt_scr[...] = n_ref[...].T
        total = jnp.zeros_like(gob_ref)
        for r in range(0, rows, br):
            mg = (BS * c_ref[r : r + br, :].astype(F32)).astype(BF)
            mg_scr[r : r + br, :] = mg
            total += jnp.sum(mg.astype(F32), axis=0, keepdims=True)
        gob_ref[...] = total
        wait_columns(dims, f_scr, f_sem, 0)

    @pl.when(j == blocks // 2)
    def _():
        wait_columns(dims, f_scr, f_sem, 1)

    for q in range(parts):
        part = o_scr.at[j, pl.ds(q * n, n), :]
        local_copy(part, part, o_sem.at[j, q]).wait()

    half = j // (blocks // 2)
    first = pl.multiple_of(lax.rem(j, blocks // 2) * d, 128)
    wf = flat2(f_scr[half, :, :, :, :, pl.ds(first, d)])
    wo = o_scr[j]
    fb = vec_ref[6:7, pl.ds(pl.multiple_of(j * d, 128), d)]
    bias_sum = jnp.zeros((1, d), F32)
    starts = list(range(0, rows, br))

    def ahead_of(r):
        return dot(n_ref[r : r + br, :], wf), dot_t(mg_scr[r : r + br, :], wo)

    def behind(r, act, gp):
        rr = slice(r, r + br)
        fwd = dot(act, wo)
        back = dot_t(gp, wf)
        acc_scr[rr, :] = jnp.where(j == 0, fwd, acc_scr[rr, :] + fwd)
        gn_ref[rr, :] = jnp.where(j == 0, back, gn_ref[rr, :] + back)

    queue = [ahead_of(starts[0])]
    waiting = None
    for i, r in enumerate(starts):
        rr = slice(r, r + br)
        if i + 1 < len(starts):
            queue.append(ahead_of(starts[i + 1]))
        (pre, ga), queue[i] = queue[i], None
        pre = pre + fb
        sq = pre * pre
        t = jnp.tanh(GC0 * pre * (1.0 + GC1 * sq))
        half_t = 0.5 * (1.0 + t)
        act = (pre * half_t).astype(BF)
        slope = half_t + (0.5 * GC0) * pre * (1.0 - t * t) * (1.0 + (3.0 * GC1) * sq)
        gp = (slope * ga).astype(BF)
        act_scr[rr, :] = act
        gp_scr[rr, :] = gp
        bias_sum += jnp.sum(gp.astype(F32), axis=0, keepdims=True)
        if waiting is not None:
            behind(*waiting)
        waiting = r, act, gp
    behind(*waiting)

    gfb_ref[...] = bias_sum
    gf_scr[j] = dot(nt_scr[...], gp_scr[...]).astype(BF).reshape(gf_scr.shape[1:])
    store_columns(dims, where_ref, gf_scr.at[j], g_own, g_oth, half, first, d, gf_sem.at[j])
    go_scr[j] = dot_0(act_scr[...], mg_scr[...]).astype(BF)
    for q in range(parts):
        at = j * parts + q
        dev, t = at // 2, lax.rem(at, 2)
        core = lax.rem(dev, 2)
        x = lax.rem(dev // 2, x_n)
        y = lax.rem(dev // (2 * x_n), y_n)
        z = dev // (2 * x_n * y_n)
        piece = lax.rem(y - yi + y_n, y_n) * x_n + lax.rem(x - xi + x_n, x_n)
        slot = lax.rem(z - zi + z_n, z_n)
        to = pl.ds(pl.multiple_of(wide + t * d, 128), d)
        for other, out in ((False, g_own), (True, g_oth)):

            @pl.when((core != ci) if other else (core == ci))
            def _():
                local_copy(go_scr.at[j, pl.ds(q * n, n), :], out.at[piece, slot, :, to], go_sem.at[j, q]).start()

    @pl.when(j == blocks - 1)
    def _():
        local_copy(mid_ref, mid_scr, mid_sem).wait()
        for r in range(0, rows, br):
            rr = slice(r, r + br)
            out_ref[rr, :] = (mid_scr[rr, :] + BS * (acc_scr[rr, :] + vec_ref[7:8, :d])).astype(BF)
        for b in range(blocks):
            wait_store(dims, gf_scr.at[b], g_own, 0, d, gf_sem.at[b])
            for q in range(parts):
                part = go_scr.at[b, pl.ds(q * n, n), :]
                local_copy(part, part, go_sem.at[b, q]).wait()


def mlp_call(dims, where, normed, cot, middle, vec, own, oth):
    rows, d = normed.shape
    n, cols = own[0].shape[1:]
    wide = cols - 2 * d
    blocks = 2 * wide // d
    count = dims[1] * dims[2]
    act = full_spec((rows, d))
    piece = jax.ShapeDtypeStruct((count, dims[0], n, cols), BF)
    return pl.pallas_call(
        functools.partial(mlp_kernel, dims, len(own)),
        grid=(blocks,),
        in_specs=[SMEM, act, act, ANY, full_spec(vec.shape)] + [ANY] * (2 * len(own)),
        out_specs=[act, act, pl.BlockSpec((1, d), lambda j: (0, j)), full_spec((1, d))] + [ANY] * 2,
        out_shape=[
            jax.ShapeDtypeStruct((rows, d), BF),
            jax.ShapeDtypeStruct((rows, d), F32),
            jax.ShapeDtypeStruct((1, blocks * d), F32),
            jax.ShapeDtypeStruct((1, d), F32),
            piece, piece,
        ],
        scratch_shapes=[
            pltpu.VMEM((rows, d), F32), pltpu.SemaphoreType.DMA(()), pltpu.VMEM((d, rows), BF), pltpu.VMEM((rows, d), BF), pltpu.VMEM((rows, d), F32),
            pltpu.VMEM((rows, d), BF), pltpu.VMEM((rows, d), BF),
        ]
        + weight_scratch(dims, n, wide)
        + [
            pltpu.VMEM((blocks, d, d), BF), pltpu.SemaphoreType.DMA((blocks, d // n)),
            pltpu.VMEM((blocks,) + dims + (n, d), BF), pltpu.SemaphoreType.DMA((blocks, count, dims[0])),
            pltpu.VMEM((blocks, d, d), BF), pltpu.SemaphoreType.DMA((blocks, d // n)),
        ],
        compiler_params=params(),
        cost_estimate=cost(24 * rows * d * wide, 30e6, 2 * rows * wide),
        name="mlp",
    )(where, normed, cot, middle, vec, *own, *oth)


def proj_back_kernel(dims, count, first, where_ref, gn_ref, mid_ref, c_ref, a0_ref, a1_ref, vec_ref, ind_ref, *refs):
    own, oth = refs[:count], refs[count : 2 * count]
    (
        gm_ref, ga_ref, gw_ref, del_ref, gg_ref, gb_ref, gpb_ref, gw_acc, w_scr, w_sem,
    ) = refs[2 * count :]
    i = pl.program_id(0)
    d = mid_ref.shape[1]
    m = d // 2

    @pl.when(i == 0)
    def _():
        load_columns(dims, where_ref, own, oth, first, m, w_scr, w_sem)
        gw_acc[...] = jnp.zeros_like(gw_acc)
        gg_ref[...] = jnp.zeros_like(gg_ref)
        gb_ref[...] = jnp.zeros_like(gb_ref)
        gpb_ref[...] = jnp.zeros_like(gpb_ref)
        for h in range(2):
            wait_columns(dims, w_scr, w_sem, h)

    dy = gn_ref[...]
    xhat, rstd = normalize(mid_ref[...])
    gg_ref[...] += jnp.sum(dy * xhat, axis=0, keepdims=True)
    gb_ref[...] += jnp.sum(dy, axis=0, keepdims=True)
    gm = c_ref[...].astype(F32) + ln_back(dy, xhat, rstd, vec_ref[4:5, :d])
    gm_ref[...] = gm
    pg = (BS * gm).astype(BF)
    gpb_ref[...] += jnp.sum(pg.astype(F32), axis=0, keepdims=True)
    a = jnp.concatenate([a0_ref[...], a1_ref[...]], axis=1)
    gw_acc[...] += dot_0(a, pg)
    ga = (dot_t(pg[:, :m], flat2(w_scr[0])) + dot_t(pg[:, m:], flat2(w_scr[1]))).astype(BF)
    ga_ref[...] = ga
    prod = ga.astype(F32) * a.astype(F32)
    high = prod.astype(BF)
    low = (prod - high.astype(F32)).astype(BF)
    del_ref[...] = dot_t(ind_ref[...], high) + dot_t(ind_ref[...], low)

    @pl.when(i == pl.num_programs(0) - 1)
    def _():
        gw_ref[...] = gw_acc[...].astype(BF)


def proj_back_call(dims, where, gn, middle, cot, att, vec, own, oth):
    rows, d = middle.shape
    br = 256
    row = pl.BlockSpec((br, d), lambda i: (i, 0))
    ind = jnp.asarray(np.arange(16)[:, None] == np.arange(d)[None, :] // HD, BF)
    one = full_spec((1, d))
    vshape = jax.ShapeDtypeStruct((1, d), F32)
    return pl.pallas_call(
        functools.partial(proj_back_kernel, dims, len(own), 3 * d // 2),
        grid=(rows // br,),
        in_specs=[SMEM, row, row, row] + [pl.BlockSpec((br, v.shape[1]), lambda i: (i, 0)) for v in att]
        + [full_spec(vec.shape), full_spec((16, d))] + [ANY] * (2 * len(own)),
        out_specs=[row, row, full_spec((d, d)), pl.BlockSpec((16, br), lambda i: (0, i)), one, one, one],
        out_shape=[
            jax.ShapeDtypeStruct((rows, d), F32),
            jax.ShapeDtypeStruct((rows, d), BF),
            jax.ShapeDtypeStruct((d, d), BF),
            jax.ShapeDtypeStruct((16, rows), F32),
            vshape, vshape, vshape,
        ],
        scratch_shapes=[pltpu.VMEM((d, d), F32)] + weight_scratch(dims, own[0].shape[1], d // 2),
        compiler_params=params(),
        cost_estimate=cost(4 * rows * d * d, rows * d * 16),
        name="proj_back",
    )(where, gn, middle, cot, *att, vec, ind, *own, *oth)


def pair_back(j_ref, do_ref, lse_ref, del_ref, row, segr_ref, segc_ref, pair, dj_ref, dk_acc, dv_acc):
    rows = j_ref.shape[0]
    scale = HD**-0.5
    lanes = slice(pair * 128, (pair + 1) * 128)
    base = pair * 384
    k = j_ref[:, 128:256] * BF(scale)
    ks = split_heads(k)
    kt = k.T
    vs = split_heads(j_ref[:, 256:384])
    qt = j_ref[:, 0:128].T
    dot_do = do_ref[:, lanes].T
    items = [(tile, h) for tile in q_tiles(rows)[::-1] for h in range(2)]

    def ahead_of(item):
        (q0, kv0, kv1, _), h = item
        q = j_ref[q0 : q0 + 256, 0:128]
        do = do_ref[q0 : q0 + 256, lanes]
        return dot_t(ks[h][kv0:kv1], q), dot_t(vs[h][kv0:kv1], do)

    def behind(tile, h, probs, ds):
        q0, kv0, kv1, _ = tile
        hh = slice(h * HD, (h + 1) * HD)
        qq = slice(q0, q0 + 256)
        dv = dot_t(dot_do[hh, qq], probs)
        dk = dot_t(qt[hh, qq], ds)
        if q0 in (LONG, LONG - 256):
            dk_acc[hh, kv0:kv1] = dk
            dv_acc[hh, kv0:kv1] = dv
        else:
            dk_acc[hh, kv0:kv1] += dk
            dv_acc[hh, kv0:kv1] += dv
        return dot(kt[hh, kv0:kv1], ds)

    queue = [ahead_of(it) for it in items[:2]]
    waiting, dqs = None, []

    def settle():
        tile, h = waiting[:2]
        dqs.append(behind(*waiting))
        if h == 1:
            q0 = tile[0]
            dj_ref[q0 : q0 + 256, base : base + 128] = jnp.concatenate(dqs[-2:], axis=0).T.astype(BF)

    for n, (tile, h) in enumerate(items):
        q0, kv0, kv1, is_long = tile
        if n + 2 < len(items):
            queue.append(ahead_of(items[n + 2]))
        (s, dp), queue[n] = queue[n], None
        lse = lse_ref[pair, h : h + 1, q0 : q0 + 256]
        dlt = del_ref[pl.ds(row + h, 1), q0 : q0 + 256]
        parts = mask_diagonal(s, q0 - kv0, is_long, segr_ref, segc_ref)
        probs = jnp.concatenate([jnp.exp(p - lse) for p in parts], axis=0)
        ds = (probs * (dp - dlt)).astype(BF)
        if waiting is not None:
            settle()
        waiting = tile, h, probs.astype(BF), ds
    settle()
    dj_ref[:, base + 128 : base + 256] = (dk_acc[...] * scale).T.astype(BF)
    dj_ref[:, base + 256 : base + 384] = dv_acc[...].T.astype(BF)


def attn_back_kernel(
    dims, count, devices, where_ref, j0_ref, j1_ref, do_ref, lse_ref, del_ref, segr_ref, segc_ref,
    x_ref, vec_ref, gwp_ref, gfb_ref, gob_ref, gg2_ref, gb2_ref, gpb_ref, gm_ref, nt_ref, *refs,
):
    own, oth, refs = refs[:count], refs[count : 2 * count], refs[2 * count :]
    gx_ref, g_own, g_oth = refs[:3]
    (
        w_scr, w_sem, nt_scr, nt_sem, gn_scr, gm_scr, gm_sem, dj_scr, dk_acc, dv_acc, gw_scr, gw_sem,
        p_scr, p_sem, t_scr, t_sem, qv_scr,
    ) = refs[3:]
    i = pl.program_id(0)
    groups = gw_scr.shape[0]
    rows, d = x_ref.shape
    br = 256
    proj_at = groups * 384
    table_at = proj_at + d // 2

    @pl.when(i == 0)
    def _():
        load_columns(dims, where_ref, own, oth, 0, groups * 384, w_scr, w_sem)
        local_copy(nt_ref, nt_scr, nt_sem).start()
        local_copy(gm_ref, gm_scr, gm_sem).start()
        for h in range(2):
            p_scr[h] = gwp_ref[:, h * (d // 2) : (h + 1) * (d // 2)].reshape(p_scr.shape[1:])
            store_columns(dims, where_ref, p_scr.at[h], g_own, g_oth, h, proj_at, d // 2, p_sem.at[h])

    for h, j_ref in enumerate((j0_ref, j1_ref)):
        row = (i * 2 + h) * 2
        pair_back(j_ref, do_ref, lse_ref, del_ref, row, segr_ref, segc_ref, h, dj_scr, dk_acc, dv_acc)

    @pl.when(i == 0)
    def _():
        local_copy(nt_ref, nt_scr, nt_sem).wait()
        for h in range(2):
            wait_columns(dims, w_scr, w_sem, h)

    first = pl.multiple_of(i * 384, 128)
    dj = dj_scr[...]
    for h in range(2):
        for t, off in ((0, 0), (2, d)):
            part = dj[:, h * 384 + t * 128 : h * 384 + (t + 1) * 128].astype(F32)
            qv_scr[:, pl.ds(pl.multiple_of(off + (i * 2 + h) * 128, 128), 128)] = jnp.sum(part, axis=0, keepdims=True)
    gw = dot(nt_scr[...], dj).astype(BF)
    for h in range(2):
        gw_scr[i, h] = gw[:, h * 384 : (h + 1) * 384].reshape(gw_scr.shape[2:])
        store_columns(dims, where_ref, gw_scr.at[i, h], g_own, g_oth, h, first, 384, gw_sem.at[i, h])
    w = jnp.concatenate([flat2(w_scr[h, :, :, :, :, pl.ds(first, 384)]) for h in range(2)], axis=1)
    for r in range(0, rows, br):
        back = dot_t(dj[r : r + br, :], w)
        gn_scr[r : r + br, :] = jnp.where(i == 0, back, gn_scr[r : r + br, :] + back)

    @pl.when(i == groups - 1)
    def _():
        local_copy(gm_ref, gm_scr, gm_sem).wait()
        gg = jnp.zeros((1, d), F32)
        gb = jnp.zeros((1, d), F32)
        for r in range(0, rows, br):
            rr = slice(r, r + br)
            xhat, rstd = normalize(x_ref[rr, :].astype(F32))
            dy = gn_scr[rr, :]
            gg += jnp.sum(dy * xhat, axis=0, keepdims=True)
            gb += jnp.sum(dy, axis=0, keepdims=True)
            gx_ref[rr, :] = (gm_scr[rr, :] + ln_back(dy, xhat, rstd, vec_ref[0:1, :d])).astype(BF)
        table = pack_vectors(
            {
                "g1": gg, "b1": gb, "qv": qv_scr[...], "fb": gfb_ref[...], "pb": gpb_ref[...],
                "g2": gg2_ref[...], "b2": gb2_ref[...], "ob": gob_ref[...],
            },
            d, devices,
        ).reshape(t_scr.shape)
        t_scr[...] = table
        for h in range(2):
            store_columns(dims, where_ref, t_scr, g_own, g_oth, h, table_at, 128, t_sem.at[h])
        for h in range(2):
            for b in range(groups):
                wait_store(dims, gw_scr.at[b, h], g_own, 0, 384, gw_sem.at[b, h])
            wait_store(dims, p_scr.at[h], g_own, proj_at, d // 2, p_sem.at[h])
            wait_store(dims, t_scr, g_own, table_at, 128, t_sem.at[h])


def attn_back_call(dims, where, joined, ga, lse, delta, seg_row, seg_col, x, vec, own, oth, vectors, gm, nt, devices):
    rows, d = x.shape
    n = own[0].shape[1]
    groups = d // 256
    act = full_spec((rows, d))
    count = dims[1] * dims[2]
    piece = jax.ShapeDtypeStruct((count, dims[0], n, groups * 384 + d // 2 + 128), BF)
    return pl.pallas_call(
        functools.partial(attn_back_kernel, dims, len(own), devices),
        grid=(groups,),
        in_specs=[
            SMEM,
            pl.BlockSpec((rows, 384), lambda i: (0, i)),
            pl.BlockSpec((rows, 384), lambda i: (0, groups + i)),
            pl.BlockSpec((rows, 256), lambda i: (0, i)),
            pl.BlockSpec((2, 2, rows), lambda i: (i, 0, 0)),
            full_spec(delta.shape), full_spec((1, 256)), full_spec((256, 1)), act, full_spec(vec.shape),
        ]
        + [full_spec(v.shape) for v in vectors] + [ANY] * (2 + 2 * len(own)),
        out_specs=[act, ANY, ANY],
        out_shape=[jax.ShapeDtypeStruct((rows, d), BF), piece, piece],
        scratch_shapes=weight_scratch(dims, n, groups * 384)
        + [
            pltpu.VMEM((d, rows), BF), pltpu.SemaphoreType.DMA(()), pltpu.VMEM((rows, d), F32),
            pltpu.VMEM((rows, d), F32), pltpu.SemaphoreType.DMA(()), pltpu.VMEM((rows, 768), BF),
            pltpu.VMEM((128, rows), F32), pltpu.VMEM((128, rows), F32),
            pltpu.VMEM((groups, 2) + dims + (n, 384), BF), pltpu.SemaphoreType.DMA((groups, 2, count, dims[0])),
            pltpu.VMEM((2,) + dims + (n, d // 2), BF), pltpu.SemaphoreType.DMA((2, count, dims[0])),
            pltpu.VMEM(dims + (n, 128), BF), pltpu.SemaphoreType.DMA((2, count, dims[0])),
            pltpu.VMEM((1, 2 * d), F32),
        ],
        compiler_params=params(),
        cost_estimate=cost(60e9, 20e6, 5.5e6),
        name="attn_back",
    )(where, joined, joined, ga, lse, delta, seg_row, seg_col, x, vec, *vectors, gm, nt, *own, *oth)


def pack_plan(counts, rows):
    c = [counts[i] for i in range(counts.shape[0])]
    ends, run = [], jnp.int32(0)
    for v in c:
        run = run + v
        ends.append(run)
    start = jnp.int32(0)
    for i in range(len(c) - 1):
        start = jnp.where(c[i] == LONG, ends[i] - c[i], start)
    rolled = jnp.arange(rows, dtype=jnp.int32)
    pos = rolled + start
    pos = jnp.where(pos >= rows, pos - rows, pos)
    seg = functools.reduce(jnp.add, [(pos >= e).astype(jnp.int32) for e in ends])
    valid = seg < len(c) - 1
    seg = jnp.where(valid, seg, 1000 + rolled)
    return start, seg[LONG:], valid


def roll_rows(array, shift):
    return lax.dynamic_slice_in_dim(jnp.concatenate([array, array], axis=0), shift, array.shape[0])


def half_columns(w, h, joined=False):
    r, cols = w.shape
    if not joined:
        return w[:, h * (cols // 2) : (h + 1) * (cols // 2)]
    pairs = cols // 384
    starts = [(t * pairs + p) * 128 for p in range(h, pairs, 2) for t in range(3)]
    return jnp.concatenate([w[:, s : s + 128] for s in starts], axis=1)


def join_columns(left, right):
    r, m = left.shape
    both = jnp.stack([v.reshape(r, m // 384, 3, 128) for v in (left, right)], axis=2)
    return both.transpose(0, 3, 1, 2, 4).reshape(r, 2 * m)


def add_all(values):
    return functools.reduce(jnp.add, [v.astype(F32) for v in values])


class Plain:
    def __init__(self, dp, fsdp):
        self.dims = (1, 1, 1)
        index = lax.axis_index("dp") * fsdp + lax.axis_index("fsdp")
        self.ci = index % 2

    def where(self):
        zero = jnp.zeros((), jnp.int32)
        return jnp.stack([zero, zero, zero, self.ci.astype(jnp.int32)])

    def pick(self, pair):
        return jnp.where(self.ci == 0, pair[0], pair[1]), jnp.where(self.ci == 0, pair[1], pair[0])

    def gather(self, w_qkv, w_proj, table, w_fc, w_out):
        whole = lambda v: lax.all_gather(v, AXES, axis=0, tiled=True)
        attn = whole(jnp.concatenate([w_qkv, w_proj, table], axis=1))
        cut = w_qkv.shape[1], w_qkv.shape[1] + w_proj.shape[1]
        fc, out = whole(w_fc), whole(w_out)
        d = out.shape[1]
        lists = [[], []]
        for h in range(2):
            qkv, proj, table = attn[:, : cut[0]], attn[:, cut[0] : cut[1]], attn[:, cut[1] :]
            lists[0].append(jnp.concatenate([half_columns(qkv, h, True), half_columns(proj, h), table], axis=1))
            lists[1].append(
                jnp.concatenate([half_columns(fc, h)] + [out[(2 * h + t) * d : (2 * h + t + 1) * d] for t in range(2)], axis=1)
            )
        listed = []
        for pair in lists:
            own, oth = self.pick(pair)
            listed.append(([own[None]], [oth[None]]))
        return listed

    def scatter(self, own, oth):
        pair = self.pick([own[0, 0], oth[0, 0]])
        m = pair[0].shape[1]
        mine = lax.psum_scatter(jnp.concatenate(pair, axis=1), AXES, scatter_dimension=0, tiled=True).astype(F32)
        return mine[:, :m], mine[:, m:]

    def scatter_hidden(self, own, oth):
        pair = self.pick([own[0, 0], oth[0, 0]])
        d = pair[0].shape[0]
        wide = pair[0].shape[1] - 2 * d
        fc = self.scatter(own[..., :wide], oth[..., :wide])
        out = jnp.concatenate([v[:, wide + t * d : wide + (t + 1) * d] for v in pair for t in range(2)], axis=0)
        return fc, lax.psum_scatter(out, AXES, scatter_dimension=0, tiled=True).astype(F32)


class Chips:
    def __init__(self, dp, fsdp):
        x_n, z_n = fsdp // 2, 4
        self.dims = (z_n, dp // z_n, x_n)
        index = lax.axis_index("dp") * fsdp + lax.axis_index("fsdp")
        self.ci = index % 2
        self.at = (index // (2 * x_n * self.dims[1]), (index // (2 * x_n)) % self.dims[1], (index // 2) % x_n, self.ci)

    def where(self):
        return jnp.stack(self.at).astype(jnp.int32)

    def pick(self, pair):
        return jnp.where(self.ci == 0, pair[0], pair[1]), jnp.where(self.ci == 0, pair[1], pair[0])

    def send(self, array, dz=0, dy=0, dx=0, dc=0):
        z_n, y_n, x_n = self.dims
        pairs = []
        for z in range(z_n):
            for y in range(y_n):
                for x in range(x_n):
                    for c in range(2):
                        here = ((z * y_n + y) * x_n + x) * 2 + c
                        there = (((z + dz) % z_n * y_n + (y + dy) % y_n) * x_n + (x + dx) % x_n) * 2 + (c + dc) % 2
                        pairs.append((here, there))
        return lax.ppermute(array, AXES, pairs)

    def trade(self, halves):
        return self.rows_of(*self.pick(halves))

    def rows_of(self, keep, give):
        return jnp.concatenate(self.pick([keep, self.send(give, dc=1)]), axis=0)

    def along_z(self, piece):
        return [piece] + [self.send(piece, dz=-k) for k in range(1, self.dims[0])]

    def swap(self, arrays):
        return [self.send(v, dc=1) for v in arrays]

    def add_core(self, own, theirs):
        return [add_all([own[i], theirs[i]]).astype(BF) for i in range(own.shape[0])]

    def rows_back(self, total):
        n = total.shape[0] // 2
        mine, give = self.pick([total[:n], total[n:]])
        return self.pick([mine, self.send(give, dc=1)])


def together(*trees):
    return lax.optimization_barrier(trees)


def prepare(tokens, lengths, cotangent):
    start, seg, valid = pack_plan(lengths[0], tokens.shape[0])
    x = roll_rows(tokens, start)
    cot = jnp.where(valid[:, None], roll_rows(cotangent, start), BF(0))
    return start, seg[None, :], seg[:, None], x, cot


def vector_table(r, ln1_gain, ln1_bias, qv_bias, proj_bias, ln2_gain, ln2_bias, fc_bias, out_bias):
    flat = [
        jnp.concatenate([ln1_gain, ln1_bias, qv_bias]), fc_bias,
        jnp.concatenate([proj_bias, ln2_gain, ln2_bias, out_bias]),
    ]
    return jnp.pad(jnp.stack(flat), ((0, r - 3), (0, 128 - 4 * r)))


def results(r, out, gx, s_fc, s_out, s_attn, table):
    d = out.shape[1]
    cut = 3 * d // 2
    s_qkv = join_columns(*[v[:, :cut] for v in s_attn])
    s_proj = jnp.concatenate([v[:, cut:] for v in s_attn], axis=1)
    row0, row1, row2 = [table[k, : 4 * r] for k in range(3)]
    return (
        out, gx,
        row0[:r], row0[r : 2 * r], s_qkv, row0[2 * r :], s_proj, row2[:r],
        row2[r : 2 * r], row2[2 * r : 3 * r], jnp.concatenate(s_fc, axis=1), row1, s_out, row2[3 * r :],
    )


def split_table(halves):
    return [v[:, :-128] for v in halves], halves[0][:, -128:]


def block_plain(
    links, tokens, lengths, ln1_gain, ln1_bias, w_qkv, qv_bias, w_proj, proj_bias, ln2_gain, ln2_bias,
    w_fc, fc_bias, w_out, out_bias, cotangent,
):
    rows, d = tokens.shape
    r = w_qkv.shape[0]
    devices = d // r
    dims, where = links.dims, links.where()
    table = vector_table(r, ln1_gain, ln1_bias, qv_bias, proj_bias, ln2_gain, ln2_bias, fc_bias, out_bias)
    attn_w, m_w = links.gather(w_qkv, w_proj, table, w_fc, w_out)
    start, seg_row, seg_col, x, cot = prepare(tokens, lengths, cotangent)
    normed, nt, vec = first_norm_call(dims, where, x, attn_w[0], devices)
    joined = qkv_call(dims, where, normed, vec, *attn_w)
    att0, lse0 = attn_call(joined, seg_row, seg_col, 0, 2)
    att1, lse1 = attn_call(joined, seg_row, seg_col, 2, d // 256 - 2)
    att = att0, att1
    middle, normed_two = proj_call(dims, where, x, att, vec, *attn_w)
    out, gn, gfb, gob, *m_g = mlp_call(dims, where, normed_two, cot, middle, vec, *m_w)
    s_fc, s_out = links.scatter_hidden(*m_g)
    gm, ga, gw_proj, delta, gg2, gb2, gpb = proj_back_call(dims, where, gn, middle, cot, att, vec, *attn_w)
    gx, *g = attn_back_call(
        dims, where, joined, ga, jnp.concatenate([lse0, lse1]), delta, seg_row, seg_col, x, vec, *attn_w,
        (gw_proj, gfb, gob, gg2, gb2, gpb), gm, nt, devices,
    )
    restore = rows - start
    return results(r, roll_rows(out, restore), roll_rows(gx, restore), s_fc, s_out, *split_table(links.scatter(*g)))


def block_chips(
    links, tokens, lengths, ln1_gain, ln1_bias, w_qkv, qv_bias, w_proj, proj_bias, ln2_gain, ln2_bias,
    w_fc, fc_bias, w_out, out_bias, cotangent,
):
    rows, d = tokens.shape
    r = w_qkv.shape[0]
    devices = d // r
    dims, where, send, swap = links.dims, links.where(), links.send, links.swap
    table = vector_table(r, ln1_gain, ln1_bias, qv_bias, proj_bias, ln2_gain, ln2_bias, fc_bias, out_bias)

    def xy(column):
        return send(column, dx=1), send(column, dy=1)

    def corner(x_part, y_part):
        return [send(x_part[:2], dy=1), send(y_part[2:], dx=1)]

    def near(b):
        return send(b[1], dx=1), send(b[2], dy=1), send(b[3], dx=1, dy=1)

    def far(parts):
        return [parts[0]] + [send(parts[j], dz=j) for j in range(1, dims[0])]

    a = links.rows_of(*cut_call(where, w_qkv, w_proj, table))
    a, tokens, lengths, cotangent, w_fc = together(a, tokens, lengths, cotangent, w_fc)
    a0 = links.along_z(a)
    fc = links.trade([half_columns(w_fc, h) for h in range(2)])
    m = jnp.concatenate([fc, w_out[: 2 * r], w_out[2 * r :]], axis=1)
    a0, m, tokens, lengths, cotangent = together(a0, m, tokens, lengths, cotangent)
    prep = prepare(tokens, lengths, cotangent)
    m0 = links.along_z(m)
    a0 = jnp.stack(a0)
    a_own = [a0, send(a0, dx=1), send(a0, dy=1), send(a0, dx=1, dy=1)]
    a_own, m0, prep = together(a_own, m0, prep)
    start, seg_row, seg_col, x, cot = prep
    m0 = jnp.stack(m0)
    a_own = [jnp.concatenate(a_own, axis=0)]
    m0, a_own = together(m0, a_own)
    attn_w = a_own, swap(a_own)
    mx, my = xy(m0)
    normed, nt, vec = first_norm_call(dims, where, x, a_own, devices)
    normed, attn_w = together(normed, attn_w)

    joined = qkv_call(dims, where, normed, vec, *attn_w)
    att0, lse0 = attn_call(joined, seg_row, seg_col, 0, 2)
    att0, joined, mx, my = together(att0, joined, mx, my)
    att1, lse1 = attn_call(joined, seg_row, seg_col, 2, d // 256 - 2)
    att = att0, att1
    middle, normed_two = proj_call(dims, where, x, att, vec, *attn_w)
    md = corner(mx, my)
    m_oth = swap([m0, mx, my])
    lse = jnp.concatenate([lse0, lse1])
    normed_two, md, m_oth, lse = together(normed_two, md, m_oth, lse)
    m_w = [m0, mx, my] + md, m_oth + swap(md)

    out, gn, gfb, gob, m_own, m_oth = mlp_call(dims, where, normed_two, cot, middle, vec, *m_w)
    gm, ga, gw_proj, delta, gg2, gb2, gpb = proj_back_call(dims, where, gn, middle, cot, att, vec, *attn_w)
    (m_oth,) = swap([m_oth])
    ga, delta, m_own, m_oth = together(ga, delta, m_own, m_oth)

    def chip_sum(i, part):
        return add_all([part(m_own[i]), part(m_oth[i])]).astype(BF)

    first = (
        chip_sum(3, lambda v: v[1:3]), chip_sum(3, lambda v: v[:1]), chip_sum(3, lambda v: v[3:]),
        chip_sum(1, lambda v: v[1:]), chip_sum(2, lambda v: v[:3]),
    )
    first, ga, delta, m_own, m_oth = together(first, ga, delta, m_own, m_oth)
    first = (
        send(first[0], dx=1, dy=1), send(first[1], dy=1), send(first[2], dx=1),
        send(first[3], dx=1), send(first[4], dy=1),
    )
    gx, g_own, g_oth = attn_back_call(
        dims, where, joined, ga, lse, delta, seg_row, seg_col, x, vec, *attn_w,
        (gw_proj, gfb, gob, gg2, gb2, gpb), gm, nt, devices,
    )
    gx, g_own, g_oth, first, m_own, m_oth, out = together(gx, g_own, g_oth, first, m_own, m_oth, out)

    (g_oth,) = swap([g_oth])
    corners, by_y, by_x, from_x, from_y = first

    def chip_total(i, j, arrived):
        return add_all([m_own[i, j], m_oth[i, j]] + arrived).astype(BF)

    x_one = send(chip_total(1, 0, [by_y[0]]), dx=1)
    y_one = send(chip_total(2, 3, [by_x[0]]), dy=1)
    b = {1: send(chip_total(0, 1, [from_x[0], from_y[1], corners[0]]), dz=1)}
    e = links.add_core(g_own, g_oth)
    e, x_one, y_one, gx, out, m_own, m_oth, b = together(e, x_one, y_one, gx, out, m_own, m_oth, b)

    e_near = near(e)
    b[0] = chip_total(0, 0, [x_one, from_y[0]])
    b[2] = send(chip_total(0, 2, [from_x[1], from_y[2], corners[1]]), dz=2)
    b[3] = send(chip_total(0, 3, [from_x[2], y_one]), dz=3)
    b = [b[j] for j in range(4)]
    gx, out = roll_rows(gx, rows - start), roll_rows(out, rows - start)
    e_near, b, e, gx, out = together(e_near, b, e, gx, out)

    e = far([add_all([e[0][j]] + [v[j] for v in e_near]).astype(BF) for j in range(dims[0])])
    total = add_all(b)
    s_fc = links.rows_back(total[:, : -2 * d])
    s_out = jnp.concatenate([total[:, -2 * d : -d], total[:, -d:]], axis=0)
    e, s_fc, s_out = together(e, s_fc, s_out)
    total = add_all(e)
    vectors = jnp.where(links.ci == 0, total[:3, -128:], total[r : r + 3, -128:])
    return results(r, out, gx, s_fc, s_out, links.rows_back(total[:, :-128]), vectors)


def solution(mesh):
    dp, fsdp = mesh.shape["dp"], mesh.shape["fsdp"]

    def per_device(*args):
        if (dp, fsdp) == (8, 4) and args[4].shape[0] % 8 == 0:
            return block_chips(Chips(dp, fsdp), *args)
        return block_plain(Plain(dp, fsdp), *args)

    row, vec = P(AXES, None), P(AXES)
    in_specs = (row, row, vec, vec, row, vec, row, vec, vec, vec, row, vec, row, vec, row)
    out_specs = (row, row, vec, vec, row, vec, row, vec, vec, vec, row, vec, row, vec)
    return jax.shard_map(
        per_device, mesh=mesh, in_specs=in_specs, out_specs=out_specs, check_vma=False
    )
```

```python
import functools
import math

import jax
import jax.numpy as jnp
import numpy as np
from jax import lax
from jax.experimental import pallas as pl
from jax.experimental.pallas import tpu as pltpu
from jax.sharding import PartitionSpec as P

HD = 64
LONG = 768
EPS = 1e-05
BS = 1.0 / math.sqrt(48.0)
NEG = -1e30
F32 = jnp.float32
BF = jnp.bfloat16
VMEM_LIMIT = 58 * 1024 * 1024
AXES = ("dp", "fsdp")
GC0 = math.sqrt(2.0 / math.pi)
GC1 = 0.044715


def dot(a, b):
    return lax.dot_general(a, b, (((1,), (0,)), ((), ())), preferred_element_type=F32)


def dot_t(a, b):
    return lax.dot_general(a, b, (((1,), (1,)), ((), ())), preferred_element_type=F32)


def dot_0(a, b):
    return lax.dot_general(a, b, (((0,), (0,)), ((), ())), preferred_element_type=F32)


def params(grid_len=1):
    return pltpu.CompilerParams(
        dimension_semantics=("arbitrary",) * grid_len, vmem_limit_bytes=VMEM_LIMIT
    )


def cost(flops, nbytes, trans=0):
    return pl.CostEstimate(flops=int(flops), bytes_accessed=int(nbytes), transcendentals=int(trans))


def normalize(values):
    centred = values - jnp.mean(values, axis=-1, keepdims=True)
    rstd = lax.rsqrt(jnp.mean(centred * centred, axis=-1, keepdims=True) + EPS)
    return centred * rstd, rstd


def ln_back(dy, xhat, rstd, gain):
    dx = dy * gain
    m1 = jnp.mean(dx, axis=-1, keepdims=True)
    m2 = jnp.mean(dx * xhat, axis=-1, keepdims=True)
    return rstd * (dx - m1 - xhat * m2)


def full_spec(shape):
    return pl.BlockSpec(shape, lambda *_: (0,) * len(shape), pipeline_mode=pl.Buffered(1))


def lane_masks(rows):
    lane = lax.broadcasted_iota(jnp.int32, (rows, 128), 1)
    return lane < HD


def split_heads(block):
    low = lane_masks(block.shape[0])
    zero = jnp.zeros_like(block)
    return jnp.where(low, block, zero), jnp.where(low, zero, block)


def q_tiles(rows):
    tiles = [(r, 0, r + 256, True) for r in range(0, LONG, 256)]
    tiles += [(LONG, LONG, rows, False)]
    return tiles


def diag_allowed(is_long, seg_row, seg_col):
    kv = lax.broadcasted_iota(jnp.int32, (256, 256), 0)
    qp = lax.broadcasted_iota(jnp.int32, (256, 256), 1)
    allowed = kv <= qp
    if not is_long:
        allowed = allowed & (seg_col == seg_row)
    return allowed


def attn_kernel(q_ref, k_ref, v_ref, segr_ref, segc_ref, o_ref, lse_ref):
    rows = q_ref.shape[0]
    ks = split_heads(k_ref[...] * BF(HD**-0.5))
    vt = v_ref[...].T
    items = [(tile, h) for tile in q_tiles(rows) for h in range(2)]

    def score(item):
        (q0, kv0, kv1, _), h = item
        return dot_t(ks[h][kv0:kv1], q_ref[q0 : q0 + 256, :])

    queue = [score(it) for it in items[:3]]
    outs = []
    for n, ((q0, kv0, kv1, is_long), h) in enumerate(items):
        if n + 3 < len(items):
            queue.append(score(items[n + 3]))
        s, queue[n] = queue[n], None
        parts = mask_diagonal(s, q0 - kv0, is_long, segr_ref, segc_ref)
        top = functools.reduce(jnp.maximum, [jnp.max(p, axis=0, keepdims=True) for p in parts])
        exps = [jnp.exp(p - top) for p in parts]
        total = functools.reduce(jnp.add, [jnp.sum(e, axis=0, keepdims=True) for e in exps])
        lse_ref[0, h : h + 1, q0 : q0 + 256] = top + jnp.log(total)
        probs = jnp.concatenate([e.astype(BF) for e in exps], axis=0)
        outs.append(dot(vt[h * HD : (h + 1) * HD, kv0:kv1], probs) * (1.0 / total))
        if h == 1:
            o_ref[q0 : q0 + 256, :] = jnp.concatenate(outs, axis=0).T.astype(BF)
            outs = []


def mask_diagonal(s, at, is_long, segr_ref, segc_ref):
    allowed = diag_allowed(is_long, segr_ref[...], segc_ref[...])
    diag = jnp.where(allowed, s[at:], NEG)
    return [s[:at], diag] if at else [diag]


def attn_call(joined, seg_row, seg_col, group0, groups):
    rows = joined.shape[0]
    pairs = joined.shape[1] // 384
    at = lambda t: pl.BlockSpec((rows, 128), lambda p: (0, pair_block(group0 * 2 + p, pairs) * 3 + t))
    return pl.pallas_call(
        attn_kernel,
        grid=(2 * groups,),
        in_specs=[at(0), at(1), at(2), full_spec((1, 256)), full_spec((256, 1))],
        out_specs=[
            pl.BlockSpec((rows, 128), lambda p: (0, p)),
            pl.BlockSpec((1, 2, rows), lambda p: (p, 0, 0)),
        ],
        out_shape=[
            jax.ShapeDtypeStruct((rows, groups * 256), BF),
            jax.ShapeDtypeStruct((2 * groups, 2, rows), F32),
        ],
        compiler_params=params(),
        cost_estimate=cost(groups * 8e9, 8e6, 5.5e6),
        name="attn",
    )(joined, joined, joined, seg_row, seg_col)


def pair_block(p, pairs):
    return (p % 2) * (pairs // 2) + p // 2


ANY = pl.BlockSpec(memory_space=pl.ANY)
SMEM = pl.BlockSpec(memory_space=pltpu.SMEM)


def local_copy(src, dst, sem):
    return pltpu.make_async_copy(src, dst, sem)


def places(dims, where_ref):
    z_n, y_n, x_n = dims
    zi, yi, xi = [where_ref[i] for i in range(3)]
    return [
        (lax.rem(y - yi + y_n, y_n) * x_n + lax.rem(x - xi + x_n, x_n)) * z_n + lax.rem(z - zi + z_n, z_n)
        for z in range(z_n)
        for y in range(y_n)
        for x in range(x_n)
    ]


def array_spans(arrays):
    at = 0
    for k, a in enumerate(arrays):
        yield k, a, pl.ds(at, a.shape[0])
        at += a.shape[0]


def load_columns(where_ref, own, oth, first, cols, dst, sem):
    ci = where_ref[3]
    for half, arrays in ((ci, own), (1 - ci, oth)):
        for k, a, span in array_spans(arrays):
            local_copy(a.at[:, :, pl.ds(first, cols)], dst.at[half, span], sem.at[half, k]).start()


def wait_columns(own, dst, sem, half):
    for k, _, span in array_spans(own):
        block = dst.at[half, span]
        local_copy(block, block, sem.at[half, k]).wait()


def whole_rows(dims, where_ref, scr, half, cols=slice(None)):
    return jnp.concatenate([scr[half, p, :, cols] for p in places(dims, where_ref)], axis=0)


def put_rows(dims, where_ref, scr, lead, value):
    n = scr.shape[-2]
    for i, p in enumerate(places(dims, where_ref)):
        scr[lead + (p,)] = value[i * n : (i + 1) * n]


def store_columns(where_ref, src, own, oth, half, first, cols, sem):
    ci = where_ref[3]
    for other, out in ((False, own), (True, oth)):

        @pl.when((half != ci) if other else (half == ci))
        def _():
            local_copy(src, out.at[:, :, pl.ds(first, cols)], sem).start()


def wait_store(src, sem):
    local_copy(src, src, sem).wait()


def weight_scratch(dims, n, cols, arrays):
    return [
        pltpu.VMEM((2, math.prod(dims), n, cols), BF),
        pltpu.SemaphoreType.DMA((2, arrays)),
    ]


def vector_plan(d, devices):
    r = d // devices
    return {
        "g1": (0, 0, r), "b1": (0, r, r), "qv": (0, 2 * r, 2 * r), "fb": (1, 0, 4 * r),
        "pb": (2, 0, r), "g2": (2, r, r), "b2": (2, 2 * r, r), "ob": (2, 3 * r, r),
    }


VECTOR_ROWS = {"g1": 0, "b1": 1, "qv": 2, "pb": 3, "g2": 4, "b2": 5, "fb": 6, "ob": 7}


def owner_of(shape, size, axis):
    c = lax.broadcasted_iota(jnp.int32, shape, axis).astype(F32)
    owner = jnp.floor((c + 0.5) * (1.0 / size))
    return owner, c - owner * size


def row_pick(devices, d, row):
    r = d // devices
    at = lax.broadcasted_iota(jnp.int32, (devices, d), 1)
    dev = lax.broadcasted_iota(jnp.int32, (devices, d), 0)
    return (at == dev * r + row).astype(BF)


def vector_maps(devices, n, first, size):
    owner, place = owner_of((devices, n), size, 1)
    mine = owner == lax.broadcasted_iota(jnp.int32, (devices, n), 0).astype(F32)
    _, place = owner_of((128, n), size, 1)
    spot = (place + first == lax.broadcasted_iota(jnp.int32, (128, n), 0).astype(F32)).astype(BF)
    return mine, spot


def unpack_vectors(table, d, devices, out_ref):
    plan = vector_plan(d, devices)
    picked = [dot(row_pick(devices, d, k), table).astype(BF) for k in range(3)]
    for name, i in VECTOR_ROWS.items():
        k, first, size = plan[name]
        n = size * devices
        mine, spot = vector_maps(devices, n, first, size)
        spread = dot(picked[k], spot)
        out_ref[i : i + 1, :n] = jnp.sum(jnp.where(mine, spread, 0.0), axis=0, keepdims=True)


def pack_vectors(rows, d, devices):
    plan = vector_plan(d, devices)
    parts = [None] * 3
    for name in VECTOR_ROWS:
        k, first, size = plan[name]
        n = size * devices
        mine, spot = vector_maps(devices, n, first, size)
        part = dot_t(jnp.where(mine, rows[name], 0.0).astype(BF), spot)
        parts[k] = part if parts[k] is None else parts[k] + part
    total = None
    for k in range(3):
        piece = dot_0(row_pick(devices, d, k), parts[k].astype(BF))
        total = piece if total is None else total + piece
    return total.astype(BF)


def cut_kernel(where_ref, w_ref, p_ref, t_ref, keep_ref, give_ref):
    ci = where_ref[3]
    pairs = w_ref.shape[1] // 384
    half = p_ref.shape[1] // 2
    for h in range(2):
        for other, out in ((False, keep_ref), (True, give_ref)):

            @pl.when((ci != h) if other else (ci == h))
            def _():
                at = 0
                for p in range(h, pairs, 2):
                    for t in range(3):
                        first = (t * pairs + p) * 128
                        out[:, at : at + 128] = w_ref[:, first : first + 128]
                        at += 128
                out[:, at : at + half] = p_ref[:, h * half : (h + 1) * half]
                out[:, at + half :] = t_ref[...]


def cut_call(where, w_qkv, w_proj, table):
    r = w_qkv.shape[0]
    cols = (w_qkv.shape[1] + w_proj.shape[1]) // 2 + 128
    shapes = [full_spec(v.shape) for v in (w_qkv, w_proj, table)]
    return pl.pallas_call(
        cut_kernel,
        grid=(1,),
        in_specs=[SMEM] + shapes,
        out_specs=[full_spec((r, cols))] * 2,
        out_shape=[jax.ShapeDtypeStruct((r, cols), BF)] * 2,
        compiler_params=params(),
        cost_estimate=cost(0, 4 * r * cols),
        name="cut",
    )(where, w_qkv, w_proj, table)


def first_norm_kernel(dims, count, devices, where_ref, x_ref, *refs):
    own = refs[:count]
    n_ref, nt_ref, vec_ref, t_scr, t_sem = refs[count:]
    rows, d = x_ref.shape
    table_at = own[0].shape[-1] - 128
    copies = [local_copy(a.at[:, :, pl.ds(table_at, 128)], t_scr.at[0, span], t_sem.at[i]) for i, a, span in array_spans(own)]
    for c in copies:
        c.start()
    for c in copies:
        c.wait()
    vec_ref[...] = jnp.zeros_like(vec_ref)
    unpack_vectors(whole_rows(dims, where_ref, t_scr, 0), d, devices, vec_ref)
    for r in range(0, rows, 256):
        xhat, _ = normalize(x_ref[r : r + 256, :].astype(F32))
        normed = (xhat * vec_ref[0:1, :d] + vec_ref[1:2, :d]).astype(BF)
        n_ref[r : r + 256, :] = normed
        nt_ref[:, r : r + 256] = normed.T


def first_norm_call(dims, where, x, own, devices):
    rows, d = x.shape
    return pl.pallas_call(
        functools.partial(first_norm_kernel, dims, len(own), devices),
        grid=(1,),
        in_specs=[SMEM, full_spec((rows, d))] + [ANY] * len(own),
        out_specs=[full_spec((rows, d)), full_spec((d, rows)), full_spec((8, 4 * d))],
        out_shape=[
            jax.ShapeDtypeStruct((rows, d), BF), jax.ShapeDtypeStruct((d, rows), BF),
            jax.ShapeDtypeStruct((8, 4 * d), F32),
        ],
        scratch_shapes=[
            pltpu.VMEM((1, math.prod(dims), own[0].shape[1], 128), BF), pltpu.SemaphoreType.DMA((len(own),)),
        ],
        compiler_params=params(),
        cost_estimate=cost(1e9, rows * d * 6),
        name="first_norm",
    )(where, x, *own)


def qkv_kernel(dims, count, where_ref, n_ref, vec_ref, *refs):
    own, oth = refs[:count], refs[count : 2 * count]
    o_ref, w_scr, w_sem, bias_scr = refs[2 * count :]
    rows, d = n_ref.shape
    cols = w_scr.shape[-1]
    step = pl.program_id(0)

    @pl.when(step == 0)
    def _():
        load_columns(where_ref, own, oth, 0, cols, w_scr, w_sem)
        zero = jnp.zeros((1, 128), F32)
        pairs = d // 128
        for p in range(pairs):
            at = pair_block(p, pairs) * 384
            half, at = at // cols, at % cols
            bias_scr[half, :, at : at + 128] = vec_ref[2:3, p * 128 : (p + 1) * 128]
            bias_scr[half, :, at + 128 : at + 256] = zero
            bias_scr[half, :, at + 256 : at + 384] = vec_ref[2:3, d + p * 128 : d + (p + 1) * 128]
        wait_columns(own, w_scr, w_sem, 0)

    @pl.when(step == 1)
    def _():
        wait_columns(own, w_scr, w_sem, 1)

    w = whole_rows(dims, where_ref, w_scr, step)
    for r in range(0, rows, 256):
        o_ref[r : r + 256, :] = (dot(n_ref[r : r + 256, :], w) + bias_scr[step]).astype(BF)


def qkv_call(dims, where, normed, vec, own, oth):
    rows, d = normed.shape
    n = own[0].shape[1]
    cols = 3 * d // 2
    return pl.pallas_call(
        functools.partial(qkv_kernel, dims, len(own)),
        grid=(2,),
        in_specs=[SMEM, full_spec((rows, d)), full_spec(vec.shape)] + [ANY] * (2 * len(own)),
        out_specs=pl.BlockSpec((rows, cols), lambda j: (0, j)),
        out_shape=jax.ShapeDtypeStruct((rows, 2 * cols), BF),
        scratch_shapes=weight_scratch(dims, n, cols, len(own)) + [pltpu.VMEM((2, 1, cols), F32)],
        compiler_params=params(),
        cost_estimate=cost(4 * rows * d * cols, rows * d * 8 + d * cols * 4),
        name="qkv",
    )(where, normed, vec, *own, *oth)


def proj_kernel(dims, count, first, where_ref, x_ref, a0_ref, a1_ref, vec_ref, *refs):
    own, oth = refs[:count], refs[count : 2 * count]
    mid_ref, n_ref, w_scr, w_sem = refs[2 * count :]
    d = x_ref.shape[1]

    @pl.when(pl.program_id(0) == 0)
    def _():
        load_columns(where_ref, own, oth, first, w_scr.shape[-1], w_scr, w_sem)
        for h in range(2):
            wait_columns(own, w_scr, w_sem, h)

    a = jnp.concatenate([a0_ref[...], a1_ref[...]], axis=1)
    branch = jnp.concatenate([dot(a, whole_rows(dims, where_ref, w_scr, h)) for h in range(2)], axis=1) + vec_ref[3:4, :d]
    middle = x_ref[...].astype(F32) + BS * branch
    mid_ref[...] = middle
    xhat, _ = normalize(middle)
    n_ref[...] = (xhat * vec_ref[4:5, :d] + vec_ref[5:6, :d]).astype(BF)


def proj_call(dims, where, x, att, vec, own, oth):
    rows, d = x.shape
    br = 256
    row = pl.BlockSpec((br, d), lambda i: (i, 0))
    return pl.pallas_call(
        functools.partial(proj_kernel, dims, len(own), 3 * d // 2),
        grid=(rows // br,),
        in_specs=[SMEM, row] + [pl.BlockSpec((br, v.shape[1]), lambda i: (i, 0)) for v in att]
        + [full_spec(vec.shape)] + [ANY] * (2 * len(own)),
        out_specs=[row, row],
        out_shape=[jax.ShapeDtypeStruct((rows, d), F32), jax.ShapeDtypeStruct((rows, d), BF)],
        scratch_shapes=weight_scratch(dims, own[0].shape[1], d // 2, len(own)),
        compiler_params=params(),
        cost_estimate=cost(2 * rows * d * d, rows * d * 10 + d * d * 2),
        name="proj",
    )(where, x, *att, vec, *own, *oth)


def mlp_kernel(dims, count, where_ref, n_ref, c_ref, mid_ref, vec_ref, *refs):
    own, oth = refs[:count], refs[count : 2 * count]
    (
        out_ref, gn_ref, gfb_ref, gob_ref, g_own, g_oth,
        mid_scr, mid_sem, nt_scr, mg_scr, acc_scr, act_scr, gp_scr, w_scr, w_sem, gf_scr, gf_sem, go_scr, go_sem,
    ) = refs[2 * count :]
    z_n, y_n, x_n = dims
    zi, yi, xi, ci = [where_ref[i] for i in range(4)]
    j = pl.program_id(0)
    rows, d = n_ref.shape
    n, total_cols = w_scr.shape[-2:]
    wide = total_cols - 2 * d
    blocks = 2 * wide // d
    parts = d // n
    br = 512

    def hidden_rows(q):
        at = j * parts + q
        dev, t = at // 2, lax.rem(at, 2)
        x, y, z = lax.rem(dev // 2, x_n), lax.rem(dev // (2 * x_n), y_n), dev // (2 * x_n * y_n)
        piece = lax.rem(y - yi + y_n, y_n) * x_n + lax.rem(x - xi + x_n, x_n)
        return lax.rem(dev, 2), piece * z_n + lax.rem(z - zi + z_n, z_n), pl.multiple_of(t * d, 128)

    @pl.when(j == 0)
    def _():
        load_columns(where_ref, own, oth, 0, total_cols, w_scr, w_sem)
        local_copy(mid_ref, mid_scr, mid_sem).start()
        nt_scr[...] = n_ref[...].T
        total = jnp.zeros_like(gob_ref)
        for r in range(0, rows, br):
            mg = (BS * c_ref[r : r + br, :].astype(F32)).astype(BF)
            mg_scr[r : r + br, :] = mg
            total += jnp.sum(mg.astype(F32), axis=0, keepdims=True)
        gob_ref[...] = total
        for h in range(2):
            wait_columns(own, w_scr, w_sem, h)

    half = j // (blocks // 2)
    first = pl.multiple_of(lax.rem(j, blocks // 2) * d, 128)
    wf = whole_rows(dims, where_ref, w_scr, half, pl.ds(first, d))
    spots = [hidden_rows(q) for q in range(parts)]
    wo = jnp.concatenate([w_scr[c, p, :, pl.ds(wide + at, d)] for c, p, at in spots], axis=0)
    fb = vec_ref[6:7, pl.ds(pl.multiple_of(j * d, 128), d)]
    bias_sum = jnp.zeros((1, d), F32)
    starts = list(range(0, rows, br))

    def ahead_of(r):
        return dot(n_ref[r : r + br, :], wf), dot_t(mg_scr[r : r + br, :], wo)

    def behind(r, act, gp):
        rr = slice(r, r + br)
        fwd = dot(act, wo)
        back = dot_t(gp, wf)
        acc_scr[rr, :] = jnp.where(j == 0, fwd, acc_scr[rr, :] + fwd)
        gn_ref[rr, :] = jnp.where(j == 0, back, gn_ref[rr, :] + back)

    queue = [ahead_of(starts[0])]
    waiting = None
    for i, r in enumerate(starts):
        rr = slice(r, r + br)
        if i + 1 < len(starts):
            queue.append(ahead_of(starts[i + 1]))
        (pre, ga), queue[i] = queue[i], None
        pre = pre + fb
        sq = pre * pre
        t = jnp.tanh(GC0 * pre * (1.0 + GC1 * sq))
        half_t = 0.5 * (1.0 + t)
        act = (pre * half_t).astype(BF)
        slope = half_t + (0.5 * GC0) * pre * (1.0 - t * t) * (1.0 + (3.0 * GC1) * sq)
        gp = (slope * ga).astype(BF)
        act_scr[rr, :] = act
        gp_scr[rr, :] = gp
        bias_sum += jnp.sum(gp.astype(F32), axis=0, keepdims=True)
        if waiting is not None:
            behind(*waiting)
        waiting = r, act, gp
    behind(*waiting)

    gfb_ref[...] = bias_sum
    put_rows(dims, where_ref, gf_scr, (j,), dot(nt_scr[...], gp_scr[...]).astype(BF))
    store_columns(where_ref, gf_scr.at[j], g_own, g_oth, half, first, d, gf_sem.at[j])
    go = dot_0(act_scr[...], mg_scr[...]).astype(BF)
    for q, (c, p, at) in enumerate(spots):
        go_scr[c, p, :, pl.ds(at, d)] = go[q * n : (q + 1) * n]

    @pl.when(j == blocks - 1)
    def _():
        for c in range(2):
            store_columns(where_ref, go_scr.at[c], g_own, g_oth, c, wide, 2 * d, go_sem.at[c])
        local_copy(mid_ref, mid_scr, mid_sem).wait()
        for r in range(0, rows, br):
            rr = slice(r, r + br)
            out_ref[rr, :] = (mid_scr[rr, :] + BS * (acc_scr[rr, :] + vec_ref[7:8, :d])).astype(BF)
        for b in range(blocks):
            wait_store(gf_scr.at[b], gf_sem.at[b])
        for c in range(2):
            wait_store(go_scr.at[c], go_sem.at[c])


def mlp_call(dims, where, normed, cot, middle, vec, own, oth):
    rows, d = normed.shape
    n, cols = own[0].shape[1:]
    wide = cols - 2 * d
    blocks = 2 * wide // d
    act = full_spec((rows, d))
    chips = math.prod(dims)
    piece = jax.ShapeDtypeStruct((chips, n, cols), BF)
    return pl.pallas_call(
        functools.partial(mlp_kernel, dims, len(own)),
        grid=(blocks,),
        in_specs=[SMEM, act, act, ANY, full_spec(vec.shape)] + [ANY] * (2 * len(own)),
        out_specs=[act, act, pl.BlockSpec((1, d), lambda j: (0, j)), full_spec((1, d))] + [ANY] * 2,
        out_shape=[
            jax.ShapeDtypeStruct((rows, d), BF),
            jax.ShapeDtypeStruct((rows, d), F32),
            jax.ShapeDtypeStruct((1, blocks * d), F32),
            jax.ShapeDtypeStruct((1, d), F32),
            piece, piece,
        ],
        scratch_shapes=[
            pltpu.VMEM((rows, d), F32), pltpu.SemaphoreType.DMA(()), pltpu.VMEM((d, rows), BF), pltpu.VMEM((rows, d), BF), pltpu.VMEM((rows, d), F32),
            pltpu.VMEM((rows, d), BF), pltpu.VMEM((rows, d), BF),
        ]
        + weight_scratch(dims, n, cols, len(own))
        + [
            pltpu.VMEM((blocks, chips, n, d), BF), pltpu.SemaphoreType.DMA((blocks,)),
            pltpu.VMEM((2, chips, n, 2 * d), BF), pltpu.SemaphoreType.DMA((2,)),
        ],
        compiler_params=params(),
        cost_estimate=cost(24 * rows * d * wide, 30e6, 2 * rows * wide),
        name="mlp",
    )(where, normed, cot, middle, vec, *own, *oth)


def proj_back_kernel(dims, count, first, where_ref, gn_ref, mid_ref, c_ref, a0_ref, a1_ref, vec_ref, ind_ref, *refs):
    own, oth = refs[:count], refs[count : 2 * count]
    (
        gm_ref, ga_ref, gw_ref, del_ref, gg_ref, gb_ref, gpb_ref, gw_acc, w_scr, w_sem,
    ) = refs[2 * count :]
    i = pl.program_id(0)
    d = mid_ref.shape[1]
    m = d // 2

    @pl.when(i == 0)
    def _():
        load_columns(where_ref, own, oth, first, m, w_scr, w_sem)
        gw_acc[...] = jnp.zeros_like(gw_acc)
        gg_ref[...] = jnp.zeros_like(gg_ref)
        gb_ref[...] = jnp.zeros_like(gb_ref)
        gpb_ref[...] = jnp.zeros_like(gpb_ref)
        for h in range(2):
            wait_columns(own, w_scr, w_sem, h)

    dy = gn_ref[...]
    xhat, rstd = normalize(mid_ref[...])
    gg_ref[...] += jnp.sum(dy * xhat, axis=0, keepdims=True)
    gb_ref[...] += jnp.sum(dy, axis=0, keepdims=True)
    gm = c_ref[...].astype(F32) + ln_back(dy, xhat, rstd, vec_ref[4:5, :d])
    gm_ref[...] = gm
    pg = (BS * gm).astype(BF)
    gpb_ref[...] += jnp.sum(pg.astype(F32), axis=0, keepdims=True)
    a = jnp.concatenate([a0_ref[...], a1_ref[...]], axis=1)
    gw_acc[...] += dot_0(a, pg)
    ga = sum(dot_t(pg[:, h * m : (h + 1) * m], whole_rows(dims, where_ref, w_scr, h)) for h in range(2)).astype(BF)
    ga_ref[...] = ga
    prod = ga.astype(F32) * a.astype(F32)
    high = prod.astype(BF)
    low = (prod - high.astype(F32)).astype(BF)
    del_ref[...] = dot_t(ind_ref[...], high) + dot_t(ind_ref[...], low)

    @pl.when(i == pl.num_programs(0) - 1)
    def _():
        gw_ref[...] = gw_acc[...].astype(BF)


def proj_back_call(dims, where, gn, middle, cot, att, vec, own, oth):
    rows, d = middle.shape
    br = 256
    row = pl.BlockSpec((br, d), lambda i: (i, 0))
    ind = jnp.asarray(np.arange(16)[:, None] == np.arange(d)[None, :] // HD, BF)
    one = full_spec((1, d))
    vshape = jax.ShapeDtypeStruct((1, d), F32)
    return pl.pallas_call(
        functools.partial(proj_back_kernel, dims, len(own), 3 * d // 2),
        grid=(rows // br,),
        in_specs=[SMEM, row, row, row] + [pl.BlockSpec((br, v.shape[1]), lambda i: (i, 0)) for v in att]
        + [full_spec(vec.shape), full_spec((16, d))] + [ANY] * (2 * len(own)),
        out_specs=[row, row, full_spec((d, d)), pl.BlockSpec((16, br), lambda i: (0, i)), one, one, one],
        out_shape=[
            jax.ShapeDtypeStruct((rows, d), F32),
            jax.ShapeDtypeStruct((rows, d), BF),
            jax.ShapeDtypeStruct((d, d), BF),
            jax.ShapeDtypeStruct((16, rows), F32),
            vshape, vshape, vshape,
        ],
        scratch_shapes=[pltpu.VMEM((d, d), F32)] + weight_scratch(dims, own[0].shape[1], d // 2, len(own)),
        compiler_params=params(),
        cost_estimate=cost(4 * rows * d * d, rows * d * 16),
        name="proj_back",
    )(where, gn, middle, cot, *att, vec, ind, *own, *oth)


def pair_back(j_ref, do_ref, lse_ref, del_ref, row, segr_ref, segc_ref, pair, dj_ref, dk_acc, dv_acc):
    rows = j_ref.shape[0]
    scale = HD**-0.5
    lanes = slice(pair * 128, (pair + 1) * 128)
    base = pair * 384
    k = j_ref[:, 128:256] * BF(scale)
    ks = split_heads(k)
    kt = k.T
    vs = split_heads(j_ref[:, 256:384])
    qt = j_ref[:, 0:128].T
    dot_do = do_ref[:, lanes].T
    items = [(tile, h) for tile in q_tiles(rows)[::-1] for h in range(2)]

    def ahead_of(item):
        (q0, kv0, kv1, _), h = item
        q = j_ref[q0 : q0 + 256, 0:128]
        do = do_ref[q0 : q0 + 256, lanes]
        return dot_t(ks[h][kv0:kv1], q), dot_t(vs[h][kv0:kv1], do)

    def behind(tile, h, probs, ds):
        q0, kv0, kv1, _ = tile
        hh = slice(h * HD, (h + 1) * HD)
        qq = slice(q0, q0 + 256)
        dv = dot_t(dot_do[hh, qq], probs)
        dk = dot_t(qt[hh, qq], ds)
        if q0 in (LONG, LONG - 256):
            dk_acc[hh, kv0:kv1] = dk
            dv_acc[hh, kv0:kv1] = dv
        else:
            dk_acc[hh, kv0:kv1] += dk
            dv_acc[hh, kv0:kv1] += dv
        return dot(kt[hh, kv0:kv1], ds)

    queue = [ahead_of(it) for it in items[:2]]
    waiting, dqs = None, []

    def settle():
        tile, h = waiting[:2]
        dqs.append(behind(*waiting))
        if h == 1:
            q0 = tile[0]
            dj_ref[q0 : q0 + 256, base : base + 128] = jnp.concatenate(dqs[-2:], axis=0).T.astype(BF)

    for n, (tile, h) in enumerate(items):
        q0, kv0, kv1, is_long = tile
        if n + 2 < len(items):
            queue.append(ahead_of(items[n + 2]))
        (s, dp), queue[n] = queue[n], None
        lse = lse_ref[pair, h : h + 1, q0 : q0 + 256]
        dlt = del_ref[pl.ds(row + h, 1), q0 : q0 + 256]
        parts = mask_diagonal(s, q0 - kv0, is_long, segr_ref, segc_ref)
        probs = jnp.concatenate([jnp.exp(p - lse) for p in parts], axis=0)
        ds = (probs * (dp - dlt)).astype(BF)
        if waiting is not None:
            settle()
        waiting = tile, h, probs.astype(BF), ds
    settle()
    dj_ref[:, base + 128 : base + 256] = (dk_acc[...] * scale).T.astype(BF)
    dj_ref[:, base + 256 : base + 384] = dv_acc[...].T.astype(BF)


def attn_back_kernel(
    dims, count, devices, where_ref, j0_ref, j1_ref, do_ref, lse_ref, del_ref, segr_ref, segc_ref,
    x_ref, vec_ref, gwp_ref, gfb_ref, gob_ref, gg2_ref, gb2_ref, gpb_ref, gm_ref, nt_ref, *refs,
):
    own, oth, refs = refs[:count], refs[count : 2 * count], refs[2 * count :]
    gx_ref, g_own, g_oth = refs[:3]
    (
        w_scr, w_sem, nt_scr, nt_sem, gn_scr, gm_scr, gm_sem, dj_scr, dk_acc, dv_acc, gw_scr, gw_sem,
        p_scr, p_sem, t_scr, t_sem, qv_scr,
    ) = refs[3:]
    i = pl.program_id(0)
    groups = gw_scr.shape[0]
    rows, d = x_ref.shape
    br = 256
    proj_at = groups * 384
    table_at = proj_at + d // 2

    @pl.when(i == 0)
    def _():
        load_columns(where_ref, own, oth, 0, groups * 384, w_scr, w_sem)
        local_copy(nt_ref, nt_scr, nt_sem).start()
        local_copy(gm_ref, gm_scr, gm_sem).start()
        for h in range(2):
            put_rows(dims, where_ref, p_scr, (h,), gwp_ref[:, h * (d // 2) : (h + 1) * (d // 2)])
            store_columns(where_ref, p_scr.at[h], g_own, g_oth, h, proj_at, d // 2, p_sem.at[h])

    for h, j_ref in enumerate((j0_ref, j1_ref)):
        row = (i * 2 + h) * 2
        pair_back(j_ref, do_ref, lse_ref, del_ref, row, segr_ref, segc_ref, h, dj_scr, dk_acc, dv_acc)

    @pl.when(i == 0)
    def _():
        local_copy(nt_ref, nt_scr, nt_sem).wait()
        for h in range(2):
            wait_columns(own, w_scr, w_sem, h)

    first = pl.multiple_of(i * 384, 128)
    dj = dj_scr[...]
    for h in range(2):
        for t, off in ((0, 0), (2, d)):
            part = dj[:, h * 384 + t * 128 : h * 384 + (t + 1) * 128].astype(F32)
            qv_scr[:, pl.ds(pl.multiple_of(off + (i * 2 + h) * 128, 128), 128)] = jnp.sum(part, axis=0, keepdims=True)
    gw = dot(nt_scr[...], dj).astype(BF)
    for h in range(2):
        put_rows(dims, where_ref, gw_scr, (i, h), gw[:, h * 384 : (h + 1) * 384])
        store_columns(where_ref, gw_scr.at[i, h], g_own, g_oth, h, first, 384, gw_sem.at[i, h])
    w = jnp.concatenate([whole_rows(dims, where_ref, w_scr, h, pl.ds(first, 384)) for h in range(2)], axis=1)
    for r in range(0, rows, br):
        back = dot_t(dj[r : r + br, :], w)
        gn_scr[r : r + br, :] = jnp.where(i == 0, back, gn_scr[r : r + br, :] + back)

    @pl.when(i == groups - 1)
    def _():
        local_copy(gm_ref, gm_scr, gm_sem).wait()
        gg = jnp.zeros((1, d), F32)
        gb = jnp.zeros((1, d), F32)
        for r in range(0, rows, br):
            rr = slice(r, r + br)
            xhat, rstd = normalize(x_ref[rr, :].astype(F32))
            dy = gn_scr[rr, :]
            gg += jnp.sum(dy * xhat, axis=0, keepdims=True)
            gb += jnp.sum(dy, axis=0, keepdims=True)
            gx_ref[rr, :] = (gm_scr[rr, :] + ln_back(dy, xhat, rstd, vec_ref[0:1, :d])).astype(BF)
        table = pack_vectors(
            {
                "g1": gg, "b1": gb, "qv": qv_scr[...], "fb": gfb_ref[...], "pb": gpb_ref[...],
                "g2": gg2_ref[...], "b2": gb2_ref[...], "ob": gob_ref[...],
            },
            d, devices,
        )
        put_rows(dims, where_ref, t_scr, (), table)
        for h in range(2):
            store_columns(where_ref, t_scr, g_own, g_oth, h, table_at, 128, t_sem.at[h])
        for h in range(2):
            for b in range(groups):
                wait_store(gw_scr.at[b, h], gw_sem.at[b, h])
            wait_store(p_scr.at[h], p_sem.at[h])
            wait_store(t_scr, t_sem.at[h])


def attn_back_call(dims, where, joined, ga, lse, delta, seg_row, seg_col, x, vec, own, oth, vectors, gm, nt, devices):
    rows, d = x.shape
    n = own[0].shape[1]
    groups = d // 256
    act = full_spec((rows, d))
    chips = math.prod(dims)
    piece = jax.ShapeDtypeStruct((chips, n, groups * 384 + d // 2 + 128), BF)
    return pl.pallas_call(
        functools.partial(attn_back_kernel, dims, len(own), devices),
        grid=(groups,),
        in_specs=[
            SMEM,
            pl.BlockSpec((rows, 384), lambda i: (0, i)),
            pl.BlockSpec((rows, 384), lambda i: (0, groups + i)),
            pl.BlockSpec((rows, 256), lambda i: (0, i)),
            pl.BlockSpec((2, 2, rows), lambda i: (i, 0, 0)),
            full_spec(delta.shape), full_spec((1, 256)), full_spec((256, 1)), act, full_spec(vec.shape),
        ]
        + [full_spec(v.shape) for v in vectors] + [ANY] * (2 + 2 * len(own)),
        out_specs=[act, ANY, ANY],
        out_shape=[jax.ShapeDtypeStruct((rows, d), BF), piece, piece],
        scratch_shapes=weight_scratch(dims, n, groups * 384, len(own))
        + [
            pltpu.VMEM((d, rows), BF), pltpu.SemaphoreType.DMA(()), pltpu.VMEM((rows, d), F32),
            pltpu.VMEM((rows, d), F32), pltpu.SemaphoreType.DMA(()), pltpu.VMEM((rows, 768), BF),
            pltpu.VMEM((128, rows), F32), pltpu.VMEM((128, rows), F32),
            pltpu.VMEM((groups, 2, chips, n, 384), BF), pltpu.SemaphoreType.DMA((groups, 2)),
            pltpu.VMEM((2, chips, n, d // 2), BF), pltpu.SemaphoreType.DMA((2,)),
            pltpu.VMEM((chips, n, 128), BF), pltpu.SemaphoreType.DMA((2,)),
            pltpu.VMEM((1, 2 * d), F32),
        ],
        compiler_params=params(),
        cost_estimate=cost(60e9, 20e6, 5.5e6),
        name="attn_back",
    )(where, joined, joined, ga, lse, delta, seg_row, seg_col, x, vec, *vectors, gm, nt, *own, *oth)


def pack_plan(counts, rows):
    c = [counts[i] for i in range(counts.shape[0])]
    ends, run = [], jnp.int32(0)
    for v in c:
        run = run + v
        ends.append(run)
    start = jnp.int32(0)
    for i in range(len(c) - 1):
        start = jnp.where(c[i] == LONG, ends[i] - c[i], start)
    rolled = jnp.arange(rows, dtype=jnp.int32)
    pos = rolled + start
    pos = jnp.where(pos >= rows, pos - rows, pos)
    seg = functools.reduce(jnp.add, [(pos >= e).astype(jnp.int32) for e in ends])
    valid = seg < len(c) - 1
    seg = jnp.where(valid, seg, 1000 + rolled)
    return start, seg[LONG:], valid


def roll_rows(array, shift):
    return lax.dynamic_slice_in_dim(jnp.concatenate([array, array], axis=0), shift, array.shape[0])


def half_columns(w, h, joined=False):
    r, cols = w.shape
    if not joined:
        return w[:, h * (cols // 2) : (h + 1) * (cols // 2)]
    pairs = cols // 384
    starts = [(t * pairs + p) * 128 for p in range(h, pairs, 2) for t in range(3)]
    return jnp.concatenate([w[:, s : s + 128] for s in starts], axis=1)


def join_columns(left, right):
    r, m = left.shape
    both = jnp.stack([v.reshape(r, m // 384, 3, 128) for v in (left, right)], axis=2)
    return both.transpose(0, 3, 1, 2, 4).reshape(r, 2 * m)


def add_all(values):
    return functools.reduce(jnp.add, [v.astype(F32) for v in values])


class Plain:
    def __init__(self, dp, fsdp):
        self.dims = (1, 1, 1)
        index = lax.axis_index("dp") * fsdp + lax.axis_index("fsdp")
        self.ci = index % 2

    def where(self):
        zero = jnp.zeros((), jnp.int32)
        return jnp.stack([zero, zero, zero, self.ci.astype(jnp.int32)])

    def pick(self, pair):
        return jnp.where(self.ci == 0, pair[0], pair[1]), jnp.where(self.ci == 0, pair[1], pair[0])

    def gather(self, w_qkv, w_proj, table, w_fc, w_out):
        whole = lambda v: lax.all_gather(v, AXES, axis=0, tiled=True)
        attn = whole(jnp.concatenate([w_qkv, w_proj, table], axis=1))
        cut = w_qkv.shape[1], w_qkv.shape[1] + w_proj.shape[1]
        fc, out = whole(w_fc), whole(w_out)
        d = out.shape[1]
        lists = [[], []]
        for h in range(2):
            qkv, proj, table = attn[:, : cut[0]], attn[:, cut[0] : cut[1]], attn[:, cut[1] :]
            lists[0].append(jnp.concatenate([half_columns(qkv, h, True), half_columns(proj, h), table], axis=1))
            lists[1].append(
                jnp.concatenate([half_columns(fc, h)] + [out[(2 * h + t) * d : (2 * h + t + 1) * d] for t in range(2)], axis=1)
            )
        listed = []
        for pair in lists:
            own, oth = self.pick(pair)
            listed.append(([own[None]], [oth[None]]))
        return listed

    def scatter(self, own, oth):
        pair = self.pick([own[0], oth[0]])
        m = pair[0].shape[1]
        mine = lax.psum_scatter(jnp.concatenate(pair, axis=1), AXES, scatter_dimension=0, tiled=True).astype(F32)
        return mine[:, :m], mine[:, m:]

    def scatter_hidden(self, own, oth):
        pair = self.pick([own[0], oth[0]])
        d = pair[0].shape[0]
        wide = pair[0].shape[1] - 2 * d
        fc = self.scatter(own[..., :wide], oth[..., :wide])
        out = jnp.concatenate([v[:, wide + t * d : wide + (t + 1) * d] for v in pair for t in range(2)], axis=0)
        return fc, lax.psum_scatter(out, AXES, scatter_dimension=0, tiled=True).astype(F32)


class Chips:
    def __init__(self, dp, fsdp):
        x_n, z_n = fsdp // 2, 4
        self.dims = (z_n, dp // z_n, x_n)
        index = lax.axis_index("dp") * fsdp + lax.axis_index("fsdp")
        self.ci = index % 2
        self.at = (index // (2 * x_n * self.dims[1]), (index // (2 * x_n)) % self.dims[1], (index // 2) % x_n, self.ci)

    def where(self):
        return jnp.stack(self.at).astype(jnp.int32)

    def pick(self, pair):
        return jnp.where(self.ci == 0, pair[0], pair[1]), jnp.where(self.ci == 0, pair[1], pair[0])

    def send(self, array, dz=0, dy=0, dx=0, dc=0):
        z_n, y_n, x_n = self.dims
        pairs = []
        for z in range(z_n):
            for y in range(y_n):
                for x in range(x_n):
                    for c in range(2):
                        here = ((z * y_n + y) * x_n + x) * 2 + c
                        there = (((z + dz) % z_n * y_n + (y + dy) % y_n) * x_n + (x + dx) % x_n) * 2 + (c + dc) % 2
                        pairs.append((here, there))
        return lax.ppermute(array, AXES, pairs)

    def trade(self, halves):
        return self.rows_of(*self.pick(halves))

    def rows_of(self, keep, give):
        return jnp.concatenate(self.pick([keep, self.send(give, dc=1)]), axis=0)

    def along_z(self, piece):
        return [piece] + [self.send(piece, dz=-k) for k in range(1, self.dims[0])]

    def swap(self, arrays):
        return [self.send(v, dc=1) for v in arrays]

    def add_core(self, own, theirs):
        return [add_all([own[i], theirs[i]]).astype(BF) for i in range(own.shape[0])]

    def rows_back(self, total):
        n = total.shape[0] // 2
        mine, give = self.pick([total[:n], total[n:]])
        return self.pick([mine, self.send(give, dc=1)])


def together(*trees):
    return lax.optimization_barrier(trees)


def prepare(tokens, lengths, cotangent):
    start, seg, valid = pack_plan(lengths[0], tokens.shape[0])
    x = roll_rows(tokens, start)
    cot = jnp.where(valid[:, None], roll_rows(cotangent, start), BF(0))
    return start, seg[None, :], seg[:, None], x, cot


def vector_table(r, ln1_gain, ln1_bias, qv_bias, proj_bias, ln2_gain, ln2_bias, fc_bias, out_bias):
    flat = [
        jnp.concatenate([ln1_gain, ln1_bias, qv_bias]), fc_bias,
        jnp.concatenate([proj_bias, ln2_gain, ln2_bias, out_bias]),
    ]
    return jnp.pad(jnp.stack(flat), ((0, r - 3), (0, 128 - 4 * r)))


def results(r, out, gx, s_fc, s_out, s_attn, table):
    d = out.shape[1]
    cut = 3 * d // 2
    s_qkv = join_columns(*[v[:, :cut] for v in s_attn])
    s_proj = jnp.concatenate([v[:, cut:] for v in s_attn], axis=1)
    row0, row1, row2 = [table[k, : 4 * r] for k in range(3)]
    return (
        out, gx,
        row0[:r], row0[r : 2 * r], s_qkv, row0[2 * r :], s_proj, row2[:r],
        row2[r : 2 * r], row2[2 * r : 3 * r], jnp.concatenate(s_fc, axis=1), row1, s_out, row2[3 * r :],
    )


def split_table(halves):
    return [v[:, :-128] for v in halves], halves[0][:, -128:]


def block_plain(
    links, tokens, lengths, ln1_gain, ln1_bias, w_qkv, qv_bias, w_proj, proj_bias, ln2_gain, ln2_bias,
    w_fc, fc_bias, w_out, out_bias, cotangent,
):
    rows, d = tokens.shape
    r = w_qkv.shape[0]
    devices = d // r
    dims, where = links.dims, links.where()
    table = vector_table(r, ln1_gain, ln1_bias, qv_bias, proj_bias, ln2_gain, ln2_bias, fc_bias, out_bias)
    attn_w, m_w = links.gather(w_qkv, w_proj, table, w_fc, w_out)
    start, seg_row, seg_col, x, cot = prepare(tokens, lengths, cotangent)
    normed, nt, vec = first_norm_call(dims, where, x, attn_w[0], devices)
    joined = qkv_call(dims, where, normed, vec, *attn_w)
    att0, lse0 = attn_call(joined, seg_row, seg_col, 0, 2)
    att1, lse1 = attn_call(joined, seg_row, seg_col, 2, d // 256 - 2)
    att = att0, att1
    middle, normed_two = proj_call(dims, where, x, att, vec, *attn_w)
    out, gn, gfb, gob, *m_g = mlp_call(dims, where, normed_two, cot, middle, vec, *m_w)
    s_fc, s_out = links.scatter_hidden(*m_g)
    gm, ga, gw_proj, delta, gg2, gb2, gpb = proj_back_call(dims, where, gn, middle, cot, att, vec, *attn_w)
    gx, *g = attn_back_call(
        dims, where, joined, ga, jnp.concatenate([lse0, lse1]), delta, seg_row, seg_col, x, vec, *attn_w,
        (gw_proj, gfb, gob, gg2, gb2, gpb), gm, nt, devices,
    )
    restore = rows - start
    return results(r, roll_rows(out, restore), roll_rows(gx, restore), s_fc, s_out, *split_table(links.scatter(*g)))


def block_chips(
    links, tokens, lengths, ln1_gain, ln1_bias, w_qkv, qv_bias, w_proj, proj_bias, ln2_gain, ln2_bias,
    w_fc, fc_bias, w_out, out_bias, cotangent,
):
    rows, d = tokens.shape
    r = w_qkv.shape[0]
    devices = d // r
    dims, where, send, swap = links.dims, links.where(), links.send, links.swap
    table = vector_table(r, ln1_gain, ln1_bias, qv_bias, proj_bias, ln2_gain, ln2_bias, fc_bias, out_bias)

    def xy(column):
        return send(column, dx=1), send(column, dy=1)

    def corner(x_part, y_part):
        return [send(x_part[:2], dy=1), send(y_part[2:], dx=1)]

    def near(b):
        return send(b[1], dx=1), send(b[2], dy=1), send(b[3], dx=1, dy=1)

    def far(parts):
        return [parts[0]] + [send(parts[j], dz=j) for j in range(1, dims[0])]

    a = links.rows_of(*cut_call(where, w_qkv, w_proj, table))
    a, tokens, lengths, cotangent, w_fc = together(a, tokens, lengths, cotangent, w_fc)
    a0 = links.along_z(a)
    fc = links.trade([half_columns(w_fc, h) for h in range(2)])
    m = jnp.concatenate([fc, w_out[: 2 * r], w_out[2 * r :]], axis=1)
    a0, m, tokens, lengths, cotangent = together(a0, m, tokens, lengths, cotangent)
    prep = prepare(tokens, lengths, cotangent)
    m0 = links.along_z(m)
    a0 = jnp.stack(a0)
    a_own = [a0, send(a0, dx=1), send(a0, dy=1), send(a0, dx=1, dy=1)]
    a_own, m0, prep = together(a_own, m0, prep)
    start, seg_row, seg_col, x, cot = prep
    m0 = jnp.stack(m0)
    a_own = [jnp.concatenate(a_own, axis=0)]
    m0, a_own = together(m0, a_own)
    attn_w = a_own, swap(a_own)
    mx, my = xy(m0)
    normed, nt, vec = first_norm_call(dims, where, x, a_own, devices)
    normed, attn_w = together(normed, attn_w)

    joined = qkv_call(dims, where, normed, vec, *attn_w)
    att0, lse0 = attn_call(joined, seg_row, seg_col, 0, 2)
    att0, joined, mx, my = together(att0, joined, mx, my)
    att1, lse1 = attn_call(joined, seg_row, seg_col, 2, d // 256 - 2)
    att = att0, att1
    middle, normed_two = proj_call(dims, where, x, att, vec, *attn_w)
    md = corner(mx, my)
    m_oth = swap([m0, mx, my])
    lse = jnp.concatenate([lse0, lse1])
    normed_two, md, m_oth, lse = together(normed_two, md, m_oth, lse)
    m_w = [m0, mx, my] + md, m_oth + swap(md)

    out, gn, gfb, gob, m_own, m_oth = mlp_call(dims, where, normed_two, cot, middle, vec, *m_w)
    gm, ga, gw_proj, delta, gg2, gb2, gpb = proj_back_call(dims, where, gn, middle, cot, att, vec, *attn_w)
    (m_oth,) = swap([m_oth])
    ga, delta, m_own, m_oth = together(ga, delta, m_own, m_oth)
    m_own, m_oth = [v.reshape(-1, dims[0], *v.shape[1:]) for v in (m_own, m_oth)]

    def chip_sum(i, part):
        return add_all([part(m_own[i]), part(m_oth[i])]).astype(BF)

    first = (
        chip_sum(3, lambda v: v[1:3]), chip_sum(3, lambda v: v[:1]), chip_sum(3, lambda v: v[3:]),
        chip_sum(1, lambda v: v[1:]), chip_sum(2, lambda v: v[:3]),
    )
    first, ga, delta, m_own, m_oth = together(first, ga, delta, m_own, m_oth)
    first = (
        send(first[0], dx=1, dy=1), send(first[1], dy=1), send(first[2], dx=1),
        send(first[3], dx=1), send(first[4], dy=1),
    )
    gx, g_own, g_oth = attn_back_call(
        dims, where, joined, ga, lse, delta, seg_row, seg_col, x, vec, *attn_w,
        (gw_proj, gfb, gob, gg2, gb2, gpb), gm, nt, devices,
    )
    gx, g_own, g_oth, first, m_own, m_oth, out = together(gx, g_own, g_oth, first, m_own, m_oth, out)

    (g_oth,) = swap([g_oth])
    corners, by_y, by_x, from_x, from_y = first

    def chip_total(i, j, arrived):
        return add_all([m_own[i, j], m_oth[i, j]] + arrived).astype(BF)

    x_one = send(chip_total(1, 0, [by_y[0]]), dx=1)
    y_one = send(chip_total(2, 3, [by_x[0]]), dy=1)
    b = {1: send(chip_total(0, 1, [from_x[0], from_y[1], corners[0]]), dz=1)}
    e = links.add_core(*[v.reshape(-1, dims[0], *v.shape[1:]) for v in (g_own, g_oth)])
    e, x_one, y_one, gx, out, m_own, m_oth, b = together(e, x_one, y_one, gx, out, m_own, m_oth, b)

    e_near = near(e)
    b[0] = chip_total(0, 0, [x_one, from_y[0]])
    b[2] = send(chip_total(0, 2, [from_x[1], from_y[2], corners[1]]), dz=2)
    b[3] = send(chip_total(0, 3, [from_x[2], y_one]), dz=3)
    b = [b[j] for j in range(4)]
    gx, out = roll_rows(gx, rows - start), roll_rows(out, rows - start)
    e_near, b, e, gx, out = together(e_near, b, e, gx, out)

    e = far([add_all([e[0][j]] + [v[j] for v in e_near]).astype(BF) for j in range(dims[0])])
    total = add_all(b)
    s_fc = links.rows_back(total[:, : -2 * d])
    s_out = jnp.concatenate([total[:, -2 * d : -d], total[:, -d:]], axis=0)
    e, s_fc, s_out = together(e, s_fc, s_out)
    total = add_all(e)
    vectors = jnp.where(links.ci == 0, total[:3, -128:], total[r : r + 3, -128:])
    return results(r, out, gx, s_fc, s_out, links.rows_back(total[:, :-128]), vectors)


def solution(mesh):
    dp, fsdp = mesh.shape["dp"], mesh.shape["fsdp"]

    def per_device(*args):
        if (dp, fsdp) == (8, 4) and args[4].shape[0] % 8 == 0:
            return block_chips(Chips(dp, fsdp), *args)
        return block_plain(Plain(dp, fsdp), *args)

    row, vec = P(AXES, None), P(AXES)
    in_specs = (row, row, vec, vec, row, vec, row, vec, vec, vec, row, vec, row, vec, row)
    out_specs = (row, row, vec, vec, row, vec, row, vec, vec, vec, row, vec, row, vec)
    return jax.shard_map(
        per_device, mesh=mesh, in_specs=in_specs, out_specs=out_specs, check_vma=False
    )
```

```python
import functools
import math

import jax
import jax.numpy as jnp
import numpy as np
from jax import lax
from jax.experimental import pallas as pl
from jax.experimental.pallas import tpu as pltpu
from jax.sharding import PartitionSpec as P

HD = 64
LONG = 768
EPS = 1e-05
BS = 1.0 / math.sqrt(48.0)
NEG = -1e30
F32 = jnp.float32
BF = jnp.bfloat16
VMEM_LIMIT = 58 * 1024 * 1024
AXES = ("dp", "fsdp")
GC0 = math.sqrt(2.0 / math.pi)
GC1 = 0.044715


def dot(a, b):
    return lax.dot_general(a, b, (((1,), (0,)), ((), ())), preferred_element_type=F32)


def dot_t(a, b):
    return lax.dot_general(a, b, (((1,), (1,)), ((), ())), preferred_element_type=F32)


def dot_0(a, b):
    return lax.dot_general(a, b, (((0,), (0,)), ((), ())), preferred_element_type=F32)


def params(grid_len=1):
    return pltpu.CompilerParams(
        dimension_semantics=("arbitrary",) * grid_len, vmem_limit_bytes=VMEM_LIMIT
    )


def cost(flops, nbytes, trans=0):
    return pl.CostEstimate(flops=int(flops), bytes_accessed=int(nbytes), transcendentals=int(trans))


def normalize(values):
    centred = values - jnp.mean(values, axis=-1, keepdims=True)
    rstd = lax.rsqrt(jnp.mean(centred * centred, axis=-1, keepdims=True) + EPS)
    return centred * rstd, rstd


def ln_back(dy, xhat, rstd, gain):
    dx = dy * gain
    m1 = jnp.mean(dx, axis=-1, keepdims=True)
    m2 = jnp.mean(dx * xhat, axis=-1, keepdims=True)
    return rstd * (dx - m1 - xhat * m2)


def full_spec(shape):
    return pl.BlockSpec(shape, lambda *_: (0,) * len(shape), pipeline_mode=pl.Buffered(1))


def lane_masks(rows):
    lane = lax.broadcasted_iota(jnp.int32, (rows, 128), 1)
    return lane < HD


def split_heads(block):
    low = lane_masks(block.shape[0])
    zero = jnp.zeros_like(block)
    return jnp.where(low, block, zero), jnp.where(low, zero, block)


def q_tiles(rows):
    tiles = [(r, 0, r + 256, True) for r in range(0, LONG, 256)]
    tiles += [(LONG, LONG, rows, False)]
    return tiles


def diag_allowed(is_long, seg_row, seg_col):
    kv = lax.broadcasted_iota(jnp.int32, (256, 256), 0)
    qp = lax.broadcasted_iota(jnp.int32, (256, 256), 1)
    allowed = kv <= qp
    if not is_long:
        allowed = allowed & (seg_col == seg_row)
    return allowed


def attn_kernel(q_ref, k_ref, v_ref, segr_ref, segc_ref, o_ref, lse_ref):
    rows = q_ref.shape[0]
    ks = split_heads(k_ref[...] * BF(HD**-0.5))
    vt = v_ref[...].T
    items = [(tile, h) for tile in q_tiles(rows) for h in range(2)]

    def score(item):
        (q0, kv0, kv1, _), h = item
        return dot_t(ks[h][kv0:kv1], q_ref[q0 : q0 + 256, :])

    queue = [score(it) for it in items[:3]]
    outs = []
    for n, ((q0, kv0, kv1, is_long), h) in enumerate(items):
        if n + 3 < len(items):
            queue.append(score(items[n + 3]))
        s, queue[n] = queue[n], None
        parts = mask_diagonal(s, q0 - kv0, is_long, segr_ref, segc_ref)
        top = functools.reduce(jnp.maximum, [jnp.max(p, axis=0, keepdims=True) for p in parts])
        exps = [jnp.exp(p - top) for p in parts]
        total = functools.reduce(jnp.add, [jnp.sum(e, axis=0, keepdims=True) for e in exps])
        lse_ref[0, h : h + 1, q0 : q0 + 256] = top + jnp.log(total)
        probs = jnp.concatenate([e.astype(BF) for e in exps], axis=0)
        outs.append(dot(vt[h * HD : (h + 1) * HD, kv0:kv1], probs) * (1.0 / total))
        if h == 1:
            o_ref[q0 : q0 + 256, :] = jnp.concatenate(outs, axis=0).T.astype(BF)
            outs = []


def mask_diagonal(s, at, is_long, segr_ref, segc_ref):
    allowed = diag_allowed(is_long, segr_ref[...], segc_ref[...])
    diag = jnp.where(allowed, s[at:], NEG)
    return [s[:at], diag] if at else [diag]


def attn_call(joined, seg_row, seg_col, group0, groups):
    rows = joined.shape[0]
    pairs = joined.shape[1] // 384
    at = lambda t: pl.BlockSpec((rows, 128), lambda p: (0, pair_block(group0 * 2 + p, pairs) * 3 + t))
    return pl.pallas_call(
        attn_kernel,
        grid=(2 * groups,),
        in_specs=[at(0), at(1), at(2), full_spec((1, 256)), full_spec((256, 1))],
        out_specs=[
            pl.BlockSpec((rows, 128), lambda p: (0, p)),
            pl.BlockSpec((1, 2, rows), lambda p: (p, 0, 0)),
        ],
        out_shape=[
            jax.ShapeDtypeStruct((rows, groups * 256), BF),
            jax.ShapeDtypeStruct((2 * groups, 2, rows), F32),
        ],
        compiler_params=params(),
        cost_estimate=cost(groups * 8e9, 8e6, 5.5e6),
        name="attn",
    )(joined, joined, joined, seg_row, seg_col)


def pair_block(p, pairs):
    return (p % 2) * (pairs // 2) + p // 2


ANY = pl.BlockSpec(memory_space=pl.ANY)
SMEM = pl.BlockSpec(memory_space=pltpu.SMEM)


def local_copy(src, dst, sem):
    return pltpu.make_async_copy(src, dst, sem)


def places(dims, where_ref):
    z_n, y_n, x_n = dims
    zi, yi, xi = [where_ref[i] for i in range(3)]
    return [
        (lax.rem(y - yi + y_n, y_n) * x_n + lax.rem(x - xi + x_n, x_n)) * z_n + lax.rem(z - zi + z_n, z_n)
        for z in range(z_n)
        for y in range(y_n)
        for x in range(x_n)
    ]


def array_spans(arrays):
    at = 0
    for k, a in enumerate(arrays):
        yield k, a, pl.ds(at, a.shape[0])
        at += a.shape[0]


def load_columns(where_ref, own, oth, first, cols, dst, sem):
    ci = where_ref[3]
    for half, arrays in ((ci, own), (1 - ci, oth)):
        for k, a, span in array_spans(arrays):
            local_copy(a.at[:, :, pl.ds(first, cols)], dst.at[half, span], sem.at[half, k]).start()


def wait_columns(own, dst, sem, half):
    for k, _, span in array_spans(own):
        block = dst.at[half, span]
        local_copy(block, block, sem.at[half, k]).wait()


def whole_rows(dims, where_ref, scr, half, cols=slice(None)):
    return jnp.concatenate([scr[half, p, :, cols] for p in places(dims, where_ref)], axis=0)


def put_rows(dims, where_ref, scr, lead, value):
    n = scr.shape[-2]
    for i, p in enumerate(places(dims, where_ref)):
        scr[lead + (p,)] = value[i * n : (i + 1) * n]


def store_columns(where_ref, src, own, oth, half, first, cols, sem):
    ci = where_ref[3]
    for other, out in ((False, own), (True, oth)):

        @pl.when((half != ci) if other else (half == ci))
        def _():
            local_copy(src, out.at[:, :, pl.ds(first, cols)], sem).start()


def wait_store(src, sem):
    local_copy(src, src, sem).wait()


def weight_scratch(dims, n, cols, arrays):
    return [
        pltpu.VMEM((2, math.prod(dims), n, cols), BF),
        pltpu.SemaphoreType.DMA((2, arrays)),
    ]


def vector_plan(d, devices):
    r = d // devices
    return {
        "g1": (0, 0, r), "b1": (0, r, r), "qv": (0, 2 * r, 2 * r), "fb": (1, 0, 4 * r),
        "pb": (2, 0, r), "g2": (2, r, r), "b2": (2, 2 * r, r), "ob": (2, 3 * r, r),
    }


VECTOR_ROWS = {"g1": 0, "b1": 1, "qv": 2, "pb": 3, "g2": 4, "b2": 5, "fb": 6, "ob": 7}


def owner_of(shape, size, axis):
    c = lax.broadcasted_iota(jnp.int32, shape, axis).astype(F32)
    owner = jnp.floor((c + 0.5) * (1.0 / size))
    return owner, c - owner * size


def row_pick(devices, d, row):
    r = d // devices
    at = lax.broadcasted_iota(jnp.int32, (devices, d), 1)
    dev = lax.broadcasted_iota(jnp.int32, (devices, d), 0)
    return (at == dev * r + row).astype(BF)


def vector_maps(devices, n, first, size):
    owner, place = owner_of((devices, n), size, 1)
    mine = owner == lax.broadcasted_iota(jnp.int32, (devices, n), 0).astype(F32)
    _, place = owner_of((128, n), size, 1)
    spot = (place + first == lax.broadcasted_iota(jnp.int32, (128, n), 0).astype(F32)).astype(BF)
    return mine, spot


def unpack_vectors(table, d, devices, out_ref):
    plan = vector_plan(d, devices)
    picked = [dot(row_pick(devices, d, k), table).astype(BF) for k in range(3)]
    for name, i in VECTOR_ROWS.items():
        k, first, size = plan[name]
        n = size * devices
        mine, spot = vector_maps(devices, n, first, size)
        spread = dot(picked[k], spot)
        out_ref[i : i + 1, :n] = jnp.sum(jnp.where(mine, spread, 0.0), axis=0, keepdims=True)


def pack_vectors(rows, d, devices):
    plan = vector_plan(d, devices)
    parts = [None] * 3
    for name in VECTOR_ROWS:
        k, first, size = plan[name]
        n = size * devices
        mine, spot = vector_maps(devices, n, first, size)
        part = dot_t(jnp.where(mine, rows[name], 0.0).astype(BF), spot)
        parts[k] = part if parts[k] is None else parts[k] + part
    total = None
    for k in range(3):
        piece = dot_0(row_pick(devices, d, k), parts[k].astype(BF))
        total = piece if total is None else total + piece
    return total.astype(BF)


def cut_kernel(where_ref, w_ref, p_ref, t_ref, f_ref, a_keep, a_give, f_keep, f_give):
    ci = where_ref[3]
    pairs = w_ref.shape[1] // 384
    half = p_ref.shape[1] // 2
    wide = f_ref.shape[1] // 2
    for h in range(2):
        for other, out, f_out in ((False, a_keep, f_keep), (True, a_give, f_give)):

            @pl.when((ci != h) if other else (ci == h))
            def _():
                at = 0
                for p in range(h, pairs, 2):
                    for t in range(3):
                        first = (t * pairs + p) * 128
                        out[:, at : at + 128] = w_ref[:, first : first + 128]
                        at += 128
                out[:, at : at + half] = p_ref[:, h * half : (h + 1) * half]
                out[:, at + half :] = t_ref[...]
                f_out[...] = f_ref[:, h * wide : (h + 1) * wide]


def cut_call(where, w_qkv, w_proj, table, w_fc):
    r = w_qkv.shape[0]
    cols = (w_qkv.shape[1] + w_proj.shape[1]) // 2 + 128
    sizes = [cols, cols, w_fc.shape[1] // 2, w_fc.shape[1] // 2]
    args = (w_qkv, w_proj, table, w_fc)
    return pl.pallas_call(
        cut_kernel,
        grid=(1,),
        in_specs=[SMEM] + [full_spec(v.shape) for v in args],
        out_specs=[full_spec((r, s)) for s in sizes],
        out_shape=[jax.ShapeDtypeStruct((r, s), BF) for s in sizes],
        compiler_params=params(),
        cost_estimate=cost(0, 4 * r * sum(sizes)),
        name="cut",
    )(where, *args)


def first_norm_kernel(dims, count, devices, where_ref, x_ref, *refs):
    own = refs[:count]
    n_ref, nt_ref, vec_ref, t_scr, t_sem = refs[count:]
    rows, d = x_ref.shape
    table_at = own[0].shape[-1] - 128
    copies = [local_copy(a.at[:, :, pl.ds(table_at, 128)], t_scr.at[0, span], t_sem.at[i]) for i, a, span in array_spans(own)]
    for c in copies:
        c.start()
    for c in copies:
        c.wait()
    vec_ref[...] = jnp.zeros_like(vec_ref)
    unpack_vectors(whole_rows(dims, where_ref, t_scr, 0), d, devices, vec_ref)
    for r in range(0, rows, 256):
        xhat, _ = normalize(x_ref[r : r + 256, :].astype(F32))
        normed = (xhat * vec_ref[0:1, :d] + vec_ref[1:2, :d]).astype(BF)
        n_ref[r : r + 256, :] = normed
        nt_ref[:, r : r + 256] = normed.T


def first_norm_call(dims, where, x, own, devices):
    rows, d = x.shape
    return pl.pallas_call(
        functools.partial(first_norm_kernel, dims, len(own), devices),
        grid=(1,),
        in_specs=[SMEM, full_spec((rows, d))] + [ANY] * len(own),
        out_specs=[full_spec((rows, d)), full_spec((d, rows)), full_spec((8, 4 * d))],
        out_shape=[
            jax.ShapeDtypeStruct((rows, d), BF), jax.ShapeDtypeStruct((d, rows), BF),
            jax.ShapeDtypeStruct((8, 4 * d), F32),
        ],
        scratch_shapes=[
            pltpu.VMEM((1, math.prod(dims), own[0].shape[1], 128), BF), pltpu.SemaphoreType.DMA((len(own),)),
        ],
        compiler_params=params(),
        cost_estimate=cost(1e9, rows * d * 6),
        name="first_norm",
    )(where, x, *own)


def qkv_kernel(dims, count, where_ref, n_ref, vec_ref, *refs):
    own, oth = refs[:count], refs[count : 2 * count]
    o_ref, w_scr, w_sem, bias_scr = refs[2 * count :]
    rows, d = n_ref.shape
    cols = w_scr.shape[-1]
    step = pl.program_id(0)

    @pl.when(step == 0)
    def _():
        load_columns(where_ref, own, oth, 0, cols, w_scr, w_sem)
        zero = jnp.zeros((1, 128), F32)
        pairs = d // 128
        for p in range(pairs):
            at = pair_block(p, pairs) * 384
            half, at = at // cols, at % cols
            bias_scr[half, :, at : at + 128] = vec_ref[2:3, p * 128 : (p + 1) * 128]
            bias_scr[half, :, at + 128 : at + 256] = zero
            bias_scr[half, :, at + 256 : at + 384] = vec_ref[2:3, d + p * 128 : d + (p + 1) * 128]
        wait_columns(own, w_scr, w_sem, 0)

    @pl.when(step == 1)
    def _():
        wait_columns(own, w_scr, w_sem, 1)

    w = whole_rows(dims, where_ref, w_scr, step)
    for r in range(0, rows, 256):
        o_ref[r : r + 256, :] = (dot(n_ref[r : r + 256, :], w) + bias_scr[step]).astype(BF)


def qkv_call(dims, where, normed, vec, own, oth):
    rows, d = normed.shape
    n = own[0].shape[1]
    cols = 3 * d // 2
    return pl.pallas_call(
        functools.partial(qkv_kernel, dims, len(own)),
        grid=(2,),
        in_specs=[SMEM, full_spec((rows, d)), full_spec(vec.shape)] + [ANY] * (2 * len(own)),
        out_specs=pl.BlockSpec((rows, cols), lambda j: (0, j)),
        out_shape=jax.ShapeDtypeStruct((rows, 2 * cols), BF),
        scratch_shapes=weight_scratch(dims, n, cols, len(own)) + [pltpu.VMEM((2, 1, cols), F32)],
        compiler_params=params(),
        cost_estimate=cost(4 * rows * d * cols, rows * d * 8 + d * cols * 4),
        name="qkv",
    )(where, normed, vec, *own, *oth)


def proj_kernel(dims, count, first, where_ref, x_ref, a0_ref, a1_ref, vec_ref, *refs):
    own, oth = refs[:count], refs[count : 2 * count]
    mid_ref, n_ref, w_scr, w_sem = refs[2 * count :]
    d = x_ref.shape[1]

    @pl.when(pl.program_id(0) == 0)
    def _():
        load_columns(where_ref, own, oth, first, w_scr.shape[-1], w_scr, w_sem)
        for h in range(2):
            wait_columns(own, w_scr, w_sem, h)

    a = jnp.concatenate([a0_ref[...], a1_ref[...]], axis=1)
    branch = jnp.concatenate([dot(a, whole_rows(dims, where_ref, w_scr, h)) for h in range(2)], axis=1) + vec_ref[3:4, :d]
    middle = x_ref[...].astype(F32) + BS * branch
    mid_ref[...] = middle
    xhat, _ = normalize(middle)
    n_ref[...] = (xhat * vec_ref[4:5, :d] + vec_ref[5:6, :d]).astype(BF)


def proj_call(dims, where, x, att, vec, own, oth):
    rows, d = x.shape
    br = 256
    row = pl.BlockSpec((br, d), lambda i: (i, 0))
    return pl.pallas_call(
        functools.partial(proj_kernel, dims, len(own), 3 * d // 2),
        grid=(rows // br,),
        in_specs=[SMEM, row] + [pl.BlockSpec((br, v.shape[1]), lambda i: (i, 0)) for v in att]
        + [full_spec(vec.shape)] + [ANY] * (2 * len(own)),
        out_specs=[row, row],
        out_shape=[jax.ShapeDtypeStruct((rows, d), F32), jax.ShapeDtypeStruct((rows, d), BF)],
        scratch_shapes=weight_scratch(dims, own[0].shape[1], d // 2, len(own)),
        compiler_params=params(),
        cost_estimate=cost(2 * rows * d * d, rows * d * 10 + d * d * 2),
        name="proj",
    )(where, x, *att, vec, *own, *oth)


def mlp_kernel(dims, count, where_ref, n_ref, c_ref, mid_ref, vec_ref, *refs):
    own, oth = refs[:count], refs[count : 2 * count]
    (
        out_ref, gn_ref, gfb_ref, gob_ref, g_own, g_oth,
        mid_scr, mid_sem, nt_scr, mg_scr, acc_scr, act_scr, gp_scr, w_scr, w_sem, gf_scr, gf_sem, go_scr, go_sem,
    ) = refs[2 * count :]
    z_n, y_n, x_n = dims
    zi, yi, xi, ci = [where_ref[i] for i in range(4)]
    j = pl.program_id(0)
    rows, d = n_ref.shape
    n, total_cols = w_scr.shape[-2:]
    wide = total_cols - 2 * d
    blocks = 2 * wide // d
    parts = d // n
    br = 512

    def hidden_rows(q):
        at = j * parts + q
        dev, t = at // 2, lax.rem(at, 2)
        x, y, z = lax.rem(dev // 2, x_n), lax.rem(dev // (2 * x_n), y_n), dev // (2 * x_n * y_n)
        piece = lax.rem(y - yi + y_n, y_n) * x_n + lax.rem(x - xi + x_n, x_n)
        return lax.rem(dev, 2), piece * z_n + lax.rem(z - zi + z_n, z_n), pl.multiple_of(t * d, 128)

    @pl.when(j == 0)
    def _():
        load_columns(where_ref, own, oth, 0, total_cols, w_scr, w_sem)
        local_copy(mid_ref, mid_scr, mid_sem).start()
        nt_scr[...] = n_ref[...].T
        total = jnp.zeros_like(gob_ref)
        for r in range(0, rows, br):
            mg = (BS * c_ref[r : r + br, :].astype(F32)).astype(BF)
            mg_scr[r : r + br, :] = mg
            total += jnp.sum(mg.astype(F32), axis=0, keepdims=True)
        gob_ref[...] = total
        for h in range(2):
            wait_columns(own, w_scr, w_sem, h)

    half = j // (blocks // 2)
    first = pl.multiple_of(lax.rem(j, blocks // 2) * d, 128)
    wf = whole_rows(dims, where_ref, w_scr, half, pl.ds(first, d))
    spots = [hidden_rows(q) for q in range(parts)]
    wo = jnp.concatenate([w_scr[c, p, :, pl.ds(wide + at, d)] for c, p, at in spots], axis=0)
    fb = vec_ref[6:7, pl.ds(pl.multiple_of(j * d, 128), d)]
    bias_sum = jnp.zeros((1, d), F32)
    starts = list(range(0, rows, br))

    def ahead_of(r):
        return dot(n_ref[r : r + br, :], wf), dot_t(mg_scr[r : r + br, :], wo)

    def behind(r, act, gp):
        rr = slice(r, r + br)
        fwd = dot(act, wo)
        back = dot_t(gp, wf)
        acc_scr[rr, :] = jnp.where(j == 0, fwd, acc_scr[rr, :] + fwd)
        gn_ref[rr, :] = jnp.where(j == 0, back, gn_ref[rr, :] + back)

    queue = [ahead_of(starts[0])]
    waiting = None
    for i, r in enumerate(starts):
        rr = slice(r, r + br)
        if i + 1 < len(starts):
            queue.append(ahead_of(starts[i + 1]))
        (pre, ga), queue[i] = queue[i], None
        pre = pre + fb
        sq = pre * pre
        t = jnp.tanh(GC0 * pre * (1.0 + GC1 * sq))
        half_t = 0.5 * (1.0 + t)
        act = (pre * half_t).astype(BF)
        slope = half_t + (0.5 * GC0) * pre * (1.0 - t * t) * (1.0 + (3.0 * GC1) * sq)
        gp = (slope * ga).astype(BF)
        act_scr[rr, :] = act
        gp_scr[rr, :] = gp
        bias_sum += jnp.sum(gp.astype(F32), axis=0, keepdims=True)
        if waiting is not None:
            behind(*waiting)
        waiting = r, act, gp
    behind(*waiting)

    gfb_ref[...] = bias_sum
    put_rows(dims, where_ref, gf_scr, (j,), dot(nt_scr[...], gp_scr[...]).astype(BF))
    store_columns(where_ref, gf_scr.at[j], g_own, g_oth, half, first, d, gf_sem.at[j])
    go = dot_0(act_scr[...], mg_scr[...]).astype(BF)
    for q, (c, p, at) in enumerate(spots):
        go_scr[c, p, :, pl.ds(at, d)] = go[q * n : (q + 1) * n]

    @pl.when(j == blocks - 1)
    def _():
        for c in range(2):
            store_columns(where_ref, go_scr.at[c], g_own, g_oth, c, wide, 2 * d, go_sem.at[c])
        local_copy(mid_ref, mid_scr, mid_sem).wait()
        for r in range(0, rows, br):
            rr = slice(r, r + br)
            out_ref[rr, :] = (mid_scr[rr, :] + BS * (acc_scr[rr, :] + vec_ref[7:8, :d])).astype(BF)
        for b in range(blocks):
            wait_store(gf_scr.at[b], gf_sem.at[b])
        for c in range(2):
            wait_store(go_scr.at[c], go_sem.at[c])


def mlp_call(dims, where, normed, cot, middle, vec, own, oth):
    rows, d = normed.shape
    n, cols = own[0].shape[1:]
    wide = cols - 2 * d
    blocks = 2 * wide // d
    act = full_spec((rows, d))
    chips = math.prod(dims)
    piece = jax.ShapeDtypeStruct((chips, n, cols), BF)
    return pl.pallas_call(
        functools.partial(mlp_kernel, dims, len(own)),
        grid=(blocks,),
        in_specs=[SMEM, act, act, ANY, full_spec(vec.shape)] + [ANY] * (2 * len(own)),
        out_specs=[act, act, pl.BlockSpec((1, d), lambda j: (0, j)), full_spec((1, d))] + [ANY] * 2,
        out_shape=[
            jax.ShapeDtypeStruct((rows, d), BF),
            jax.ShapeDtypeStruct((rows, d), F32),
            jax.ShapeDtypeStruct((1, blocks * d), F32),
            jax.ShapeDtypeStruct((1, d), F32),
            piece, piece,
        ],
        scratch_shapes=[
            pltpu.VMEM((rows, d), F32), pltpu.SemaphoreType.DMA(()), pltpu.VMEM((d, rows), BF), pltpu.VMEM((rows, d), BF), pltpu.VMEM((rows, d), F32),
            pltpu.VMEM((rows, d), BF), pltpu.VMEM((rows, d), BF),
        ]
        + weight_scratch(dims, n, cols, len(own))
        + [
            pltpu.VMEM((blocks, chips, n, d), BF), pltpu.SemaphoreType.DMA((blocks,)),
            pltpu.VMEM((2, chips, n, 2 * d), BF), pltpu.SemaphoreType.DMA((2,)),
        ],
        compiler_params=params(),
        cost_estimate=cost(24 * rows * d * wide, 30e6, 2 * rows * wide),
        name="mlp",
    )(where, normed, cot, middle, vec, *own, *oth)


def proj_back_kernel(dims, count, first, where_ref, gn_ref, mid_ref, c_ref, a0_ref, a1_ref, vec_ref, ind_ref, *refs):
    own, oth = refs[:count], refs[count : 2 * count]
    (
        gm_ref, ga_ref, gw_ref, del_ref, gg_ref, gb_ref, gpb_ref, gw_acc, w_scr, w_sem,
    ) = refs[2 * count :]
    i = pl.program_id(0)
    d = mid_ref.shape[1]
    m = d // 2

    @pl.when(i == 0)
    def _():
        load_columns(where_ref, own, oth, first, m, w_scr, w_sem)
        gw_acc[...] = jnp.zeros_like(gw_acc)
        gg_ref[...] = jnp.zeros_like(gg_ref)
        gb_ref[...] = jnp.zeros_like(gb_ref)
        gpb_ref[...] = jnp.zeros_like(gpb_ref)
        for h in range(2):
            wait_columns(own, w_scr, w_sem, h)

    dy = gn_ref[...]
    xhat, rstd = normalize(mid_ref[...])
    gg_ref[...] += jnp.sum(dy * xhat, axis=0, keepdims=True)
    gb_ref[...] += jnp.sum(dy, axis=0, keepdims=True)
    gm = c_ref[...].astype(F32) + ln_back(dy, xhat, rstd, vec_ref[4:5, :d])
    gm_ref[...] = gm
    pg = (BS * gm).astype(BF)
    gpb_ref[...] += jnp.sum(pg.astype(F32), axis=0, keepdims=True)
    a = jnp.concatenate([a0_ref[...], a1_ref[...]], axis=1)
    gw_acc[...] += dot_0(a, pg)
    ga = sum(dot_t(pg[:, h * m : (h + 1) * m], whole_rows(dims, where_ref, w_scr, h)) for h in range(2)).astype(BF)
    ga_ref[...] = ga
    prod = ga.astype(F32) * a.astype(F32)
    high = prod.astype(BF)
    low = (prod - high.astype(F32)).astype(BF)
    del_ref[...] = dot_t(ind_ref[...], high) + dot_t(ind_ref[...], low)

    @pl.when(i == pl.num_programs(0) - 1)
    def _():
        gw_ref[...] = gw_acc[...].astype(BF)


def proj_back_call(dims, where, gn, middle, cot, att, vec, own, oth):
    rows, d = middle.shape
    br = 256
    row = pl.BlockSpec((br, d), lambda i: (i, 0))
    ind = jnp.asarray(np.arange(16)[:, None] == np.arange(d)[None, :] // HD, BF)
    one = full_spec((1, d))
    vshape = jax.ShapeDtypeStruct((1, d), F32)
    return pl.pallas_call(
        functools.partial(proj_back_kernel, dims, len(own), 3 * d // 2),
        grid=(rows // br,),
        in_specs=[SMEM, row, row, row] + [pl.BlockSpec((br, v.shape[1]), lambda i: (i, 0)) for v in att]
        + [full_spec(vec.shape), full_spec((16, d))] + [ANY] * (2 * len(own)),
        out_specs=[row, row, full_spec((d, d)), pl.BlockSpec((16, br), lambda i: (0, i)), one, one, one],
        out_shape=[
            jax.ShapeDtypeStruct((rows, d), F32),
            jax.ShapeDtypeStruct((rows, d), BF),
            jax.ShapeDtypeStruct((d, d), BF),
            jax.ShapeDtypeStruct((16, rows), F32),
            vshape, vshape, vshape,
        ],
        scratch_shapes=[pltpu.VMEM((d, d), F32)] + weight_scratch(dims, own[0].shape[1], d // 2, len(own)),
        compiler_params=params(),
        cost_estimate=cost(4 * rows * d * d, rows * d * 16),
        name="proj_back",
    )(where, gn, middle, cot, *att, vec, ind, *own, *oth)


def pair_back(j_ref, do_ref, lse_ref, del_ref, row, segr_ref, segc_ref, pair, dj_ref, dk_acc, dv_acc):
    rows = j_ref.shape[0]
    scale = HD**-0.5
    lanes = slice(pair * 128, (pair + 1) * 128)
    base = pair * 384
    k = j_ref[:, 128:256] * BF(scale)
    ks = split_heads(k)
    kt = k.T
    vs = split_heads(j_ref[:, 256:384])
    qt = j_ref[:, 0:128].T
    dot_do = do_ref[:, lanes].T
    items = [(tile, h) for tile in q_tiles(rows)[::-1] for h in range(2)]

    def ahead_of(item):
        (q0, kv0, kv1, _), h = item
        q = j_ref[q0 : q0 + 256, 0:128]
        do = do_ref[q0 : q0 + 256, lanes]
        return dot_t(ks[h][kv0:kv1], q), dot_t(vs[h][kv0:kv1], do)

    def behind(tile, h, probs, ds):
        q0, kv0, kv1, _ = tile
        hh = slice(h * HD, (h + 1) * HD)
        qq = slice(q0, q0 + 256)
        dv = dot_t(dot_do[hh, qq], probs)
        dk = dot_t(qt[hh, qq], ds)
        if q0 in (LONG, LONG - 256):
            dk_acc[hh, kv0:kv1] = dk
            dv_acc[hh, kv0:kv1] = dv
        else:
            dk_acc[hh, kv0:kv1] += dk
            dv_acc[hh, kv0:kv1] += dv
        return dot(kt[hh, kv0:kv1], ds)

    queue = [ahead_of(it) for it in items[:2]]
    waiting, dqs = None, []

    def settle():
        tile, h = waiting[:2]
        dqs.append(behind(*waiting))
        if h == 1:
            q0 = tile[0]
            dj_ref[q0 : q0 + 256, base : base + 128] = jnp.concatenate(dqs[-2:], axis=0).T.astype(BF)

    for n, (tile, h) in enumerate(items):
        q0, kv0, kv1, is_long = tile
        if n + 2 < len(items):
            queue.append(ahead_of(items[n + 2]))
        (s, dp), queue[n] = queue[n], None
        lse = lse_ref[pair, h : h + 1, q0 : q0 + 256]
        dlt = del_ref[pl.ds(row + h, 1), q0 : q0 + 256]
        parts = mask_diagonal(s, q0 - kv0, is_long, segr_ref, segc_ref)
        probs = jnp.concatenate([jnp.exp(p - lse) for p in parts], axis=0)
        ds = (probs * (dp - dlt)).astype(BF)
        if waiting is not None:
            settle()
        waiting = tile, h, probs.astype(BF), ds
    settle()
    dj_ref[:, base + 128 : base + 256] = (dk_acc[...] * scale).T.astype(BF)
    dj_ref[:, base + 256 : base + 384] = dv_acc[...].T.astype(BF)


def attn_back_kernel(
    dims, count, devices, where_ref, j0_ref, j1_ref, do_ref, lse_ref, del_ref, segr_ref, segc_ref,
    x_ref, vec_ref, gwp_ref, gfb_ref, gob_ref, gg2_ref, gb2_ref, gpb_ref, gm_ref, nt_ref, *refs,
):
    own, oth, refs = refs[:count], refs[count : 2 * count], refs[2 * count :]
    gx_ref, g_own, g_oth = refs[:3]
    (
        w_scr, w_sem, nt_scr, nt_sem, gn_scr, gm_scr, gm_sem, dj_scr, dk_acc, dv_acc, gw_scr, gw_sem,
        p_scr, p_sem, t_scr, t_sem, qv_scr,
    ) = refs[3:]
    i = pl.program_id(0)
    groups = gw_scr.shape[0]
    rows, d = x_ref.shape
    br = 256
    proj_at = groups * 384
    table_at = proj_at + d // 2

    @pl.when(i == 0)
    def _():
        load_columns(where_ref, own, oth, 0, groups * 384, w_scr, w_sem)
        local_copy(nt_ref, nt_scr, nt_sem).start()
        local_copy(gm_ref, gm_scr, gm_sem).start()
        for h in range(2):
            put_rows(dims, where_ref, p_scr, (h,), gwp_ref[:, h * (d // 2) : (h + 1) * (d // 2)])
            store_columns(where_ref, p_scr.at[h], g_own, g_oth, h, proj_at, d // 2, p_sem.at[h])

    for h, j_ref in enumerate((j0_ref, j1_ref)):
        row = (i * 2 + h) * 2
        pair_back(j_ref, do_ref, lse_ref, del_ref, row, segr_ref, segc_ref, h, dj_scr, dk_acc, dv_acc)

    @pl.when(i == 0)
    def _():
        local_copy(nt_ref, nt_scr, nt_sem).wait()
        for h in range(2):
            wait_columns(own, w_scr, w_sem, h)

    first = pl.multiple_of(i * 384, 128)
    dj = dj_scr[...]
    for h in range(2):
        for t, off in ((0, 0), (2, d)):
            part = dj[:, h * 384 + t * 128 : h * 384 + (t + 1) * 128].astype(F32)
            qv_scr[:, pl.ds(pl.multiple_of(off + (i * 2 + h) * 128, 128), 128)] = jnp.sum(part, axis=0, keepdims=True)
    gw = dot(nt_scr[...], dj).astype(BF)
    for h in range(2):
        put_rows(dims, where_ref, gw_scr, (i, h), gw[:, h * 384 : (h + 1) * 384])
        store_columns(where_ref, gw_scr.at[i, h], g_own, g_oth, h, first, 384, gw_sem.at[i, h])
    w = jnp.concatenate([whole_rows(dims, where_ref, w_scr, h, pl.ds(first, 384)) for h in range(2)], axis=1)
    for r in range(0, rows, br):
        back = dot_t(dj[r : r + br, :], w)
        gn_scr[r : r + br, :] = jnp.where(i == 0, back, gn_scr[r : r + br, :] + back)

    @pl.when(i == groups - 1)
    def _():
        local_copy(gm_ref, gm_scr, gm_sem).wait()
        gg = jnp.zeros((1, d), F32)
        gb = jnp.zeros((1, d), F32)
        for r in range(0, rows, br):
            rr = slice(r, r + br)
            xhat, rstd = normalize(x_ref[rr, :].astype(F32))
            dy = gn_scr[rr, :]
            gg += jnp.sum(dy * xhat, axis=0, keepdims=True)
            gb += jnp.sum(dy, axis=0, keepdims=True)
            gx_ref[rr, :] = (gm_scr[rr, :] + ln_back(dy, xhat, rstd, vec_ref[0:1, :d])).astype(BF)
        table = pack_vectors(
            {
                "g1": gg, "b1": gb, "qv": qv_scr[...], "fb": gfb_ref[...], "pb": gpb_ref[...],
                "g2": gg2_ref[...], "b2": gb2_ref[...], "ob": gob_ref[...],
            },
            d, devices,
        )
        put_rows(dims, where_ref, t_scr, (), table)
        for h in range(2):
            store_columns(where_ref, t_scr, g_own, g_oth, h, table_at, 128, t_sem.at[h])
        for h in range(2):
            for b in range(groups):
                wait_store(gw_scr.at[b, h], gw_sem.at[b, h])
            wait_store(p_scr.at[h], p_sem.at[h])
            wait_store(t_scr, t_sem.at[h])


def attn_back_call(dims, where, joined, ga, lse, delta, seg_row, seg_col, x, vec, own, oth, vectors, gm, nt, devices):
    rows, d = x.shape
    n = own[0].shape[1]
    groups = d // 256
    act = full_spec((rows, d))
    chips = math.prod(dims)
    piece = jax.ShapeDtypeStruct((chips, n, groups * 384 + d // 2 + 128), BF)
    return pl.pallas_call(
        functools.partial(attn_back_kernel, dims, len(own), devices),
        grid=(groups,),
        in_specs=[
            SMEM,
            pl.BlockSpec((rows, 384), lambda i: (0, i)),
            pl.BlockSpec((rows, 384), lambda i: (0, groups + i)),
            pl.BlockSpec((rows, 256), lambda i: (0, i)),
            pl.BlockSpec((2, 2, rows), lambda i: (i, 0, 0)),
            full_spec(delta.shape), full_spec((1, 256)), full_spec((256, 1)), act, full_spec(vec.shape),
        ]
        + [full_spec(v.shape) for v in vectors] + [ANY] * (2 + 2 * len(own)),
        out_specs=[act, ANY, ANY],
        out_shape=[jax.ShapeDtypeStruct((rows, d), BF), piece, piece],
        scratch_shapes=weight_scratch(dims, n, groups * 384, len(own))
        + [
            pltpu.VMEM((d, rows), BF), pltpu.SemaphoreType.DMA(()), pltpu.VMEM((rows, d), F32),
            pltpu.VMEM((rows, d), F32), pltpu.SemaphoreType.DMA(()), pltpu.VMEM((rows, 768), BF),
            pltpu.VMEM((128, rows), F32), pltpu.VMEM((128, rows), F32),
            pltpu.VMEM((groups, 2, chips, n, 384), BF), pltpu.SemaphoreType.DMA((groups, 2)),
            pltpu.VMEM((2, chips, n, d // 2), BF), pltpu.SemaphoreType.DMA((2,)),
            pltpu.VMEM((chips, n, 128), BF), pltpu.SemaphoreType.DMA((2,)),
            pltpu.VMEM((1, 2 * d), F32),
        ],
        compiler_params=params(),
        cost_estimate=cost(60e9, 20e6, 5.5e6),
        name="attn_back",
    )(where, joined, joined, ga, lse, delta, seg_row, seg_col, x, vec, *vectors, gm, nt, *own, *oth)


def pack_plan(counts, rows):
    c = [counts[i] for i in range(counts.shape[0])]
    ends, run = [], jnp.int32(0)
    for v in c:
        run = run + v
        ends.append(run)
    start = jnp.int32(0)
    for i in range(len(c) - 1):
        start = jnp.where(c[i] == LONG, ends[i] - c[i], start)
    rolled = jnp.arange(rows, dtype=jnp.int32)
    pos = rolled + start
    pos = jnp.where(pos >= rows, pos - rows, pos)
    seg = functools.reduce(jnp.add, [(pos >= e).astype(jnp.int32) for e in ends])
    valid = seg < len(c) - 1
    seg = jnp.where(valid, seg, 1000 + rolled)
    return start, seg[LONG:], valid


def roll_rows(array, shift):
    return lax.dynamic_slice_in_dim(jnp.concatenate([array, array], axis=0), shift, array.shape[0])


def half_columns(w, h, joined=False):
    r, cols = w.shape
    if not joined:
        return w[:, h * (cols // 2) : (h + 1) * (cols // 2)]
    pairs = cols // 384
    starts = [(t * pairs + p) * 128 for p in range(h, pairs, 2) for t in range(3)]
    return jnp.concatenate([w[:, s : s + 128] for s in starts], axis=1)


def join_columns(left, right):
    r, m = left.shape
    both = jnp.stack([v.reshape(r, m // 384, 3, 128) for v in (left, right)], axis=2)
    return both.transpose(0, 3, 1, 2, 4).reshape(r, 2 * m)


def add_all(values):
    return functools.reduce(jnp.add, [v.astype(F32) for v in values])


class Plain:
    def __init__(self, dp, fsdp):
        self.dims = (1, 1, 1)
        index = lax.axis_index("dp") * fsdp + lax.axis_index("fsdp")
        self.ci = index % 2

    def where(self):
        zero = jnp.zeros((), jnp.int32)
        return jnp.stack([zero, zero, zero, self.ci.astype(jnp.int32)])

    def pick(self, pair):
        return jnp.where(self.ci == 0, pair[0], pair[1]), jnp.where(self.ci == 0, pair[1], pair[0])

    def gather(self, w_qkv, w_proj, table, w_fc, w_out):
        whole = lambda v: lax.all_gather(v, AXES, axis=0, tiled=True)
        attn = whole(jnp.concatenate([w_qkv, w_proj, table], axis=1))
        cut = w_qkv.shape[1], w_qkv.shape[1] + w_proj.shape[1]
        fc, out = whole(w_fc), whole(w_out)
        d = out.shape[1]
        lists = [[], []]
        for h in range(2):
            qkv, proj, table = attn[:, : cut[0]], attn[:, cut[0] : cut[1]], attn[:, cut[1] :]
            lists[0].append(jnp.concatenate([half_columns(qkv, h, True), half_columns(proj, h), table], axis=1))
            lists[1].append(
                jnp.concatenate([half_columns(fc, h)] + [out[(2 * h + t) * d : (2 * h + t + 1) * d] for t in range(2)], axis=1)
            )
        listed = []
        for pair in lists:
            own, oth = self.pick(pair)
            listed.append(([own[None]], [oth[None]]))
        return listed

    def scatter(self, own, oth):
        pair = self.pick([own[0], oth[0]])
        m = pair[0].shape[1]
        mine = lax.psum_scatter(jnp.concatenate(pair, axis=1), AXES, scatter_dimension=0, tiled=True).astype(F32)
        return mine[:, :m], mine[:, m:]

    def scatter_hidden(self, own, oth):
        pair = self.pick([own[0], oth[0]])
        d = pair[0].shape[0]
        wide = pair[0].shape[1] - 2 * d
        fc = self.scatter(own[..., :wide], oth[..., :wide])
        out = jnp.concatenate([v[:, wide + t * d : wide + (t + 1) * d] for v in pair for t in range(2)], axis=0)
        return fc, lax.psum_scatter(out, AXES, scatter_dimension=0, tiled=True).astype(F32)


class Chips:
    def __init__(self, dp, fsdp):
        x_n, z_n = fsdp // 2, 4
        self.dims = (z_n, dp // z_n, x_n)
        index = lax.axis_index("dp") * fsdp + lax.axis_index("fsdp")
        self.ci = index % 2
        self.at = (index // (2 * x_n * self.dims[1]), (index // (2 * x_n)) % self.dims[1], (index // 2) % x_n, self.ci)

    def where(self):
        return jnp.stack(self.at).astype(jnp.int32)

    def pick(self, pair):
        return jnp.where(self.ci == 0, pair[0], pair[1]), jnp.where(self.ci == 0, pair[1], pair[0])

    def send(self, array, dz=0, dy=0, dx=0, dc=0):
        z_n, y_n, x_n = self.dims
        pairs = []
        for z in range(z_n):
            for y in range(y_n):
                for x in range(x_n):
                    for c in range(2):
                        here = ((z * y_n + y) * x_n + x) * 2 + c
                        there = (((z + dz) % z_n * y_n + (y + dy) % y_n) * x_n + (x + dx) % x_n) * 2 + (c + dc) % 2
                        pairs.append((here, there))
        return lax.ppermute(array, AXES, pairs)

    def trade(self, halves):
        return self.rows_of(*self.pick(halves))

    def rows_of(self, keep, give):
        return jnp.concatenate(self.pick([keep, self.send(give, dc=1)]), axis=0)

    def along_z(self, piece):
        return [piece] + [self.send(piece, dz=-k) for k in range(1, self.dims[0])]

    def swap(self, arrays):
        return [self.send(v, dc=1) for v in arrays]

    def add_core(self, own, theirs):
        return [add_all([own[i], theirs[i]]).astype(BF) for i in range(own.shape[0])]

    def rows_back(self, total):
        n = total.shape[0] // 2
        mine, give = self.pick([total[:n], total[n:]])
        return self.pick([mine, self.send(give, dc=1)])


def together(*trees):
    return lax.optimization_barrier(trees)


def prepare(tokens, lengths, cotangent):
    start, seg, valid = pack_plan(lengths[0], tokens.shape[0])
    x = roll_rows(tokens, start)
    cot = jnp.where(valid[:, None], roll_rows(cotangent, start), BF(0))
    return start, seg[None, :], seg[:, None], x, cot


def vector_table(r, ln1_gain, ln1_bias, qv_bias, proj_bias, ln2_gain, ln2_bias, fc_bias, out_bias):
    flat = [
        jnp.concatenate([ln1_gain, ln1_bias, qv_bias]), fc_bias,
        jnp.concatenate([proj_bias, ln2_gain, ln2_bias, out_bias]),
    ]
    return jnp.pad(jnp.stack(flat), ((0, r - 3), (0, 128 - 4 * r)))


def results(r, out, gx, s_fc, s_out, s_attn, table):
    d = out.shape[1]
    cut = 3 * d // 2
    s_qkv = join_columns(*[v[:, :cut] for v in s_attn])
    s_proj = jnp.concatenate([v[:, cut:] for v in s_attn], axis=1)
    row0, row1, row2 = [table[k, : 4 * r] for k in range(3)]
    return (
        out, gx,
        row0[:r], row0[r : 2 * r], s_qkv, row0[2 * r :], s_proj, row2[:r],
        row2[r : 2 * r], row2[2 * r : 3 * r], jnp.concatenate(s_fc, axis=1), row1, s_out, row2[3 * r :],
    )


def split_table(halves):
    return [v[:, :-128] for v in halves], halves[0][:, -128:]


def block_plain(
    links, tokens, lengths, ln1_gain, ln1_bias, w_qkv, qv_bias, w_proj, proj_bias, ln2_gain, ln2_bias,
    w_fc, fc_bias, w_out, out_bias, cotangent,
):
    rows, d = tokens.shape
    r = w_qkv.shape[0]
    devices = d // r
    dims, where = links.dims, links.where()
    table = vector_table(r, ln1_gain, ln1_bias, qv_bias, proj_bias, ln2_gain, ln2_bias, fc_bias, out_bias)
    attn_w, m_w = links.gather(w_qkv, w_proj, table, w_fc, w_out)
    start, seg_row, seg_col, x, cot = prepare(tokens, lengths, cotangent)
    normed, nt, vec = first_norm_call(dims, where, x, attn_w[0], devices)
    joined = qkv_call(dims, where, normed, vec, *attn_w)
    att0, lse0 = attn_call(joined, seg_row, seg_col, 0, 2)
    att1, lse1 = attn_call(joined, seg_row, seg_col, 2, d // 256 - 2)
    att = att0, att1
    middle, normed_two = proj_call(dims, where, x, att, vec, *attn_w)
    out, gn, gfb, gob, *m_g = mlp_call(dims, where, normed_two, cot, middle, vec, *m_w)
    s_fc, s_out = links.scatter_hidden(*m_g)
    gm, ga, gw_proj, delta, gg2, gb2, gpb = proj_back_call(dims, where, gn, middle, cot, att, vec, *attn_w)
    gx, *g = attn_back_call(
        dims, where, joined, ga, jnp.concatenate([lse0, lse1]), delta, seg_row, seg_col, x, vec, *attn_w,
        (gw_proj, gfb, gob, gg2, gb2, gpb), gm, nt, devices,
    )
    restore = rows - start
    return results(r, roll_rows(out, restore), roll_rows(gx, restore), s_fc, s_out, *split_table(links.scatter(*g)))


def block_chips(
    links, tokens, lengths, ln1_gain, ln1_bias, w_qkv, qv_bias, w_proj, proj_bias, ln2_gain, ln2_bias,
    w_fc, fc_bias, w_out, out_bias, cotangent,
):
    rows, d = tokens.shape
    r = w_qkv.shape[0]
    devices = d // r
    dims, where, send, swap = links.dims, links.where(), links.send, links.swap
    table = vector_table(r, ln1_gain, ln1_bias, qv_bias, proj_bias, ln2_gain, ln2_bias, fc_bias, out_bias)

    def xy(column):
        return send(column, dx=1), send(column, dy=1)

    def corner(x_part, y_part):
        return [send(x_part[:2], dy=1), send(y_part[2:], dx=1)]

    def near(b):
        return send(b[1], dx=1), send(b[2], dy=1), send(b[3], dx=1, dy=1)

    def far(parts):
        return [parts[0]] + [send(parts[j], dz=j) for j in range(1, dims[0])]

    a_keep, a_give, f_keep, f_give = cut_call(where, w_qkv, w_proj, table, w_fc)
    a = links.rows_of(a_keep, a_give)
    a, tokens, lengths, cotangent, f_keep, f_give = together(a, tokens, lengths, cotangent, f_keep, f_give)
    a0 = links.along_z(a)
    fc = links.rows_of(f_keep, f_give)
    a0, fc, w_out, tokens, lengths, cotangent = together(a0, fc, w_out, tokens, lengths, cotangent)
    prep = prepare(tokens, lengths, cotangent)
    a0 = jnp.stack(a0)
    a0, fc, w_out = together(a0, fc, w_out)
    m = jnp.concatenate([fc, w_out[: 2 * r], w_out[2 * r :]], axis=1)
    a_own = [a0, send(a0, dx=1), send(a0, dy=1), send(a0, dx=1, dy=1)]
    m0 = links.along_z(m)
    a_own, m0, prep = together(a_own, m0, prep)
    start, seg_row, seg_col, x, cot = prep
    m0 = jnp.stack(m0)
    m0, a_own = together(m0, a_own)
    a_own = [jnp.concatenate(a_own, axis=0)]
    attn_w = a_own, swap(a_own)
    mx, my = xy(m0)
    normed, nt, vec = first_norm_call(dims, where, x, a_own, devices)
    normed, attn_w = together(normed, attn_w)

    joined = qkv_call(dims, where, normed, vec, *attn_w)
    att0, lse0 = attn_call(joined, seg_row, seg_col, 0, 2)
    att0, joined, mx, my = together(att0, joined, mx, my)
    att1, lse1 = attn_call(joined, seg_row, seg_col, 2, d // 256 - 2)
    att = att0, att1
    middle, normed_two = proj_call(dims, where, x, att, vec, *attn_w)
    md = corner(mx, my)
    m_oth = swap([m0, mx, my])
    lse = jnp.concatenate([lse0, lse1])
    normed_two, md, m_oth, lse = together(normed_two, md, m_oth, lse)
    m_w = [m0, mx, my] + md, m_oth + swap(md)

    out, gn, gfb, gob, m_own, m_oth = mlp_call(dims, where, normed_two, cot, middle, vec, *m_w)
    gm, ga, gw_proj, delta, gg2, gb2, gpb = proj_back_call(dims, where, gn, middle, cot, att, vec, *attn_w)
    (m_oth,) = swap([m_oth])
    ga, delta, m_own, m_oth = together(ga, delta, m_own, m_oth)
    m_own, m_oth = [v.reshape(-1, dims[0], *v.shape[1:]) for v in (m_own, m_oth)]

    def chip_sum(i, part):
        return add_all([part(m_own[i]), part(m_oth[i])]).astype(BF)

    first = (
        chip_sum(3, lambda v: v[1:3]), chip_sum(3, lambda v: v[:1]), chip_sum(3, lambda v: v[3:]),
        chip_sum(1, lambda v: v[1:]), chip_sum(2, lambda v: v[:3]),
    )
    first, ga, delta, m_own, m_oth = together(first, ga, delta, m_own, m_oth)
    first = (
        send(first[0], dx=1, dy=1), send(first[1], dy=1), send(first[2], dx=1),
        send(first[3], dx=1), send(first[4], dy=1),
    )
    gx, g_own, g_oth = attn_back_call(
        dims, where, joined, ga, lse, delta, seg_row, seg_col, x, vec, *attn_w,
        (gw_proj, gfb, gob, gg2, gb2, gpb), gm, nt, devices,
    )
    gx, g_own, g_oth, first, m_own, m_oth, out = together(gx, g_own, g_oth, first, m_own, m_oth, out)

    (g_oth,) = swap([g_oth])
    corners, by_y, by_x, from_x, from_y = first

    def chip_total(i, j, arrived):
        return add_all([m_own[i, j], m_oth[i, j]] + arrived).astype(BF)

    x_one = send(chip_total(1, 0, [by_y[0]]), dx=1)
    y_one = send(chip_total(2, 3, [by_x[0]]), dy=1)
    b = {1: send(chip_total(0, 1, [from_x[0], from_y[1], corners[0]]), dz=1)}
    e = links.add_core(*[v.reshape(-1, dims[0], *v.shape[1:]) for v in (g_own, g_oth)])
    e, x_one, y_one, gx, out, m_own, m_oth, b = together(e, x_one, y_one, gx, out, m_own, m_oth, b)

    e_near = near(e)
    b[0] = chip_total(0, 0, [x_one, from_y[0]])
    b[2] = send(chip_total(0, 2, [from_x[1], from_y[2], corners[1]]), dz=2)
    b[3] = send(chip_total(0, 3, [from_x[2], y_one]), dz=3)
    b = [b[j] for j in range(4)]
    gx, out = roll_rows(gx, rows - start), roll_rows(out, rows - start)
    e_near, b, e, gx, out = together(e_near, b, e, gx, out)

    e = far([add_all([e[0][j]] + [v[j] for v in e_near]).astype(BF) for j in range(dims[0])])
    total = add_all(b)
    s_fc = links.rows_back(total[:, : -2 * d])
    s_out = jnp.concatenate([total[:, -2 * d : -d], total[:, -d:]], axis=0)
    e, s_fc, s_out = together(e, s_fc, s_out)
    total = add_all(e)
    vectors = jnp.where(links.ci == 0, total[:3, -128:], total[r : r + 3, -128:])
    return results(r, out, gx, s_fc, s_out, links.rows_back(total[:, :-128]), vectors)


def solution(mesh):
    dp, fsdp = mesh.shape["dp"], mesh.shape["fsdp"]

    def per_device(*args):
        if (dp, fsdp) == (8, 4) and args[4].shape[0] % 8 == 0:
            return block_chips(Chips(dp, fsdp), *args)
        return block_plain(Plain(dp, fsdp), *args)

    row, vec = P(AXES, None), P(AXES)
    in_specs = (row, row, vec, vec, row, vec, row, vec, vec, vec, row, vec, row, vec, row)
    out_specs = (row, row, vec, vec, row, vec, row, vec, vec, vec, row, vec, row, vec)
    return jax.shard_map(
        per_device, mesh=mesh, in_specs=in_specs, out_specs=out_specs, check_vma=False
    )
```

```python
import functools
import math

import jax
import jax.numpy as jnp
import numpy as np
from jax import lax
from jax.experimental import pallas as pl
from jax.experimental.pallas import tpu as pltpu
from jax.sharding import PartitionSpec as P

HD = 64
LONG = 768
EPS = 1e-05
BS = 1.0 / math.sqrt(48.0)
NEG = -1e30
F32 = jnp.float32
BF = jnp.bfloat16
VMEM_LIMIT = 58 * 1024 * 1024
AXES = ("dp", "fsdp")
GC0 = math.sqrt(2.0 / math.pi)
GC1 = 0.044715


def dot(a, b):
    return lax.dot_general(a, b, (((1,), (0,)), ((), ())), preferred_element_type=F32)


def dot_t(a, b):
    return lax.dot_general(a, b, (((1,), (1,)), ((), ())), preferred_element_type=F32)


def dot_0(a, b):
    return lax.dot_general(a, b, (((0,), (0,)), ((), ())), preferred_element_type=F32)


def params(grid_len=1):
    return pltpu.CompilerParams(
        dimension_semantics=("arbitrary",) * grid_len, vmem_limit_bytes=VMEM_LIMIT
    )


def cost(flops, nbytes, trans=0):
    return pl.CostEstimate(flops=int(flops), bytes_accessed=int(nbytes), transcendentals=int(trans))


def normalize(values):
    centred = values - jnp.mean(values, axis=-1, keepdims=True)
    rstd = lax.rsqrt(jnp.mean(centred * centred, axis=-1, keepdims=True) + EPS)
    return centred * rstd, rstd


def ln_back(dy, xhat, rstd, gain):
    dx = dy * gain
    m1 = jnp.mean(dx, axis=-1, keepdims=True)
    m2 = jnp.mean(dx * xhat, axis=-1, keepdims=True)
    return rstd * (dx - m1 - xhat * m2)


def full_spec(shape):
    return pl.BlockSpec(shape, lambda *_: (0,) * len(shape), pipeline_mode=pl.Buffered(1))


def lane_masks(rows):
    lane = lax.broadcasted_iota(jnp.int32, (rows, 128), 1)
    return lane < HD


def split_heads(block):
    low = lane_masks(block.shape[0])
    zero = jnp.zeros_like(block)
    return jnp.where(low, block, zero), jnp.where(low, zero, block)


def q_tiles(rows):
    tiles = [(r, 0, r + 256, True) for r in range(0, LONG, 256)]
    tiles += [(LONG, LONG, rows, False)]
    return tiles


def diag_allowed(is_long, seg_row, seg_col):
    kv = lax.broadcasted_iota(jnp.int32, (256, 256), 0)
    qp = lax.broadcasted_iota(jnp.int32, (256, 256), 1)
    allowed = kv <= qp
    if not is_long:
        allowed = allowed & (seg_col == seg_row)
    return allowed


def attn_kernel(q_ref, k_ref, v_ref, segr_ref, segc_ref, o_ref, lse_ref):
    rows = q_ref.shape[0]
    ks = split_heads(k_ref[...] * BF(HD**-0.5))
    vt = v_ref[...].T
    items = [(tile, h) for tile in q_tiles(rows) for h in range(2)]

    def score(item):
        (q0, kv0, kv1, _), h = item
        return dot_t(ks[h][kv0:kv1], q_ref[q0 : q0 + 256, :])

    queue = [score(it) for it in items[:3]]
    outs = []
    for n, ((q0, kv0, kv1, is_long), h) in enumerate(items):
        if n + 3 < len(items):
            queue.append(score(items[n + 3]))
        s, queue[n] = queue[n], None
        parts = mask_diagonal(s, q0 - kv0, is_long, segr_ref, segc_ref)
        top = functools.reduce(jnp.maximum, [jnp.max(p, axis=0, keepdims=True) for p in parts])
        exps = [jnp.exp(p - top) for p in parts]
        total = functools.reduce(jnp.add, [jnp.sum(e, axis=0, keepdims=True) for e in exps])
        lse_ref[0, h : h + 1, q0 : q0 + 256] = top + jnp.log(total)
        probs = jnp.concatenate([e.astype(BF) for e in exps], axis=0)
        outs.append(dot(vt[h * HD : (h + 1) * HD, kv0:kv1], probs) * (1.0 / total))
        if h == 1:
            o_ref[q0 : q0 + 256, :] = jnp.concatenate(outs, axis=0).T.astype(BF)
            outs = []


def mask_diagonal(s, at, is_long, segr_ref, segc_ref):
    allowed = diag_allowed(is_long, segr_ref[...], segc_ref[...])
    diag = jnp.where(allowed, s[at:], NEG)
    return [s[:at], diag] if at else [diag]


def attn_call(joined, seg_row, seg_col, group0, groups):
    rows = joined.shape[0]
    pairs = joined.shape[1] // 384
    at = lambda t: pl.BlockSpec((rows, 128), lambda p: (0, pair_block(group0 * 2 + p, pairs) * 3 + t))
    return pl.pallas_call(
        attn_kernel,
        grid=(2 * groups,),
        in_specs=[at(0), at(1), at(2), full_spec((1, 256)), full_spec((256, 1))],
        out_specs=[
            pl.BlockSpec((rows, 128), lambda p: (0, p)),
            pl.BlockSpec((1, 2, rows), lambda p: (p, 0, 0)),
        ],
        out_shape=[
            jax.ShapeDtypeStruct((rows, groups * 256), BF),
            jax.ShapeDtypeStruct((2 * groups, 2, rows), F32),
        ],
        compiler_params=params(),
        cost_estimate=cost(groups * 8e9, 8e6, 5.5e6),
        name="attn",
    )(joined, joined, joined, seg_row, seg_col)


def pair_block(p, pairs):
    return (p % 2) * (pairs // 2) + p // 2


ANY = pl.BlockSpec(memory_space=pl.ANY)
SMEM = pl.BlockSpec(memory_space=pltpu.SMEM)


def local_copy(src, dst, sem):
    return pltpu.make_async_copy(src, dst, sem)


def places(dims, where_ref):
    z_n, y_n, x_n = dims
    zi, yi, xi = [where_ref[i] for i in range(3)]
    return [
        (lax.rem(y - yi + y_n, y_n) * x_n + lax.rem(x - xi + x_n, x_n)) * z_n + lax.rem(z - zi + z_n, z_n)
        for z in range(z_n)
        for y in range(y_n)
        for x in range(x_n)
    ]


def leaving(dims, place):
    if dims != (4, 2, 2):
        return place
    for first, step in ((14, -6), (12, 0), (10, 4), (8, 2)):
        place = jnp.where((place >= first) & (place < first + 2), place + step + 100, place)
    return jnp.where(place >= 100, place - 100, place)


def array_spans(arrays):
    at = 0
    for k, a in enumerate(arrays):
        yield k, a, pl.ds(at, a.shape[0])
        at += a.shape[0]


def load_columns(where_ref, own, oth, first, cols, dst, sem):
    ci = where_ref[3]
    for half, arrays in ((ci, own), (1 - ci, oth)):
        for k, a, span in array_spans(arrays):
            local_copy(a.at[:, :, pl.ds(first, cols)], dst.at[half, span], sem.at[half, k]).start()


def wait_columns(own, dst, sem, half):
    for k, _, span in array_spans(own):
        block = dst.at[half, span]
        local_copy(block, block, sem.at[half, k]).wait()


def whole_rows(dims, where_ref, scr, half, cols=slice(None)):
    return jnp.concatenate([scr[half, p, :, cols] for p in places(dims, where_ref)], axis=0)


def put_rows(dims, where_ref, scr, lead, value, order=lambda p: p):
    n = scr.shape[-2]
    for i, p in enumerate(places(dims, where_ref)):
        scr[lead + (order(p),)] = value[i * n : (i + 1) * n]


def store_columns(where_ref, src, own, oth, half, first, cols, sem):
    ci = where_ref[3]
    for other, out in ((False, own), (True, oth)):

        @pl.when((half != ci) if other else (half == ci))
        def _():
            local_copy(src, out.at[:, :, pl.ds(first, cols)], sem).start()


def wait_store(src, sem):
    local_copy(src, src, sem).wait()


def weight_scratch(dims, n, cols, arrays):
    return [
        pltpu.VMEM((2, math.prod(dims), n, cols), BF),
        pltpu.SemaphoreType.DMA((2, arrays)),
    ]


def vector_plan(d, devices):
    r = d // devices
    return {
        "g1": (0, 0, r), "b1": (0, r, r), "qv": (0, 2 * r, 2 * r), "fb": (1, 0, 4 * r),
        "pb": (2, 0, r), "g2": (2, r, r), "b2": (2, 2 * r, r), "ob": (2, 3 * r, r),
    }


VECTOR_ROWS = {"g1": 0, "b1": 1, "qv": 2, "pb": 3, "g2": 4, "b2": 5, "fb": 6, "ob": 7}


def owner_of(shape, size, axis):
    c = lax.broadcasted_iota(jnp.int32, shape, axis).astype(F32)
    owner = jnp.floor((c + 0.5) * (1.0 / size))
    return owner, c - owner * size


def row_pick(devices, d, row):
    r = d // devices
    at = lax.broadcasted_iota(jnp.int32, (devices, d), 1)
    dev = lax.broadcasted_iota(jnp.int32, (devices, d), 0)
    return (at == dev * r + row).astype(BF)


def vector_maps(devices, n, first, size):
    owner, place = owner_of((devices, n), size, 1)
    mine = owner == lax.broadcasted_iota(jnp.int32, (devices, n), 0).astype(F32)
    _, place = owner_of((128, n), size, 1)
    spot = (place + first == lax.broadcasted_iota(jnp.int32, (128, n), 0).astype(F32)).astype(BF)
    return mine, spot


def unpack_vectors(table, d, devices, out_ref):
    plan = vector_plan(d, devices)
    picked = [dot(row_pick(devices, d, k), table).astype(BF) for k in range(3)]
    for name, i in VECTOR_ROWS.items():
        k, first, size = plan[name]
        n = size * devices
        mine, spot = vector_maps(devices, n, first, size)
        spread = dot(picked[k], spot)
        out_ref[i : i + 1, :n] = jnp.sum(jnp.where(mine, spread, 0.0), axis=0, keepdims=True)


def pack_vectors(rows, d, devices):
    plan = vector_plan(d, devices)
    parts = [None] * 3
    for name in VECTOR_ROWS:
        k, first, size = plan[name]
        n = size * devices
        mine, spot = vector_maps(devices, n, first, size)
        part = dot_t(jnp.where(mine, rows[name], 0.0).astype(BF), spot)
        parts[k] = part if parts[k] is None else parts[k] + part
    total = None
    for k in range(3):
        piece = dot_0(row_pick(devices, d, k), parts[k].astype(BF))
        total = piece if total is None else total + piece
    return total.astype(BF)


def cut_kernel(where_ref, w_ref, p_ref, t_ref, f_ref, a_keep, a_give, f_keep, f_give):
    ci = where_ref[3]
    pairs = w_ref.shape[1] // 384
    half = p_ref.shape[1] // 2
    wide = f_ref.shape[1] // 2
    for h in range(2):
        for other, out, f_out in ((False, a_keep, f_keep), (True, a_give, f_give)):

            @pl.when((ci != h) if other else (ci == h))
            def _():
                at = 0
                for p in range(h, pairs, 2):
                    for t in range(3):
                        first = (t * pairs + p) * 128
                        out[:, at : at + 128] = w_ref[:, first : first + 128]
                        at += 128
                out[:, at : at + half] = p_ref[:, h * half : (h + 1) * half]
                out[:, at + half :] = t_ref[...]
                f_out[...] = f_ref[:, h * wide : (h + 1) * wide]


def cut_call(where, w_qkv, w_proj, table, w_fc):
    r = w_qkv.shape[0]
    cols = (w_qkv.shape[1] + w_proj.shape[1]) // 2 + 128
    sizes = [cols, cols, w_fc.shape[1] // 2, w_fc.shape[1] // 2]
    args = (w_qkv, w_proj, table, w_fc)
    return pl.pallas_call(
        cut_kernel,
        grid=(1,),
        in_specs=[SMEM] + [full_spec(v.shape) for v in args],
        out_specs=[full_spec((r, s)) for s in sizes],
        out_shape=[jax.ShapeDtypeStruct((r, s), BF) for s in sizes],
        compiler_params=params(),
        cost_estimate=cost(0, 4 * r * sum(sizes)),
        name="cut",
    )(where, *args)


def first_norm_kernel(dims, count, devices, where_ref, x_ref, *refs):
    own = refs[:count]
    n_ref, nt_ref, vec_ref, t_scr, t_sem = refs[count:]
    rows, d = x_ref.shape
    table_at = own[0].shape[-1] - 128
    copies = [local_copy(a.at[:, :, pl.ds(table_at, 128)], t_scr.at[0, span], t_sem.at[i]) for i, a, span in array_spans(own)]
    for c in copies:
        c.start()
    for c in copies:
        c.wait()
    vec_ref[...] = jnp.zeros_like(vec_ref)
    unpack_vectors(whole_rows(dims, where_ref, t_scr, 0), d, devices, vec_ref)
    for r in range(0, rows, 256):
        xhat, _ = normalize(x_ref[r : r + 256, :].astype(F32))
        normed = (xhat * vec_ref[0:1, :d] + vec_ref[1:2, :d]).astype(BF)
        n_ref[r : r + 256, :] = normed
        nt_ref[:, r : r + 256] = normed.T


def first_norm_call(dims, where, x, own, devices):
    rows, d = x.shape
    return pl.pallas_call(
        functools.partial(first_norm_kernel, dims, len(own), devices),
        grid=(1,),
        in_specs=[SMEM, full_spec((rows, d))] + [ANY] * len(own),
        out_specs=[full_spec((rows, d)), full_spec((d, rows)), full_spec((8, 4 * d))],
        out_shape=[
            jax.ShapeDtypeStruct((rows, d), BF), jax.ShapeDtypeStruct((d, rows), BF),
            jax.ShapeDtypeStruct((8, 4 * d), F32),
        ],
        scratch_shapes=[
            pltpu.VMEM((1, math.prod(dims), own[0].shape[1], 128), BF), pltpu.SemaphoreType.DMA((len(own),)),
        ],
        compiler_params=params(),
        cost_estimate=cost(1e9, rows * d * 6),
        name="first_norm",
    )(where, x, *own)


def qkv_kernel(dims, count, where_ref, n_ref, vec_ref, *refs):
    own, oth = refs[:count], refs[count : 2 * count]
    o_ref, w_scr, w_sem, bias_scr = refs[2 * count :]
    rows, d = n_ref.shape
    cols = w_scr.shape[-1]
    step = pl.program_id(0)

    @pl.when(step == 0)
    def _():
        load_columns(where_ref, own, oth, 0, cols, w_scr, w_sem)
        zero = jnp.zeros((1, 128), F32)
        pairs = d // 128
        for p in range(pairs):
            at = pair_block(p, pairs) * 384
            half, at = at // cols, at % cols
            bias_scr[half, :, at : at + 128] = vec_ref[2:3, p * 128 : (p + 1) * 128]
            bias_scr[half, :, at + 128 : at + 256] = zero
            bias_scr[half, :, at + 256 : at + 384] = vec_ref[2:3, d + p * 128 : d + (p + 1) * 128]
        wait_columns(own, w_scr, w_sem, 0)

    @pl.when(step == 1)
    def _():
        wait_columns(own, w_scr, w_sem, 1)

    w = whole_rows(dims, where_ref, w_scr, step)
    for r in range(0, rows, 256):
        o_ref[r : r + 256, :] = (dot(n_ref[r : r + 256, :], w) + bias_scr[step]).astype(BF)


def qkv_call(dims, where, normed, vec, own, oth):
    rows, d = normed.shape
    n = own[0].shape[1]
    cols = 3 * d // 2
    return pl.pallas_call(
        functools.partial(qkv_kernel, dims, len(own)),
        grid=(2,),
        in_specs=[SMEM, full_spec((rows, d)), full_spec(vec.shape)] + [ANY] * (2 * len(own)),
        out_specs=pl.BlockSpec((rows, cols), lambda j: (0, j)),
        out_shape=jax.ShapeDtypeStruct((rows, 2 * cols), BF),
        scratch_shapes=weight_scratch(dims, n, cols, len(own)) + [pltpu.VMEM((2, 1, cols), F32)],
        compiler_params=params(),
        cost_estimate=cost(4 * rows * d * cols, rows * d * 8 + d * cols * 4),
        name="qkv",
    )(where, normed, vec, *own, *oth)


def proj_kernel(dims, count, first, where_ref, x_ref, a0_ref, a1_ref, vec_ref, *refs):
    own, oth = refs[:count], refs[count : 2 * count]
    mid_ref, n_ref, w_scr, w_sem = refs[2 * count :]
    d = x_ref.shape[1]

    @pl.when(pl.program_id(0) == 0)
    def _():
        load_columns(where_ref, own, oth, first, w_scr.shape[-1], w_scr, w_sem)
        for h in range(2):
            wait_columns(own, w_scr, w_sem, h)

    a = jnp.concatenate([a0_ref[...], a1_ref[...]], axis=1)
    branch = jnp.concatenate([dot(a, whole_rows(dims, where_ref, w_scr, h)) for h in range(2)], axis=1) + vec_ref[3:4, :d]
    middle = x_ref[...].astype(F32) + BS * branch
    mid_ref[...] = middle
    xhat, _ = normalize(middle)
    n_ref[...] = (xhat * vec_ref[4:5, :d] + vec_ref[5:6, :d]).astype(BF)


def proj_call(dims, where, x, att, vec, own, oth):
    rows, d = x.shape
    br = 256
    row = pl.BlockSpec((br, d), lambda i: (i, 0))
    return pl.pallas_call(
        functools.partial(proj_kernel, dims, len(own), 3 * d // 2),
        grid=(rows // br,),
        in_specs=[SMEM, row] + [pl.BlockSpec((br, v.shape[1]), lambda i: (i, 0)) for v in att]
        + [full_spec(vec.shape)] + [ANY] * (2 * len(own)),
        out_specs=[row, row],
        out_shape=[jax.ShapeDtypeStruct((rows, d), F32), jax.ShapeDtypeStruct((rows, d), BF)],
        scratch_shapes=weight_scratch(dims, own[0].shape[1], d // 2, len(own)),
        compiler_params=params(),
        cost_estimate=cost(2 * rows * d * d, rows * d * 10 + d * d * 2),
        name="proj",
    )(where, x, *att, vec, *own, *oth)


def mlp_kernel(dims, count, where_ref, n_ref, c_ref, mid_ref, vec_ref, *refs):
    own, oth = refs[:count], refs[count : 2 * count]
    (
        out_ref, gn_ref, gfb_ref, gob_ref, g_own, g_oth,
        mid_scr, mid_sem, nt_scr, mg_scr, acc_scr, act_scr, gp_scr, w_scr, w_sem, gf_scr, gf_sem, go_scr, go_sem,
    ) = refs[2 * count :]
    z_n, y_n, x_n = dims
    zi, yi, xi, ci = [where_ref[i] for i in range(4)]
    j = pl.program_id(0)
    rows, d = n_ref.shape
    n, total_cols = w_scr.shape[-2:]
    wide = total_cols - 2 * d
    blocks = 2 * wide // d
    parts = d // n
    br = 512

    def hidden_rows(q):
        at = j * parts + q
        dev, t = at // 2, lax.rem(at, 2)
        x, y, z = lax.rem(dev // 2, x_n), lax.rem(dev // (2 * x_n), y_n), dev // (2 * x_n * y_n)
        piece = lax.rem(y - yi + y_n, y_n) * x_n + lax.rem(x - xi + x_n, x_n)
        return lax.rem(dev, 2), piece * z_n + lax.rem(z - zi + z_n, z_n), pl.multiple_of(t * d, 128)

    @pl.when(j == 0)
    def _():
        load_columns(where_ref, own, oth, 0, total_cols, w_scr, w_sem)
        local_copy(mid_ref, mid_scr, mid_sem).start()
        nt_scr[...] = n_ref[...].T
        total = jnp.zeros_like(gob_ref)
        for r in range(0, rows, br):
            mg = (BS * c_ref[r : r + br, :].astype(F32)).astype(BF)
            mg_scr[r : r + br, :] = mg
            total += jnp.sum(mg.astype(F32), axis=0, keepdims=True)
        gob_ref[...] = total
        for h in range(2):
            wait_columns(own, w_scr, w_sem, h)

    half = j // (blocks // 2)
    first = pl.multiple_of(lax.rem(j, blocks // 2) * d, 128)
    wf = whole_rows(dims, where_ref, w_scr, half, pl.ds(first, d))
    spots = [hidden_rows(q) for q in range(parts)]
    wo = jnp.concatenate([w_scr[c, p, :, pl.ds(wide + at, d)] for c, p, at in spots], axis=0)
    fb = vec_ref[6:7, pl.ds(pl.multiple_of(j * d, 128), d)]
    bias_sum = jnp.zeros((1, d), F32)
    starts = list(range(0, rows, br))

    def ahead_of(r):
        return dot(n_ref[r : r + br, :], wf), dot_t(mg_scr[r : r + br, :], wo)

    def behind(r, act, gp):
        rr = slice(r, r + br)
        fwd = dot(act, wo)
        back = dot_t(gp, wf)
        acc_scr[rr, :] = jnp.where(j == 0, fwd, acc_scr[rr, :] + fwd)
        gn_ref[rr, :] = jnp.where(j == 0, back, gn_ref[rr, :] + back)

    queue = [ahead_of(starts[0])]
    waiting = None
    for i, r in enumerate(starts):
        rr = slice(r, r + br)
        if i + 1 < len(starts):
            queue.append(ahead_of(starts[i + 1]))
        (pre, ga), queue[i] = queue[i], None
        pre = pre + fb
        sq = pre * pre
        t = jnp.tanh(GC0 * pre * (1.0 + GC1 * sq))
        half_t = 0.5 * (1.0 + t)
        act = (pre * half_t).astype(BF)
        slope = half_t + (0.5 * GC0) * pre * (1.0 - t * t) * (1.0 + (3.0 * GC1) * sq)
        gp = (slope * ga).astype(BF)
        act_scr[rr, :] = act
        gp_scr[rr, :] = gp
        bias_sum += jnp.sum(gp.astype(F32), axis=0, keepdims=True)
        if waiting is not None:
            behind(*waiting)
        waiting = r, act, gp
    behind(*waiting)

    gfb_ref[...] = bias_sum
    order = functools.partial(leaving, dims)
    put_rows(dims, where_ref, gf_scr, (j,), dot(nt_scr[...], gp_scr[...]).astype(BF), order)
    store_columns(where_ref, gf_scr.at[j], g_own, g_oth, half, first, d, gf_sem.at[j])
    go = dot_0(act_scr[...], mg_scr[...]).astype(BF)
    for q, (c, p, at) in enumerate(spots):
        go_scr[c, order(p), :, pl.ds(at, d)] = go[q * n : (q + 1) * n]

    @pl.when(j == blocks - 1)
    def _():
        for c in range(2):
            store_columns(where_ref, go_scr.at[c], g_own, g_oth, c, wide, 2 * d, go_sem.at[c])
        local_copy(mid_ref, mid_scr, mid_sem).wait()
        for r in range(0, rows, br):
            rr = slice(r, r + br)
            out_ref[rr, :] = (mid_scr[rr, :] + BS * (acc_scr[rr, :] + vec_ref[7:8, :d])).astype(BF)
        for b in range(blocks):
            wait_store(gf_scr.at[b], gf_sem.at[b])
        for c in range(2):
            wait_store(go_scr.at[c], go_sem.at[c])


def mlp_call(dims, where, normed, cot, middle, vec, own, oth):
    rows, d = normed.shape
    n, cols = own[0].shape[1:]
    wide = cols - 2 * d
    blocks = 2 * wide // d
    act = full_spec((rows, d))
    chips = math.prod(dims)
    piece = jax.ShapeDtypeStruct((chips, n, cols), BF)
    return pl.pallas_call(
        functools.partial(mlp_kernel, dims, len(own)),
        grid=(blocks,),
        in_specs=[SMEM, act, act, ANY, full_spec(vec.shape)] + [ANY] * (2 * len(own)),
        out_specs=[act, act, pl.BlockSpec((1, d), lambda j: (0, j)), full_spec((1, d))] + [ANY] * 2,
        out_shape=[
            jax.ShapeDtypeStruct((rows, d), BF),
            jax.ShapeDtypeStruct((rows, d), F32),
            jax.ShapeDtypeStruct((1, blocks * d), F32),
            jax.ShapeDtypeStruct((1, d), F32),
            piece, piece,
        ],
        scratch_shapes=[
            pltpu.VMEM((rows, d), F32), pltpu.SemaphoreType.DMA(()), pltpu.VMEM((d, rows), BF), pltpu.VMEM((rows, d), BF), pltpu.VMEM((rows, d), F32),
            pltpu.VMEM((rows, d), BF), pltpu.VMEM((rows, d), BF),
        ]
        + weight_scratch(dims, n, cols, len(own))
        + [
            pltpu.VMEM((blocks, chips, n, d), BF), pltpu.SemaphoreType.DMA((blocks,)),
            pltpu.VMEM((2, chips, n, 2 * d), BF), pltpu.SemaphoreType.DMA((2,)),
        ],
        compiler_params=params(),
        cost_estimate=cost(24 * rows * d * wide, 30e6, 2 * rows * wide),
        name="mlp",
    )(where, normed, cot, middle, vec, *own, *oth)


def proj_back_kernel(dims, count, first, where_ref, gn_ref, mid_ref, c_ref, a0_ref, a1_ref, vec_ref, ind_ref, *refs):
    own, oth = refs[:count], refs[count : 2 * count]
    (
        gm_ref, ga_ref, gw_ref, del_ref, gg_ref, gb_ref, gpb_ref, gw_acc, w_scr, w_sem,
    ) = refs[2 * count :]
    i = pl.program_id(0)
    d = mid_ref.shape[1]
    m = d // 2

    @pl.when(i == 0)
    def _():
        load_columns(where_ref, own, oth, first, m, w_scr, w_sem)
        gw_acc[...] = jnp.zeros_like(gw_acc)
        gg_ref[...] = jnp.zeros_like(gg_ref)
        gb_ref[...] = jnp.zeros_like(gb_ref)
        gpb_ref[...] = jnp.zeros_like(gpb_ref)
        for h in range(2):
            wait_columns(own, w_scr, w_sem, h)

    dy = gn_ref[...]
    xhat, rstd = normalize(mid_ref[...])
    gg_ref[...] += jnp.sum(dy * xhat, axis=0, keepdims=True)
    gb_ref[...] += jnp.sum(dy, axis=0, keepdims=True)
    gm = c_ref[...].astype(F32) + ln_back(dy, xhat, rstd, vec_ref[4:5, :d])
    gm_ref[...] = gm
    pg = (BS * gm).astype(BF)
    gpb_ref[...] += jnp.sum(pg.astype(F32), axis=0, keepdims=True)
    a = jnp.concatenate([a0_ref[...], a1_ref[...]], axis=1)
    gw_acc[...] += dot_0(a, pg)
    ga = sum(dot_t(pg[:, h * m : (h + 1) * m], whole_rows(dims, where_ref, w_scr, h)) for h in range(2)).astype(BF)
    ga_ref[...] = ga
    prod = ga.astype(F32) * a.astype(F32)
    high = prod.astype(BF)
    low = (prod - high.astype(F32)).astype(BF)
    del_ref[...] = dot_t(ind_ref[...], high) + dot_t(ind_ref[...], low)

    @pl.when(i == pl.num_programs(0) - 1)
    def _():
        gw_ref[...] = gw_acc[...].astype(BF)


def proj_back_call(dims, where, gn, middle, cot, att, vec, own, oth):
    rows, d = middle.shape
    br = 256
    row = pl.BlockSpec((br, d), lambda i: (i, 0))
    ind = jnp.asarray(np.arange(16)[:, None] == np.arange(d)[None, :] // HD, BF)
    one = full_spec((1, d))
    vshape = jax.ShapeDtypeStruct((1, d), F32)
    return pl.pallas_call(
        functools.partial(proj_back_kernel, dims, len(own), 3 * d // 2),
        grid=(rows // br,),
        in_specs=[SMEM, row, row, row] + [pl.BlockSpec((br, v.shape[1]), lambda i: (i, 0)) for v in att]
        + [full_spec(vec.shape), full_spec((16, d))] + [ANY] * (2 * len(own)),
        out_specs=[row, row, full_spec((d, d)), pl.BlockSpec((16, br), lambda i: (0, i)), one, one, one],
        out_shape=[
            jax.ShapeDtypeStruct((rows, d), F32),
            jax.ShapeDtypeStruct((rows, d), BF),
            jax.ShapeDtypeStruct((d, d), BF),
            jax.ShapeDtypeStruct((16, rows), F32),
            vshape, vshape, vshape,
        ],
        scratch_shapes=[pltpu.VMEM((d, d), F32)] + weight_scratch(dims, own[0].shape[1], d // 2, len(own)),
        compiler_params=params(),
        cost_estimate=cost(4 * rows * d * d, rows * d * 16),
        name="proj_back",
    )(where, gn, middle, cot, *att, vec, ind, *own, *oth)


def pair_back(j_ref, do_ref, lse_ref, del_ref, row, segr_ref, segc_ref, pair, dj_ref, dk_acc, dv_acc):
    rows = j_ref.shape[0]
    scale = HD**-0.5
    lanes = slice(pair * 128, (pair + 1) * 128)
    base = pair * 384
    k = j_ref[:, 128:256] * BF(scale)
    ks = split_heads(k)
    kt = k.T
    vs = split_heads(j_ref[:, 256:384])
    qt = j_ref[:, 0:128].T
    dot_do = do_ref[:, lanes].T
    items = [(tile, h) for tile in q_tiles(rows)[::-1] for h in range(2)]

    def ahead_of(item):
        (q0, kv0, kv1, _), h = item
        q = j_ref[q0 : q0 + 256, 0:128]
        do = do_ref[q0 : q0 + 256, lanes]
        return dot_t(ks[h][kv0:kv1], q), dot_t(vs[h][kv0:kv1], do)

    def behind(tile, h, probs, ds):
        q0, kv0, kv1, _ = tile
        hh = slice(h * HD, (h + 1) * HD)
        qq = slice(q0, q0 + 256)
        dv = dot_t(dot_do[hh, qq], probs)
        dk = dot_t(qt[hh, qq], ds)
        if q0 in (LONG, LONG - 256):
            dk_acc[hh, kv0:kv1] = dk
            dv_acc[hh, kv0:kv1] = dv
        else:
            dk_acc[hh, kv0:kv1] += dk
            dv_acc[hh, kv0:kv1] += dv
        return dot(kt[hh, kv0:kv1], ds)

    queue = [ahead_of(it) for it in items[:2]]
    waiting, dqs = None, []

    def settle():
        tile, h = waiting[:2]
        dqs.append(behind(*waiting))
        if h == 1:
            q0 = tile[0]
            dj_ref[q0 : q0 + 256, base : base + 128] = jnp.concatenate(dqs[-2:], axis=0).T.astype(BF)

    for n, (tile, h) in enumerate(items):
        q0, kv0, kv1, is_long = tile
        if n + 2 < len(items):
            queue.append(ahead_of(items[n + 2]))
        (s, dp), queue[n] = queue[n], None
        lse = lse_ref[pair, h : h + 1, q0 : q0 + 256]
        dlt = del_ref[pl.ds(row + h, 1), q0 : q0 + 256]
        parts = mask_diagonal(s, q0 - kv0, is_long, segr_ref, segc_ref)
        probs = jnp.concatenate([jnp.exp(p - lse) for p in parts], axis=0)
        ds = (probs * (dp - dlt)).astype(BF)
        if waiting is not None:
            settle()
        waiting = tile, h, probs.astype(BF), ds
    settle()
    dj_ref[:, base + 128 : base + 256] = (dk_acc[...] * scale).T.astype(BF)
    dj_ref[:, base + 256 : base + 384] = dv_acc[...].T.astype(BF)


def attn_back_kernel(
    dims, count, devices, where_ref, j0_ref, j1_ref, do_ref, lse_ref, del_ref, segr_ref, segc_ref,
    x_ref, vec_ref, gwp_ref, gfb_ref, gob_ref, gg2_ref, gb2_ref, gpb_ref, gm_ref, nt_ref, *refs,
):
    own, oth, refs = refs[:count], refs[count : 2 * count], refs[2 * count :]
    gx_ref, g_own, g_oth = refs[:3]
    (
        w_scr, w_sem, nt_scr, nt_sem, gn_scr, gm_scr, gm_sem, dj_scr, dk_acc, dv_acc, gw_scr, gw_sem,
        p_scr, p_sem, t_scr, t_sem, qv_scr,
    ) = refs[3:]
    i = pl.program_id(0)
    groups = gw_scr.shape[0]
    rows, d = x_ref.shape
    br = 256
    proj_at = groups * 384
    table_at = proj_at + d // 2

    @pl.when(i == 0)
    def _():
        load_columns(where_ref, own, oth, 0, groups * 384, w_scr, w_sem)
        local_copy(nt_ref, nt_scr, nt_sem).start()
        local_copy(gm_ref, gm_scr, gm_sem).start()
        for h in range(2):
            put_rows(dims, where_ref, p_scr, (h,), gwp_ref[:, h * (d // 2) : (h + 1) * (d // 2)])
            store_columns(where_ref, p_scr.at[h], g_own, g_oth, h, proj_at, d // 2, p_sem.at[h])

    for h, j_ref in enumerate((j0_ref, j1_ref)):
        row = (i * 2 + h) * 2
        pair_back(j_ref, do_ref, lse_ref, del_ref, row, segr_ref, segc_ref, h, dj_scr, dk_acc, dv_acc)

    @pl.when(i == 0)
    def _():
        local_copy(nt_ref, nt_scr, nt_sem).wait()
        for h in range(2):
            wait_columns(own, w_scr, w_sem, h)

    first = pl.multiple_of(i * 384, 128)
    dj = dj_scr[...]
    for h in range(2):
        for t, off in ((0, 0), (2, d)):
            part = dj[:, h * 384 + t * 128 : h * 384 + (t + 1) * 128].astype(F32)
            qv_scr[:, pl.ds(pl.multiple_of(off + (i * 2 + h) * 128, 128), 128)] = jnp.sum(part, axis=0, keepdims=True)
    gw = dot(nt_scr[...], dj).astype(BF)
    for h in range(2):
        put_rows(dims, where_ref, gw_scr, (i, h), gw[:, h * 384 : (h + 1) * 384])
        store_columns(where_ref, gw_scr.at[i, h], g_own, g_oth, h, first, 384, gw_sem.at[i, h])
    w = jnp.concatenate([whole_rows(dims, where_ref, w_scr, h, pl.ds(first, 384)) for h in range(2)], axis=1)
    for r in range(0, rows, br):
        back = dot_t(dj[r : r + br, :], w)
        gn_scr[r : r + br, :] = jnp.where(i == 0, back, gn_scr[r : r + br, :] + back)

    @pl.when(i == groups - 1)
    def _():
        local_copy(gm_ref, gm_scr, gm_sem).wait()
        gg = jnp.zeros((1, d), F32)
        gb = jnp.zeros((1, d), F32)
        for r in range(0, rows, br):
            rr = slice(r, r + br)
            xhat, rstd = normalize(x_ref[rr, :].astype(F32))
            dy = gn_scr[rr, :]
            gg += jnp.sum(dy * xhat, axis=0, keepdims=True)
            gb += jnp.sum(dy, axis=0, keepdims=True)
            gx_ref[rr, :] = (gm_scr[rr, :] + ln_back(dy, xhat, rstd, vec_ref[0:1, :d])).astype(BF)
        table = pack_vectors(
            {
                "g1": gg, "b1": gb, "qv": qv_scr[...], "fb": gfb_ref[...], "pb": gpb_ref[...],
                "g2": gg2_ref[...], "b2": gb2_ref[...], "ob": gob_ref[...],
            },
            d, devices,
        )
        put_rows(dims, where_ref, t_scr, (), table)
        for h in range(2):
            store_columns(where_ref, t_scr, g_own, g_oth, h, table_at, 128, t_sem.at[h])
        for h in range(2):
            for b in range(groups):
                wait_store(gw_scr.at[b, h], gw_sem.at[b, h])
            wait_store(p_scr.at[h], p_sem.at[h])
            wait_store(t_scr, t_sem.at[h])


def attn_back_call(dims, where, joined, ga, lse, delta, seg_row, seg_col, x, vec, own, oth, vectors, gm, nt, devices):
    rows, d = x.shape
    n = own[0].shape[1]
    groups = d // 256
    act = full_spec((rows, d))
    chips = math.prod(dims)
    piece = jax.ShapeDtypeStruct((chips, n, groups * 384 + d // 2 + 128), BF)
    return pl.pallas_call(
        functools.partial(attn_back_kernel, dims, len(own), devices),
        grid=(groups,),
        in_specs=[
            SMEM,
            pl.BlockSpec((rows, 384), lambda i: (0, i)),
            pl.BlockSpec((rows, 384), lambda i: (0, groups + i)),
            pl.BlockSpec((rows, 256), lambda i: (0, i)),
            pl.BlockSpec((2, 2, rows), lambda i: (i, 0, 0)),
            full_spec(delta.shape), full_spec((1, 256)), full_spec((256, 1)), act, full_spec(vec.shape),
        ]
        + [full_spec(v.shape) for v in vectors] + [ANY] * (2 + 2 * len(own)),
        out_specs=[act, ANY, ANY],
        out_shape=[jax.ShapeDtypeStruct((rows, d), BF), piece, piece],
        scratch_shapes=weight_scratch(dims, n, groups * 384, len(own))
        + [
            pltpu.VMEM((d, rows), BF), pltpu.SemaphoreType.DMA(()), pltpu.VMEM((rows, d), F32),
            pltpu.VMEM((rows, d), F32), pltpu.SemaphoreType.DMA(()), pltpu.VMEM((rows, 768), BF),
            pltpu.VMEM((128, rows), F32), pltpu.VMEM((128, rows), F32),
            pltpu.VMEM((groups, 2, chips, n, 384), BF), pltpu.SemaphoreType.DMA((groups, 2)),
            pltpu.VMEM((2, chips, n, d // 2), BF), pltpu.SemaphoreType.DMA((2,)),
            pltpu.VMEM((chips, n, 128), BF), pltpu.SemaphoreType.DMA((2,)),
            pltpu.VMEM((1, 2 * d), F32),
        ],
        compiler_params=params(),
        cost_estimate=cost(60e9, 20e6, 5.5e6),
        name="attn_back",
    )(where, joined, joined, ga, lse, delta, seg_row, seg_col, x, vec, *vectors, gm, nt, *own, *oth)


def pack_plan(counts, rows):
    c = [counts[i] for i in range(counts.shape[0])]
    ends, run = [], jnp.int32(0)
    for v in c:
        run = run + v
        ends.append(run)
    start = jnp.int32(0)
    for i in range(len(c) - 1):
        start = jnp.where(c[i] == LONG, ends[i] - c[i], start)
    rolled = jnp.arange(rows, dtype=jnp.int32)
    pos = rolled + start
    pos = jnp.where(pos >= rows, pos - rows, pos)
    seg = functools.reduce(jnp.add, [(pos >= e).astype(jnp.int32) for e in ends])
    valid = seg < len(c) - 1
    seg = jnp.where(valid, seg, 1000 + rolled)
    return start, seg[LONG:], valid


def roll_rows(array, shift):
    return lax.dynamic_slice_in_dim(jnp.concatenate([array, array], axis=0), shift, array.shape[0])


def half_columns(w, h, joined=False):
    r, cols = w.shape
    if not joined:
        return w[:, h * (cols // 2) : (h + 1) * (cols // 2)]
    pairs = cols // 384
    starts = [(t * pairs + p) * 128 for p in range(h, pairs, 2) for t in range(3)]
    return jnp.concatenate([w[:, s : s + 128] for s in starts], axis=1)


def join_columns(left, right):
    r, m = left.shape
    both = jnp.stack([v.reshape(r, m // 384, 3, 128) for v in (left, right)], axis=2)
    return both.transpose(0, 3, 1, 2, 4).reshape(r, 2 * m)


def add_all(values):
    return functools.reduce(jnp.add, [v.astype(F32) for v in values])


class Plain:
    def __init__(self, dp, fsdp):
        self.dims = (1, 1, 1)
        index = lax.axis_index("dp") * fsdp + lax.axis_index("fsdp")
        self.ci = index % 2

    def where(self):
        zero = jnp.zeros((), jnp.int32)
        return jnp.stack([zero, zero, zero, self.ci.astype(jnp.int32)])

    def pick(self, pair):
        return jnp.where(self.ci == 0, pair[0], pair[1]), jnp.where(self.ci == 0, pair[1], pair[0])

    def gather(self, w_qkv, w_proj, table, w_fc, w_out):
        whole = lambda v: lax.all_gather(v, AXES, axis=0, tiled=True)
        attn = whole(jnp.concatenate([w_qkv, w_proj, table], axis=1))
        cut = w_qkv.shape[1], w_qkv.shape[1] + w_proj.shape[1]
        fc, out = whole(w_fc), whole(w_out)
        d = out.shape[1]
        lists = [[], []]
        for h in range(2):
            qkv, proj, table = attn[:, : cut[0]], attn[:, cut[0] : cut[1]], attn[:, cut[1] :]
            lists[0].append(jnp.concatenate([half_columns(qkv, h, True), half_columns(proj, h), table], axis=1))
            lists[1].append(
                jnp.concatenate([half_columns(fc, h)] + [out[(2 * h + t) * d : (2 * h + t + 1) * d] for t in range(2)], axis=1)
            )
        listed = []
        for pair in lists:
            own, oth = self.pick(pair)
            listed.append(([own[None]], [oth[None]]))
        return listed

    def scatter(self, own, oth):
        pair = self.pick([own[0], oth[0]])
        m = pair[0].shape[1]
        mine = lax.psum_scatter(jnp.concatenate(pair, axis=1), AXES, scatter_dimension=0, tiled=True).astype(F32)
        return mine[:, :m], mine[:, m:]

    def scatter_hidden(self, own, oth):
        pair = self.pick([own[0], oth[0]])
        d = pair[0].shape[0]
        wide = pair[0].shape[1] - 2 * d
        fc = self.scatter(own[..., :wide], oth[..., :wide])
        out = jnp.concatenate([v[:, wide + t * d : wide + (t + 1) * d] for v in pair for t in range(2)], axis=0)
        return fc, lax.psum_scatter(out, AXES, scatter_dimension=0, tiled=True).astype(F32)


class Chips:
    def __init__(self, dp, fsdp):
        x_n, z_n = fsdp // 2, 4
        self.dims = (z_n, dp // z_n, x_n)
        index = lax.axis_index("dp") * fsdp + lax.axis_index("fsdp")
        self.ci = index % 2
        self.at = (index // (2 * x_n * self.dims[1]), (index // (2 * x_n)) % self.dims[1], (index // 2) % x_n, self.ci)

    def where(self):
        return jnp.stack(self.at).astype(jnp.int32)

    def pick(self, pair):
        return jnp.where(self.ci == 0, pair[0], pair[1]), jnp.where(self.ci == 0, pair[1], pair[0])

    def send(self, array, dz=0, dy=0, dx=0, dc=0):
        z_n, y_n, x_n = self.dims
        pairs = []
        for z in range(z_n):
            for y in range(y_n):
                for x in range(x_n):
                    for c in range(2):
                        here = ((z * y_n + y) * x_n + x) * 2 + c
                        there = (((z + dz) % z_n * y_n + (y + dy) % y_n) * x_n + (x + dx) % x_n) * 2 + (c + dc) % 2
                        pairs.append((here, there))
        return lax.ppermute(array, AXES, pairs)

    def trade(self, halves):
        return self.rows_of(*self.pick(halves))

    def rows_of(self, keep, give):
        return jnp.concatenate(self.pick([keep, self.send(give, dc=1)]), axis=0)

    def along_z(self, piece):
        return [piece] + [self.send(piece, dz=-k) for k in range(1, self.dims[0])]

    def swap(self, arrays):
        return [self.send(v, dc=1) for v in arrays]

    def add_core(self, own, theirs):
        return [add_all([own[i], theirs[i]]).astype(BF) for i in range(own.shape[0])]

    def rows_back(self, total):
        n = total.shape[0] // 2
        mine, give = self.pick([total[:n], total[n:]])
        return self.pick([mine, self.send(give, dc=1)])


def together(*trees):
    return lax.optimization_barrier(trees)


def prepare(tokens, lengths, cotangent):
    start, seg, valid = pack_plan(lengths[0], tokens.shape[0])
    x = roll_rows(tokens, start)
    cot = jnp.where(valid[:, None], roll_rows(cotangent, start), BF(0))
    return start, seg[None, :], seg[:, None], x, cot


def vector_table(r, ln1_gain, ln1_bias, qv_bias, proj_bias, ln2_gain, ln2_bias, fc_bias, out_bias):
    flat = [
        jnp.concatenate([ln1_gain, ln1_bias, qv_bias]), fc_bias,
        jnp.concatenate([proj_bias, ln2_gain, ln2_bias, out_bias]),
    ]
    return jnp.pad(jnp.stack(flat), ((0, r - 3), (0, 128 - 4 * r)))


def results(r, out, gx, s_fc, s_out, s_attn, table):
    d = out.shape[1]
    cut = 3 * d // 2
    s_qkv = join_columns(*[v[:, :cut] for v in s_attn])
    s_proj = jnp.concatenate([v[:, cut:] for v in s_attn], axis=1)
    row0, row1, row2 = [table[k, : 4 * r] for k in range(3)]
    return (
        out, gx,
        row0[:r], row0[r : 2 * r], s_qkv, row0[2 * r :], s_proj, row2[:r],
        row2[r : 2 * r], row2[2 * r : 3 * r], jnp.concatenate(s_fc, axis=1), row1, s_out, row2[3 * r :],
    )


def split_table(halves):
    return [v[:, :-128] for v in halves], halves[0][:, -128:]


def block_plain(
    links, tokens, lengths, ln1_gain, ln1_bias, w_qkv, qv_bias, w_proj, proj_bias, ln2_gain, ln2_bias,
    w_fc, fc_bias, w_out, out_bias, cotangent,
):
    rows, d = tokens.shape
    r = w_qkv.shape[0]
    devices = d // r
    dims, where = links.dims, links.where()
    table = vector_table(r, ln1_gain, ln1_bias, qv_bias, proj_bias, ln2_gain, ln2_bias, fc_bias, out_bias)
    attn_w, m_w = links.gather(w_qkv, w_proj, table, w_fc, w_out)
    start, seg_row, seg_col, x, cot = prepare(tokens, lengths, cotangent)
    normed, nt, vec = first_norm_call(dims, where, x, attn_w[0], devices)
    joined = qkv_call(dims, where, normed, vec, *attn_w)
    att0, lse0 = attn_call(joined, seg_row, seg_col, 0, 2)
    att1, lse1 = attn_call(joined, seg_row, seg_col, 2, d // 256 - 2)
    att = att0, att1
    middle, normed_two = proj_call(dims, where, x, att, vec, *attn_w)
    out, gn, gfb, gob, *m_g = mlp_call(dims, where, normed_two, cot, middle, vec, *m_w)
    s_fc, s_out = links.scatter_hidden(*m_g)
    gm, ga, gw_proj, delta, gg2, gb2, gpb = proj_back_call(dims, where, gn, middle, cot, att, vec, *attn_w)
    gx, *g = attn_back_call(
        dims, where, joined, ga, jnp.concatenate([lse0, lse1]), delta, seg_row, seg_col, x, vec, *attn_w,
        (gw_proj, gfb, gob, gg2, gb2, gpb), gm, nt, devices,
    )
    restore = rows - start
    return results(r, roll_rows(out, restore), roll_rows(gx, restore), s_fc, s_out, *split_table(links.scatter(*g)))


def block_chips(
    links, tokens, lengths, ln1_gain, ln1_bias, w_qkv, qv_bias, w_proj, proj_bias, ln2_gain, ln2_bias,
    w_fc, fc_bias, w_out, out_bias, cotangent,
):
    rows, d = tokens.shape
    r = w_qkv.shape[0]
    devices = d // r
    dims, where, send, swap = links.dims, links.where(), links.send, links.swap
    table = vector_table(r, ln1_gain, ln1_bias, qv_bias, proj_bias, ln2_gain, ln2_bias, fc_bias, out_bias)

    def xy(column):
        return send(column, dx=1), send(column, dy=1)

    def corner(x_part, y_part):
        return [send(x_part[:2], dy=1), send(y_part[2:], dx=1)]

    def near(b):
        return send(b[1], dx=1), send(b[2], dy=1), send(b[3], dx=1, dy=1)

    def far(parts):
        return [parts[0]] + [send(parts[j], dz=j) for j in range(1, dims[0])]

    a_keep, a_give, f_keep, f_give = cut_call(where, w_qkv, w_proj, table, w_fc)
    a = links.rows_of(a_keep, a_give)
    a, tokens, lengths, cotangent, f_keep, f_give = together(a, tokens, lengths, cotangent, f_keep, f_give)
    a0 = links.along_z(a)
    fc = links.rows_of(f_keep, f_give)
    a0, fc, w_out, tokens, lengths, cotangent = together(a0, fc, w_out, tokens, lengths, cotangent)
    prep = prepare(tokens, lengths, cotangent)
    a0 = jnp.stack(a0)
    a0, fc, w_out = together(a0, fc, w_out)
    m = jnp.concatenate([fc, w_out[: 2 * r], w_out[2 * r :]], axis=1)
    a_own = [a0, send(a0, dx=1), send(a0, dy=1), send(a0, dx=1, dy=1)]
    m0 = links.along_z(m)
    a_own, m0, prep = together(a_own, m0, prep)
    start, seg_row, seg_col, x, cot = prep
    m0 = jnp.stack(m0)
    m0, a_own = together(m0, a_own)
    a_own = [jnp.concatenate(a_own, axis=0)]
    attn_w = a_own, swap(a_own)
    mx, my = xy(m0)
    normed, nt, vec = first_norm_call(dims, where, x, a_own, devices)
    normed, attn_w = together(normed, attn_w)

    joined = qkv_call(dims, where, normed, vec, *attn_w)
    att0, lse0 = attn_call(joined, seg_row, seg_col, 0, 2)
    att0, joined, mx, my = together(att0, joined, mx, my)
    att1, lse1 = attn_call(joined, seg_row, seg_col, 2, d // 256 - 2)
    att = att0, att1
    middle, normed_two = proj_call(dims, where, x, att, vec, *attn_w)
    md = corner(mx, my)
    m_oth = swap([m0, mx, my])
    lse = jnp.concatenate([lse0, lse1])
    normed_two, md, m_oth, lse = together(normed_two, md, m_oth, lse)
    m_w = [m0, mx, my] + md, m_oth + swap(md)

    out, gn, gfb, gob, m_own, m_oth = mlp_call(dims, where, normed_two, cot, middle, vec, *m_w)
    gm, ga, gw_proj, delta, gg2, gb2, gpb = proj_back_call(dims, where, gn, middle, cot, att, vec, *attn_w)
    (m_oth,) = swap([m_oth])
    ga, delta, m_own, m_oth = together(ga, delta, m_own, m_oth)

    def chip_sum(span, *more):
        return add_all([m_own[span], m_oth[span], *more]).astype(BF)

    first = chip_sum(slice(6, 10)), chip_sum(slice(10, 14))
    first, ga, delta, m_own, m_oth = together(first, ga, delta, m_own, m_oth)
    first = send(first[0], dx=1), send(first[1], dy=1)
    gx, g_own, g_oth = attn_back_call(
        dims, where, joined, ga, lse, delta, seg_row, seg_col, x, vec, *attn_w,
        (gw_proj, gfb, gob, gg2, gb2, gpb), gm, nt, devices,
    )
    gx, g_own, g_oth, first, m_own, m_oth, out = together(gx, g_own, g_oth, first, m_own, m_oth, out)

    (g_oth,) = swap([g_oth])
    from_x, from_y = first
    x_low = send(chip_sum(slice(4, 6), from_y[2:]), dx=1)
    y_high = send(chip_sum(slice(14, 16), from_x[2:]), dy=1)
    e = links.add_core(*[v.reshape(-1, dims[0], *v.shape[1:]) for v in (g_own, g_oth)])
    e, x_low, y_high, gx, out, m_own, m_oth = together(e, x_low, y_high, gx, out, m_own, m_oth)

    e_near = near(e)
    arrived = [(x_low, from_y), (from_x, y_high)]
    b = [chip_sum(j, *[v[j % 2] for v in arrived[j // 2]]) for j in range(dims[0])]
    b[1:3] = [send(b[j], dz=j) for j in (1, 2)]
    gx, out = roll_rows(gx, rows - start), roll_rows(out, rows - start)
    e_near, b, e, gx, out = together(e_near, b, e, gx, out)

    b[3] = send(b[3], dz=3)
    e = far([add_all([e[0][j]] + [v[j] for v in e_near]).astype(BF) for j in range(dims[0])])
    total = add_all(b)
    s_fc = links.rows_back(total[:, : -2 * d])
    s_out = jnp.concatenate([total[:, -2 * d : -d], total[:, -d:]], axis=0)
    e, s_fc, s_out = together(e, s_fc, s_out)
    total = add_all(e)
    vectors = jnp.where(links.ci == 0, total[:3, -128:], total[r : r + 3, -128:])
    return results(r, out, gx, s_fc, s_out, links.rows_back(total[:, :-128]), vectors)


def solution(mesh):
    dp, fsdp = mesh.shape["dp"], mesh.shape["fsdp"]

    def per_device(*args):
        if (dp, fsdp) == (8, 4) and args[4].shape[0] % 8 == 0:
            return block_chips(Chips(dp, fsdp), *args)
        return block_plain(Plain(dp, fsdp), *args)

    row, vec = P(AXES, None), P(AXES)
    in_specs = (row, row, vec, vec, row, vec, row, vec, vec, vec, row, vec, row, vec, row)
    out_specs = (row, row, vec, vec, row, vec, row, vec, vec, vec, row, vec, row, vec)
    return jax.shard_map(
        per_device, mesh=mesh, in_specs=in_specs, out_specs=out_specs, check_vma=False
    )
```
